32 devices in a mesh: gx: 4 (over z), gy: 2 (over y), gz: 4 (over x, core).
Axes of the slice: x: 2, y: 2, z: 4, core: 2. Of those that a mesh axis runs over, the one named last changes fastest.
Arguments:
- enthalpy: float32 [32, 64, 512], P('gx', 'gy', 'gz'), may hold values from -6 to 6
- conductivity: float32 [32, 64, 512], P('gx', 'gy', 'gz'), may hold values from 0.25 to 1
- phase: float32 [4, 2, 4, 16, 16, 256], P('gx', 'gy', 'gz'), may hold values from -1 to 1
- solute: float32 [4, 2, 4, 16, 16, 256], P('gx', 'gy', 'gz'), may hold values from -3 to 3
- tile_source: int32 [4, 2, 4, 16, 1], P('gx', 'gy', 'gz'), may hold values from 0 to 3; in each aligned block of 16 rows (0 to 15, 16 to 31, ..., all dimensions but the last counted through in order) at most 8 rows name the same one
- tile_block: int32 [4, 2, 4, 16], P('gx', 'gy', 'gz'), may hold values from 0 to 63
- tile_neighbour: int32 [4, 2, 4, 16, 6], P('gx', 'gy', 'gz'), may hold values from -1 to 63, as said below
Outputs:
- enthalpy_out: float32 [32, 64, 512], P('gx', 'gy', 'gz')
- phase_out: float32 [4, 2, 4, 16, 16, 256], P('gx', 'gy', 'gz')
- solute_out: float32 [4, 2, 4, 16, 16, 256], P('gx', 'gy', 'gz')
The draws below stay inside these ranges and needn't reach their ends.
Inputs may be any that keep to these rules, and one draw needn't show every extreme that they name: `tile_source`: on one device at most 8 slots name the same brick, and some device reaches 8 in every draw. `tile_neighbour`: entries are tile numbers 16 * owner + slot among the tiles with the same gy and gz indices, or -1. A tile is never its own neighbour. If face f of tile a names tile b, face f xor 1 of tile b names tile a. For each face, at most 6 tiles of one owner name tiles of one same other owner, and some owner reaches 6 in every draw.
All inputs are finite; a program needn't handle non-finite values.
Results may differ from the reference program's by a relative error of at most 0.000084.
Values sent between devices are 32-bit elements; how exact they have to be, the bound alone decides.
No kernel may reach another device: no remote copies, remote signals or barrier semaphores. Data moves between devices by JAX's collectives and lax.ppermute only.
A program may use at most 64 MiB of HBM per device.

```python
import math
import jax
import jax.numpy as jnp
import numpy as np

BX = 8
BY = 32
BZ = 128
CB = 8
TE = 16
SLOTS = 16
HEAT_STEPS = 2
PHASE_STEPS = 4
NX = 32
NY = 64
NZ = 512
BLK = 64
CAP = 8
N_GX = 4
N_GY = 2
N_GZ = 4


def face_pairs(key):
    first_key, second_key, third_key = jax.random.split(key, 3)
    total = N_GX * SLOTS
    slot_order = jax.random.permutation(first_key, SLOTS).astype(jnp.int32)
    offset_base = jax.random.randint(second_key, (), 0, N_GX - 1).astype(jnp.int32)
    slots = jnp.arange(SLOTS, dtype=jnp.int32)
    step_of_slot = 1 + (slots + offset_base) % (N_GX - 1)
    owners = jnp.arange(N_GX, dtype=jnp.int32)[:, None]
    destination_holder = (owners + step_of_slot[None, :]) % N_GX
    target = (destination_holder * SLOTS + slot_order[None, :]).reshape(total)
    retained = jax.random.randint(third_key, (N_GX, SLOTS), 0, 4) > 0
    retained = (retained | (owners == 0)).reshape(total)
    counting = jnp.arange(total, dtype=jnp.int32)
    upper = jnp.where(retained, target, -1)
    lower = jnp.full((total,), -1, jnp.int32).at[target].set(jnp.where(retained, counting, -1))
    return jnp.stack([lower, upper], axis=-1)


def draw_tile_neighbour(key, part):
    key = jax.random.fold_in(key, 11)
    line_count = N_GY * N_GZ
    keys = jax.random.split(key, line_count * 3)
    paired = jax.vmap(face_pairs)(keys)
    paired = paired.reshape(line_count, 3, N_GX * SLOTS, 2)
    paired = jnp.transpose(paired, (0, 2, 1, 3)).reshape(N_GY, N_GZ, N_GX, SLOTS, 6)
    return jnp.transpose(paired, (2, 0, 1, 3, 4)).astype(jnp.int32)


def plant(result, key, low, largest):
    place = [jax.random.randint(jax.random.fold_in(key, axis), (), 0, length) for axis, length in enumerate(result.shape)]
    longest = result.shape.index(max(result.shape))
    next_to = place[:longest] + [(place[longest] + 1) % result.shape[longest]] + place[longest + 1:]
    return result.at[tuple(place)].set(low).at[tuple(next_to)].set(largest)


def level_of(stream_key, extent, cuts, low, top_value):
    level = 1.0
    for axis_at, blocks in cuts:
        heights = jax.random.uniform(jax.random.fold_in(jax.random.fold_in(stream_key, 6), axis_at), (blocks,), jnp.float32, low / len(cuts), top_value / len(cuts))
        level = level * jnp.repeat(jnp.exp(heights), extent[axis_at] // blocks).reshape((-1,) + (1,) * (len(extent) - 1 - axis_at))
    return level


def shared_out(own_key, own, number, rows, amount, top, most, skew):
    order = jax.random.permutation(own_key, amount)
    packed, common = shares(amount, rows * top, most, skew, True), shares(amount, rows * top, most, skew, False)
    places = jnp.arange(amount)

    def named(sizes, offset_by):
        used = int((sizes > 0).sum())
        fixed = max(1, used // 4)
        passed = fixed + (places - fixed + offset_by * (used - fixed)) % max(1, amount - fixed)
        return jnp.zeros((amount,), jnp.int32).at[order[jnp.where(places < fixed, places, passed)]].set(jnp.asarray(sizes, jnp.int32))

    sizes = jnp.where(number % 4 == 0, named(packed, number // 4), named(common, number - number // 4 - 1))
    mixed = jax.random.permutation(jax.random.fold_in(own, 3), amount)
    giver, taker = mixed[0:amount // 2 * 2:2], mixed[1:amount // 2 * 2:2]
    margin = jnp.minimum(sizes[giver] - 1, most - sizes[taker]) // 2
    margin = jnp.where((giver == order[0]) | (taker == order[0]) | (sizes[taker] == 0), 0, jnp.maximum(margin, 0))
    passed = jax.random.randint(jax.random.fold_in(own, 4), (amount // 2,), 0, 1 << 20) % (margin + 1)
    sizes = sizes.at[giver].add(-passed).at[taker].add(passed)
    items = jnp.searchsorted(jnp.cumsum(sizes), jnp.arange(rows * top), side="right").astype(jnp.int32)
    grid = items.reshape(top, rows).T
    grid = grid[jax.random.permutation(jax.random.fold_in(own, 1), rows)]
    offset_by = jax.random.randint(jax.random.fold_in(own, 2), (rows, 1), 0, top)
    return jnp.take_along_axis(grid, (jnp.arange(top)[None, :] + offset_by) % top, axis=1)


def shares(amount, total, most, skew, full):
    weights = [(1 << 20) // math.isqrt(standing ** skew) + 1 for standing in range(1, amount + 1)]
    largest = most if full else min(most, max(-(-total // amount), total * weights[0] // sum(weights)))
    least = 1 if total - largest >= amount - 1 else 0
    counts, surplus = [largest] + [least] * (amount - 1), total - largest - least * (amount - 1)
    while surplus > 0:
        candidates = [i for i in range(1, amount) if counts[i] < largest] or [i for i in range(1, amount) if counts[i] < most]
        pool, budget = sum([weights[i] for i in candidates]), surplus
        for i in candidates:
            extra = min(most - counts[i], max(1, budget * weights[i] // pool), surplus)
            counts[i] = counts[i] + extra
            surplus = surplus - extra
    return np.array(counts)


def normal_values(rng, dims, scale, limit, pieces=(), held_as=jnp.bfloat16):
    drawn = scale * jax.random.normal(rng, dims, jnp.float32)
    if pieces:
        drawn = drawn * level_of(rng, dims, pieces, -0.22, 0.18)
    return jnp.clip(drawn, -limit, limit).astype(held_as)


def setup_inputs(seed: int = 0) -> dict:
    streams_of = jax.random.split(jax.random.key(seed), 8)
    enthalpy = normal_values(streams_of[0], (NX, NY, NZ), 1.5, 6.0, ((0, 4), (1, 2), (2, 4)), jnp.float32)
    conductivity = jnp.clip(jnp.exp(math.log(1.0) - 1.3862944 * jax.random.uniform(streams_of[1], (NX, NY, NZ), jnp.float32) ** level_of(streams_of[1], (NX, NY, NZ), ((0, 4), (1, 2), (2, 4)), -0.2, 0.2)), 0.25, 1.0)
    phase = jnp.clip(jax.random.uniform(streams_of[2], (N_GX, N_GY, N_GZ, SLOTS, TE, TE * TE), jnp.float32, -1.0, 1.0) * level_of(streams_of[2], (N_GX, N_GY, N_GZ, SLOTS, TE, TE * TE), ((0, 4), (1, 2), (2, 4)), -0.4, 0.0), -1.0, 1.0)
    solute = normal_values(streams_of[3], (N_GX, N_GY, N_GZ, SLOTS, TE, TE * TE), 0.5, 3.0, ((0, 4), (1, 2), (2, 4)), jnp.float32)
    tile_source_keys = jax.random.split(jax.random.fold_in(streams_of[4], 1), N_GX * N_GY * N_GZ * SLOTS // SLOTS)
    tile_source_turns = jax.random.permutation(jax.random.fold_in(streams_of[4], 3), N_GX * N_GY * N_GZ * SLOTS // SLOTS)
    tile_source = jax.vmap(lambda own, number: shared_out(jax.random.fold_in(streams_of[4], 2), own, number, SLOTS, N_GX, 1, CAP, 2))(tile_source_keys, tile_source_turns).reshape((N_GX, N_GY, N_GZ, SLOTS, 1))
    tile_block = plant(jax.random.randint(streams_of[5], (N_GX, N_GY, N_GZ, SLOTS), 0, BLK), jax.random.fold_in(streams_of[5], 1), 0, BLK - 1).astype(jnp.int32)
    tile_neighbour = draw_tile_neighbour(jax.random.fold_in(streams_of[7], 71), 0)
    return {"enthalpy": enthalpy, "conductivity": conductivity, "phase": phase, "solute": solute, "tile_source": tile_source, "tile_block": tile_block, "tile_neighbour": tile_neighbour}


RATE = 0.16
ORDER_SPEED = 0.1
SOLUTE_RATE = 0.15
COUPLING = 0.5
REJECTION = 0.5


def thermal_level_of_energy(thermal_energy_lattice):
    return jnp.minimum(thermal_energy_lattice, 0.0) + jnp.maximum(thermal_energy_lattice - 1.0, 0.0)


def conduct(thermal_energy_lattice, conductivity):
    energy_quantity = thermal_level_of_energy(thermal_energy_lattice)
    padded = jnp.pad(energy_quantity, 1)
    beside = padded[2:, 1:-1, 1:-1] + padded[:-2, 1:-1, 1:-1]
    beside = beside + padded[1:-1, 2:, 1:-1] + padded[1:-1, :-2, 1:-1]
    beside = beside + padded[1:-1, 1:-1, 2:] + padded[1:-1, 1:-1, :-2]
    return thermal_energy_lattice + RATE * conductivity * (beside - 6.0 * energy_quantity)


def refine(coarse):
    shape = coarse.shape
    spread = jnp.broadcast_to(coarse[..., :, None, :, None, :, None], shape[:-3] + (shape[-3], 2, shape[-2], 2, shape[-1], 2))
    return spread.reshape(shape[:-3] + (2 * shape[-3], 2 * shape[-2], 2 * shape[-1]))


def boundary(field):
    return jnp.stack([field[..., 0, :, :], field[..., -1, :, :], field[..., :, 0, :], field[..., :, -1, :], field[..., :, :, 0], field[..., :, :, -1]], axis=-3)


def laplace(field, ghosts):
    lower_x = jnp.concatenate([ghosts[..., 0, None, :, :], field[..., :-1, :, :]], axis=-3)
    upper_x = jnp.concatenate([field[..., 1:, :, :], ghosts[..., 1, None, :, :]], axis=-3)
    lower_y = jnp.concatenate([ghosts[..., 2, :, None, :], field[..., :, :-1, :]], axis=-2)
    upper_y = jnp.concatenate([field[..., :, 1:, :], ghosts[..., 3, :, None, :]], axis=-2)
    lower_z = jnp.concatenate([ghosts[..., 4, :, :, None], field[..., :, :, :-1]], axis=-1)
    upper_z = jnp.concatenate([field[..., :, :, 1:], ghosts[..., 5, :, :, None]], axis=-1)
    return lower_x + upper_x + lower_y + upper_y + lower_z + upper_z - 6.0 * field


def advance(phase_field, solute_field, fine_heat, phase_halo_cells, solute_ghost):
    phase_lap = laplace(phase_field, phase_halo_cells)
    solute_lap = laplace(solute_field, solute_ghost)
    squared = 1.0 - phase_field * phase_field
    new_phase = phase_field + ORDER_SPEED * (phase_lap + phase_field - phase_field * phase_field * phase_field - COUPLING * (fine_heat + solute_field) * squared * squared)
    new_solute = solute_field + SOLUTE_RATE * solute_lap + REJECTION * (new_phase - phase_field)
    return new_phase, new_solute


def destination_lines(field):
    moved = jnp.transpose(field, (1, 2, 0, 3, 4, 5, 6))
    return moved.reshape(N_GY * N_GZ, N_GX * SLOTS, TE, TE, TE)


def from_rows(field):
    shaped = field.reshape(N_GY, N_GZ, N_GX, SLOTS, TE, TE * TE)
    return jnp.transpose(shaped, (2, 0, 1, 3, 4, 5))


def fetch_ghosts(layers, neighbours):
    row_index = jnp.arange(N_GY * N_GZ, dtype=jnp.int32)[:, None, None]
    opposite = (jnp.arange(6, dtype=jnp.int32) ^ 1)[None, None, :]
    taken = layers[row_index, jnp.maximum(neighbours, 0), opposite]
    return jnp.where((neighbours >= 0)[..., None, None], taken, layers)


def reference(enthalpy, conductivity, phase, solute, tile_source, tile_block, tile_neighbour):
    existing_condition = enthalpy
    for iteration in range(HEAT_STEPS):
        existing_condition = conduct(existing_condition, conductivity)
    energy_quantity = thermal_level_of_energy(existing_condition)
    blocks = energy_quantity.reshape(N_GX, BX // CB, CB, N_GY, BY // CB, CB, N_GZ, BZ // CB, CB)
    blocks = jnp.transpose(blocks, (0, 3, 6, 1, 4, 7, 2, 5, 8)).reshape(N_GX, N_GY, N_GZ, BLK, CB, CB, CB)
    gy_index = jnp.arange(N_GY, dtype=jnp.int32)[None, :, None, None]
    gz_index = jnp.arange(N_GZ, dtype=jnp.int32)[None, None, :, None]
    coarse = blocks[tile_source[..., 0], gy_index, gz_index, tile_block]
    fine_heat = destination_lines(refine(coarse))
    phase_rows = destination_lines(phase.reshape(N_GX, N_GY, N_GZ, SLOTS, TE, TE, TE))
    solute_rows = destination_lines(solute.reshape(N_GX, N_GY, N_GZ, SLOTS, TE, TE, TE))
    neighbours = jnp.transpose(tile_neighbour, (1, 2, 0, 3, 4)).reshape(N_GY * N_GZ, N_GX * SLOTS, 6)
    for iteration in range(PHASE_STEPS):
        phase_halo_cells = fetch_ghosts(boundary(phase_rows), neighbours)
        solute_ghost = fetch_ghosts(boundary(solute_rows), neighbours)
        phase_rows, solute_rows = advance(phase_rows, solute_rows, fine_heat, phase_halo_cells, solute_ghost)
    return existing_condition, from_rows(phase_rows), from_rows(solute_rows)
```

```python
import functools

import jax
import jax.numpy as jnp
import numpy as np
from jax import lax
from jax.experimental import pallas as pl
from jax.experimental.pallas import tpu as pltpu
from jax.sharding import PartitionSpec as P

CB = 8
TE = 16
PLANE = TE * TE
SLOTS = 16
FACES = 6
PHASE_STEPS = 4
REC = 24

RATE = 0.16
ORDER_SPEED = 0.1
SOLUTE_RATE = 0.15
COUPLING = 0.5
REJECTION = 0.5

F32 = jnp.float32
BF16 = jnp.bfloat16
VMEM = pl.BlockSpec(memory_space=pltpu.VMEM)
SMEM = pl.BlockSpec(memory_space=pltpu.SMEM)
PARAMS = pltpu.CompilerParams(vmem_limit_bytes=16 * 1024 * 1024)


def plane_lane(face):
    j = np.arange(TE)
    return [j, PLANE - TE + j, j * TE, j * TE + TE - 1][face - 2]


def constant_tables():
    pick = np.zeros((2, PLANE, 256), np.float32)
    place = np.zeros((2, 128, PLANE), np.float32)
    for field in range(2):
        for face in range(2, 6):
            at = field * 64 + (face - 2) * TE + np.arange(TE)
            pick[field, plane_lane(face ^ 1), at] = 1.0
            pick[field, plane_lane(face), 128 + at] = 1.0
            place[field, at, plane_lane(face)] = 1.0
    y, z = np.divmod(np.arange(PLANE), TE)
    dy, dz = np.abs(y[:, None] - y[None, :]), np.abs(z[:, None] - z[None, :])
    stencil = ((dy + dz) == 1).astype(np.float32)
    lane = np.arange(128)
    spread = (lane[:, None] % CB == z[None, :] // 2).astype(np.float32)
    return pick, place, stencil, spread


def tables():
    pick, place, stencil, spread = constant_tables()
    picks = np.concatenate([pick[0], pick[0], pick[1], pick[1]], axis=0)
    laps = [np.concatenate([stencil, stencil, place[f], place[f]], axis=0) for f in range(2)]
    spreads = np.concatenate([spread, spread], axis=0)
    return (
        jnp.asarray(picks, BF16),
        jnp.asarray(laps[0], BF16),
        jnp.asarray(laps[1], BF16),
        jnp.asarray(spreads, BF16),
    )


def halves(value):
    high = value.astype(BF16)
    return high, (value - high.astype(F32)).astype(BF16)


def dot(a, b):
    return jnp.dot(a, b, preferred_element_type=F32)


def temperature(h):
    return jnp.minimum(h, 0.0) + jnp.maximum(h - 1.0, 0.0)


def iota(shape, dim):
    return lax.broadcasted_iota(jnp.int32, shape, dim)


def write_faces(t, xlo, xhi, ylo, yhi, zlo, zhi):
    bx, by, bz = t.shape
    xlo[...] = t[0]
    xhi[...] = t[bx - 1]
    for x in range(bx):
        ylo[x : x + 1, :] = t[x, 0:1, :]
        yhi[x : x + 1, :] = t[x, by - 1 : by, :]
    diagonal = iota((bx, by, bz), 1) == iota((bx, by, bz), 2)
    zlo[...] = jnp.sum(jnp.where(diagonal, t[:, :, 0:1], 0.0), axis=1)
    zhi[...] = jnp.sum(jnp.where(diagonal, t[:, :, bz - 1 : bz], 0.0), axis=1)


def conduct(h, k, xlo, xhi, ylo, yhi, zlo, zhi):
    bx, by, bz = h.shape
    t = temperature(h)
    row, lane = iota((bx, by, bz), 1), iota((bx, by, bz), 2)
    diagonal = row == lane
    total = jnp.concatenate([xlo[None], t[:-1]], axis=0) + jnp.concatenate([t[1:], xhi[None]], axis=0)
    total += jnp.where(row == 0, ylo[:, None, :], pltpu.roll(t, 1, 1))
    total += jnp.where(row == by - 1, yhi[:, None, :], pltpu.roll(t, by - 1, 1))
    zl = jnp.sum(jnp.where(diagonal, zlo[:, None, :], 0.0), axis=2, keepdims=True)
    zh = jnp.sum(jnp.where(diagonal, zhi[:, None, :], 0.0), axis=2, keepdims=True)
    total += jnp.where(lane == 0, zl, pltpu.roll(t, 1, 2))
    total += jnp.where(lane == bz - 1, zh, pltpu.roll(t, bz - 1, 2))
    return h + RATE * k * (total - 6.0 * t)


def faces_kernel(h, *faces):
    write_faces(temperature(h[...]), *faces)


def first_heat_kernel(h, k, xlo, xhi, ylo, yhi, zlo, zhi, out, *faces):
    halo = [r[...] for r in (xlo, xhi, ylo, yhi, zlo, zhi)]
    h1 = conduct(h[...], k[...], *halo)
    out[...] = h1
    write_faces(temperature(h1), *faces)


def block_layout(cap):
    parts = 128 // CB // cap
    return parts, CB // parts


def second_heat_kernel(cap, request, h, k, xlo, xhi, ylo, yhi, zlo, zhi, out, send, held):
    halo = [r[...] for r in (xlo, xhi, ylo, yhi, zlo, zhi)]
    h2 = conduct(h[...], k[...], *halo)
    out[...] = h2
    bx, by, bz = h2.shape
    held[...] = temperature(h2).reshape(bx, by // CB, CB, bz)
    parts, deep = block_layout(cap)
    nby, nbz = by // CB, bz // CB
    group = iota((deep, CB, bz), 2) // CB
    for owner in range(send.shape[0]):
        total = jnp.zeros((deep, CB, bz), F32)
        for rank in range(cap):
            block = request[owner * cap + rank]
            a, b, c = block // (nby * nbz), (block // nbz) % nby, block % nbz
            for part in range(parts):
                at = rank * parts + part
                patch = held[pl.ds(a * CB + part * deep, deep), b]
                moved = pltpu.roll(patch, (CB * at - CB * c + bz) % bz, 2)
                total = jnp.where(group == at, moved, total)
        send[owner] = total.reshape(deep * CB, bz)


def axis_shift(lo_face, hi_face, axis):
    count = lax.axis_size(axis)
    if count == 2:
        first = lax.axis_index(axis) == 0
        got = lax.ppermute(jnp.where(first, hi_face, lo_face), axis, [(0, 1), (1, 0)])
        zero = jnp.zeros_like(got)
        return jnp.where(first, zero, got), jnp.where(first, got, zero)
    forward = [(i, i + 1) for i in range(count - 1)]
    backward = [(b, a) for a, b in forward]
    return lax.ppermute(hi_face, axis, forward), lax.ppermute(lo_face, axis, backward)


def exchange(faces):
    xlo, xhi, ylo, yhi, zlo, zhi = faces
    return (
        *axis_shift(xlo, xhi, "gx"),
        *axis_shift(ylo, yhi, "gy"),
        *axis_shift(zlo, zhi, "gz"),
    )


def write_records(phase, solute, picks, own):
    flat = [f.reshape(SLOTS * TE, PLANE) for f in (phase, solute)]
    parts = jnp.concatenate([*halves(flat[0]), *halves(flat[1])], axis=1)
    planes = dot(parts, picks)
    own[0:SLOTS, 0:TE, :] = planes[:, 0:128].reshape(SLOTS, TE, 128)
    own[SLOTS : 2 * SLOTS, 0:TE, :] = planes[:, 128:256].reshape(SLOTS, TE, 128)
    for face in range(2):
        for number, field in enumerate((phase, solute)):
            for half in range(2):
                row = TE + face * 4 + number * 2 + half
                lanes = slice(half * 128, half * 128 + 128)
                near, far = (0, TE - 1) if face == 0 else (TE - 1, 0)
                own[0:SLOTS, row : row + 1, :] = field[:, far : far + 1, lanes]
                own[SLOTS : 2 * SLOTS, row : row + 1, :] = field[:, near : near + 1, lanes]


def merge_record(source, number):
    side = (iota((TE, 128), 1) % 64) // TE
    out = source[number(2), 0:TE, :]
    for face in range(3, 6):
        out = jnp.where(side == face - 2, source[number(face), 0:TE, :], out)
    edge = jnp.where(
        iota((8, 128), 0) < 4, source[number(0), TE:REC, :], source[number(1), TE:REC, :]
    )
    return out, edge


def pack(own, send_index, send):
    records = send_index.shape[0] // FACES
    for record in range(records):
        out, edge = merge_record(own, lambda face: send_index[record * FACES + face])
        send[record, 0:TE, :] = out
        send[record, TE:REC, :] = edge


def first_pack_kernel(send_index, phase, solute, picks, own, send):
    write_records(phase[...], solute[...], picks[...], own)
    pack(own, send_index, send)


def take_heat(cap, place, blocks, spreads, held, heat):
    parts, deep = block_layout(cap)
    group = iota((CB, 128), 1) // CB
    for slot in range(SLOTS):
        source, rank = place[slot], place[SLOTS + slot]
        for x in range(CB):
            row = (x % deep) * CB
            patch = blocks[source, row : row + CB, :]
            held[slot * CB + x] = jnp.where(group == rank * parts + x // deep, patch, 0.0)
    rows = held[...].reshape(SLOTS * CB * CB, 128)
    wide = dot(jnp.concatenate(halves(rows), axis=1), spreads)
    wide = wide.reshape(SLOTS * CB, CB, PLANE)
    keep = iota(wide.shape, 1) == iota(wide.shape, 2) // TE // 2
    coarse = jnp.sum(jnp.where(keep, wide, 0.0), axis=1)
    for half in range(2):
        for odd in range(2):
            heat[half, pl.ds(odd, SLOTS * CB, 2), :] = coarse[:, half * 128 : half * 128 + 128]


def step(receive_index, phase, solute, heat, got, own, laps, all_records, ghosts):
    records = got.shape[0]
    all_records[0:records] = got[...]
    all_records[records : records + 2 * SLOTS] = own[...]
    for slot in range(SLOTS):
        out, edge = merge_record(all_records, lambda face: receive_index[slot * FACES + face])
        ghosts[slot, 0:TE, :] = out
        ghosts[slot, TE:REC, :] = edge
    beside = jnp.concatenate(halves(ghosts[:, 0:TE, :].reshape(SLOTS * TE, 128)), axis=1)
    row = iota((SLOTS, TE, PLANE), 1)
    lap = []
    for number, (field, table) in enumerate(((phase, laps[0]), (solute, laps[1]))):
        flat = field.reshape(SLOTS * TE, PLANE)
        total = dot(jnp.concatenate([*halves(flat), beside], axis=1), table)
        total = total.reshape(SLOTS, TE, PLANE) - 6.0 * field
        sides = []
        for face in range(2):
            at = TE + face * 4 + number * 2
            sides.append(
                jnp.concatenate([ghosts[:, at : at + 1, :], ghosts[:, at + 1 : at + 2, :]], axis=2)
            )
        total += jnp.where(row == 0, sides[0], pltpu.roll(field, 1, 1))
        total += jnp.where(row == TE - 1, sides[1], pltpu.roll(field, TE - 1, 1))
        lap.append(total)
    warm = jnp.concatenate([heat[0], heat[1]], axis=1).reshape(SLOTS, TE, PLANE)
    squared = 1.0 - phase * phase
    new_phase = phase + ORDER_SPEED * (
        lap[0] + phase - phase * phase * phase - COUPLING * (warm + solute) * squared * squared
    )
    new_solute = solute + SOLUTE_RATE * lap[1] + REJECTION * (new_phase - phase)
    return new_phase, new_solute


def first_step_kernel(
    cap, receive_index, send_index, place, phase, solute, blocks, got, own, picks, lap0, lap1, spreads,
    phase_out, solute_out, heat_out, own_out, send, all_records, ghosts, held,
):
    take_heat(cap, place, blocks, spreads[...], held, heat_out)
    new_phase, new_solute = step(
        receive_index, phase[...], solute[...], heat_out[...], got, own, (lap0[...], lap1[...]),
        all_records, ghosts,
    )
    phase_out[...] = new_phase
    solute_out[...] = new_solute
    write_records(new_phase, new_solute, picks[...], own_out)
    pack(own_out, send_index, send)


def middle_step_kernel(
    receive_index, send_index, phase, solute, heat, got, own, picks, lap0, lap1,
    phase_out, solute_out, own_out, send, all_records, ghosts,
):
    new_phase, new_solute = step(
        receive_index, phase[...], solute[...], heat[...], got, own, (lap0[...], lap1[...]),
        all_records, ghosts,
    )
    phase_out[...] = new_phase
    solute_out[...] = new_solute
    write_records(new_phase, new_solute, picks[...], own_out)
    pack(own_out, send_index, send)


def last_step_kernel(
    receive_index, phase, solute, heat, got, own, lap0, lap1, phase_out, solute_out, all_records, ghosts
):
    new_phase, new_solute = step(
        receive_index, phase[...], solute[...], heat[...], got, own, (lap0[...], lap1[...]),
        all_records, ghosts,
    )
    phase_out[...] = new_phase
    solute_out[...] = new_solute


def call(kernel, in_specs, out_shapes, scratch=()):
    return pl.pallas_call(
        kernel,
        out_shape=out_shapes,
        in_specs=in_specs,
        out_specs=jax.tree.map(lambda _: VMEM, out_shapes),
        scratch_shapes=list(scratch),
        compiler_params=PARAMS,
    )


def shape(*dims):
    return jax.ShapeDtypeStruct(dims, F32)


def tile_indices(neighbour, cap, me):
    count = lax.axis_size("gx")
    owner = neighbour >> 4
    other = (neighbour >= 0) & (owner != me)
    slot = jnp.arange(SLOTS, dtype=jnp.int32)
    alike = (owner[None] == owner[:, None]) & other[None]
    receive_rank = jnp.sum((alike & (neighbour[None] < neighbour[:, None])).astype(jnp.int32), axis=1)
    send_rank = jnp.sum(
        (alike & (slot[None, :, None] < slot[:, None, None])).astype(jnp.int32), axis=1
    )
    records = count * cap
    receive = jnp.where(
        neighbour < 0,
        records + SLOTS + slot[:, None],
        jnp.where(owner == me, records + (neighbour & (SLOTS - 1)), owner * cap + receive_rank),
    )
    key = jnp.where(other, owner * cap + send_rank, -1)
    hit = key[None] == jnp.arange(records, dtype=jnp.int32)[:, None, None]
    sender = jnp.sum(jnp.where(hit, slot[None, :, None], 0), axis=1)
    sender = sender.reshape(records, 3, 2)[:, :, ::-1]
    return receive.reshape(-1), sender.reshape(-1)


def local(enthalpy, conductivity, phase, solute, tile_source, tile_block, tile_neighbour):
    count = lax.axis_size("gx")
    me = lax.axis_index("gx")
    plane_cap = -(-SLOTS // (count - 1))
    block_cap = 2 * SLOTS // count
    bx, by, bz = enthalpy.shape
    picks, lap0, lap1, spreads = tables()

    face_shapes = [shape(by, bz)] * 2 + [shape(bx, bz)] * 4
    faces = call(faces_kernel, [VMEM], face_shapes)(enthalpy)
    halo = exchange(faces)

    neighbour = tile_neighbour.reshape(SLOTS, FACES)
    receive_index, send_index = tile_indices(neighbour, plane_cap, me)
    phase_field = phase.reshape(SLOTS, TE, PLANE)
    solute_field = solute.reshape(SLOTS, TE, PLANE)
    records = count * plane_cap
    own_shape, send_shape = shape(2 * SLOTS, REC, 128), shape(records, REC, 128)
    own, send = call(first_pack_kernel, [SMEM, VMEM, VMEM, VMEM], [own_shape, send_shape])(
        send_index, phase_field, solute_field, picks
    )
    sources = tile_source.reshape(SLOTS)
    wanted = tile_block.reshape(SLOTS)
    slot = jnp.arange(SLOTS, dtype=jnp.int32)
    ranks = jnp.sum(
        ((sources[None] == sources[:, None]) & (slot[None] < slot[:, None])).astype(jnp.int32), axis=1
    )
    key = sources * block_cap + ranks
    all_keys = jnp.arange(count * block_cap, dtype=jnp.int32)
    request = jnp.sum(jnp.where(key[None] == all_keys[:, None], wanted[None], 0), axis=1)
    request = lax.all_to_all(
        request.reshape(count, block_cap), "gx", split_axis=0, concat_axis=0, tiled=True
    ).reshape(-1)
    got = lax.all_to_all(send, "gx", split_axis=0, concat_axis=0, tiled=True)

    brick = shape(bx, by, bz)
    h1, *faces = call(first_heat_kernel, [VMEM] * 8, [brick] + face_shapes)(
        enthalpy, conductivity, *halo
    )
    halo = exchange(faces)
    _, deep = block_layout(block_cap)
    block_rows = deep * CB
    h2, found = call(
        functools.partial(second_heat_kernel, block_cap),
        [SMEM] + [VMEM] * 8,
        [brick, shape(count, block_rows, bz)],
        [pltpu.VMEM((bx, by // CB, CB, bz), F32)],
    )(request, h1, conductivity, *halo)
    blocks = lax.all_to_all(found, "gx", split_axis=0, concat_axis=0, tiled=True)

    place = jnp.concatenate([sources, ranks])
    field = shape(SLOTS, TE, PLANE)
    step_scratch = [
        pltpu.VMEM((records + 2 * SLOTS, REC, 128), F32),
        pltpu.VMEM((SLOTS, REC, 128), F32),
    ]
    phase_field, solute_field, heat, own, send = call(
        functools.partial(first_step_kernel, block_cap),
        [SMEM] * 3 + [VMEM] * 9,
        [field, field, shape(2, SLOTS * TE, 128), own_shape, send_shape],
        step_scratch + [pltpu.VMEM((SLOTS * CB, CB, 128), F32)],
    )(
        receive_index, send_index, place, phase_field, solute_field, blocks, got, own, picks, lap0, lap1,
        spreads,
    )
    for _ in range(PHASE_STEPS - 2):
        got = lax.all_to_all(send, "gx", split_axis=0, concat_axis=0, tiled=True)
        phase_field, solute_field, own, send = call(
            middle_step_kernel, [SMEM] * 2 + [VMEM] * 8, [field, field, own_shape, send_shape], step_scratch
        )(receive_index, send_index, phase_field, solute_field, heat, got, own, picks, lap0, lap1)
    got = lax.all_to_all(send, "gx", split_axis=0, concat_axis=0, tiled=True)
    phase_field, solute_field = call(
        last_step_kernel, [SMEM] + [VMEM] * 7, [field, field], step_scratch
    )(receive_index, phase_field, solute_field, heat, got, own, lap0, lap1)
    return h2, phase_field.reshape(phase.shape), solute_field.reshape(solute.shape)


def solution(mesh):
    grid = P("gx", "gy", "gz")
    tiles = P("gx", "gy", "gz", None, None, None)
    return jax.shard_map(
        local,
        mesh=mesh,
        in_specs=(
            grid,
            grid,
            tiles,
            tiles,
            P("gx", "gy", "gz", None, None),
            P("gx", "gy", "gz", None),
            P("gx", "gy", "gz", None, None),
        ),
        out_specs=(grid, tiles, tiles),
        check_vma=False,
    )
```

```python
import functools

import jax
import jax.numpy as jnp
import numpy as np
from jax import lax
from jax.experimental import pallas as pl
from jax.experimental.pallas import tpu as pltpu
from jax.sharding import PartitionSpec as P

CB = 8
TE = 16
PLANE = TE * TE
SLOTS = 16
FACES = 6
PHASE_STEPS = 4
REC = 24

RATE = 0.16
ORDER_SPEED = 0.1
SOLUTE_RATE = 0.15
COUPLING = 0.5
REJECTION = 0.5

F32 = jnp.float32
BF16 = jnp.bfloat16
VMEM = pl.BlockSpec(memory_space=pltpu.VMEM)
SMEM = pl.BlockSpec(memory_space=pltpu.SMEM)
PARAMS = pltpu.CompilerParams(vmem_limit_bytes=16 * 1024 * 1024)


def plane_lane(face):
    j = np.arange(TE)
    return [j, PLANE - TE + j, j * TE, j * TE + TE - 1][face - 2]


def constant_tables():
    pick = np.zeros((2, PLANE, 256), np.float32)
    place = np.zeros((2, 128, PLANE), np.float32)
    for field in range(2):
        for face in range(2, 6):
            at = field * 64 + (face - 2) * TE + np.arange(TE)
            pick[field, plane_lane(face ^ 1), at] = 1.0
            pick[field, plane_lane(face), 128 + at] = 1.0
            place[field, at, plane_lane(face)] = 1.0
    y, z = np.divmod(np.arange(PLANE), TE)
    dy, dz = np.abs(y[:, None] - y[None, :]), np.abs(z[:, None] - z[None, :])
    stencil = ((dy + dz) == 1).astype(np.float32)
    lane = np.arange(128)
    spread = (lane[:, None] % CB == z[None, :] // 2).astype(np.float32)
    return pick, place, stencil, spread


def tables():
    pick, place, stencil, spread = constant_tables()
    picks = np.concatenate([pick[0], pick[0], pick[1], pick[1]], axis=0)
    laps = [np.concatenate([stencil, stencil, place[f], place[f]], axis=0) for f in range(2)]
    spreads = np.concatenate([spread, spread], axis=0)
    return (
        jnp.asarray(picks, BF16),
        jnp.asarray(laps[0], BF16),
        jnp.asarray(laps[1], BF16),
        jnp.asarray(spreads, BF16),
    )


def halves(value):
    high = value.astype(BF16)
    return high, (value - high.astype(F32)).astype(BF16)


def dot(a, b):
    return jnp.dot(a, b, preferred_element_type=F32)


def temperature(h):
    return jnp.minimum(h, 0.0) + jnp.maximum(h - 1.0, 0.0)


def iota(shape, dim):
    return lax.broadcasted_iota(jnp.int32, shape, dim)


def to_lanes(column):
    bx, by, _ = column.shape
    diagonal = iota((bx, by, 128), 1) == iota((bx, by, 128), 2)
    return jnp.sum(jnp.where(diagonal, column, 0.0), axis=1)


def to_column(line, by):
    bx = line.shape[0]
    diagonal = iota((bx, by, 128), 1) == iota((bx, by, 128), 2)
    return jnp.sum(jnp.where(diagonal, line[:, None, :], 0.0), axis=2, keepdims=True)


def conduct(h, k, xlo, xhi, ylo, yhi, zlo, zhi):
    bx, by, bz = h.shape
    t = temperature(h)
    row, lane = iota((bx, by, bz), 1), iota((bx, by, bz), 2)
    if bx > 1:
        total = jnp.concatenate([xlo, t[:-1]], axis=0) + jnp.concatenate([t[1:], xhi], axis=0)
    else:
        total = xlo + xhi
    total += jnp.where(row == 0, ylo[:, None, :], pltpu.roll(t, 1, 1))
    total += jnp.where(row == by - 1, yhi[:, None, :], pltpu.roll(t, by - 1, 1))
    total += jnp.where(lane == 0, to_column(zlo, by), pltpu.roll(t, 1, 2))
    total += jnp.where(lane == bz - 1, to_column(zhi, by), pltpu.roll(t, bz - 1, 2))
    return h + RATE * k * (total - 6.0 * t)


def sublanes(value, y):
    return jnp.concatenate([value[x, y : y + 1, :] for x in range(value.shape[0])], axis=0)


def side_blocks(h, k):
    by, bz = h.shape[1:]
    return [
        (sublanes(h, 0), sublanes(h, 1), sublanes(k, 0)),
        (sublanes(h, by - 1), sublanes(h, by - 2), sublanes(k, by - 1)),
        (to_lanes(h[:, :, 0:1]), to_lanes(h[:, :, 1:2]), to_lanes(k[:, :, 0:1])),
        (to_lanes(h[:, :, bz - 1 : bz]), to_lanes(h[:, :, bz - 2 : bz - 1]), to_lanes(k[:, :, bz - 1 : bz])),
    ]


def sides_kernel(sizes, h, k, send):
    ny, nz = sizes
    my_y, my_z = lax.axis_index("gy"), lax.axis_index("gz")
    bx = h.shape[0]
    blocks = side_blocks(h[...], k[...])
    for y in range(ny):
        for z in range(nz):
            for part in range(3):
                ylo, yhi, zlo, zhi = [block[part] for block in blocks]
                chosen = jnp.where(
                    my_y == y, jnp.where(z < my_z, zlo, zhi), jnp.where(y < my_y, ylo, yhi)
                )
                send[y * nz + z, part * bx : part * bx + bx, :] = chosen


def side_reader(sizes, got, bx):
    ny, nz = sizes
    my_y, my_z = lax.axis_index("gy"), lax.axis_index("gz")

    def read(dy, dz, part=0):
        y, z = my_y + dy, my_z + dz
        inside = (y >= 0) & (y < ny) & (z >= 0) & (z < nz)
        at = jnp.where(inside, y * nz + z, 0)
        return jnp.where(inside, got[at, part * bx : part * bx + bx, :], 0.0)

    return read


def layers_kernel(sizes, h, k, got, _, low, high):
    bx, by, bz = h.shape
    read = side_reader(sizes, got, bx)
    around = [read(-1, 0), read(1, 0), read(0, -1), read(0, 1)]
    for out, near, far in ((low, 0, 1), (high, bx - 1, bx - 2)):
        out[0:by, :] = h[near]
        out[by : 2 * by, :] = h[far]
        out[2 * by : 3 * by, :] = k[near]
        for number, side in enumerate(around):
            out[3 * by + number : 3 * by + number + 1, :] = side[near : near + 1, :]


def block_layout(cap):
    parts = 128 // CB // cap
    return parts, CB // parts


def flat_step(h, k, inner, outer, first, last, before, after, length):
    bx, lanes = h.shape
    t = temperature(h)
    row, lane = iota(h.shape, 0), iota(h.shape, 1)
    total = temperature(inner) + temperature(outer)
    total += jnp.where(row == 0, temperature(first), pltpu.roll(t, 1, 0))
    total += jnp.where(row == bx - 1, temperature(last), pltpu.roll(t, bx - 1, 0))
    total += jnp.where(lane == 0, temperature(before), pltpu.roll(t, 1, 1))
    total += jnp.where(lane == length - 1, temperature(after), pltpu.roll(t, lanes - 1, 1))
    return h + RATE * k * (total - 6.0 * t)


def heat_kernel(cap, sizes, request, h, k, got, low, high, out, send, held):
    bx, by, bz = h.shape
    h0, k0 = h[...], k[...]
    read = side_reader(sizes, got, bx)
    layers = []
    for r in (low, high):
        layers.append([r[part * by : part * by + by, :][None] for part in range(3)])
    lines = [[r[3 * by + n : 3 * by + n + 1, :] for n in range(4)] for r in (low, high)]
    y_sides = [[read(d, 0, part) for part in range(3)] for d in (-1, 1)]
    z_sides = [[read(0, d, part) for part in range(3)] for d in (-1, 1)]
    corner = [[read(dy, dz) for dz in (-1, 1)] for dy in (-1, 1)]
    to_first = [[pltpu.roll(c[0], 1, 1), c[1]] for c in corner]
    y_inner = [sublanes(h0, 0), sublanes(h0, by - 1)]
    z_inner = [to_lanes(h0[:, :, 0:1]), to_lanes(h0[:, :, bz - 1 : bz])]

    sides = [temperature(layers[0][0]), temperature(layers[1][0])]
    sides += [temperature(side[0]) for side in y_sides + z_sides]
    h1 = conduct(h0, k0, *sides)
    next_sides = []
    for side in range(2):
        near, far, near_k = layers[side]
        across = [temperature(far), temperature(h0[0:1])]
        if side:
            across = [temperature(h0[bx - 1 : bx]), temperature(far)]
        next_sides.append(conduct(near, near_k, *across, *[temperature(line) for line in lines[side]]))
    for side in range(2):
        near, far, near_k = y_sides[side]
        ends = [to_first[side][0], pltpu.roll(to_first[side][1], bz - 1, 1)]
        next_sides.append(
            flat_step(near, near_k, y_inner[side], far, lines[0][side], lines[1][side], *ends, bz)
        )
    for side in range(2):
        near, far, near_k = z_sides[side]
        ends = [to_first[0][side], pltpu.roll(to_first[1][side], by - 1, 1)]
        next_sides.append(
            flat_step(near, near_k, z_inner[side], far, lines[0][2 + side], lines[1][2 + side], *ends, by)
        )
    h2 = conduct(h1, k0, *[temperature(side) for side in next_sides])
    out[...] = h2

    held[...] = temperature(h2).reshape(bx, by // CB, CB, bz)
    parts, deep = block_layout(cap)
    nby, nbz = by // CB, bz // CB
    group = iota((deep, CB, bz), 2) // CB
    for owner in range(send.shape[0]):
        total = jnp.zeros((deep, CB, bz), F32)
        for rank in range(cap):
            block = request[owner * cap + rank]
            a, b, c = block // (nby * nbz), (block // nbz) % nby, block % nbz
            for part in range(parts):
                at = rank * parts + part
                patch = held[pl.ds(a * CB + part * deep, deep), b]
                moved = pltpu.roll(patch, (CB * at - CB * c + bz) % bz, 2)
                total = jnp.where(group == at, moved, total)
        send[owner] = total.reshape(deep * CB, bz)


def write_records(phase, solute, picks, own):
    flat = [f.reshape(SLOTS * TE, PLANE) for f in (phase, solute)]
    parts = jnp.concatenate([*halves(flat[0]), *halves(flat[1])], axis=1)
    planes = dot(parts, picks)
    own[0:SLOTS, 0:TE, :] = planes[:, 0:128].reshape(SLOTS, TE, 128)
    own[SLOTS : 2 * SLOTS, 0:TE, :] = planes[:, 128:256].reshape(SLOTS, TE, 128)
    for face in range(2):
        for number, field in enumerate((phase, solute)):
            for half in range(2):
                row = TE + face * 4 + number * 2 + half
                lanes = slice(half * 128, half * 128 + 128)
                near, far = (0, TE - 1) if face == 0 else (TE - 1, 0)
                own[0:SLOTS, row : row + 1, :] = field[:, far : far + 1, lanes]
                own[SLOTS : 2 * SLOTS, row : row + 1, :] = field[:, near : near + 1, lanes]


def merge_record(source, number):
    side = (iota((TE, 128), 1) % 64) // TE
    out = source[number(2), 0:TE, :]
    for face in range(3, 6):
        out = jnp.where(side == face - 2, source[number(face), 0:TE, :], out)
    edge = jnp.where(
        iota((8, 128), 0) < 4, source[number(0), TE:REC, :], source[number(1), TE:REC, :]
    )
    return out, edge


def pack(own, send_index, send):
    records = send_index.shape[0] // FACES
    cap = records // send.shape[0]
    for record in range(records):
        out, edge = merge_record(own, lambda face: send_index[record * FACES + face])
        owner, row = record // cap, record % cap * REC
        send[owner, row : row + TE, :] = out
        send[owner, row + TE : row + REC, :] = edge


def first_pack_kernel(send_index, place, wanted, phase, solute, picks, own, send):
    write_records(phase[...], solute[...], picks[...], own)
    pack(own, send_index, send)
    count, rows, _ = send.shape
    lane = iota((8, 128), 1)
    for owner in range(count):
        asked = jnp.zeros((8, 128), F32)
        for slot in range(SLOTS):
            here = jnp.where(place[slot] == owner, place[SLOTS + slot], -1)
            asked = jnp.where(lane == here, wanted[slot].astype(F32), asked)
        send[owner, rows - 8 : rows, :] = asked


def take_heat(cap, place, blocks, spreads, held, heat):
    parts, deep = block_layout(cap)
    group = iota((CB, 128), 1) // CB
    for slot in range(SLOTS):
        source, rank = place[slot], place[SLOTS + slot]
        for x in range(CB):
            row = (x % deep) * CB
            patch = blocks[source, row : row + CB, :]
            held[slot * CB + x] = jnp.where(group == rank * parts + x // deep, patch, 0.0)
    rows = held[...].reshape(SLOTS * CB * CB, 128)
    wide = dot(jnp.concatenate(halves(rows), axis=1), spreads)
    wide = wide.reshape(SLOTS * CB, CB, PLANE)
    keep = iota(wide.shape, 1) == iota(wide.shape, 2) // TE // 2
    coarse = jnp.sum(jnp.where(keep, wide, 0.0), axis=1)
    for half in range(2):
        for odd in range(2):
            heat[half, pl.ds(odd, SLOTS * CB, 2), :] = coarse[:, half * 128 : half * 128 + 128]


def step(receive_index, phase, solute, heat, got, own, laps, all_records, ghosts):
    records = all_records.shape[0] - 2 * SLOTS
    count = got.shape[0]
    cap = records // count
    for owner in range(count):
        mine = got[owner, 0 : cap * REC, :]
        all_records[owner * cap : owner * cap + cap] = mine.reshape(cap, REC, 128)
    all_records[records : records + 2 * SLOTS] = own[...]
    for slot in range(SLOTS):
        out, edge = merge_record(all_records, lambda face: receive_index[slot * FACES + face])
        ghosts[slot, 0:TE, :] = out
        ghosts[slot, TE:REC, :] = edge
    beside = jnp.concatenate(halves(ghosts[:, 0:TE, :].reshape(SLOTS * TE, 128)), axis=1)
    row = iota((SLOTS, TE, PLANE), 1)
    lap = []
    for number, (field, table) in enumerate(((phase, laps[0]), (solute, laps[1]))):
        flat = field.reshape(SLOTS * TE, PLANE)
        total = dot(jnp.concatenate([*halves(flat), beside], axis=1), table)
        total = total.reshape(SLOTS, TE, PLANE) - 6.0 * field
        sides = []
        for face in range(2):
            at = TE + face * 4 + number * 2
            sides.append(
                jnp.concatenate([ghosts[:, at : at + 1, :], ghosts[:, at + 1 : at + 2, :]], axis=2)
            )
        total += jnp.where(row == 0, sides[0], pltpu.roll(field, 1, 1))
        total += jnp.where(row == TE - 1, sides[1], pltpu.roll(field, TE - 1, 1))
        lap.append(total)
    warm = jnp.concatenate([heat[0], heat[1]], axis=1).reshape(SLOTS, TE, PLANE)
    squared = 1.0 - phase * phase
    new_phase = phase + ORDER_SPEED * (
        lap[0] + phase - phase * phase * phase - COUPLING * (warm + solute) * squared * squared
    )
    new_solute = solute + SOLUTE_RATE * lap[1] + REJECTION * (new_phase - phase)
    return new_phase, new_solute


def first_step_kernel(
    cap, receive_index, send_index, place, phase, solute, blocks, got, own, picks, lap0, lap1, spreads,
    phase_out, solute_out, heat_out, own_out, send, all_records, ghosts, held,
):
    take_heat(cap, place, blocks, spreads[...], held, heat_out)
    new_phase, new_solute = step(
        receive_index, phase[...], solute[...], heat_out[...], got, own, (lap0[...], lap1[...]),
        all_records, ghosts,
    )
    phase_out[...] = new_phase
    solute_out[...] = new_solute
    write_records(new_phase, new_solute, picks[...], own_out)
    pack(own_out, send_index, send)


def middle_step_kernel(
    receive_index, send_index, phase, solute, heat, got, own, picks, lap0, lap1,
    phase_out, solute_out, own_out, send, all_records, ghosts,
):
    new_phase, new_solute = step(
        receive_index, phase[...], solute[...], heat[...], got, own, (lap0[...], lap1[...]),
        all_records, ghosts,
    )
    phase_out[...] = new_phase
    solute_out[...] = new_solute
    write_records(new_phase, new_solute, picks[...], own_out)
    pack(own_out, send_index, send)


def last_step_kernel(
    receive_index, phase, solute, heat, got, own, lap0, lap1, phase_out, solute_out, all_records, ghosts
):
    new_phase, new_solute = step(
        receive_index, phase[...], solute[...], heat[...], got, own, (lap0[...], lap1[...]),
        all_records, ghosts,
    )
    phase_out[...] = new_phase
    solute_out[...] = new_solute


def call(kernel, in_specs, out_shapes, scratch=()):
    return pl.pallas_call(
        kernel,
        out_shape=out_shapes,
        in_specs=in_specs,
        out_specs=jax.tree.map(lambda _: VMEM, out_shapes),
        scratch_shapes=list(scratch),
        compiler_params=PARAMS,
    )


def shape(*dims):
    return jax.ShapeDtypeStruct(dims, F32)


def tile_indices(neighbour, cap, me):
    count = lax.axis_size("gx")
    owner = neighbour >> 4
    other = (neighbour >= 0) & (owner != me)
    slot = jnp.arange(SLOTS, dtype=jnp.int32)
    alike = (owner[None] == owner[:, None]) & other[None]
    receive_rank = jnp.sum((alike & (neighbour[None] < neighbour[:, None])).astype(jnp.int32), axis=1)
    send_rank = jnp.sum(
        (alike & (slot[None, :, None] < slot[:, None, None])).astype(jnp.int32), axis=1
    )
    records = count * cap
    receive = jnp.where(
        neighbour < 0,
        records + SLOTS + slot[:, None],
        jnp.where(owner == me, records + (neighbour & (SLOTS - 1)), owner * cap + receive_rank),
    )
    key = jnp.where(other, owner * cap + send_rank, -1)
    hit = key[None] == jnp.arange(records, dtype=jnp.int32)[:, None, None]
    sender = jnp.sum(jnp.where(hit, slot[None, :, None], 0), axis=1)
    sender = sender.reshape(records, 3, 2)[:, :, ::-1]
    return receive.reshape(-1), sender.reshape(-1)


def local(enthalpy, conductivity, phase, solute, tile_source, tile_block, tile_neighbour):
    count = lax.axis_size("gx")
    sizes = (lax.axis_size("gy"), lax.axis_size("gz"))
    me = lax.axis_index("gx")
    plane_cap = -(-SLOTS // (count - 1))
    block_cap = 2 * SLOTS // count
    bx, by, bz = enthalpy.shape
    picks, lap0, lap1, spreads = tables()

    sides = call(
        functools.partial(sides_kernel, sizes), [VMEM] * 2, shape(sizes[0] * sizes[1], 3 * bx, 128)
    )(enthalpy, conductivity)
    sides = lax.all_to_all(sides, ("gy", "gz"), split_axis=0, concat_axis=0, tiled=True)

    sources = tile_source.reshape(SLOTS)
    wanted = tile_block.reshape(SLOTS)
    slot = jnp.arange(SLOTS, dtype=jnp.int32)
    ranks = jnp.sum(
        ((sources[None] == sources[:, None]) & (slot[None] < slot[:, None])).astype(jnp.int32), axis=1
    )
    place = jnp.concatenate([sources, ranks])
    neighbour = tile_neighbour.reshape(SLOTS, FACES)
    receive_index, send_index = tile_indices(neighbour, plane_cap, me)
    phase_field = phase.reshape(SLOTS, TE, PLANE)
    solute_field = solute.reshape(SLOTS, TE, PLANE)
    records = count * plane_cap
    own_shape, send_shape = shape(2 * SLOTS, REC, 128), shape(count, plane_cap * REC, 128)
    own, send = call(
        first_pack_kernel,
        [SMEM] * 3 + [VMEM] * 3,
        [own_shape, shape(count, plane_cap * REC + 8, 128)],
    )(send_index, place, wanted, phase_field, solute_field, picks)
    got = lax.all_to_all(send, "gx", split_axis=0, concat_axis=0, tiled=True)
    request = got[:, plane_cap * REC, :block_cap].astype(jnp.int32).reshape(-1)

    layer = shape(3 * by + 8, bz)
    low, high = call(
        functools.partial(layers_kernel, sizes),
        [VMEM] * 3 + [pl.BlockSpec(memory_space=pl.ANY)],
        [layer, layer],
    )(enthalpy, conductivity, sides, send)
    forward = [(i, i + 1) for i in range(count - 1)]
    backward = [(b, a) for a, b in forward]
    from_low = lax.ppermute(high, "gx", forward)
    from_high = lax.ppermute(low, "gx", backward)
    _, deep = block_layout(block_cap)
    heat_out, found = call(
        functools.partial(heat_kernel, block_cap, sizes),
        [SMEM] + [VMEM] * 5,
        [shape(bx, by, bz), shape(count, deep * CB, bz)],
        [pltpu.VMEM((bx, by // CB, CB, bz), F32)],
    )(request, enthalpy, conductivity, sides, from_low, from_high)
    blocks = lax.all_to_all(found, "gx", split_axis=0, concat_axis=0, tiled=True)

    field = shape(SLOTS, TE, PLANE)
    step_scratch = [
        pltpu.VMEM((records + 2 * SLOTS, REC, 128), F32),
        pltpu.VMEM((SLOTS, REC, 128), F32),
    ]
    phase_field, solute_field, heat, own, send = call(
        functools.partial(first_step_kernel, block_cap),
        [SMEM] * 3 + [VMEM] * 9,
        [field, field, shape(2, SLOTS * TE, 128), own_shape, send_shape],
        step_scratch + [pltpu.VMEM((SLOTS * CB, CB, 128), F32)],
    )(
        receive_index, send_index, place, phase_field, solute_field, blocks, got, own, picks, lap0, lap1,
        spreads,
    )
    for _ in range(PHASE_STEPS - 2):
        got = lax.all_to_all(send, "gx", split_axis=0, concat_axis=0, tiled=True)
        phase_field, solute_field, own, send = call(
            middle_step_kernel, [SMEM] * 2 + [VMEM] * 8, [field, field, own_shape, send_shape], step_scratch
        )(receive_index, send_index, phase_field, solute_field, heat, got, own, picks, lap0, lap1)
    got = lax.all_to_all(send, "gx", split_axis=0, concat_axis=0, tiled=True)
    phase_field, solute_field = call(
        last_step_kernel, [SMEM] + [VMEM] * 7, [field, field], step_scratch
    )(receive_index, phase_field, solute_field, heat, got, own, lap0, lap1)
    return heat_out, phase_field.reshape(phase.shape), solute_field.reshape(solute.shape)


def solution(mesh):
    grid = P("gx", "gy", "gz")
    tiles = P("gx", "gy", "gz", None, None, None)
    return jax.shard_map(
        local,
        mesh=mesh,
        in_specs=(
            grid,
            grid,
            tiles,
            tiles,
            P("gx", "gy", "gz", None, None),
            P("gx", "gy", "gz", None),
            P("gx", "gy", "gz", None, None),
        ),
        out_specs=(grid, tiles, tiles),
        check_vma=False,
    )
```

```python
import functools

import jax
import jax.numpy as jnp
import numpy as np
from jax import lax
from jax.experimental import pallas as pl
from jax.experimental.pallas import tpu as pltpu
from jax.sharding import PartitionSpec as P

CB = 8
TE = 16
PLANE = TE * TE
SLOTS = 16
FACES = 6
PHASE_STEPS = 4
REC = 24

RATE = 0.16
ORDER_SPEED = 0.1
SOLUTE_RATE = 0.15
COUPLING = 0.5
REJECTION = 0.5

F32 = jnp.float32
BF16 = jnp.bfloat16
VMEM = pl.BlockSpec(memory_space=pltpu.VMEM)
SMEM = pl.BlockSpec(memory_space=pltpu.SMEM)
HBM = pl.BlockSpec(memory_space=pltpu.HBM)
PARAMS = pltpu.CompilerParams(vmem_limit_bytes=16 * 1024 * 1024)


def plane_lane(face):
    j = np.arange(TE)
    return [j, PLANE - TE + j, j * TE, j * TE + TE - 1][face - 2]


def constant_tables():
    pick = np.zeros((2, PLANE, 256), np.float32)
    place = np.zeros((2, 128, PLANE), np.float32)
    for field in range(2):
        for face in range(2, 6):
            at = field * 64 + (face - 2) * TE + np.arange(TE)
            pick[field, plane_lane(face ^ 1), at] = 1.0
            pick[field, plane_lane(face), 128 + at] = 1.0
            place[field, at, plane_lane(face)] = 1.0
    y, z = np.divmod(np.arange(PLANE), TE)
    dy, dz = np.abs(y[:, None] - y[None, :]), np.abs(z[:, None] - z[None, :])
    stencil = ((dy + dz) == 1).astype(np.float32)
    lane = np.arange(128)
    spread = (lane[:, None] % CB == z[None, :] // 2).astype(np.float32)
    return pick, place, stencil, spread


def tables():
    pick, place, stencil, spread = constant_tables()
    picks = np.concatenate([pick[0], pick[0], pick[1], pick[1]], axis=0)
    laps = [np.concatenate([stencil, stencil, place[f], place[f]], axis=0) for f in range(2)]
    spreads = np.concatenate([spread, spread], axis=0)
    return (
        jnp.asarray(picks, BF16),
        jnp.asarray(laps[0], BF16),
        jnp.asarray(laps[1], BF16),
        jnp.asarray(spreads, BF16),
    )


def halves(value):
    high = value.astype(BF16)
    return high, (value - high.astype(F32)).astype(BF16)


def dot(a, b):
    return jnp.dot(a, b, preferred_element_type=F32)


def temperature(h):
    return jnp.minimum(h, 0.0) + jnp.maximum(h - 1.0, 0.0)


def iota(shape, dim):
    return lax.broadcasted_iota(jnp.int32, shape, dim)


def to_lanes(column):
    bx, by, _ = column.shape
    diagonal = iota((bx, by, 128), 1) == iota((bx, by, 128), 2)
    return jnp.sum(jnp.where(diagonal, column, 0.0), axis=1)


def to_column(line, by):
    bx = line.shape[0]
    diagonal = iota((bx, by, 128), 1) == iota((bx, by, 128), 2)
    return jnp.sum(jnp.where(diagonal, line[:, None, :], 0.0), axis=2, keepdims=True)


def conduct(h, k, xlo, xhi, ylo, yhi, zlo, zhi):
    bx, by, bz = h.shape
    t = temperature(h)
    row, lane = iota((bx, by, bz), 1), iota((bx, by, bz), 2)
    if bx > 1:
        total = jnp.concatenate([xlo, t[:-1]], axis=0) + jnp.concatenate([t[1:], xhi], axis=0)
    else:
        total = xlo + xhi
    total += jnp.where(row == 0, ylo[:, None, :], pltpu.roll(t, 1, 1))
    total += jnp.where(row == by - 1, yhi[:, None, :], pltpu.roll(t, by - 1, 1))
    total += jnp.where(lane == 0, to_column(zlo, by), pltpu.roll(t, 1, 2))
    total += jnp.where(lane == bz - 1, to_column(zhi, by), pltpu.roll(t, bz - 1, 2))
    return h + RATE * k * (total - 6.0 * t)


def sublanes(value, y):
    return jnp.concatenate([value[x, y : y + 1, :] for x in range(value.shape[0])], axis=0)


def side_blocks(h, k):
    by, bz = h.shape[1:]
    return [
        (sublanes(h, 0), sublanes(h, 1), sublanes(k, 0)),
        (sublanes(h, by - 1), sublanes(h, by - 2), sublanes(k, by - 1)),
        (to_lanes(h[:, :, 0:1]), to_lanes(h[:, :, 1:2]), to_lanes(k[:, :, 0:1])),
        (to_lanes(h[:, :, bz - 1 : bz]), to_lanes(h[:, :, bz - 2 : bz - 1]), to_lanes(k[:, :, bz - 1 : bz])),
    ]


def ask(sources, wanted, asked, place):
    lane = iota(asked.shape[1:], 1)
    ranks = []
    for slot in range(SLOTS):
        alike = [jnp.where(sources[other] == sources[slot], 1, 0) for other in range(slot)]
        ranks.append(sum(alike, jnp.int32(0)))
        place[slot] = sources[slot]
        place[SLOTS + slot] = ranks[slot]
    for owner in range(asked.shape[0]):
        row = jnp.zeros(lane.shape, jnp.int32)
        for slot in range(SLOTS):
            row = jnp.where(lane == jnp.where(sources[slot] == owner, ranks[slot], -1), wanted[slot], row)
        asked[owner] = row


def sides_kernel(sizes, sources, wanted, h_far, k_far, send, asked, place, h, k, sems):
    ny, nz = sizes
    my_y, my_z = lax.axis_index("gy"), lax.axis_index("gz")
    bx = h.shape[0]
    copies = []
    for x in range(bx):
        copies.append(pltpu.make_async_copy(h_far.at[x], h.at[x], sems.at[x]))
        copies.append(pltpu.make_async_copy(k_far.at[x], k.at[x], sems.at[bx + x]))
    for copy in copies:
        copy.start()
    ask(sources, wanted, asked, place)
    for copy in copies:
        copy.wait()
    blocks = side_blocks(h[...], k[...])
    for y in range(ny):
        for z in range(nz):
            for part in range(3):
                ylo, yhi, zlo, zhi = [block[part] for block in blocks]
                chosen = jnp.where(
                    my_y == y, jnp.where(z < my_z, zlo, zhi), jnp.where(y < my_y, ylo, yhi)
                )
                send[y * nz + z, part * bx : part * bx + bx, :] = chosen


def side_reader(sizes, got, bx):
    ny, nz = sizes
    my_y, my_z = lax.axis_index("gy"), lax.axis_index("gz")

    def read(dy, dz, part=0):
        y, z = my_y + dy, my_z + dz
        inside = (y >= 0) & (y < ny) & (z >= 0) & (z < nz)
        at = jnp.where(inside, y * nz + z, 0)
        return jnp.where(inside, got[at, part * bx : part * bx + bx, :], 0.0)

    return read


def layers_kernel(sizes, h, k, got, low, high):
    bx, by, bz = h.shape
    read = side_reader(sizes, got, bx)
    around = [read(-1, 0), read(1, 0), read(0, -1), read(0, 1)]
    for out, near, far in ((low, 0, 1), (high, bx - 1, bx - 2)):
        out[0:by, :] = h[near]
        out[by : 2 * by, :] = h[far]
        out[2 * by : 3 * by, :] = k[near]
        for number, side in enumerate(around):
            out[3 * by + number : 3 * by + number + 1, :] = side[near : near + 1, :]


def block_layout(cap):
    parts = 128 // CB // cap
    return parts, CB // parts


def flat_step(h, k, inner, outer, first, last, before, after, length):
    bx, lanes = h.shape
    t = temperature(h)
    row, lane = iota(h.shape, 0), iota(h.shape, 1)
    total = temperature(inner) + temperature(outer)
    total += jnp.where(row == 0, temperature(first), pltpu.roll(t, 1, 0))
    total += jnp.where(row == bx - 1, temperature(last), pltpu.roll(t, bx - 1, 0))
    total += jnp.where(lane == 0, temperature(before), pltpu.roll(t, 1, 1))
    total += jnp.where(lane == length - 1, temperature(after), pltpu.roll(t, lanes - 1, 1))
    return h + RATE * k * (total - 6.0 * t)


def heat_kernel(cap, sizes, request, h, k, got, low, high, packed, out, send, held):
    bx, by, bz = h.shape
    h0, k0 = h[...], k[...]
    read = side_reader(sizes, got, bx)
    layers = []
    for r in (low, high):
        layers.append([r[part * by : part * by + by, :][None] for part in range(3)])
    lines = [[r[3 * by + n : 3 * by + n + 1, :] for n in range(4)] for r in (low, high)]
    y_sides = [[read(d, 0, part) for part in range(3)] for d in (-1, 1)]
    z_sides = [[read(0, d, part) for part in range(3)] for d in (-1, 1)]
    corner = [[read(dy, dz) for dz in (-1, 1)] for dy in (-1, 1)]
    to_first = [[pltpu.roll(c[0], 1, 1), c[1]] for c in corner]
    y_inner = [sublanes(h0, 0), sublanes(h0, by - 1)]
    z_inner = [to_lanes(h0[:, :, 0:1]), to_lanes(h0[:, :, bz - 1 : bz])]

    sides = [temperature(layers[0][0]), temperature(layers[1][0])]
    sides += [temperature(side[0]) for side in y_sides + z_sides]
    h1 = conduct(h0, k0, *sides)
    next_sides = []
    for side in range(2):
        near, far, near_k = layers[side]
        across = [temperature(far), temperature(h0[0:1])]
        if side:
            across = [temperature(h0[bx - 1 : bx]), temperature(far)]
        next_sides.append(conduct(near, near_k, *across, *[temperature(line) for line in lines[side]]))
    for side in range(2):
        near, far, near_k = y_sides[side]
        ends = [to_first[side][0], pltpu.roll(to_first[side][1], bz - 1, 1)]
        next_sides.append(
            flat_step(near, near_k, y_inner[side], far, lines[0][side], lines[1][side], *ends, bz)
        )
    for side in range(2):
        near, far, near_k = z_sides[side]
        ends = [to_first[0][side], pltpu.roll(to_first[1][side], by - 1, 1)]
        next_sides.append(
            flat_step(near, near_k, z_inner[side], far, lines[0][2 + side], lines[1][2 + side], *ends, by)
        )
    h2 = conduct(h1, k0, *[temperature(side) for side in next_sides])
    out[...] = h2

    held[...] = temperature(h2).reshape(bx, by // CB, CB, bz)
    parts, deep = block_layout(cap)
    nby, nbz = by // CB, bz // CB
    group = iota((deep, CB, bz), 2) // CB
    for owner in range(send.shape[0]):
        total = jnp.zeros((deep, CB, bz), F32)
        for rank in range(cap):
            block = request[owner * cap + rank]
            a, b, c = block // (nby * nbz), (block // nbz) % nby, block % nbz
            for part in range(parts):
                at = rank * parts + part
                patch = held[pl.ds(a * CB + part * deep, deep), b]
                moved = pltpu.roll(patch, (CB * at - CB * c + bz) % bz, 2)
                total = jnp.where(group == at, moved, total)
        behind = packed.shape[1]
        send[owner, 0:behind, :] = packed[owner]
        send[owner, behind:, :] = total.reshape(deep * CB, bz)


def write_records(phase, solute, picks, own):
    flat = [f.reshape(SLOTS * TE, PLANE) for f in (phase, solute)]
    parts = jnp.concatenate([*halves(flat[0]), *halves(flat[1])], axis=1)
    planes = dot(parts, picks)
    own[0:SLOTS, 0:TE, :] = planes[:, 0:128].reshape(SLOTS, TE, 128)
    own[SLOTS : 2 * SLOTS, 0:TE, :] = planes[:, 128:256].reshape(SLOTS, TE, 128)
    for face in range(2):
        for number, field in enumerate((phase, solute)):
            for half in range(2):
                row = TE + face * 4 + number * 2 + half
                lanes = slice(half * 128, half * 128 + 128)
                near, far = (0, TE - 1) if face == 0 else (TE - 1, 0)
                own[0:SLOTS, row : row + 1, :] = field[:, far : far + 1, lanes]
                own[SLOTS : 2 * SLOTS, row : row + 1, :] = field[:, near : near + 1, lanes]


def merge_record(source, number):
    side = (iota((TE, 128), 1) % 64) // TE
    out = source[number(2), 0:TE, :]
    for face in range(3, 6):
        out = jnp.where(side == face - 2, source[number(face), 0:TE, :], out)
    edge = jnp.where(
        iota((8, 128), 0) < 4, source[number(0), TE:REC, :], source[number(1), TE:REC, :]
    )
    return out, edge


def pack(own, send_index, send):
    records = send_index.shape[0] // FACES
    cap = records // send.shape[0]
    for record in range(records):
        out, edge = merge_record(own, lambda face: send_index[record * FACES + face])
        owner, row = record // cap, record % cap * REC
        send[owner, row : row + TE, :] = out
        send[owner, row + TE : row + REC, :] = edge


def first_pack_kernel(send_index, phase, solute, picks, own, send):
    write_records(phase[...], solute[...], picks[...], own)
    pack(own, send_index, send)


def take_heat(cap, place, got, spreads, held, heat):
    parts, deep = block_layout(cap)
    first = got.shape[1] - deep * CB
    group = iota((CB, 128), 1) // CB
    for slot in range(SLOTS):
        source, rank = place[slot], place[SLOTS + slot]
        for x in range(CB):
            row = first + (x % deep) * CB
            patch = got[source, row : row + CB, :]
            held[slot * CB + x] = jnp.where(group == rank * parts + x // deep, patch, 0.0)
    rows = held[...].reshape(SLOTS * CB * CB, 128)
    wide = dot(jnp.concatenate(halves(rows), axis=1), spreads)
    wide = wide.reshape(SLOTS * CB, CB, PLANE)
    keep = iota(wide.shape, 1) == iota(wide.shape, 2) // TE // 2
    coarse = jnp.sum(jnp.where(keep, wide, 0.0), axis=1)
    for half in range(2):
        for odd in range(2):
            heat[half, pl.ds(odd, SLOTS * CB, 2), :] = coarse[:, half * 128 : half * 128 + 128]


def step(receive_index, phase, solute, heat, got, own, laps, all_records, ghosts):
    records = all_records.shape[0] - 2 * SLOTS
    count = got.shape[0]
    cap = records // count
    for owner in range(count):
        mine = got[owner, 0 : cap * REC, :]
        all_records[owner * cap : owner * cap + cap] = mine.reshape(cap, REC, 128)
    all_records[records : records + 2 * SLOTS] = own[...]
    for slot in range(SLOTS):
        out, edge = merge_record(all_records, lambda face: receive_index[slot * FACES + face])
        ghosts[slot, 0:TE, :] = out
        ghosts[slot, TE:REC, :] = edge
    beside = jnp.concatenate(halves(ghosts[:, 0:TE, :].reshape(SLOTS * TE, 128)), axis=1)
    row = iota((SLOTS, TE, PLANE), 1)
    lap = []
    for number, (field, table) in enumerate(((phase, laps[0]), (solute, laps[1]))):
        flat = field.reshape(SLOTS * TE, PLANE)
        total = dot(jnp.concatenate([*halves(flat), beside], axis=1), table)
        total = total.reshape(SLOTS, TE, PLANE) - 6.0 * field
        sides = []
        for face in range(2):
            at = TE + face * 4 + number * 2
            sides.append(
                jnp.concatenate([ghosts[:, at : at + 1, :], ghosts[:, at + 1 : at + 2, :]], axis=2)
            )
        total += jnp.where(row == 0, sides[0], pltpu.roll(field, 1, 1))
        total += jnp.where(row == TE - 1, sides[1], pltpu.roll(field, TE - 1, 1))
        lap.append(total)
    warm = jnp.concatenate([heat[0], heat[1]], axis=1).reshape(SLOTS, TE, PLANE)
    squared = 1.0 - phase * phase
    new_phase = phase + ORDER_SPEED * (
        lap[0] + phase - phase * phase * phase - COUPLING * (warm + solute) * squared * squared
    )
    new_solute = solute + SOLUTE_RATE * lap[1] + REJECTION * (new_phase - phase)
    return new_phase, new_solute


def first_step_kernel(
    cap, receive_index, send_index, place, phase, solute, got, own, picks, lap0, lap1, spreads, brick,
    phase_out, solute_out, heat_out, own_out, send, brick_out, all_records, ghosts, held, sem,
):
    copy = pltpu.make_async_copy(brick, brick_out, sem)
    copy.start()
    take_heat(cap, place, got, spreads[...], held, heat_out)
    new_phase, new_solute = step(
        receive_index, phase[...], solute[...], heat_out[...], got, own, (lap0[...], lap1[...]),
        all_records, ghosts,
    )
    phase_out[...] = new_phase
    solute_out[...] = new_solute
    write_records(new_phase, new_solute, picks[...], own_out)
    pack(own_out, send_index, send)
    copy.wait()


def middle_step_kernel(
    receive_index, send_index, phase, solute, heat, got, own, picks, lap0, lap1,
    phase_out, solute_out, own_out, send, all_records, ghosts,
):
    new_phase, new_solute = step(
        receive_index, phase[...], solute[...], heat[...], got, own, (lap0[...], lap1[...]),
        all_records, ghosts,
    )
    phase_out[...] = new_phase
    solute_out[...] = new_solute
    write_records(new_phase, new_solute, picks[...], own_out)
    pack(own_out, send_index, send)


def last_step_kernel(
    receive_index, phase, solute, heat, got, own, lap0, lap1, phase_out, solute_out, all_records, ghosts
):
    new_phase, new_solute = step(
        receive_index, phase[...], solute[...], heat[...], got, own, (lap0[...], lap1[...]),
        all_records, ghosts,
    )
    phase_out[...] = new_phase
    solute_out[...] = new_solute


def call(kernel, in_specs, out_shapes, scratch=(), out_specs=None):
    return pl.pallas_call(
        kernel,
        out_shape=out_shapes,
        in_specs=in_specs,
        out_specs=out_specs or jax.tree.map(lambda _: VMEM, out_shapes),
        scratch_shapes=list(scratch),
        compiler_params=PARAMS,
    )


def shape(*dims):
    return jax.ShapeDtypeStruct(dims, F32)


def tile_indices(neighbour, cap, me):
    count = lax.axis_size("gx")
    owner = neighbour >> 4
    other = (neighbour >= 0) & (owner != me)
    slot = jnp.arange(SLOTS, dtype=jnp.int32)
    alike = (owner[None] == owner[:, None]) & other[None]
    receive_rank = jnp.sum((alike & (neighbour[None] < neighbour[:, None])).astype(jnp.int32), axis=1)
    send_rank = jnp.sum(
        (alike & (slot[None, :, None] < slot[:, None, None])).astype(jnp.int32), axis=1
    )
    records = count * cap
    receive = jnp.where(
        neighbour < 0,
        records + SLOTS + slot[:, None],
        jnp.where(owner == me, records + (neighbour & (SLOTS - 1)), owner * cap + receive_rank),
    )
    key = jnp.where(other, owner * cap + send_rank, -1)
    hit = key[None] == jnp.arange(records, dtype=jnp.int32)[:, None, None]
    sender = jnp.sum(jnp.where(hit, slot[None, :, None], 0), axis=1)
    sender = sender.reshape(records, 3, 2)[:, :, ::-1]
    return receive.reshape(-1), sender.reshape(-1)


def local(enthalpy, conductivity, phase, solute, tile_source, tile_block, tile_neighbour):
    count = lax.axis_size("gx")
    sizes = (lax.axis_size("gy"), lax.axis_size("gz"))
    me = lax.axis_index("gx")
    plane_cap = -(-SLOTS // (count - 1))
    block_cap = 2 * SLOTS // count
    bx, by, bz = enthalpy.shape
    picks, lap0, lap1, spreads = tables()

    sources = tile_source.reshape(SLOTS)
    wanted = tile_block.reshape(SLOTS)
    integers = jax.ShapeDtypeStruct((count, 8, 128), jnp.int32)
    sides, asked, place = call(
        functools.partial(sides_kernel, sizes),
        [SMEM] * 2 + [HBM] * 2,
        [
            shape(sizes[0] * sizes[1], 3 * bx, 128),
            integers,
            jax.ShapeDtypeStruct((2 * SLOTS,), jnp.int32),
        ],
        [pltpu.VMEM((bx, by, bz), F32)] * 2 + [pltpu.SemaphoreType.DMA((2 * bx,))],
        [VMEM, VMEM, SMEM],
    )(sources, wanted, enthalpy, conductivity)
    sides = lax.all_to_all(sides, ("gy", "gz"), split_axis=0, concat_axis=0, tiled=True)
    asked = lax.all_to_all(asked, "gx", split_axis=0, concat_axis=0, tiled=True)
    request = asked[:, 0, :block_cap].reshape(-1)

    neighbour = tile_neighbour.reshape(SLOTS, FACES)
    receive_index, send_index = tile_indices(neighbour, plane_cap, me)
    phase_field = phase.reshape(SLOTS, TE, PLANE)
    solute_field = solute.reshape(SLOTS, TE, PLANE)
    records = count * plane_cap
    own_shape, send_shape = shape(2 * SLOTS, REC, 128), shape(count, plane_cap * REC, 128)
    own, packed = call(first_pack_kernel, [SMEM] + [VMEM] * 3, [own_shape, send_shape])(
        send_index, phase_field, solute_field, picks
    )

    layer = shape(3 * by + 8, bz)
    low, high = call(functools.partial(layers_kernel, sizes), [VMEM] * 3, [layer, layer])(
        enthalpy, conductivity, sides
    )
    forward = [(i, i + 1) for i in range(count - 1)]
    backward = [(b, a) for a, b in forward]
    from_low = lax.ppermute(high, "gx", forward)
    from_high = lax.ppermute(low, "gx", backward)
    _, deep = block_layout(block_cap)
    brick = shape(bx, by, bz)
    heated, send = call(
        functools.partial(heat_kernel, block_cap, sizes),
        [SMEM] + [VMEM] * 6,
        [brick, shape(count, plane_cap * REC + deep * CB, 128)],
        [pltpu.VMEM((bx, by // CB, CB, bz), F32)],
    )(request, enthalpy, conductivity, sides, from_low, from_high, packed)
    got = lax.all_to_all(send, "gx", split_axis=0, concat_axis=0, tiled=True)

    field = shape(SLOTS, TE, PLANE)
    step_scratch = [
        pltpu.VMEM((records + 2 * SLOTS, REC, 128), F32),
        pltpu.VMEM((SLOTS, REC, 128), F32),
    ]
    phase_field, solute_field, heat, own, send, heat_out = call(
        functools.partial(first_step_kernel, block_cap),
        [SMEM] * 3 + [VMEM] * 9,
        [field, field, shape(2, SLOTS * TE, 128), own_shape, send_shape, brick],
        step_scratch + [pltpu.VMEM((SLOTS * CB, CB, 128), F32), pltpu.SemaphoreType.DMA],
        [VMEM] * 5 + [HBM],
    )(
        receive_index, send_index, place, phase_field, solute_field, got, own, picks, lap0, lap1, spreads,
        heated,
    )
    for _ in range(PHASE_STEPS - 2):
        got = lax.all_to_all(send, "gx", split_axis=0, concat_axis=0, tiled=True)
        phase_field, solute_field, own, send = call(
            middle_step_kernel, [SMEM] * 2 + [VMEM] * 8, [field, field, own_shape, send_shape], step_scratch
        )(receive_index, send_index, phase_field, solute_field, heat, got, own, picks, lap0, lap1)
    got = lax.all_to_all(send, "gx", split_axis=0, concat_axis=0, tiled=True)
    phase_field, solute_field = call(
        last_step_kernel, [SMEM] + [VMEM] * 7, [field, field], step_scratch
    )(receive_index, phase_field, solute_field, heat, got, own, lap0, lap1)
    return heat_out, phase_field.reshape(phase.shape), solute_field.reshape(solute.shape)


def solution(mesh):
    grid = P("gx", "gy", "gz")
    tiles = P("gx", "gy", "gz", None, None, None)
    return jax.shard_map(
        local,
        mesh=mesh,
        in_specs=(
            grid,
            grid,
            tiles,
            tiles,
            P("gx", "gy", "gz", None, None),
            P("gx", "gy", "gz", None),
            P("gx", "gy", "gz", None, None),
        ),
        out_specs=(grid, tiles, tiles),
        check_vma=False,
    )
```

```python
import functools

import jax
import jax.numpy as jnp
import numpy as np
from jax import lax
from jax.experimental import pallas as pl
from jax.experimental.pallas import tpu as pltpu
from jax.sharding import PartitionSpec as P

CB = 8
TE = 16
PLANE = TE * TE
SLOTS = 16
FACES = 6
PHASE_STEPS = 4
REC = 24

RATE = 0.16
ORDER_SPEED = 0.1
SOLUTE_RATE = 0.15
COUPLING = 0.5
REJECTION = 0.5

F32 = jnp.float32
BF16 = jnp.bfloat16
VMEM = pl.BlockSpec(memory_space=pltpu.VMEM)
SMEM = pl.BlockSpec(memory_space=pltpu.SMEM)
ANY = pl.BlockSpec(memory_space=pl.ANY)


def plane_lane(face):
    j = np.arange(TE)
    return [j, PLANE - TE + j, j * TE, j * TE + TE - 1][face - 2]


def constant_tables():
    pick = np.zeros((2, PLANE, 256), np.float32)
    place = np.zeros((2, 128, PLANE), np.float32)
    for field in range(2):
        for face in range(2, 6):
            at = field * 64 + (face - 2) * TE + np.arange(TE)
            pick[field, plane_lane(face ^ 1), at] = 1.0
            pick[field, plane_lane(face), 128 + at] = 1.0
            place[field, at, plane_lane(face)] = 1.0
    y, z = np.divmod(np.arange(PLANE), TE)
    dy, dz = np.abs(y[:, None] - y[None, :]), np.abs(z[:, None] - z[None, :])
    stencil = ((dy + dz) == 1).astype(np.float32)
    lane = np.arange(128)
    spread = (lane[:, None] % CB == z[None, :] // 2).astype(np.float32)
    return pick, place, stencil, spread


def tables():
    pick, place, stencil, spread = constant_tables()
    picks = np.concatenate([pick[0], pick[0], pick[1], pick[1]], axis=0)
    laps = [np.concatenate([stencil, stencil, place[f], place[f]], axis=0) for f in range(2)]
    spreads = np.concatenate([spread, spread], axis=0)
    return (
        jnp.asarray(picks, BF16),
        jnp.asarray(laps[0], BF16),
        jnp.asarray(laps[1], BF16),
        jnp.asarray(spreads, BF16),
    )


def halves(value):
    high = value.astype(BF16)
    return high, (value - high.astype(F32)).astype(BF16)


def dot(a, b):
    return jnp.dot(a, b, preferred_element_type=F32)


def temperature(h):
    return jnp.minimum(h, 0.0) + jnp.maximum(h - 1.0, 0.0)


def iota(shape, dim):
    return lax.broadcasted_iota(jnp.int32, shape, dim)


def to_lanes(column):
    bx, by, _ = column.shape
    diagonal = iota((bx, by, 128), 1) == iota((bx, by, 128), 2)
    return jnp.sum(jnp.where(diagonal, column, 0.0), axis=1)


def to_column(line, by):
    bx = line.shape[0]
    diagonal = iota((bx, by, 128), 1) == iota((bx, by, 128), 2)
    return jnp.sum(jnp.where(diagonal, line[:, None, :], 0.0), axis=2, keepdims=True)


def conduct(h, k, xlo, xhi, ylo, yhi, zlo, zhi):
    bx, by, bz = h.shape
    t = temperature(h)
    row, lane = iota((bx, by, bz), 1), iota((bx, by, bz), 2)
    if bx > 1:
        total = jnp.concatenate([xlo, t[:-1]], axis=0) + jnp.concatenate([t[1:], xhi], axis=0)
    else:
        total = xlo + xhi
    total += jnp.where(row == 0, ylo[:, None, :], pltpu.roll(t, 1, 1))
    total += jnp.where(row == by - 1, yhi[:, None, :], pltpu.roll(t, by - 1, 1))
    total += jnp.where(lane == 0, to_column(zlo, by), pltpu.roll(t, 1, 2))
    total += jnp.where(lane == bz - 1, to_column(zhi, by), pltpu.roll(t, bz - 1, 2))
    return h + RATE * k * (total - 6.0 * t)


def sublanes(value, y):
    return jnp.concatenate([value[x, y : y + 1, :] for x in range(value.shape[0])], axis=0)


def side_blocks(h, k):
    by, bz = h.shape[1:]
    return [
        (sublanes(h, 0), sublanes(h, 1), sublanes(k, 0)),
        (sublanes(h, by - 1), sublanes(h, by - 2), sublanes(k, by - 1)),
        (to_lanes(h[:, :, 0:1]), to_lanes(h[:, :, 1:2]), to_lanes(k[:, :, 0:1])),
        (to_lanes(h[:, :, bz - 1 : bz]), to_lanes(h[:, :, bz - 2 : bz - 1]), to_lanes(k[:, :, bz - 1 : bz])),
    ]


def column_of(row):
    square = (row.shape[1], row.shape[1])
    return jnp.sum(jnp.where(iota(square, 0) == iota(square, 1), row, 0.0), axis=1, keepdims=True)


def write_tables(block_cap, source, block, neighbour, asked, table, senders):
    me = lax.axis_index("gx").astype(F32)
    count, records = asked.shape[0], senders.shape[0]
    cap = float(records // count)
    square = (SLOTS, SLOTS)
    before = iota(square, 0) < iota(square, 1)
    slot = iota((1, SLOTS), 1).astype(F32)
    source_row, block_column = source[...].astype(F32), column_of(block[...].astype(F32))
    source_column = column_of(source_row)
    rank = jnp.sum(
        jnp.where((source_column == source_row) & before, 1.0, 0.0), axis=0, keepdims=True
    )
    rank_column = column_of(rank)
    lane = iota((SLOTS, 128), 1).astype(F32)
    for owner in range(count):
        hit = (source_column == float(owner)) & (rank_column == lane)
        asked[owner : owner + 1, :] = jnp.sum(jnp.where(hit, block_column, 0.0), axis=0, keepdims=True)
    table[6:7, 0:SLOTS] = source[...]
    table[7:8, 0:SLOTS] = rank.astype(jnp.int32)
    sent = jnp.zeros((records, 128), F32)
    for face in range(FACES):
        number = neighbour[face]
        owner_row, number_row = (number >> 4).astype(F32), number.astype(F32)
        owner_column, number_column = column_of(owner_row), column_of(number_row)
        other_row = (number_row >= 0.0) & (owner_row != me)
        alike = (owner_column == owner_row) & (owner_column >= 0.0) & (owner_column != me)
        receive_rank = jnp.sum(
            jnp.where(alike & (number_column < number_row), 1.0, 0.0), axis=0, keepdims=True
        )
        send_rank = jnp.sum(jnp.where(alike & before, 1.0, 0.0), axis=0, keepdims=True)
        here = records + (number_row - owner_row * SLOTS)
        receive = jnp.where(owner_row == me, here, owner_row * cap + receive_rank)
        receive = jnp.where(number_row < 0.0, records + SLOTS + slot, receive)
        table[face : face + 1, 0:SLOTS] = receive.astype(jnp.int32)
        key = jnp.where(other_row, owner_row * cap + send_rank, -1.0)
        hit = iota((records, SLOTS), 0).astype(F32) == key
        tile = jnp.sum(jnp.where(hit, slot, 0.0), axis=1, keepdims=True)
        sent = jnp.where(iota(sent.shape, 1) == (face ^ 1), tile, sent)
    senders[...] = sent.astype(jnp.int32)


def sides_kernel(
    sizes, block_cap, source, block, neighbour, h_far, k_far, send, asked, table, senders, h, k, sems
):
    ny, nz = sizes
    my_y, my_z = lax.axis_index("gy"), lax.axis_index("gz")
    bx = h.shape[0]
    copies = []
    for x in range(bx):
        copies.append(pltpu.make_async_copy(h_far.at[x], h.at[x], sems.at[x]))
        copies.append(pltpu.make_async_copy(k_far.at[x], k.at[x], sems.at[bx + x]))
    for copy in copies:
        copy.start()
    write_tables(block_cap, source, block, neighbour, asked, table, senders)
    for copy in copies:
        copy.wait()
    blocks = side_blocks(h[...], k[...])
    for y in range(ny):
        for z in range(nz):
            for part in range(3):
                ylo, yhi, zlo, zhi = [block[part] for block in blocks]
                chosen = jnp.where(
                    my_y == y, jnp.where(z < my_z, zlo, zhi), jnp.where(y < my_y, ylo, yhi)
                )
                send[y * nz + z, part * bx : part * bx + bx, :] = chosen


def side_reader(sizes, got, bx):
    ny, nz = sizes
    my_y, my_z = lax.axis_index("gy"), lax.axis_index("gz")

    def read(dy, dz, part=0):
        y, z = my_y + dy, my_z + dz
        inside = (y >= 0) & (y < ny) & (z >= 0) & (z < nz)
        at = jnp.where(inside, y * nz + z, 0)
        return jnp.where(inside, got[at, part * bx : part * bx + bx, :], 0.0)

    return read


def layers_kernel(sizes, h, k, got, asked, _, send):
    bx, by, bz = h.shape
    me = lax.axis_index("gx")
    read = side_reader(sizes, got, bx)
    around = [read(-1, 0), read(1, 0), read(0, -1), read(0, 1)]
    for owner in range(send.shape[0]):
        low = owner < me
        layers = [(h[0], h[bx - 1]), (h[1], h[bx - 2]), (k[0], k[bx - 1])]
        for part, (lower, upper) in enumerate(layers):
            send[owner, part * by : part * by + by, :] = jnp.where(low, lower, upper)
        for number, side in enumerate(around):
            line = jnp.where(low, side[0:1, :], side[bx - 1 : bx, :])
            send[owner, 3 * by + number : 3 * by + number + 1, :] = line
        send[owner, 3 * by + 4 : 3 * by + 5, :] = asked[owner : owner + 1, :]
        send[owner, 3 * by + 5 : 3 * by + 8, :] = jnp.zeros((3, bz), F32)


def block_layout(cap):
    parts = 128 // CB // cap
    return parts, CB // parts


def flat_step(h, k, inner, outer, first, last, before, after, length):
    bx, lanes = h.shape
    t = temperature(h)
    row, lane = iota(h.shape, 0), iota(h.shape, 1)
    total = temperature(inner) + temperature(outer)
    total += jnp.where(row == 0, temperature(first), pltpu.roll(t, 1, 0))
    total += jnp.where(row == bx - 1, temperature(last), pltpu.roll(t, bx - 1, 0))
    total += jnp.where(lane == 0, temperature(before), pltpu.roll(t, 1, 1))
    total += jnp.where(lane == length - 1, temperature(after), pltpu.roll(t, lanes - 1, 1))
    return h + RATE * k * (total - 6.0 * t)


def heat_kernel(cap, sizes, request, h, k, got, got_x, packed, out, send, held):
    bx, by, bz = h.shape
    h0, k0 = h[...], k[...]
    read = side_reader(sizes, got, bx)
    count, me = got_x.shape[0], lax.axis_index("gx")
    layers, lines = [], []
    for owner in (me - 1, me + 1):
        inside = (owner >= 0) & (owner < count)
        beside = jnp.where(inside, got_x[jnp.where(inside, owner, 0)], 0.0)
        layers.append([beside[part * by : part * by + by, :][None] for part in range(3)])
        lines.append([beside[3 * by + n : 3 * by + n + 1, :] for n in range(4)])
    y_sides = [[read(d, 0, part) for part in range(3)] for d in (-1, 1)]
    z_sides = [[read(0, d, part) for part in range(3)] for d in (-1, 1)]
    corner = [[read(dy, dz) for dz in (-1, 1)] for dy in (-1, 1)]
    to_first = [[pltpu.roll(c[0], 1, 1), c[1]] for c in corner]
    y_inner = [sublanes(h0, 0), sublanes(h0, by - 1)]
    z_inner = [to_lanes(h0[:, :, 0:1]), to_lanes(h0[:, :, bz - 1 : bz])]

    sides = [temperature(layers[0][0]), temperature(layers[1][0])]
    sides += [temperature(side[0]) for side in y_sides + z_sides]
    h1 = conduct(h0, k0, *sides)
    next_sides = []
    for side in range(2):
        near, far, near_k = layers[side]
        across = [temperature(far), temperature(h0[0:1])]
        if side:
            across = [temperature(h0[bx - 1 : bx]), temperature(far)]
        next_sides.append(conduct(near, near_k, *across, *[temperature(line) for line in lines[side]]))
    for side in range(2):
        near, far, near_k = y_sides[side]
        ends = [to_first[side][0], pltpu.roll(to_first[side][1], bz - 1, 1)]
        next_sides.append(
            flat_step(near, near_k, y_inner[side], far, lines[0][side], lines[1][side], *ends, bz)
        )
    for side in range(2):
        near, far, near_k = z_sides[side]
        ends = [to_first[0][side], pltpu.roll(to_first[1][side], by - 1, 1)]
        next_sides.append(
            flat_step(near, near_k, z_inner[side], far, lines[0][2 + side], lines[1][2 + side], *ends, by)
        )
    h2 = conduct(h1, k0, *[temperature(side) for side in next_sides])
    out[...] = h2

    held[...] = temperature(h2).reshape(bx, by // CB, CB, bz)
    parts, deep = block_layout(cap)
    nby, nbz = by // CB, bz // CB
    group = iota((deep, CB, bz), 2) // CB
    for owner in range(send.shape[0]):
        total = jnp.zeros((deep, CB, bz), F32)
        for rank in range(cap):
            block = request[owner, rank]
            a, b, c = block // (nby * nbz), (block // nbz) % nby, block % nbz
            for part in range(parts):
                at = rank * parts + part
                patch = held[pl.ds(a * CB + part * deep, deep), b]
                moved = pltpu.roll(patch, (CB * at - CB * c + bz) % bz, 2)
                total = jnp.where(group == at, moved, total)
        behind = packed.shape[1]
        send[owner, 0:behind, :] = packed[owner]
        send[owner, behind:, :] = total.reshape(deep * CB, bz)


def write_records(phase, solute, picks, own):
    flat = [f.reshape(SLOTS * TE, PLANE) for f in (phase, solute)]
    parts = jnp.concatenate([*halves(flat[0]), *halves(flat[1])], axis=1)
    planes = dot(parts, picks)
    own[0:SLOTS, 0:TE, :] = planes[:, 0:128].reshape(SLOTS, TE, 128)
    own[SLOTS : 2 * SLOTS, 0:TE, :] = planes[:, 128:256].reshape(SLOTS, TE, 128)
    for face in range(2):
        for number, field in enumerate((phase, solute)):
            for half in range(2):
                row = TE + face * 4 + number * 2 + half
                lanes = slice(half * 128, half * 128 + 128)
                near, far = (0, TE - 1) if face == 0 else (TE - 1, 0)
                own[0:SLOTS, row : row + 1, :] = field[:, far : far + 1, lanes]
                own[SLOTS : 2 * SLOTS, row : row + 1, :] = field[:, near : near + 1, lanes]


def merge_record(source, number):
    side = (iota((TE, 128), 1) % 64) // TE
    out = source[number(2), 0:TE, :]
    for face in range(3, 6):
        out = jnp.where(side == face - 2, source[number(face), 0:TE, :], out)
    edge = jnp.where(
        iota((8, 128), 0) < 4, source[number(0), TE:REC, :], source[number(1), TE:REC, :]
    )
    return out, edge


def pack(own, senders, send):
    records = senders.shape[0]
    cap = records // send.shape[0]
    for record in range(records):
        out, edge = merge_record(own, lambda face: senders[record, face])
        owner, row = record // cap, record % cap * REC
        send[owner, row : row + TE, :] = out
        send[owner, row + TE : row + REC, :] = edge


def first_pack_kernel(senders, phase, solute, picks, own, send):
    write_records(phase[...], solute[...], picks[...], own)
    pack(own, senders, send)


def take_heat(cap, table, got, spreads, held, heat):
    parts, deep = block_layout(cap)
    first = got.shape[1] - deep * CB
    group = iota((CB, 128), 1) // CB
    for slot in range(SLOTS):
        source, rank = table[6, slot], table[7, slot]
        for x in range(CB):
            row = first + (x % deep) * CB
            patch = got[source, row : row + CB, :]
            held[slot * CB + x] = jnp.where(group == rank * parts + x // deep, patch, 0.0)
    rows = held[...].reshape(SLOTS * CB * CB, 128)
    wide = dot(jnp.concatenate(halves(rows), axis=1), spreads)
    wide = wide.reshape(SLOTS * CB, CB, PLANE)
    keep = iota(wide.shape, 1) == iota(wide.shape, 2) // TE // 2
    coarse = jnp.sum(jnp.where(keep, wide, 0.0), axis=1)
    for half in range(2):
        for odd in range(2):
            heat[half, pl.ds(odd, SLOTS * CB, 2), :] = coarse[:, half * 128 : half * 128 + 128]


def step(table, phase, solute, heat, got, own, laps, all_records, ghosts):
    records = all_records.shape[0] - 2 * SLOTS
    count = got.shape[0]
    cap = records // count
    for owner in range(count):
        mine = got[owner, 0 : cap * REC, :]
        all_records[owner * cap : owner * cap + cap] = mine.reshape(cap, REC, 128)
    all_records[records : records + 2 * SLOTS] = own[...]
    for slot in range(SLOTS):
        out, edge = merge_record(all_records, lambda face: table[face, slot])
        ghosts[slot, 0:TE, :] = out
        ghosts[slot, TE:REC, :] = edge
    beside = jnp.concatenate(halves(ghosts[:, 0:TE, :].reshape(SLOTS * TE, 128)), axis=1)
    row = iota((SLOTS, TE, PLANE), 1)
    lap = []
    for number, (field, table) in enumerate(((phase, laps[0]), (solute, laps[1]))):
        flat = field.reshape(SLOTS * TE, PLANE)
        total = dot(jnp.concatenate([*halves(flat), beside], axis=1), table)
        total = total.reshape(SLOTS, TE, PLANE) - 6.0 * field
        sides = []
        for face in range(2):
            at = TE + face * 4 + number * 2
            sides.append(
                jnp.concatenate([ghosts[:, at : at + 1, :], ghosts[:, at + 1 : at + 2, :]], axis=2)
            )
        total += jnp.where(row == 0, sides[0], pltpu.roll(field, 1, 1))
        total += jnp.where(row == TE - 1, sides[1], pltpu.roll(field, TE - 1, 1))
        lap.append(total)
    warm = jnp.concatenate([heat[0], heat[1]], axis=1).reshape(SLOTS, TE, PLANE)
    squared = 1.0 - phase * phase
    new_phase = phase + ORDER_SPEED * (
        lap[0] + phase - phase * phase * phase - COUPLING * (warm + solute) * squared * squared
    )
    new_solute = solute + SOLUTE_RATE * lap[1] + REJECTION * (new_phase - phase)
    return new_phase, new_solute


def first_step_kernel(
    cap, table, senders, phase, solute, got, own, picks, lap0, lap1, spreads, brick,
    phase_out, solute_out, heat_out, own_out, send, brick_out, all_records, ghosts, held, sem,
):
    copy = pltpu.make_async_copy(brick, brick_out, sem)
    copy.start()
    take_heat(cap, table, got, spreads[...], held, heat_out)
    new_phase, new_solute = step(
        table, phase[...], solute[...], heat_out[...], got, own, (lap0[...], lap1[...]),
        all_records, ghosts,
    )
    phase_out[...] = new_phase
    solute_out[...] = new_solute
    write_records(new_phase, new_solute, picks[...], own_out)
    pack(own_out, senders, send)
    copy.wait()


def middle_step_kernel(
    table, senders, phase, solute, heat, got, own, picks, lap0, lap1,
    phase_out, solute_out, own_out, send, all_records, ghosts,
):
    new_phase, new_solute = step(
        table, phase[...], solute[...], heat[...], got, own, (lap0[...], lap1[...]),
        all_records, ghosts,
    )
    phase_out[...] = new_phase
    solute_out[...] = new_solute
    write_records(new_phase, new_solute, picks[...], own_out)
    pack(own_out, senders, send)


def last_step_kernel(
    table, phase, solute, heat, got, own, lap0, lap1, phase_out, solute_out, all_records, ghosts
):
    new_phase, new_solute = step(
        table, phase[...], solute[...], heat[...], got, own, (lap0[...], lap1[...]),
        all_records, ghosts,
    )
    phase_out[...] = new_phase
    solute_out[...] = new_solute


def call(kernel, in_specs, out_shapes, scratch=(), out_specs=None, mib=16):
    return pl.pallas_call(
        kernel,
        out_shape=out_shapes,
        in_specs=in_specs,
        out_specs=out_specs or jax.tree.map(lambda _: VMEM, out_shapes),
        scratch_shapes=list(scratch),
        compiler_params=pltpu.CompilerParams(vmem_limit_bytes=mib * 1024 * 1024),
    )


def shape(*dims):
    return jax.ShapeDtypeStruct(dims, F32)


def local(enthalpy, conductivity, phase, solute, tile_source, tile_block, tile_neighbour):
    count = lax.axis_size("gx")
    sizes = (lax.axis_size("gy"), lax.axis_size("gz"))
    plane_cap = -(-SLOTS // (count - 1))
    block_cap = 2 * SLOTS // count
    records = count * plane_cap
    bx, by, bz = enthalpy.shape
    picks, lap0, lap1, spreads = tables()

    integers = functools.partial(jax.ShapeDtypeStruct, dtype=jnp.int32)
    sides, asked, table, senders = call(
        functools.partial(sides_kernel, sizes, block_cap),
        [VMEM] * 3 + [ANY] * 2,
        [
            shape(sizes[0] * sizes[1], 3 * bx, 128),
            shape(count, 128),
            integers((8, 128)),
            integers((records, 128)),
        ],
        [pltpu.VMEM((bx, by, bz), F32)] * 2 + [pltpu.SemaphoreType.DMA((2 * bx,))],
        mib=56,
    )(
        tile_source.reshape(1, SLOTS),
        tile_block.reshape(1, SLOTS),
        jnp.transpose(tile_neighbour, (0, 1, 4, 2, 3)).reshape(FACES, 1, SLOTS),
        enthalpy,
        conductivity,
    )
    sides = lax.all_to_all(sides, ("gy", "gz"), split_axis=0, concat_axis=0, tiled=True)

    phase_field = phase.reshape(SLOTS, TE, PLANE)
    solute_field = solute.reshape(SLOTS, TE, PLANE)
    own_shape, send_shape = shape(2 * SLOTS, REC, 128), shape(count, plane_cap * REC, 128)
    own, packed = call(first_pack_kernel, [SMEM] + [VMEM] * 3, [own_shape, send_shape])(
        senders, phase_field, solute_field, picks
    )

    layers = call(
        functools.partial(layers_kernel, sizes),
        [VMEM] * 4 + [ANY],
        shape(count, 3 * by + 8, bz),
    )(enthalpy, conductivity, sides, asked, packed)
    layers = lax.all_to_all(layers, "gx", split_axis=0, concat_axis=0, tiled=True)
    request = layers[:, 3 * by + 4, :block_cap].astype(jnp.int32)
    _, deep = block_layout(block_cap)
    brick = shape(bx, by, bz)
    heated, send = call(
        functools.partial(heat_kernel, block_cap, sizes),
        [SMEM] + [VMEM] * 5,
        [brick, shape(count, plane_cap * REC + deep * CB, 128)],
        [pltpu.VMEM((bx, by // CB, CB, bz), F32)],
    )(request, enthalpy, conductivity, sides, layers, packed)
    got = lax.all_to_all(send, "gx", split_axis=0, concat_axis=0, tiled=True)

    field = shape(SLOTS, TE, PLANE)
    step_scratch = [
        pltpu.VMEM((records + 2 * SLOTS, REC, 128), F32),
        pltpu.VMEM((SLOTS, REC, 128), F32),
    ]
    phase_field, solute_field, heat, own, send, heat_out = call(
        functools.partial(first_step_kernel, block_cap),
        [SMEM] * 2 + [VMEM] * 9,
        [field, field, shape(2, SLOTS * TE, 128), own_shape, send_shape, brick],
        step_scratch + [pltpu.VMEM((SLOTS * CB, CB, 128), F32), pltpu.SemaphoreType.DMA],
        [VMEM] * 5 + [ANY],
    )(
        table, senders, phase_field, solute_field, got, own, picks, lap0, lap1, spreads,
        heated,
    )
    for _ in range(PHASE_STEPS - 2):
        got = lax.all_to_all(send, "gx", split_axis=0, concat_axis=0, tiled=True)
        phase_field, solute_field, own, send = call(
            middle_step_kernel, [SMEM] * 2 + [VMEM] * 8, [field, field, own_shape, send_shape], step_scratch
        )(table, senders, phase_field, solute_field, heat, got, own, picks, lap0, lap1)
    got = lax.all_to_all(send, "gx", split_axis=0, concat_axis=0, tiled=True)
    phase_field, solute_field = call(
        last_step_kernel, [SMEM] + [VMEM] * 7, [field, field], step_scratch
    )(table, phase_field, solute_field, heat, got, own, lap0, lap1)
    return heat_out, phase_field.reshape(phase.shape), solute_field.reshape(solute.shape)


def solution(mesh):
    grid = P("gx", "gy", "gz")
    tiles = P("gx", "gy", "gz", None, None, None)
    return jax.shard_map(
        local,
        mesh=mesh,
        in_specs=(
            grid,
            grid,
            tiles,
            tiles,
            P("gx", "gy", "gz", None, None),
            P("gx", "gy", "gz", None),
            P("gx", "gy", "gz", None, None),
        ),
        out_specs=(grid, tiles, tiles),
        check_vma=False,
    )
```

```python
import functools

import jax
import jax.numpy as jnp
import numpy as np
from jax import lax
from jax.experimental import pallas as pl
from jax.experimental.pallas import tpu as pltpu
from jax.sharding import PartitionSpec as P

CB = 8
TE = 16
PLANE = TE * TE
SLOTS = 16
FACES = 6
PHASE_STEPS = 4
REC = 24

RATE = 0.16
ORDER_SPEED = 0.1
SOLUTE_RATE = 0.15
COUPLING = 0.5
REJECTION = 0.5

F32 = jnp.float32
BF16 = jnp.bfloat16
VMEM = pl.BlockSpec(memory_space=pltpu.VMEM)
SMEM = pl.BlockSpec(memory_space=pltpu.SMEM)
ANY = pl.BlockSpec(memory_space=pl.ANY)


def plane_lane(face):
    j = np.arange(TE)
    return [j, PLANE - TE + j, j * TE, j * TE + TE - 1][face - 2]


def constant_tables():
    pick = np.zeros((2, PLANE, 256), np.float32)
    place = np.zeros((2, 128, PLANE), np.float32)
    for field in range(2):
        for face in range(2, 6):
            at = field * 64 + (face - 2) * TE + np.arange(TE)
            pick[field, plane_lane(face ^ 1), at] = 1.0
            pick[field, plane_lane(face), 128 + at] = 1.0
            place[field, at, plane_lane(face)] = 1.0
    y, z = np.divmod(np.arange(PLANE), TE)
    dy, dz = np.abs(y[:, None] - y[None, :]), np.abs(z[:, None] - z[None, :])
    stencil = ((dy + dz) == 1).astype(np.float32)
    lane = np.arange(128)
    spread = (lane[:, None] % CB == z[None, :] // 2).astype(np.float32)
    return pick, place, stencil, spread


def tables():
    pick, place, stencil, spread = constant_tables()
    place = np.concatenate([place[0], place[1]], axis=1)
    return (
        jnp.asarray(np.concatenate([pick[0], pick[1]], axis=0), BF16),
        jnp.asarray(stencil, BF16),
        jnp.asarray(np.concatenate([place, place], axis=0), BF16),
        jnp.asarray(np.concatenate([spread, spread], axis=0), BF16),
    )


def halves(value):
    high = value.astype(BF16)
    return high, (value - high.astype(F32)).astype(BF16)


def dot(a, b):
    return jnp.dot(a, b, preferred_element_type=F32)


def temperature(h):
    return jnp.minimum(h, 0.0) + jnp.maximum(h - 1.0, 0.0)


def iota(shape, dim):
    return lax.broadcasted_iota(jnp.int32, shape, dim)


def to_lanes(column):
    bx, by, _ = column.shape
    diagonal = iota((bx, by, 128), 1) == iota((bx, by, 128), 2)
    return jnp.sum(jnp.where(diagonal, column, 0.0), axis=1)


def to_column(line, by):
    bx = line.shape[0]
    diagonal = iota((bx, by, 128), 1) == iota((bx, by, 128), 2)
    return jnp.sum(jnp.where(diagonal, line[:, None, :], 0.0), axis=2, keepdims=True)


def conduct(h, k, xlo, xhi, ylo, yhi, zlo, zhi):
    bx, by, bz = h.shape
    t = temperature(h)
    row, lane = iota((bx, by, bz), 1), iota((bx, by, bz), 2)
    if bx > 1:
        total = jnp.concatenate([xlo, t[:-1]], axis=0) + jnp.concatenate([t[1:], xhi], axis=0)
    else:
        total = xlo + xhi
    total += jnp.where(row == 0, ylo[:, None, :], pltpu.roll(t, 1, 1))
    total += jnp.where(row == by - 1, yhi[:, None, :], pltpu.roll(t, by - 1, 1))
    total += jnp.where(lane == 0, to_column(zlo, by), pltpu.roll(t, 1, 2))
    total += jnp.where(lane == bz - 1, to_column(zhi, by), pltpu.roll(t, bz - 1, 2))
    return h + RATE * k * (total - 6.0 * t)


def sublanes(value, y):
    return jnp.concatenate([value[x, y : y + 1, :] for x in range(value.shape[0])], axis=0)


def side_blocks(h, k):
    by, bz = h.shape[1:]
    return [
        (sublanes(h, 0), sublanes(h, 1), sublanes(k, 0)),
        (sublanes(h, by - 1), sublanes(h, by - 2), sublanes(k, by - 1)),
        (to_lanes(h[:, :, 0:1]), to_lanes(h[:, :, 1:2]), to_lanes(k[:, :, 0:1])),
        (to_lanes(h[:, :, bz - 1 : bz]), to_lanes(h[:, :, bz - 2 : bz - 1]), to_lanes(k[:, :, bz - 1 : bz])),
    ]


def column_of(row):
    square = (row.shape[1], row.shape[1])
    return jnp.sum(jnp.where(iota(square, 0) == iota(square, 1), row, 0.0), axis=1, keepdims=True)


def write_tables(plane_cap, source, block, neighbour, asked, table):
    me = lax.axis_index("gx").astype(F32)
    count = asked.shape[0]
    records = count * plane_cap
    cap = float(plane_cap)
    square = (SLOTS, SLOTS)
    before = iota(square, 0) < iota(square, 1)
    slot = iota((1, SLOTS), 1).astype(F32)
    source_row, block_column = source[...].astype(F32), column_of(block[...].astype(F32))
    source_column = column_of(source_row)
    rank = jnp.sum(
        jnp.where((source_column == source_row) & before, 1.0, 0.0), axis=0, keepdims=True
    )
    rank_column = column_of(rank)
    lane = iota((SLOTS, 128), 1).astype(F32)
    for shift in range(count):
        owner = me + float(shift)
        owner = jnp.where(owner >= float(count), owner - float(count), owner)
        hit = (source_column == owner) & (rank_column == lane)
        asked[shift : shift + 1, :] = jnp.sum(jnp.where(hit, block_column, 0.0), axis=0, keepdims=True)
    table[6:7, 0:SLOTS] = source[...]
    table[7:8, 0:SLOTS] = rank.astype(jnp.int32)
    slot_column = iota((SLOTS, records), 0).astype(F32)
    for face in range(FACES):
        number = neighbour[face]
        owner_row, number_row = (number >> 4).astype(F32), number.astype(F32)
        owner_column, number_column = column_of(owner_row), column_of(number_row)
        other_row = (number_row >= 0.0) & (owner_row != me)
        alike = (owner_column == owner_row) & (owner_column >= 0.0) & (owner_column != me)
        receive_rank = jnp.sum(
            jnp.where(alike & (number_column < number_row), 1.0, 0.0), axis=0, keepdims=True
        )
        send_rank = jnp.sum(jnp.where(alike & before, 1.0, 0.0), axis=0, keepdims=True)
        here = records + (number_row - owner_row * SLOTS)
        receive = jnp.where(owner_row == me, here, owner_row * cap + receive_rank)
        receive = jnp.where(number_row < 0.0, records + SLOTS + slot, receive)
        table[face : face + 1, 0:SLOTS] = receive.astype(jnp.int32)
        key = jnp.where(other_row, owner_row * cap + send_rank, -1.0)
        hit = iota((SLOTS, records), 1).astype(F32) == column_of(key)
        tile = jnp.sum(jnp.where(hit, slot_column, 0.0), axis=0, keepdims=True)
        table[face ^ 1 : (face ^ 1) + 1, SLOTS : SLOTS + records] = tile.astype(jnp.int32)


def sides_kernel(
    sizes, plane_cap, source, block, neighbour, h_far, k_far, send, asked, table, h, k, sems
):
    ny, nz = sizes
    my_y, my_z = lax.axis_index("gy"), lax.axis_index("gz")
    bx = h.shape[0]
    copies = []
    for x in range(bx):
        copies.append(pltpu.make_async_copy(h_far.at[x], h.at[x], sems.at[x]))
        copies.append(pltpu.make_async_copy(k_far.at[x], k.at[x], sems.at[bx + x]))
    for copy in copies:
        copy.start()
    write_tables(plane_cap, source, block, neighbour, asked, table)
    for copy in copies:
        copy.wait()
    blocks = side_blocks(h[...], k[...])
    for y in range(ny):
        for z in range(nz):
            for part in range(3):
                ylo, yhi, zlo, zhi = [block[part] for block in blocks]
                chosen = jnp.where(
                    my_y == y, jnp.where(z < my_z, zlo, zhi), jnp.where(y < my_y, ylo, yhi)
                )
                send[y * nz + z, part * bx : part * bx + bx, :] = chosen


def side_reader(sizes, got, bx):
    ny, nz = sizes
    my_y, my_z = lax.axis_index("gy"), lax.axis_index("gz")

    def read(dy, dz, part=0):
        y, z = my_y + dy, my_z + dz
        inside = (y >= 0) & (y < ny) & (z >= 0) & (z < nz)
        at = jnp.where(inside, y * nz + z, 0)
        return jnp.where(inside, got[at, part * bx : part * bx + bx, :], 0.0)

    return read


def layers_kernel(sizes, h, k, got, asked, _, down, up, *farther):
    bx, by, bz = h.shape
    count = asked.shape[0]
    read = side_reader(sizes, got, bx)
    around = [read(-1, 0), read(1, 0), read(0, -1), read(0, 1)]
    for out, near, far, shift in ((down, 0, 1, count - 1), (up, bx - 1, bx - 2, 1)):
        out[0:by, :] = h[near]
        out[by : 2 * by, :] = h[far]
        out[2 * by : 3 * by, :] = k[near]
        for number, side in enumerate(around):
            out[3 * by + number : 3 * by + number + 1, :] = side[near : near + 1, :]
        out[3 * by + 4 : 3 * by + 5, :] = asked[shift : shift + 1, :]
        out[3 * by + 5 : 3 * by + 8, :] = jnp.zeros((3, bz), F32)
    for number, out in enumerate(farther):
        out[...] = jnp.broadcast_to(asked[2 + number : 3 + number, :], out.shape)


def block_layout(cap):
    parts = 128 // CB // cap
    return parts, CB // parts


def flat_step(h, k, inner, outer, first, last, before, after, length):
    bx, lanes = h.shape
    t = temperature(h)
    row, lane = iota(h.shape, 0), iota(h.shape, 1)
    total = temperature(inner) + temperature(outer)
    total += jnp.where(row == 0, temperature(first), pltpu.roll(t, 1, 0))
    total += jnp.where(row == bx - 1, temperature(last), pltpu.roll(t, bx - 1, 0))
    total += jnp.where(lane == 0, temperature(before), pltpu.roll(t, 1, 1))
    total += jnp.where(lane == length - 1, temperature(after), pltpu.roll(t, lanes - 1, 1))
    return h + RATE * k * (total - 6.0 * t)


def heat_kernel(cap, sizes, request, h, k, got, low, high, packed, out, send, held):
    bx, by, bz = h.shape
    h0, k0 = h[...], k[...]
    read = side_reader(sizes, got, bx)
    count, me = send.shape[0], lax.axis_index("gx")
    layers, lines = [], []
    for beside, inside in ((low, me > 0), (high, me < count - 1)):
        beside = jnp.where(inside, beside[...], 0.0)
        layers.append([beside[part * by : part * by + by, :][None] for part in range(3)])
        lines.append([beside[3 * by + n : 3 * by + n + 1, :] for n in range(4)])
    y_sides = [[read(d, 0, part) for part in range(3)] for d in (-1, 1)]
    z_sides = [[read(0, d, part) for part in range(3)] for d in (-1, 1)]
    corner = [[read(dy, dz) for dz in (-1, 1)] for dy in (-1, 1)]
    to_first = [[pltpu.roll(c[0], 1, 1), c[1]] for c in corner]
    y_inner = [sublanes(h0, 0), sublanes(h0, by - 1)]
    z_inner = [to_lanes(h0[:, :, 0:1]), to_lanes(h0[:, :, bz - 1 : bz])]

    sides = [temperature(layers[0][0]), temperature(layers[1][0])]
    sides += [temperature(side[0]) for side in y_sides + z_sides]
    h1 = conduct(h0, k0, *sides)
    next_sides = []
    for side in range(2):
        near, far, near_k = layers[side]
        across = [temperature(far), temperature(h0[0:1])]
        if side:
            across = [temperature(h0[bx - 1 : bx]), temperature(far)]
        next_sides.append(conduct(near, near_k, *across, *[temperature(line) for line in lines[side]]))
    for side in range(2):
        near, far, near_k = y_sides[side]
        ends = [to_first[side][0], pltpu.roll(to_first[side][1], bz - 1, 1)]
        next_sides.append(
            flat_step(near, near_k, y_inner[side], far, lines[0][side], lines[1][side], *ends, bz)
        )
    for side in range(2):
        near, far, near_k = z_sides[side]
        ends = [to_first[0][side], pltpu.roll(to_first[1][side], by - 1, 1)]
        next_sides.append(
            flat_step(near, near_k, z_inner[side], far, lines[0][2 + side], lines[1][2 + side], *ends, by)
        )
    h2 = conduct(h1, k0, *[temperature(side) for side in next_sides])
    out[...] = h2

    held[...] = temperature(h2).reshape(bx, by // CB, CB, bz)
    parts, deep = block_layout(cap)
    nby, nbz = by // CB, bz // CB
    group = iota((deep, CB, bz), 2) // CB
    for owner in range(count):
        shift = lax.rem(me - owner + count, count)
        total = jnp.zeros((deep, CB, bz), F32)
        for rank in range(cap):
            block = request[shift, rank]
            a, b, c = block // (nby * nbz), (block // nbz) % nby, block % nbz
            for part in range(parts):
                at = rank * parts + part
                patch = held[pl.ds(a * CB + part * deep, deep), b]
                moved = pltpu.roll(patch, (CB * at - CB * c + bz) % bz, 2)
                total = jnp.where(group == at, moved, total)
        behind = packed.shape[1]
        send[owner, 0:behind, :] = packed[owner]
        send[owner, behind:, :] = total.reshape(deep * CB, bz)


def write_records(phase, solute, picks, own):
    flat = [f.reshape(SLOTS * TE, PLANE) for f in (phase, solute)]
    high, low = halves(jnp.concatenate(flat, axis=1))
    planes = dot(high, picks) + dot(low, picks)
    own[0:SLOTS, 0:TE, :] = planes[:, 0:128].reshape(SLOTS, TE, 128)
    own[SLOTS : 2 * SLOTS, 0:TE, :] = planes[:, 128:256].reshape(SLOTS, TE, 128)
    for face in range(2):
        for number, field in enumerate((phase, solute)):
            for half in range(2):
                row = TE + face * 4 + number * 2 + half
                lanes = slice(half * 128, half * 128 + 128)
                near, far = (0, TE - 1) if face == 0 else (TE - 1, 0)
                own[0:SLOTS, row : row + 1, :] = field[:, far : far + 1, lanes]
                own[SLOTS : 2 * SLOTS, row : row + 1, :] = field[:, near : near + 1, lanes]


def merge_record(source, number):
    side = (iota((TE, 128), 1) % 64) // TE
    out = source[number(2), 0:TE, :]
    for face in range(3, 6):
        out = jnp.where(side == face - 2, source[number(face), 0:TE, :], out)
    edge = jnp.where(
        iota((8, 128), 0) < 4, source[number(0), TE:REC, :], source[number(1), TE:REC, :]
    )
    return out, edge


def pack(own, table, send):
    records = send.shape[0] * (send.shape[1] // REC)
    cap = records // send.shape[0]
    for record in range(records):
        out, edge = merge_record(own, lambda face: table[face, SLOTS + record])
        owner, row = record // cap, record % cap * REC
        send[owner, row : row + TE, :] = out
        send[owner, row + TE : row + REC, :] = edge


def first_pack_kernel(table, phase, solute, picks, own, send):
    write_records(phase[...], solute[...], picks[...], own)
    pack(own, table, send)


def take_heat(cap, table, got, spreads, held, heat):
    parts, deep = block_layout(cap)
    first = got.shape[1] - deep * CB
    group = iota((CB, 128), 1) // CB
    for slot in range(SLOTS):
        source, rank = table[6, slot], table[7, slot]
        for x in range(CB):
            row = first + (x % deep) * CB
            patch = got[source, row : row + CB, :]
            held[slot * CB + x] = jnp.where(group == rank * parts + x // deep, patch, 0.0)
    rows = held[...].reshape(SLOTS * CB * CB, 128)
    wide = dot(jnp.concatenate(halves(rows), axis=1), spreads)
    wide = wide.reshape(SLOTS * CB, CB, PLANE)
    keep = iota(wide.shape, 1) == iota(wide.shape, 2) // TE // 2
    coarse = jnp.sum(jnp.where(keep, wide, 0.0), axis=1)
    for half in range(2):
        for odd in range(2):
            heat[half, pl.ds(odd, SLOTS * CB, 2), :] = coarse[:, half * 128 : half * 128 + 128]


def step(table, phase, solute, heat, got, own, stencil, places, all_records, ghosts):
    records = all_records.shape[0] - 2 * SLOTS
    count = got.shape[0]
    cap = records // count
    for owner in range(count):
        mine = got[owner, 0 : cap * REC, :]
        all_records[owner * cap : owner * cap + cap] = mine.reshape(cap, REC, 128)
    all_records[records : records + 2 * SLOTS] = own[...]
    for slot in range(SLOTS):
        out, edge = merge_record(all_records, lambda face: table[face, slot])
        ghosts[slot, 0:TE, :] = out
        ghosts[slot, TE:REC, :] = edge
    beside = jnp.concatenate(halves(ghosts[:, 0:TE, :].reshape(SLOTS * TE, 128)), axis=1)
    beside = dot(beside, places)
    row = iota((SLOTS, TE, PLANE), 1)
    lap = []
    for number, field in enumerate((phase, solute)):
        high, low = halves(field.reshape(SLOTS * TE, PLANE))
        total = dot(high, stencil) + dot(low, stencil)
        total += beside[:, number * PLANE : number * PLANE + PLANE]
        total = total.reshape(SLOTS, TE, PLANE) - 6.0 * field
        sides = []
        for face in range(2):
            at = TE + face * 4 + number * 2
            sides.append(
                jnp.concatenate([ghosts[:, at : at + 1, :], ghosts[:, at + 1 : at + 2, :]], axis=2)
            )
        total += jnp.where(row == 0, sides[0], pltpu.roll(field, 1, 1))
        total += jnp.where(row == TE - 1, sides[1], pltpu.roll(field, TE - 1, 1))
        lap.append(total)
    warm = jnp.concatenate([heat[0], heat[1]], axis=1).reshape(SLOTS, TE, PLANE)
    squared = 1.0 - phase * phase
    new_phase = phase + ORDER_SPEED * (
        lap[0] + phase - phase * phase * phase - COUPLING * (warm + solute) * squared * squared
    )
    new_solute = solute + SOLUTE_RATE * lap[1] + REJECTION * (new_phase - phase)
    return new_phase, new_solute


def first_step_kernel(
    cap, table, phase, solute, got, own, picks, stencil, places, spreads, brick,
    phase_out, solute_out, heat_out, own_out, send, brick_out, all_records, ghosts, held, sem,
):
    copy = pltpu.make_async_copy(brick, brick_out, sem)
    copy.start()
    take_heat(cap, table, got, spreads[...], held, heat_out)
    new_phase, new_solute = step(
        table, phase[...], solute[...], heat_out[...], got, own, stencil[...], places[...],
        all_records, ghosts,
    )
    phase_out[...] = new_phase
    solute_out[...] = new_solute
    write_records(new_phase, new_solute, picks[...], own_out)
    pack(own_out, table, send)
    copy.wait()


def middle_step_kernel(
    table, phase, solute, heat, got, own, picks, stencil, places,
    phase_out, solute_out, own_out, send, all_records, ghosts,
):
    new_phase, new_solute = step(
        table, phase[...], solute[...], heat[...], got, own, stencil[...], places[...],
        all_records, ghosts,
    )
    phase_out[...] = new_phase
    solute_out[...] = new_solute
    write_records(new_phase, new_solute, picks[...], own_out)
    pack(own_out, table, send)


def last_step_kernel(
    table, phase, solute, heat, got, own, stencil, places, phase_out, solute_out, all_records, ghosts
):
    new_phase, new_solute = step(
        table, phase[...], solute[...], heat[...], got, own, stencil[...], places[...],
        all_records, ghosts,
    )
    phase_out[...] = new_phase
    solute_out[...] = new_solute


def call(kernel, in_specs, out_shapes, scratch=(), out_specs=None, mib=16):
    return pl.pallas_call(
        kernel,
        out_shape=out_shapes,
        in_specs=in_specs,
        out_specs=out_specs or jax.tree.map(lambda _: VMEM, out_shapes),
        scratch_shapes=list(scratch),
        compiler_params=pltpu.CompilerParams(vmem_limit_bytes=mib * 1024 * 1024),
    )


def shape(*dims):
    return jax.ShapeDtypeStruct(dims, F32)


def local(enthalpy, conductivity, phase, solute, tile_source, tile_block, tile_neighbour):
    count = lax.axis_size("gx")
    sizes = (lax.axis_size("gy"), lax.axis_size("gz"))
    plane_cap = -(-SLOTS // (count - 1))
    block_cap = 2 * SLOTS // count
    records = count * plane_cap
    bx, by, bz = enthalpy.shape
    picks, stencil, places, spreads = tables()

    integers = functools.partial(jax.ShapeDtypeStruct, dtype=jnp.int32)
    sides, asked, table = call(
        functools.partial(sides_kernel, sizes, plane_cap),
        [VMEM] * 3 + [ANY] * 2,
        [
            shape(sizes[0] * sizes[1], 3 * bx, 128),
            shape(count, 128),
            integers((8, 128)),
        ],
        [pltpu.VMEM((bx, by, bz), F32)] * 2 + [pltpu.SemaphoreType.DMA((2 * bx,))],
        mib=56,
    )(
        tile_source.reshape(1, SLOTS),
        tile_block.reshape(1, SLOTS),
        jnp.transpose(tile_neighbour, (0, 1, 4, 2, 3)).reshape(FACES, 1, SLOTS),
        enthalpy,
        conductivity,
    )
    sides = lax.all_to_all(sides, ("gy", "gz"), split_axis=0, concat_axis=0, tiled=True)

    phase_field = phase.reshape(SLOTS, TE, PLANE)
    solute_field = solute.reshape(SLOTS, TE, PLANE)
    own_shape, send_shape = shape(2 * SLOTS, REC, 128), shape(count, plane_cap * REC, 128)
    own, packed = call(first_pack_kernel, [SMEM] + [VMEM] * 3, [own_shape, send_shape])(
        table, phase_field, solute_field, picks
    )

    layer = shape(3 * by + 8, bz)
    down, up, *farther = call(
        functools.partial(layers_kernel, sizes),
        [VMEM] * 4 + [ANY],
        [layer, layer] + [shape(8, 128)] * (count - 3),
    )(enthalpy, conductivity, sides, asked, packed)

    def pass_on(value, shift):
        return lax.ppermute(value, "gx", [(i, (i + shift) % count) for i in range(count)])

    from_low, from_high = pass_on(up, 1), pass_on(down, count - 1)
    farther = [pass_on(value, 2 + number) for number, value in enumerate(farther)]
    row = 3 * by + 4
    request = [asked[0:1], from_low[row : row + 1]]
    request += [value[0:1] for value in farther] + [from_high[row : row + 1]]
    request = jnp.concatenate(request, axis=0)[:, :block_cap].astype(jnp.int32)
    _, deep = block_layout(block_cap)
    brick = shape(bx, by, bz)
    heated, send = call(
        functools.partial(heat_kernel, block_cap, sizes),
        [SMEM] + [VMEM] * 6,
        [brick, shape(count, plane_cap * REC + deep * CB, 128)],
        [pltpu.VMEM((bx, by // CB, CB, bz), F32)],
    )(request, enthalpy, conductivity, sides, from_low, from_high, packed)
    got = lax.all_to_all(send, "gx", split_axis=0, concat_axis=0, tiled=True)

    field = shape(SLOTS, TE, PLANE)
    step_scratch = [
        pltpu.VMEM((records + 2 * SLOTS, REC, 128), F32),
        pltpu.VMEM((SLOTS, REC, 128), F32),
    ]
    phase_field, solute_field, heat, own, send, heat_out = call(
        functools.partial(first_step_kernel, block_cap),
        [SMEM] + [VMEM] * 9,
        [field, field, shape(2, SLOTS * TE, 128), own_shape, send_shape, brick],
        step_scratch + [pltpu.VMEM((SLOTS * CB, CB, 128), F32), pltpu.SemaphoreType.DMA],
        [VMEM] * 5 + [ANY],
    )(
        table, phase_field, solute_field, got, own, picks, stencil, places, spreads,
        heated,
    )
    for _ in range(PHASE_STEPS - 2):
        got = lax.all_to_all(send, "gx", split_axis=0, concat_axis=0, tiled=True)
        phase_field, solute_field, own, send = call(
            middle_step_kernel, [SMEM] + [VMEM] * 8, [field, field, own_shape, send_shape], step_scratch
        )(table, phase_field, solute_field, heat, got, own, picks, stencil, places)
    got = lax.all_to_all(send, "gx", split_axis=0, concat_axis=0, tiled=True)
    phase_field, solute_field = call(
        last_step_kernel, [SMEM] + [VMEM] * 7, [field, field], step_scratch
    )(table, phase_field, solute_field, heat, got, own, stencil, places)
    return heat_out, phase_field.reshape(phase.shape), solute_field.reshape(solute.shape)


def solution(mesh):
    grid = P("gx", "gy", "gz")
    tiles = P("gx", "gy", "gz", None, None, None)
    return jax.shard_map(
        local,
        mesh=mesh,
        in_specs=(
            grid,
            grid,
            tiles,
            tiles,
            P("gx", "gy", "gz", None, None),
            P("gx", "gy", "gz", None),
            P("gx", "gy", "gz", None, None),
        ),
        out_specs=(grid, tiles, tiles),
        check_vma=False,
    )
```

```python
import functools

import jax
import jax.numpy as jnp
import numpy as np
from jax import lax
from jax.experimental import pallas as pl
from jax.experimental.pallas import tpu as pltpu
from jax.sharding import PartitionSpec as P

CB = 8
TE = 16
PLANE = TE * TE
SLOTS = 16
FACES = 6
PHASE_STEPS = 4
REC = 24

RATE = 0.16
ORDER_SPEED = 0.1
SOLUTE_RATE = 0.15
COUPLING = 0.5
REJECTION = 0.5

F32 = jnp.float32
BF16 = jnp.bfloat16
VMEM = pl.BlockSpec(memory_space=pltpu.VMEM)
SMEM = pl.BlockSpec(memory_space=pltpu.SMEM)
ANY = pl.BlockSpec(memory_space=pl.ANY)


def plane_lane(face):
    j = np.arange(TE)
    return [j, PLANE - TE + j, j * TE, j * TE + TE - 1][face - 2]


def constant_tables():
    pick = np.zeros((2, PLANE, 256), np.float32)
    place = np.zeros((2, 128, PLANE), np.float32)
    for field in range(2):
        for face in range(2, 6):
            at = field * 64 + (face - 2) * TE + np.arange(TE)
            pick[field, plane_lane(face ^ 1), at] = 1.0
            pick[field, plane_lane(face), 128 + at] = 1.0
            place[field, at, plane_lane(face)] = 1.0
    y, z = np.divmod(np.arange(PLANE), TE)
    dy, dz = np.abs(y[:, None] - y[None, :]), np.abs(z[:, None] - z[None, :])
    stencil = ((dy + dz) == 1).astype(np.float32)
    lane = np.arange(128)
    spread = (lane[:, None] % CB == z[None, :] // 2).astype(np.float32)
    return pick, place, stencil, spread


def tables():
    pick, place, stencil, spread = constant_tables()
    place = np.concatenate([place[0], place[1]], axis=1)
    return (
        jnp.asarray(np.concatenate([pick[0], pick[1]], axis=0), BF16),
        jnp.asarray(stencil, BF16),
        jnp.asarray(np.concatenate([place, place], axis=0), BF16),
        jnp.asarray(np.concatenate([spread, spread], axis=0), BF16),
    )


def halves(value):
    high = value.astype(BF16)
    return high, (value - high.astype(F32)).astype(BF16)


def dot(a, b):
    return jnp.dot(a, b, preferred_element_type=F32)


def temperature(h):
    return jnp.minimum(h, 0.0) + jnp.maximum(h - 1.0, 0.0)


def iota(shape, dim):
    return lax.broadcasted_iota(jnp.int32, shape, dim)


def to_lanes(column):
    bx, by, _ = column.shape
    diagonal = iota((bx, by, 128), 1) == iota((bx, by, 128), 2)
    return jnp.sum(jnp.where(diagonal, column, 0.0), axis=1)


def to_column(line, by):
    bx = line.shape[0]
    diagonal = iota((bx, by, 128), 1) == iota((bx, by, 128), 2)
    return jnp.sum(jnp.where(diagonal, line[:, None, :], 0.0), axis=2, keepdims=True)


def conduct(h, k, xlo, xhi, ylo, yhi, zlo, zhi):
    bx, by, bz = h.shape
    t = temperature(h)
    row, lane = iota((bx, by, bz), 1), iota((bx, by, bz), 2)
    if bx > 1:
        total = jnp.concatenate([xlo, t[:-1]], axis=0) + jnp.concatenate([t[1:], xhi], axis=0)
    else:
        total = xlo + xhi
    total += jnp.where(row == 0, ylo[:, None, :], pltpu.roll(t, 1, 1))
    total += jnp.where(row == by - 1, yhi[:, None, :], pltpu.roll(t, by - 1, 1))
    total += jnp.where(lane == 0, to_column(zlo, by), pltpu.roll(t, 1, 2))
    total += jnp.where(lane == bz - 1, to_column(zhi, by), pltpu.roll(t, bz - 1, 2))
    return h + RATE * k * (total - 6.0 * t)


def sublanes(value, y):
    return jnp.concatenate([value[x, y : y + 1, :] for x in range(value.shape[0])], axis=0)


def side_blocks(h, k):
    by, bz = h.shape[1:]
    return [
        (sublanes(h, 0), sublanes(h, 1), sublanes(k, 0)),
        (sublanes(h, by - 1), sublanes(h, by - 2), sublanes(k, by - 1)),
        (to_lanes(h[:, :, 0:1]), to_lanes(h[:, :, 1:2]), to_lanes(k[:, :, 0:1])),
        (to_lanes(h[:, :, bz - 1 : bz]), to_lanes(h[:, :, bz - 2 : bz - 1]), to_lanes(k[:, :, bz - 1 : bz])),
    ]


def column_of(row):
    square = (row.shape[1], row.shape[1])
    return jnp.sum(jnp.where(iota(square, 0) == iota(square, 1), row, 0.0), axis=1, keepdims=True)


def write_tables(plane_cap, source, block, neighbour, asked, table):
    me = lax.axis_index("gx").astype(F32)
    count = asked.shape[0]
    records = (count - 1) * plane_cap
    cap = float(plane_cap)

    def wrapped(shift):
        return jnp.where(shift < 0.0, shift + float(count), shift)

    square = (SLOTS, SLOTS)
    before = iota(square, 0) < iota(square, 1)
    slot = iota((1, SLOTS), 1).astype(F32)
    source_row, block_column = source[...].astype(F32), column_of(block[...].astype(F32))
    source_column = column_of(source_row)
    rank = jnp.sum(
        jnp.where((source_column == source_row) & before, 1.0, 0.0), axis=0, keepdims=True
    )
    rank_column = column_of(rank)
    lane = iota((SLOTS, 128), 1).astype(F32)
    for shift in range(count):
        hit = (wrapped(source_column - me) == float(shift)) & (rank_column == lane)
        asked[shift : shift + 1, :] = jnp.sum(jnp.where(hit, block_column, 0.0), axis=0, keepdims=True)
    table[6:7, 0:SLOTS] = wrapped(me - source_row).astype(jnp.int32)
    table[7:8, 0:SLOTS] = rank.astype(jnp.int32)
    slot_column = iota((SLOTS, records), 0).astype(F32)
    for face in range(FACES):
        number = neighbour[face]
        owner_row, number_row = (number >> 4).astype(F32), number.astype(F32)
        owner_column, number_column = column_of(owner_row), column_of(number_row)
        other_row = (number_row >= 0.0) & (owner_row != me)
        alike = (owner_column == owner_row) & (owner_column >= 0.0) & (owner_column != me)
        receive_rank = jnp.sum(
            jnp.where(alike & (number_column < number_row), 1.0, 0.0), axis=0, keepdims=True
        )
        send_rank = jnp.sum(jnp.where(alike & before, 1.0, 0.0), axis=0, keepdims=True)
        here = records + (number_row - owner_row * SLOTS)
        there = (wrapped(me - owner_row) - 1.0) * cap + receive_rank
        receive = jnp.where(owner_row == me, here, there)
        receive = jnp.where(number_row < 0.0, records + SLOTS + slot, receive)
        table[face : face + 1, 0:SLOTS] = receive.astype(jnp.int32)
        key = jnp.where(other_row, (wrapped(owner_row - me) - 1.0) * cap + send_rank, -1.0)
        hit = iota((SLOTS, records), 1).astype(F32) == column_of(key)
        tile = jnp.sum(jnp.where(hit, slot_column, 0.0), axis=0, keepdims=True)
        table[face ^ 1 : (face ^ 1) + 1, SLOTS : SLOTS + records] = tile.astype(jnp.int32)


def sides_kernel(
    sizes, plane_cap, source, block, neighbour, h_far, k_far, send, asked, table, h, k, sems
):
    ny, nz = sizes
    my_y, my_z = lax.axis_index("gy"), lax.axis_index("gz")
    bx = h.shape[0]
    copies = []
    for x in range(bx):
        copies.append(pltpu.make_async_copy(h_far.at[x], h.at[x], sems.at[x]))
        copies.append(pltpu.make_async_copy(k_far.at[x], k.at[x], sems.at[bx + x]))
    for copy in copies:
        copy.start()
    write_tables(plane_cap, source, block, neighbour, asked, table)
    for copy in copies:
        copy.wait()
    blocks = side_blocks(h[...], k[...])
    for y in range(ny):
        for z in range(nz):
            for part in range(3):
                ylo, yhi, zlo, zhi = [block[part] for block in blocks]
                chosen = jnp.where(
                    my_y == y, jnp.where(z < my_z, zlo, zhi), jnp.where(y < my_y, ylo, yhi)
                )
                send[y * nz + z, part * bx : part * bx + bx, :] = chosen


def side_reader(sizes, got, bx):
    ny, nz = sizes
    my_y, my_z = lax.axis_index("gy"), lax.axis_index("gz")

    def read(dy, dz, part=0):
        y, z = my_y + dy, my_z + dz
        inside = (y >= 0) & (y < ny) & (z >= 0) & (z < nz)
        at = jnp.where(inside, y * nz + z, 0)
        return jnp.where(inside, got[at, part * bx : part * bx + bx, :], 0.0)

    return read


def layers_kernel(sizes, h, k, got, asked, _, down, up, *farther):
    bx, by, bz = h.shape
    count = asked.shape[0]
    read = side_reader(sizes, got, bx)
    around = [read(-1, 0), read(1, 0), read(0, -1), read(0, 1)]
    for out, near, far, shift in ((down, 0, 1, count - 1), (up, bx - 1, bx - 2, 1)):
        out[0:by, :] = h[near]
        out[by : 2 * by, :] = h[far]
        out[2 * by : 3 * by, :] = k[near]
        for number, side in enumerate(around):
            out[3 * by + number : 3 * by + number + 1, :] = side[near : near + 1, :]
        out[3 * by + 4 : 3 * by + 5, :] = asked[shift : shift + 1, :]
        out[3 * by + 5 : 3 * by + 8, :] = jnp.zeros((3, bz), F32)
    for number, out in enumerate(farther):
        out[...] = jnp.broadcast_to(asked[2 + number : 3 + number, :], out.shape)


def block_layout(cap):
    parts = 128 // CB // cap
    return parts, CB // parts


def flat_step(h, k, inner, outer, first, last, before, after, length):
    bx, lanes = h.shape
    t = temperature(h)
    row, lane = iota(h.shape, 0), iota(h.shape, 1)
    total = temperature(inner) + temperature(outer)
    total += jnp.where(row == 0, temperature(first), pltpu.roll(t, 1, 0))
    total += jnp.where(row == bx - 1, temperature(last), pltpu.roll(t, bx - 1, 0))
    total += jnp.where(lane == 0, temperature(before), pltpu.roll(t, 1, 1))
    total += jnp.where(lane == length - 1, temperature(after), pltpu.roll(t, lanes - 1, 1))
    return h + RATE * k * (total - 6.0 * t)


def heat_kernel(cap, sizes, request, h, k, got, low, high, *rest):
    count = lax.axis_size("gx")
    packed, (out, found, *send, held) = rest[: count - 1], rest[count - 1 :]

    bx, by, bz = h.shape
    h0, k0 = h[...], k[...]
    read = side_reader(sizes, got, bx)
    me = lax.axis_index("gx")
    layers, lines = [], []
    for beside, inside in ((low, me > 0), (high, me < count - 1)):
        beside = jnp.where(inside, beside[...], 0.0)
        layers.append([beside[part * by : part * by + by, :][None] for part in range(3)])
        lines.append([beside[3 * by + n : 3 * by + n + 1, :] for n in range(4)])
    y_sides = [[read(d, 0, part) for part in range(3)] for d in (-1, 1)]
    z_sides = [[read(0, d, part) for part in range(3)] for d in (-1, 1)]
    corner = [[read(dy, dz) for dz in (-1, 1)] for dy in (-1, 1)]
    to_first = [[pltpu.roll(c[0], 1, 1), c[1]] for c in corner]
    y_inner = [sublanes(h0, 0), sublanes(h0, by - 1)]
    z_inner = [to_lanes(h0[:, :, 0:1]), to_lanes(h0[:, :, bz - 1 : bz])]

    sides = [temperature(layers[0][0]), temperature(layers[1][0])]
    sides += [temperature(side[0]) for side in y_sides + z_sides]
    h1 = conduct(h0, k0, *sides)
    next_sides = []
    for side in range(2):
        near, far, near_k = layers[side]
        across = [temperature(far), temperature(h0[0:1])]
        if side:
            across = [temperature(h0[bx - 1 : bx]), temperature(far)]
        next_sides.append(conduct(near, near_k, *across, *[temperature(line) for line in lines[side]]))
    for side in range(2):
        near, far, near_k = y_sides[side]
        ends = [to_first[side][0], pltpu.roll(to_first[side][1], bz - 1, 1)]
        next_sides.append(
            flat_step(near, near_k, y_inner[side], far, lines[0][side], lines[1][side], *ends, bz)
        )
    for side in range(2):
        near, far, near_k = z_sides[side]
        ends = [to_first[0][side], pltpu.roll(to_first[1][side], by - 1, 1)]
        next_sides.append(
            flat_step(near, near_k, z_inner[side], far, lines[0][2 + side], lines[1][2 + side], *ends, by)
        )
    h2 = conduct(h1, k0, *[temperature(side) for side in next_sides])
    out[...] = h2

    held[...] = temperature(h2).reshape(bx, by // CB, CB, bz)
    parts, deep = block_layout(cap)
    nby, nbz = by // CB, bz // CB
    group = iota((deep, CB, bz), 2) // CB
    for shift in range(count):
        total = jnp.zeros((deep, CB, bz), F32)
        for rank in range(cap):
            block = request[(count - shift) % count, rank]
            a, b, c = block // (nby * nbz), (block // nbz) % nby, block % nbz
            for part in range(parts):
                at = rank * parts + part
                patch = held[pl.ds(a * CB + part * deep, deep), b]
                moved = pltpu.roll(patch, (CB * at - CB * c + bz) % bz, 2)
                total = jnp.where(group == at, moved, total)
        total = total.reshape(deep * CB, bz)
        if shift == 0:
            found[...] = total
        else:
            behind = packed[shift - 1].shape[0]
            send[shift - 1][0:behind, :] = packed[shift - 1][...]
            send[shift - 1][behind:, :] = total


def write_records(phase, solute, picks, own):
    flat = [f.reshape(SLOTS * TE, PLANE) for f in (phase, solute)]
    high, low = halves(jnp.concatenate(flat, axis=1))
    planes = dot(high, picks) + dot(low, picks)
    own[0:SLOTS, 0:TE, :] = planes[:, 0:128].reshape(SLOTS, TE, 128)
    own[SLOTS : 2 * SLOTS, 0:TE, :] = planes[:, 128:256].reshape(SLOTS, TE, 128)
    for face in range(2):
        for number, field in enumerate((phase, solute)):
            for half in range(2):
                row = TE + face * 4 + number * 2 + half
                lanes = slice(half * 128, half * 128 + 128)
                near, far = (0, TE - 1) if face == 0 else (TE - 1, 0)
                own[0:SLOTS, row : row + 1, :] = field[:, far : far + 1, lanes]
                own[SLOTS : 2 * SLOTS, row : row + 1, :] = field[:, near : near + 1, lanes]


def merge_record(source, number):
    side = (iota((TE, 128), 1) % 64) // TE
    out = source[number(2), 0:TE, :]
    for face in range(3, 6):
        out = jnp.where(side == face - 2, source[number(face), 0:TE, :], out)
    edge = jnp.where(
        iota((8, 128), 0) < 4, source[number(0), TE:REC, :], source[number(1), TE:REC, :]
    )
    return out, edge


def pack(own, table, send):
    cap = send[0].shape[0] // REC
    for number, out in enumerate(send):
        for rank in range(cap):
            record = number * cap + rank
            planes, edge = merge_record(own, lambda face: table[face, SLOTS + record])
            out[rank * REC : rank * REC + TE, :] = planes
            out[rank * REC + TE : rank * REC + REC, :] = edge


def first_pack_kernel(table, phase, solute, picks, own, *send):
    write_records(phase[...], solute[...], picks[...], own)
    pack(own, table, send)


def take_heat(cap, table, found, got, spreads, blocks, held, heat):
    parts, deep = block_layout(cap)
    blocks[0] = found[...]
    for number, value in enumerate(got):
        blocks[1 + number] = value[value.shape[0] - deep * CB :, :]
    group = iota((CB, 128), 1) // CB
    for slot in range(SLOTS):
        back, rank = table[6, slot], table[7, slot]
        for x in range(CB):
            row = (x % deep) * CB
            patch = blocks[back, row : row + CB, :]
            held[slot * CB + x] = jnp.where(group == rank * parts + x // deep, patch, 0.0)
    rows = held[...].reshape(SLOTS * CB * CB, 128)
    wide = dot(jnp.concatenate(halves(rows), axis=1), spreads)
    wide = wide.reshape(SLOTS * CB, CB, PLANE)
    keep = iota(wide.shape, 1) == iota(wide.shape, 2) // TE // 2
    coarse = jnp.sum(jnp.where(keep, wide, 0.0), axis=1)
    for half in range(2):
        for odd in range(2):
            heat[half, pl.ds(odd, SLOTS * CB, 2), :] = coarse[:, half * 128 : half * 128 + 128]


def step(table, phase, solute, heat, got, own, stencil, places, all_records, ghosts):
    records = all_records.shape[0] - 2 * SLOTS
    cap = records // len(got)
    for number, value in enumerate(got):
        all_records[number * cap : number * cap + cap] = value[0 : cap * REC, :].reshape(cap, REC, 128)
    all_records[records : records + 2 * SLOTS] = own[...]
    for slot in range(SLOTS):
        out, edge = merge_record(all_records, lambda face: table[face, slot])
        ghosts[slot, 0:TE, :] = out
        ghosts[slot, TE:REC, :] = edge
    beside = jnp.concatenate(halves(ghosts[:, 0:TE, :].reshape(SLOTS * TE, 128)), axis=1)
    beside = dot(beside, places)
    row = iota((SLOTS, TE, PLANE), 1)
    lap = []
    for number, field in enumerate((phase, solute)):
        high, low = halves(field.reshape(SLOTS * TE, PLANE))
        total = dot(high, stencil) + dot(low, stencil)
        total += beside[:, number * PLANE : number * PLANE + PLANE]
        total = total.reshape(SLOTS, TE, PLANE) - 6.0 * field
        sides = []
        for face in range(2):
            at = TE + face * 4 + number * 2
            sides.append(
                jnp.concatenate([ghosts[:, at : at + 1, :], ghosts[:, at + 1 : at + 2, :]], axis=2)
            )
        total += jnp.where(row == 0, sides[0], pltpu.roll(field, 1, 1))
        total += jnp.where(row == TE - 1, sides[1], pltpu.roll(field, TE - 1, 1))
        lap.append(total)
    warm = jnp.concatenate([heat[0], heat[1]], axis=1).reshape(SLOTS, TE, PLANE)
    squared = 1.0 - phase * phase
    new_phase = phase + ORDER_SPEED * (
        lap[0] + phase - phase * phase * phase - COUPLING * (warm + solute) * squared * squared
    )
    new_solute = solute + SOLUTE_RATE * lap[1] + REJECTION * (new_phase - phase)
    return new_phase, new_solute


def first_step_kernel(cap, table, phase, solute, own, picks, stencil, places, spreads, brick, found, *rest):
    others = lax.axis_size("gx") - 1
    got, rest = rest[:others], rest[others:]
    phase_out, solute_out, heat_out, own_out, brick_out, *rest = rest
    send, (all_records, ghosts, blocks, held, sem) = rest[:others], rest[others:]
    copy = pltpu.make_async_copy(brick, brick_out, sem)
    copy.start()
    take_heat(cap, table, found, got, spreads[...], blocks, held, heat_out)
    new_phase, new_solute = step(
        table, phase[...], solute[...], heat_out[...], got, own, stencil[...], places[...],
        all_records, ghosts,
    )
    phase_out[...] = new_phase
    solute_out[...] = new_solute
    write_records(new_phase, new_solute, picks[...], own_out)
    pack(own_out, table, send)
    copy.wait()


def middle_step_kernel(table, phase, solute, heat, own, picks, stencil, places, *rest):
    others = lax.axis_size("gx") - 1
    got, (phase_out, solute_out, own_out, *rest) = rest[:others], rest[others:]
    send, (all_records, ghosts) = rest[:others], rest[others:]
    new_phase, new_solute = step(
        table, phase[...], solute[...], heat[...], got, own, stencil[...], places[...],
        all_records, ghosts,
    )
    phase_out[...] = new_phase
    solute_out[...] = new_solute
    write_records(new_phase, new_solute, picks[...], own_out)
    pack(own_out, table, send)


def last_step_kernel(table, phase, solute, heat, own, stencil, places, *rest):
    others = lax.axis_size("gx") - 1
    got, (phase_out, solute_out, all_records, ghosts) = rest[:others], rest[others:]
    new_phase, new_solute = step(
        table, phase[...], solute[...], heat[...], got, own, stencil[...], places[...],
        all_records, ghosts,
    )
    phase_out[...] = new_phase
    solute_out[...] = new_solute


def call(kernel, in_specs, out_shapes, scratch=(), out_specs=None, mib=16):
    return pl.pallas_call(
        kernel,
        out_shape=out_shapes,
        in_specs=in_specs,
        out_specs=out_specs or jax.tree.map(lambda _: VMEM, out_shapes),
        scratch_shapes=list(scratch),
        compiler_params=pltpu.CompilerParams(vmem_limit_bytes=mib * 1024 * 1024),
    )


def shape(*dims):
    return jax.ShapeDtypeStruct(dims, F32)


def local(enthalpy, conductivity, phase, solute, tile_source, tile_block, tile_neighbour):
    count = lax.axis_size("gx")
    sizes = (lax.axis_size("gy"), lax.axis_size("gz"))
    plane_cap = -(-SLOTS // (count - 1))
    block_cap = 2 * SLOTS // count
    others = count - 1
    records = others * plane_cap
    bx, by, bz = enthalpy.shape
    picks, stencil, places, spreads = tables()

    integers = functools.partial(jax.ShapeDtypeStruct, dtype=jnp.int32)
    sides, asked, table = call(
        functools.partial(sides_kernel, sizes, plane_cap),
        [VMEM] * 3 + [ANY] * 2,
        [
            shape(sizes[0] * sizes[1], 3 * bx, 128),
            shape(count, 128),
            integers((8, 128)),
        ],
        [pltpu.VMEM((bx, by, bz), F32)] * 2 + [pltpu.SemaphoreType.DMA((2 * bx,))],
        mib=56,
    )(
        tile_source.reshape(1, SLOTS),
        tile_block.reshape(1, SLOTS),
        jnp.transpose(tile_neighbour, (0, 1, 4, 2, 3)).reshape(FACES, 1, SLOTS),
        enthalpy,
        conductivity,
    )
    sides = lax.all_to_all(sides, ("gy", "gz"), split_axis=0, concat_axis=0, tiled=True)

    phase_field = phase.reshape(SLOTS, TE, PLANE)
    solute_field = solute.reshape(SLOTS, TE, PLANE)
    own_shape, send_shapes = shape(2 * SLOTS, REC, 128), [shape(plane_cap * REC, 128)] * others
    own, *packed = call(first_pack_kernel, [SMEM] + [VMEM] * 3, [own_shape, *send_shapes])(
        table, phase_field, solute_field, picks
    )

    layer = shape(3 * by + 8, bz)
    down, up, *farther = call(
        functools.partial(layers_kernel, sizes),
        [VMEM] * 4 + [ANY],
        [layer, layer] + [shape(8, 128)] * (count - 3),
    )(enthalpy, conductivity, sides, asked, packed[0])

    def pass_on(value, shift):
        return lax.ppermute(value, "gx", [(i, (i + shift) % count) for i in range(count)])

    from_low, from_high = pass_on(up, 1), pass_on(down, count - 1)
    farther = [pass_on(value, 2 + number) for number, value in enumerate(farther)]
    row = 3 * by + 4
    request = [asked[0:1], from_low[row : row + 1]]
    request += [value[0:1] for value in farther] + [from_high[row : row + 1]]
    request = jnp.concatenate(request, axis=0)[:, :block_cap].astype(jnp.int32)
    _, deep = block_layout(block_cap)
    brick = shape(bx, by, bz)
    heated, found, *send = call(
        functools.partial(heat_kernel, block_cap, sizes),
        [SMEM] + [VMEM] * (5 + others),
        [brick, shape(deep * CB, 128)] + [shape(plane_cap * REC + deep * CB, 128)] * others,
        [pltpu.VMEM((bx, by // CB, CB, bz), F32)],
    )(request, enthalpy, conductivity, sides, from_low, from_high, *packed)

    def exchange(values):
        return [pass_on(value, 1 + number) for number, value in enumerate(values)]

    got = exchange(send)
    field = shape(SLOTS, TE, PLANE)
    step_scratch = [
        pltpu.VMEM((records + 2 * SLOTS, REC, 128), F32),
        pltpu.VMEM((SLOTS, REC, 128), F32),
    ]
    phase_field, solute_field, heat, own, heat_out, *send = call(
        functools.partial(first_step_kernel, block_cap),
        [SMEM] + [VMEM] * (9 + others),
        [field, field, shape(2, SLOTS * TE, 128), own_shape, brick, *send_shapes],
        step_scratch
        + [
            pltpu.VMEM((count, deep * CB, 128), F32),
            pltpu.VMEM((SLOTS * CB, CB, 128), F32),
            pltpu.SemaphoreType.DMA,
        ],
        [VMEM] * 4 + [ANY] + [VMEM] * others,
    )(table, phase_field, solute_field, own, picks, stencil, places, spreads, heated, found, *got)
    for _ in range(PHASE_STEPS - 2):
        got = exchange(send)
        phase_field, solute_field, own, *send = call(
            middle_step_kernel,
            [SMEM] + [VMEM] * (7 + others),
            [field, field, own_shape, *send_shapes],
            step_scratch,
        )(table, phase_field, solute_field, heat, own, picks, stencil, places, *got)
    got = exchange(send)
    phase_field, solute_field = call(
        last_step_kernel, [SMEM] + [VMEM] * (6 + others), [field, field], step_scratch
    )(table, phase_field, solute_field, heat, own, stencil, places, *got)
    return heat_out, phase_field.reshape(phase.shape), solute_field.reshape(solute.shape)


def solution(mesh):
    grid = P("gx", "gy", "gz")
    tiles = P("gx", "gy", "gz", None, None, None)
    return jax.shard_map(
        local,
        mesh=mesh,
        in_specs=(
            grid,
            grid,
            tiles,
            tiles,
            P("gx", "gy", "gz", None, None),
            P("gx", "gy", "gz", None),
            P("gx", "gy", "gz", None, None),
        ),
        out_specs=(grid, tiles, tiles),
        check_vma=False,
    )
```

```python
import functools

import jax
import jax.numpy as jnp
import numpy as np
from jax import lax
from jax.experimental import pallas as pl
from jax.experimental.pallas import tpu as pltpu
from jax.sharding import PartitionSpec as P

CB = 8
TE = 16
PLANE = TE * TE
SLOTS = 16
FACES = 6
PHASE_STEPS = 4
REC = 24

RATE = 0.16
ORDER_SPEED = 0.1
SOLUTE_RATE = 0.15
COUPLING = 0.5
REJECTION = 0.5

F32 = jnp.float32
BF16 = jnp.bfloat16
VMEM = pl.BlockSpec(memory_space=pltpu.VMEM)
SMEM = pl.BlockSpec(memory_space=pltpu.SMEM)
ANY = pl.BlockSpec(memory_space=pl.ANY)


def plane_lane(face):
    j = np.arange(TE)
    return [j, PLANE - TE + j, j * TE, j * TE + TE - 1][face - 2]


def constant_tables():
    pick = np.zeros((2, PLANE, 256), np.float32)
    place = np.zeros((2, 128, PLANE), np.float32)
    for field in range(2):
        for face in range(2, 6):
            at = field * 64 + (face - 2) * TE + np.arange(TE)
            pick[field, plane_lane(face ^ 1), at] = 1.0
            pick[field, plane_lane(face), 128 + at] = 1.0
            place[field, at, plane_lane(face)] = 1.0
    y, z = np.divmod(np.arange(PLANE), TE)
    dy, dz = np.abs(y[:, None] - y[None, :]), np.abs(z[:, None] - z[None, :])
    stencil = ((dy + dz) == 1).astype(np.float32)
    lane = np.arange(128)
    spread = (lane[:, None] % CB == z[None, :] // 2).astype(np.float32)
    return pick, place, stencil, spread


def tables():
    pick, place, stencil, spread = constant_tables()
    place = np.concatenate([place[0], place[1]], axis=1)
    return (
        jnp.asarray(np.concatenate([pick[0], pick[1]], axis=0), BF16),
        jnp.asarray(stencil, BF16),
        jnp.asarray(np.concatenate([place, place], axis=0), BF16),
        jnp.asarray(np.concatenate([spread, spread], axis=0), BF16),
    )


def halves(value):
    high = value.astype(BF16)
    return high, (value - high.astype(F32)).astype(BF16)


def dot(a, b):
    return jnp.dot(a, b, preferred_element_type=F32)


def temperature(h):
    return jnp.minimum(h, 0.0) + jnp.maximum(h - 1.0, 0.0)


def iota(shape, dim):
    return lax.broadcasted_iota(jnp.int32, shape, dim)


def to_lanes(column):
    bx, by, _ = column.shape
    diagonal = iota((bx, by, 128), 1) == iota((bx, by, 128), 2)
    return jnp.sum(jnp.where(diagonal, column, 0.0), axis=1)


def to_column(line, by):
    bx = line.shape[0]
    diagonal = iota((bx, by, 128), 1) == iota((bx, by, 128), 2)
    return jnp.sum(jnp.where(diagonal, line[:, None, :], 0.0), axis=2, keepdims=True)


def conduct(h, k, xlo, xhi, ylo, yhi, zlo, zhi):
    bx, by, bz = h.shape
    t = temperature(h)
    row, lane = iota((bx, by, bz), 1), iota((bx, by, bz), 2)
    if bx > 1:
        total = jnp.concatenate([xlo, t[:-1]], axis=0) + jnp.concatenate([t[1:], xhi], axis=0)
    else:
        total = xlo + xhi
    total += jnp.where(row == 0, ylo[:, None, :], pltpu.roll(t, 1, 1))
    total += jnp.where(row == by - 1, yhi[:, None, :], pltpu.roll(t, by - 1, 1))
    total += jnp.where(lane == 0, to_column(zlo, by), pltpu.roll(t, 1, 2))
    total += jnp.where(lane == bz - 1, to_column(zhi, by), pltpu.roll(t, bz - 1, 2))
    return h + RATE * k * (total - 6.0 * t)


def sublanes(value, y):
    return jnp.concatenate([value[x, y : y + 1, :] for x in range(value.shape[0])], axis=0)


def side_blocks(h, k):
    by, bz = h.shape[1:]
    return [
        (sublanes(h, 0), sublanes(h, 1), sublanes(k, 0)),
        (sublanes(h, by - 1), sublanes(h, by - 2), sublanes(k, by - 1)),
        (to_lanes(h[:, :, 0:1]), to_lanes(h[:, :, 1:2]), to_lanes(k[:, :, 0:1])),
        (to_lanes(h[:, :, bz - 1 : bz]), to_lanes(h[:, :, bz - 2 : bz - 1]), to_lanes(k[:, :, bz - 1 : bz])),
    ]


def column_of(row):
    square = (row.shape[1], row.shape[1])
    return jnp.sum(jnp.where(iota(square, 0) == iota(square, 1), row, 0.0), axis=1, keepdims=True)


def write_tables(plane_cap, source, block, neighbour, asked, table):
    me = lax.axis_index("gx").astype(F32)
    count = len(asked)
    records = (count - 1) * plane_cap
    cap = float(plane_cap)

    def wrapped(shift):
        return jnp.where(shift < 0.0, shift + float(count), shift)

    square = (SLOTS, SLOTS)
    before = iota(square, 0) < iota(square, 1)
    slot = iota((1, SLOTS), 1).astype(F32)
    source_row, block_column = source[...].astype(F32), column_of(block[...].astype(F32))
    source_column = column_of(source_row)
    rank = jnp.sum(
        jnp.where((source_column == source_row) & before, 1.0, 0.0), axis=0, keepdims=True
    )
    rank_column = column_of(rank)
    lane = iota((SLOTS, 128), 1).astype(F32)
    for shift in range(count):
        hit = (wrapped(source_column - me) == float(shift)) & (rank_column == lane)
        row = jnp.sum(jnp.where(hit, block_column, 0.0), axis=0, keepdims=True)
        asked[shift][...] = jnp.broadcast_to(row, asked[shift].shape)
    table[6:7, 0:SLOTS] = wrapped(me - source_row).astype(jnp.int32)
    table[7:8, 0:SLOTS] = rank.astype(jnp.int32)
    slot_column = iota((SLOTS, records), 0).astype(F32)
    for face in range(FACES):
        number = neighbour[face]
        owner_row, number_row = (number >> 4).astype(F32), number.astype(F32)
        owner_column, number_column = column_of(owner_row), column_of(number_row)
        other_row = (number_row >= 0.0) & (owner_row != me)
        alike = (owner_column == owner_row) & (owner_column >= 0.0) & (owner_column != me)
        receive_rank = jnp.sum(
            jnp.where(alike & (number_column < number_row), 1.0, 0.0), axis=0, keepdims=True
        )
        send_rank = jnp.sum(jnp.where(alike & before, 1.0, 0.0), axis=0, keepdims=True)
        here = records + (number_row - owner_row * SLOTS)
        there = (wrapped(me - owner_row) - 1.0) * cap + receive_rank
        receive = jnp.where(owner_row == me, here, there)
        receive = jnp.where(number_row < 0.0, records + SLOTS + slot, receive)
        table[face : face + 1, 0:SLOTS] = receive.astype(jnp.int32)
        key = jnp.where(other_row, (wrapped(owner_row - me) - 1.0) * cap + send_rank, -1.0)
        hit = iota((SLOTS, records), 1).astype(F32) == column_of(key)
        tile = jnp.sum(jnp.where(hit, slot_column, 0.0), axis=0, keepdims=True)
        table[face ^ 1 : (face ^ 1) + 1, SLOTS : SLOTS + records] = tile.astype(jnp.int32)


def sides_kernel(sizes, plane_cap, source_far, block_far, neighbour_far, h_far, k_far, *rest):
    *rest, source, block, neighbour, h, k, sems = rest
    ny = sizes[0]
    moves = side_moves(sizes)
    sends, table, asked = rest[: len(moves)], rest[len(moves)], rest[len(moves) + 1 :]
    my_y = lax.axis_index("gy")
    bx = h.shape[0]
    small = [(source_far, source), (block_far, block), (neighbour_far, neighbour)]
    copies = [pltpu.make_async_copy(*pair, sems.at[2 * bx + n]) for n, pair in enumerate(small)]
    large = []
    for x in range(bx):
        large.append(pltpu.make_async_copy(h_far.at[x], h.at[x], sems.at[x]))
        large.append(pltpu.make_async_copy(k_far.at[x], k.at[x], sems.at[bx + x]))
    for copy in copies + large:
        copy.start()
    for copy in copies:
        copy.wait()
    write_tables(plane_cap, source, block, neighbour, asked, table)
    for copy in large:
        copy.wait()
    ylo, yhi, zlo, zhi = side_blocks(h[...], k[...])
    if ny == 2:
        yhi = [jnp.where(my_y == 0, up, down) for up, down in zip(yhi, ylo)]
    for (dy, dz), out in zip(moves, sends):
        side = (yhi if dy > 0 else ylo) if dy else (zhi if dz > 0 else zlo)
        for part in range(1 if dy and dz else 3):
            out[part * bx : part * bx + bx, :] = side[part]


def side_moves(sizes):
    ways = [1] if sizes[0] == 2 else [-1, 1]
    return [(dy, 0) for dy in ways] + [(0, -1), (0, 1)] + [(dy, dz) for dy in ways for dz in (-1, 1)]


def send_side(value, sizes, dy, dz):
    ny, nz = sizes
    pairs = []
    for y in range(ny):
        for z in range(nz):
            to_y, to_z = y + dy, z + dz
            if ny == 2:
                to_y %= 2
            if 0 <= to_y < ny and 0 <= to_z < nz:
                pairs.append((y * nz + z, to_y * nz + to_z))
    return lax.ppermute(value, ("gy", "gz"), pairs)


def side_reader(sizes, got, bx):
    moves = side_moves(sizes)
    my_y = lax.axis_index("gy")

    def read(dy, dz, part=0):
        if sizes[0] > 2 or dy == 0:
            value = got[moves.index((-dy, -dz))]
            return value[part * bx : part * bx + bx, :]
        value = got[moves.index((1, -dz))]
        return jnp.where(my_y == max(dy, 0) ^ 1, value[part * bx : part * bx + bx, :], 0.0)

    return read


def layers_kernel(sizes, h, k, *rest):
    *got, down, up = rest
    bx, by, bz = h.shape
    read = side_reader(sizes, got, bx)
    around = [read(-1, 0), read(1, 0), read(0, -1), read(0, 1)]
    for out, near, far in ((down, 0, 1), (up, bx - 1, bx - 2)):
        out[0:by, :] = h[near]
        out[by : 2 * by, :] = h[far]
        out[2 * by : 3 * by, :] = k[near]
        for number, side in enumerate(around):
            out[3 * by + number : 3 * by + number + 1, :] = side[near : near + 1, :]
        out[3 * by + 4 : 3 * by + 8, :] = jnp.zeros((4, bz), F32)


def block_layout(cap):
    parts = 128 // CB // cap
    return parts, CB // parts


def flat_step(h, k, inner, outer, first, last, before, after, length):
    bx, lanes = h.shape
    t = temperature(h)
    row, lane = iota(h.shape, 0), iota(h.shape, 1)
    total = temperature(inner) + temperature(outer)
    total += jnp.where(row == 0, temperature(first), pltpu.roll(t, 1, 0))
    total += jnp.where(row == bx - 1, temperature(last), pltpu.roll(t, bx - 1, 0))
    total += jnp.where(lane == 0, temperature(before), pltpu.roll(t, 1, 1))
    total += jnp.where(lane == length - 1, temperature(after), pltpu.roll(t, lanes - 1, 1))
    return h + RATE * k * (total - 6.0 * t)


def heat_kernel(cap, sizes, request, h, k, low, high, *rest):
    count = lax.axis_size("gx")
    others, sides = count - 1, len(side_moves(sizes))
    got, packed, (out, found, *send, held) = rest[:sides], rest[sides : sides + others], rest[sides + others :]

    bx, by, bz = h.shape
    h0, k0 = h[...], k[...]
    read = side_reader(sizes, got, bx)
    layers, lines = [], []
    for beside in (low, high):
        layers.append([beside[part * by : part * by + by, :][None] for part in range(3)])
        lines.append([beside[3 * by + n : 3 * by + n + 1, :] for n in range(4)])
    y_sides = [[read(d, 0, part) for part in range(3)] for d in (-1, 1)]
    z_sides = [[read(0, d, part) for part in range(3)] for d in (-1, 1)]
    corner = [[read(dy, dz) for dz in (-1, 1)] for dy in (-1, 1)]
    to_first = [[pltpu.roll(c[0], 1, 1), c[1]] for c in corner]
    y_inner = [sublanes(h0, 0), sublanes(h0, by - 1)]
    z_inner = [to_lanes(h0[:, :, 0:1]), to_lanes(h0[:, :, bz - 1 : bz])]

    sides = [temperature(layers[0][0]), temperature(layers[1][0])]
    sides += [temperature(side[0]) for side in y_sides + z_sides]
    h1 = conduct(h0, k0, *sides)
    next_sides = []
    for side in range(2):
        near, far, near_k = layers[side]
        across = [temperature(far), temperature(h0[0:1])]
        if side:
            across = [temperature(h0[bx - 1 : bx]), temperature(far)]
        next_sides.append(conduct(near, near_k, *across, *[temperature(line) for line in lines[side]]))
    for side in range(2):
        near, far, near_k = y_sides[side]
        ends = [to_first[side][0], pltpu.roll(to_first[side][1], bz - 1, 1)]
        next_sides.append(
            flat_step(near, near_k, y_inner[side], far, lines[0][side], lines[1][side], *ends, bz)
        )
    for side in range(2):
        near, far, near_k = z_sides[side]
        ends = [to_first[0][side], pltpu.roll(to_first[1][side], by - 1, 1)]
        next_sides.append(
            flat_step(near, near_k, z_inner[side], far, lines[0][2 + side], lines[1][2 + side], *ends, by)
        )
    h2 = conduct(h1, k0, *[temperature(side) for side in next_sides])
    out[...] = h2

    held[...] = temperature(h2).reshape(bx, by // CB, CB, bz)
    parts, deep = block_layout(cap)
    nby, nbz = by // CB, bz // CB
    group = iota((deep, CB, bz), 2) // CB
    for shift in range(count):
        total = jnp.zeros((deep, CB, bz), F32)
        for rank in range(cap):
            block = request[(count - shift) % count, rank]
            a, b, c = block // (nby * nbz), (block // nbz) % nby, block % nbz
            for part in range(parts):
                at = rank * parts + part
                patch = held[pl.ds(a * CB + part * deep, deep), b]
                moved = pltpu.roll(patch, (CB * at - CB * c + bz) % bz, 2)
                total = jnp.where(group == at, moved, total)
        total = total.reshape(deep * CB, bz)
        if shift == 0:
            found[...] = total
        else:
            behind = packed[shift - 1].shape[0]
            send[shift - 1][0:behind, :] = packed[shift - 1][...]
            send[shift - 1][behind:, :] = total


def write_records(phase, solute, picks, own):
    flat = [f.reshape(SLOTS * TE, PLANE) for f in (phase, solute)]
    high, low = halves(jnp.concatenate(flat, axis=1))
    planes = dot(high, picks) + dot(low, picks)
    own[0:SLOTS, 0:TE, :] = planes[:, 0:128].reshape(SLOTS, TE, 128)
    own[SLOTS : 2 * SLOTS, 0:TE, :] = planes[:, 128:256].reshape(SLOTS, TE, 128)
    for face in range(2):
        for number, field in enumerate((phase, solute)):
            for half in range(2):
                row = TE + face * 4 + number * 2 + half
                lanes = slice(half * 128, half * 128 + 128)
                near, far = (0, TE - 1) if face == 0 else (TE - 1, 0)
                own[0:SLOTS, row : row + 1, :] = field[:, far : far + 1, lanes]
                own[SLOTS : 2 * SLOTS, row : row + 1, :] = field[:, near : near + 1, lanes]


def merge_record(source, number):
    side = (iota((TE, 128), 1) % 64) // TE
    out = source[number(2), 0:TE, :]
    for face in range(3, 6):
        out = jnp.where(side == face - 2, source[number(face), 0:TE, :], out)
    edge = jnp.where(
        iota((8, 128), 0) < 4, source[number(0), TE:REC, :], source[number(1), TE:REC, :]
    )
    return out, edge


def pack(own, table, send):
    cap = send[0].shape[0] // REC
    for number, out in enumerate(send):
        for rank in range(cap):
            record = number * cap + rank
            planes, edge = merge_record(own, lambda face: table[face, SLOTS + record])
            out[rank * REC : rank * REC + TE, :] = planes
            out[rank * REC + TE : rank * REC + REC, :] = edge


def first_pack_kernel(table, phase, solute, picks, own, *send):
    write_records(phase[...], solute[...], picks[...], own)
    pack(own, table, send)


def take_heat(cap, table, found, got, spreads, blocks, held, heat):
    parts, deep = block_layout(cap)
    blocks[0] = found[...]
    for number, value in enumerate(got):
        blocks[1 + number] = value[value.shape[0] - deep * CB :, :]
    group = iota((CB, 128), 1) // CB
    for slot in range(SLOTS):
        back, rank = table[6, slot], table[7, slot]
        for x in range(CB):
            row = (x % deep) * CB
            patch = blocks[back, row : row + CB, :]
            held[slot * CB + x] = jnp.where(group == rank * parts + x // deep, patch, 0.0)
    rows = held[...].reshape(SLOTS * CB * CB, 128)
    wide = dot(jnp.concatenate(halves(rows), axis=1), spreads)
    wide = wide.reshape(SLOTS * CB, CB, PLANE)
    keep = iota(wide.shape, 1) == iota(wide.shape, 2) // TE // 2
    coarse = jnp.sum(jnp.where(keep, wide, 0.0), axis=1)
    for half in range(2):
        for odd in range(2):
            heat[half, pl.ds(odd, SLOTS * CB, 2), :] = coarse[:, half * 128 : half * 128 + 128]


def step(table, phase, solute, heat, got, own, stencil, places, all_records, ghosts):
    records = all_records.shape[0] - 2 * SLOTS
    cap = records // len(got)
    for number, value in enumerate(got):
        all_records[number * cap : number * cap + cap] = value[0 : cap * REC, :].reshape(cap, REC, 128)
    all_records[records : records + 2 * SLOTS] = own[...]
    for slot in range(SLOTS):
        out, edge = merge_record(all_records, lambda face: table[face, slot])
        ghosts[slot, 0:TE, :] = out
        ghosts[slot, TE:REC, :] = edge
    beside = jnp.concatenate(halves(ghosts[:, 0:TE, :].reshape(SLOTS * TE, 128)), axis=1)
    beside = dot(beside, places)
    row = iota((SLOTS, TE, PLANE), 1)
    lap = []
    for number, field in enumerate((phase, solute)):
        high, low = halves(field.reshape(SLOTS * TE, PLANE))
        total = dot(high, stencil) + dot(low, stencil)
        total += beside[:, number * PLANE : number * PLANE + PLANE]
        total = total.reshape(SLOTS, TE, PLANE) - 6.0 * field
        sides = []
        for face in range(2):
            at = TE + face * 4 + number * 2
            sides.append(
                jnp.concatenate([ghosts[:, at : at + 1, :], ghosts[:, at + 1 : at + 2, :]], axis=2)
            )
        total += jnp.where(row == 0, sides[0], pltpu.roll(field, 1, 1))
        total += jnp.where(row == TE - 1, sides[1], pltpu.roll(field, TE - 1, 1))
        lap.append(total)
    warm = jnp.concatenate([heat[0], heat[1]], axis=1).reshape(SLOTS, TE, PLANE)
    squared = 1.0 - phase * phase
    new_phase = phase + ORDER_SPEED * (
        lap[0] + phase - phase * phase * phase - COUPLING * (warm + solute) * squared * squared
    )
    new_solute = solute + SOLUTE_RATE * lap[1] + REJECTION * (new_phase - phase)
    return new_phase, new_solute


def first_step_kernel(cap, table, phase, solute, own, picks, stencil, places, spreads, found, *rest):
    others = lax.axis_size("gx") - 1
    got, rest = rest[:others], rest[others:]
    phase_out, solute_out, heat_out, own_out, *rest = rest
    send, (all_records, ghosts, blocks, held) = rest[:others], rest[others:]
    take_heat(cap, table, found, got, spreads[...], blocks, held, heat_out)
    new_phase, new_solute = step(
        table, phase[...], solute[...], heat_out[...], got, own, stencil[...], places[...],
        all_records, ghosts,
    )
    phase_out[...] = new_phase
    solute_out[...] = new_solute
    write_records(new_phase, new_solute, picks[...], own_out)
    pack(own_out, table, send)


def write_out_kernel(value, out, sem):
    copy = pltpu.make_async_copy(value, out, sem)
    copy.start()
    copy.wait()


def middle_step_kernel(table, phase, solute, heat, own, picks, stencil, places, *rest):
    others = lax.axis_size("gx") - 1
    got, (phase_out, solute_out, own_out, *rest) = rest[:others], rest[others:]
    send, (all_records, ghosts) = rest[:others], rest[others:]
    new_phase, new_solute = step(
        table, phase[...], solute[...], heat[...], got, own, stencil[...], places[...],
        all_records, ghosts,
    )
    phase_out[...] = new_phase
    solute_out[...] = new_solute
    write_records(new_phase, new_solute, picks[...], own_out)
    pack(own_out, table, send)


def last_step_kernel(table, phase, solute, heat, own, stencil, places, *rest):
    others = lax.axis_size("gx") - 1
    got, (phase_out, solute_out, all_records, ghosts) = rest[:others], rest[others:]
    new_phase, new_solute = step(
        table, phase[...], solute[...], heat[...], got, own, stencil[...], places[...],
        all_records, ghosts,
    )
    phase_out[...] = new_phase
    solute_out[...] = new_solute


def call(kernel, in_specs, out_shapes, scratch=(), out_specs=None, mib=16):
    return pl.pallas_call(
        kernel,
        out_shape=out_shapes,
        in_specs=in_specs,
        out_specs=out_specs or jax.tree.map(lambda _: VMEM, out_shapes),
        scratch_shapes=list(scratch),
        compiler_params=pltpu.CompilerParams(vmem_limit_bytes=mib * 1024 * 1024),
    )


def shape(*dims):
    return jax.ShapeDtypeStruct(dims, F32)


def local(enthalpy, conductivity, phase, solute, tile_source, tile_block, tile_neighbour):
    count = lax.axis_size("gx")
    sizes = (lax.axis_size("gy"), lax.axis_size("gz"))
    plane_cap = -(-SLOTS // (count - 1))
    block_cap = 2 * SLOTS // count
    others = count - 1
    records = others * plane_cap
    bx, by, bz = enthalpy.shape
    picks, stencil, places, spreads = tables()

    integers = functools.partial(jax.ShapeDtypeStruct, dtype=jnp.int32)
    moves = side_moves(sizes)
    side_shapes = [shape(bx if dy and dz else 3 * bx, 128) for dy, dz in moves]
    first = call(
        functools.partial(sides_kernel, sizes, plane_cap),
        [ANY] * 5,
        [*side_shapes, integers((8, 128)), *[shape(8, 128)] * count],
        [
            pltpu.VMEM((1, SLOTS), jnp.int32),
            pltpu.VMEM((1, SLOTS), jnp.int32),
            pltpu.VMEM((FACES, 1, SLOTS), jnp.int32),
            pltpu.VMEM((bx, by, bz), F32),
            pltpu.VMEM((bx, by, bz), F32),
            pltpu.SemaphoreType.DMA((2 * bx + 3,)),
        ],
        mib=56,
    )(
        tile_source.reshape(1, SLOTS),
        tile_block.reshape(1, SLOTS),
        jnp.transpose(tile_neighbour, (0, 1, 4, 2, 3)).reshape(FACES, 1, SLOTS),
        enthalpy,
        conductivity,
    )
    sides, table, asked = first[: len(moves)], first[len(moves)], first[len(moves) + 1 :]
    sides = [send_side(value, sizes, *move) for value, move in zip(sides, moves)]

    def exchange(values):
        return [
            lax.ppermute(value, "gx", [(i, (i + shift) % count) for i in range(count)])
            for shift, value in enumerate(values, 1)
        ]

    request = [asked[0], *exchange(asked[1:])]
    request = jnp.stack([value[0, :block_cap] for value in request]).astype(jnp.int32)

    phase_field = phase.reshape(SLOTS, TE, PLANE)
    solute_field = solute.reshape(SLOTS, TE, PLANE)
    own_shape, send_shapes = shape(2 * SLOTS, REC, 128), [shape(plane_cap * REC, 128)] * others
    own, *packed = call(first_pack_kernel, [SMEM] + [VMEM] * 3, [own_shape, *send_shapes])(
        table, phase_field, solute_field, picks
    )

    layer = shape(3 * by + 8, bz)
    down, up = call(
        functools.partial(layers_kernel, sizes), [VMEM] * (2 + len(sides)), [layer, layer]
    )(enthalpy, conductivity, *sides)
    forward = [(i, i + 1) for i in range(others)]
    from_low = lax.ppermute(up, "gx", forward)
    from_high = lax.ppermute(down, "gx", [(b, a) for a, b in forward])
    _, deep = block_layout(block_cap)
    brick = shape(bx, by, bz)
    heated, found, *send = call(
        functools.partial(heat_kernel, block_cap, sizes),
        [SMEM] + [VMEM] * (4 + len(sides) + others),
        [brick, shape(deep * CB, 128)] + [shape(plane_cap * REC + deep * CB, 128)] * others,
        [pltpu.VMEM((bx, by // CB, CB, bz), F32)],
    )(request, enthalpy, conductivity, from_low, from_high, *sides, *packed)

    (heat_out,) = call(write_out_kernel, [ANY], [brick], [pltpu.SemaphoreType.DMA], [ANY])(heated)

    got = exchange(send)
    field = shape(SLOTS, TE, PLANE)
    step_scratch = [
        pltpu.VMEM((records + 2 * SLOTS, REC, 128), F32),
        pltpu.VMEM((SLOTS, REC, 128), F32),
    ]
    phase_field, solute_field, heat, own, *send = call(
        functools.partial(first_step_kernel, block_cap),
        [SMEM] + [VMEM] * (8 + others),
        [field, field, shape(2, SLOTS * TE, 128), own_shape, *send_shapes],
        step_scratch
        + [
            pltpu.VMEM((count, deep * CB, 128), F32),
            pltpu.VMEM((SLOTS * CB, CB, 128), F32),
        ],
    )(table, phase_field, solute_field, own, picks, stencil, places, spreads, found, *got)
    for _ in range(PHASE_STEPS - 2):
        got = exchange(send)
        phase_field, solute_field, own, *send = call(
            middle_step_kernel,
            [SMEM] + [VMEM] * (7 + others),
            [field, field, own_shape, *send_shapes],
            step_scratch,
        )(table, phase_field, solute_field, heat, own, picks, stencil, places, *got)
    got = exchange(send)
    phase_field, solute_field = call(
        last_step_kernel, [SMEM] + [VMEM] * (6 + others), [field, field], step_scratch
    )(table, phase_field, solute_field, heat, own, stencil, places, *got)
    return heat_out, phase_field.reshape(phase.shape), solute_field.reshape(solute.shape)


def solution(mesh):
    grid = P("gx", "gy", "gz")
    tiles = P("gx", "gy", "gz", None, None, None)
    return jax.shard_map(
        local,
        mesh=mesh,
        in_specs=(
            grid,
            grid,
            tiles,
            tiles,
            P("gx", "gy", "gz", None, None),
            P("gx", "gy", "gz", None),
            P("gx", "gy", "gz", None, None),
        ),
        out_specs=(grid, tiles, tiles),
        check_vma=False,
    )
```

```python
import functools

import jax
import jax.numpy as jnp
import numpy as np
from jax import lax
from jax.experimental import pallas as pl
from jax.experimental.pallas import tpu as pltpu
from jax.sharding import PartitionSpec as P

CB = 8
TE = 16
PLANE = TE * TE
SLOTS = 16
FACES = 6
PHASE_STEPS = 4
REC = 24

RATE = 0.16
ORDER_SPEED = 0.1
SOLUTE_RATE = 0.15
COUPLING = 0.5
REJECTION = 0.5

F32 = jnp.float32
BF16 = jnp.bfloat16
VMEM = pl.BlockSpec(memory_space=pltpu.VMEM)
SMEM = pl.BlockSpec(memory_space=pltpu.SMEM)
ANY = pl.BlockSpec(memory_space=pl.ANY)


def plane_lane(face):
    j = np.arange(TE)
    return [j, PLANE - TE + j, j * TE, j * TE + TE - 1][face - 2]


def constant_tables():
    pick = np.zeros((2, PLANE, 256), np.float32)
    place = np.zeros((2, 128, PLANE), np.float32)
    for field in range(2):
        for face in range(2, 6):
            at = field * 64 + (face - 2) * TE + np.arange(TE)
            pick[field, plane_lane(face ^ 1), at] = 1.0
            pick[field, plane_lane(face), 128 + at] = 1.0
            place[field, at, plane_lane(face)] = 1.0
    y, z = np.divmod(np.arange(PLANE), TE)
    dy, dz = np.abs(y[:, None] - y[None, :]), np.abs(z[:, None] - z[None, :])
    stencil = ((dy + dz) == 1).astype(np.float32)
    lane = np.arange(128)
    spread = (lane[:, None] % CB == z[None, :] // 2).astype(np.float32)
    return pick, place, stencil, spread


def tables():
    pick, place, stencil, spread = constant_tables()
    place = np.concatenate([place[0], place[1]], axis=1)
    return (
        jnp.asarray(np.concatenate([pick[0], pick[1]], axis=0), BF16),
        jnp.asarray(stencil, BF16),
        jnp.asarray(np.concatenate([place, place], axis=0), BF16),
        jnp.asarray(np.concatenate([spread, spread], axis=0), BF16),
    )


def halves(value):
    high = value.astype(BF16)
    return high, (value - high.astype(F32)).astype(BF16)


def dot(a, b):
    return jnp.dot(a, b, preferred_element_type=F32)


def temperature(h):
    return jnp.minimum(h, 0.0) + jnp.maximum(h - 1.0, 0.0)


def iota(shape, dim):
    return lax.broadcasted_iota(jnp.int32, shape, dim)


def to_lanes(column):
    bx, by, _ = column.shape
    diagonal = iota((bx, by, 128), 1) == iota((bx, by, 128), 2)
    return jnp.sum(jnp.where(diagonal, column, 0.0), axis=1)


def to_column(line, by):
    bx = line.shape[0]
    diagonal = iota((bx, by, 128), 1) == iota((bx, by, 128), 2)
    return jnp.sum(jnp.where(diagonal, line[:, None, :], 0.0), axis=2, keepdims=True)


def conduct(h, k, xlo, xhi, ylo, yhi, zlo, zhi):
    bx, by, bz = h.shape
    t = temperature(h)
    row, lane = iota((bx, by, bz), 1), iota((bx, by, bz), 2)
    if bx > 1:
        total = jnp.concatenate([xlo, t[:-1]], axis=0) + jnp.concatenate([t[1:], xhi], axis=0)
    else:
        total = xlo + xhi
    total += jnp.where(row == 0, ylo[:, None, :], pltpu.roll(t, 1, 1))
    total += jnp.where(row == by - 1, yhi[:, None, :], pltpu.roll(t, by - 1, 1))
    total += jnp.where(lane == 0, to_column(zlo, by), pltpu.roll(t, 1, 2))
    total += jnp.where(lane == bz - 1, to_column(zhi, by), pltpu.roll(t, bz - 1, 2))
    return h + RATE * k * (total - 6.0 * t)


def sublanes(value, y):
    return jnp.concatenate([value[x, y : y + 1, :] for x in range(value.shape[0])], axis=0)


def side_blocks(h, k):
    by, bz = h.shape[1:]
    return [
        (sublanes(h, 0), sublanes(h, 1), sublanes(k, 0)),
        (sublanes(h, by - 1), sublanes(h, by - 2), sublanes(k, by - 1)),
        (to_lanes(h[:, :, 0:1]), to_lanes(h[:, :, 1:2]), to_lanes(k[:, :, 0:1])),
        (to_lanes(h[:, :, bz - 1 : bz]), to_lanes(h[:, :, bz - 2 : bz - 1]), to_lanes(k[:, :, bz - 1 : bz])),
    ]


def column_of(row):
    square = (row.shape[1], row.shape[1])
    return jnp.sum(jnp.where(iota(square, 0) == iota(square, 1), row, 0.0), axis=1, keepdims=True)


def write_tables(plane_cap, source, block, neighbour, asked, table):
    me = lax.axis_index("gx").astype(F32)
    count = len(asked)
    records = (count - 1) * plane_cap
    cap = float(plane_cap)

    def wrapped(shift):
        return jnp.where(shift < 0.0, shift + float(count), shift)

    square = (SLOTS, SLOTS)
    before = iota(square, 0) < iota(square, 1)
    slot = iota((1, SLOTS), 1).astype(F32)
    source_row, block_column = source[...].astype(F32), column_of(block[...].astype(F32))
    source_column = column_of(source_row)
    rank = jnp.sum(
        jnp.where((source_column == source_row) & before, 1.0, 0.0), axis=0, keepdims=True
    )
    rank_column = column_of(rank)
    lane = iota((SLOTS, 128), 1).astype(F32)
    for shift in range(count):
        hit = (wrapped(source_column - me) == float(shift)) & (rank_column == lane)
        row = jnp.sum(jnp.where(hit, block_column, 0.0), axis=0, keepdims=True)
        asked[shift][...] = jnp.broadcast_to(row, asked[shift].shape)
    table[6:7, 0:SLOTS] = wrapped(me - source_row).astype(jnp.int32)
    table[7:8, 0:SLOTS] = rank.astype(jnp.int32)
    slot_column = iota((SLOTS, records), 0).astype(F32)
    for face in range(FACES):
        number = neighbour[face]
        owner_row, number_row = (number >> 4).astype(F32), number.astype(F32)
        owner_column, number_column = column_of(owner_row), column_of(number_row)
        other_row = (number_row >= 0.0) & (owner_row != me)
        alike = (owner_column == owner_row) & (owner_column >= 0.0) & (owner_column != me)
        receive_rank = jnp.sum(
            jnp.where(alike & (number_column < number_row), 1.0, 0.0), axis=0, keepdims=True
        )
        send_rank = jnp.sum(jnp.where(alike & before, 1.0, 0.0), axis=0, keepdims=True)
        here = records + (number_row - owner_row * SLOTS)
        there = (wrapped(me - owner_row) - 1.0) * cap + receive_rank
        receive = jnp.where(owner_row == me, here, there)
        receive = jnp.where(number_row < 0.0, records + SLOTS + slot, receive)
        table[face : face + 1, 0:SLOTS] = receive.astype(jnp.int32)
        key = jnp.where(other_row, (wrapped(owner_row - me) - 1.0) * cap + send_rank, -1.0)
        hit = iota((SLOTS, records), 1).astype(F32) == column_of(key)
        tile = jnp.sum(jnp.where(hit, slot_column, 0.0), axis=0, keepdims=True)
        table[face ^ 1 : (face ^ 1) + 1, SLOTS : SLOTS + records] = tile.astype(jnp.int32)


def sides_kernel(
    sizes, plane_cap, source_far, block_far, neighbour_far, h_far, k_far, send, table, *rest
):
    *asked, source, block, neighbour, h, k, sems = rest
    ny, nz = sizes
    my_y, my_z = lax.axis_index("gy"), lax.axis_index("gz")
    bx = h.shape[0]
    small = [(source_far, source), (block_far, block), (neighbour_far, neighbour)]
    copies = [pltpu.make_async_copy(*pair, sems.at[2 * bx + n]) for n, pair in enumerate(small)]
    large = []
    for x in range(bx):
        large.append(pltpu.make_async_copy(h_far.at[x], h.at[x], sems.at[x]))
        large.append(pltpu.make_async_copy(k_far.at[x], k.at[x], sems.at[bx + x]))
    for copy in copies + large:
        copy.start()
    for copy in copies:
        copy.wait()
    write_tables(plane_cap, source, block, neighbour, asked, table)
    for copy in large:
        copy.wait()
    blocks = side_blocks(h[...], k[...])
    for y in range(ny):
        for z in range(nz):
            for part in range(3):
                ylo, yhi, zlo, zhi = [block[part] for block in blocks]
                chosen = jnp.where(
                    my_y == y, jnp.where(z < my_z, zlo, zhi), jnp.where(y < my_y, ylo, yhi)
                )
                send[y * nz + z, part * bx : part * bx + bx, :] = chosen


def side_reader(sizes, got, bx):
    ny, nz = sizes
    my_y, my_z = lax.axis_index("gy"), lax.axis_index("gz")

    def read(dy, dz, part=0):
        y, z = my_y + dy, my_z + dz
        inside = (y >= 0) & (y < ny) & (z >= 0) & (z < nz)
        at = jnp.where(inside, y * nz + z, 0)
        return jnp.where(inside, got[at, part * bx : part * bx + bx, :], 0.0)

    return read


def layers_kernel(sizes, h, k, got, ask_up, ask_down, *rest):
    down, up = rest[-2:]
    bx, by, bz = h.shape
    read = side_reader(sizes, got, bx)
    around = [read(-1, 0), read(1, 0), read(0, -1), read(0, 1)]
    for out, near, far, ask in ((down, 0, 1, ask_down), (up, bx - 1, bx - 2, ask_up)):
        out[0:by, :] = h[near]
        out[by : 2 * by, :] = h[far]
        out[2 * by : 3 * by, :] = k[near]
        for number, side in enumerate(around):
            out[3 * by + number : 3 * by + number + 1, :] = side[near : near + 1, :]
        out[3 * by + 4 : 3 * by + 8, :] = ask[0:4, :]


def block_layout(cap):
    parts = 128 // CB // cap
    return parts, CB // parts


def flat_step(h, k, inner, outer, first, last, before, after, length):
    bx, lanes = h.shape
    t = temperature(h)
    row, lane = iota(h.shape, 0), iota(h.shape, 1)
    total = temperature(inner) + temperature(outer)
    total += jnp.where(row == 0, temperature(first), pltpu.roll(t, 1, 0))
    total += jnp.where(row == bx - 1, temperature(last), pltpu.roll(t, bx - 1, 0))
    total += jnp.where(lane == 0, temperature(before), pltpu.roll(t, 1, 1))
    total += jnp.where(lane == length - 1, temperature(after), pltpu.roll(t, lanes - 1, 1))
    return h + RATE * k * (total - 6.0 * t)


def heat_kernel(cap, sizes, request, h, k, got, low, high, *rest):
    count = lax.axis_size("gx")
    packed, (out, found, *send, held) = rest[: count - 1], rest[count - 1 :]

    bx, by, bz = h.shape
    h0, k0 = h[...], k[...]
    read = side_reader(sizes, got, bx)
    me = lax.axis_index("gx")
    layers, lines = [], []
    for beside, inside in ((low, me > 0), (high, me < count - 1)):
        beside = jnp.where(inside, beside[...], 0.0)
        layers.append([beside[part * by : part * by + by, :][None] for part in range(3)])
        lines.append([beside[3 * by + n : 3 * by + n + 1, :] for n in range(4)])
    y_sides = [[read(d, 0, part) for part in range(3)] for d in (-1, 1)]
    z_sides = [[read(0, d, part) for part in range(3)] for d in (-1, 1)]
    corner = [[read(dy, dz) for dz in (-1, 1)] for dy in (-1, 1)]
    to_first = [[pltpu.roll(c[0], 1, 1), c[1]] for c in corner]
    y_inner = [sublanes(h0, 0), sublanes(h0, by - 1)]
    z_inner = [to_lanes(h0[:, :, 0:1]), to_lanes(h0[:, :, bz - 1 : bz])]

    sides = [temperature(layers[0][0]), temperature(layers[1][0])]
    sides += [temperature(side[0]) for side in y_sides + z_sides]
    h1 = conduct(h0, k0, *sides)
    next_sides = []
    for side in range(2):
        near, far, near_k = layers[side]
        across = [temperature(far), temperature(h0[0:1])]
        if side:
            across = [temperature(h0[bx - 1 : bx]), temperature(far)]
        next_sides.append(conduct(near, near_k, *across, *[temperature(line) for line in lines[side]]))
    for side in range(2):
        near, far, near_k = y_sides[side]
        ends = [to_first[side][0], pltpu.roll(to_first[side][1], bz - 1, 1)]
        next_sides.append(
            flat_step(near, near_k, y_inner[side], far, lines[0][side], lines[1][side], *ends, bz)
        )
    for side in range(2):
        near, far, near_k = z_sides[side]
        ends = [to_first[0][side], pltpu.roll(to_first[1][side], by - 1, 1)]
        next_sides.append(
            flat_step(near, near_k, z_inner[side], far, lines[0][2 + side], lines[1][2 + side], *ends, by)
        )
    h2 = conduct(h1, k0, *[temperature(side) for side in next_sides])
    out[...] = h2

    held[...] = temperature(h2).reshape(bx, by // CB, CB, bz)
    parts, deep = block_layout(cap)
    nby, nbz = by // CB, bz // CB
    group = iota((deep, CB, bz), 2) // CB
    for shift in range(count):
        total = jnp.zeros((deep, CB, bz), F32)
        for rank in range(cap):
            block = request[(count - shift) % count, rank]
            a, b, c = block // (nby * nbz), (block // nbz) % nby, block % nbz
            for part in range(parts):
                at = rank * parts + part
                patch = held[pl.ds(a * CB + part * deep, deep), b]
                moved = pltpu.roll(patch, (CB * at - CB * c + bz) % bz, 2)
                total = jnp.where(group == at, moved, total)
        total = total.reshape(deep * CB, bz)
        if shift == 0:
            found[...] = total
        else:
            behind = packed[shift - 1].shape[0]
            send[shift - 1][0:behind, :] = packed[shift - 1][...]
            send[shift - 1][behind:, :] = total


def write_records(phase, solute, picks, own):
    flat = [f.reshape(SLOTS * TE, PLANE) for f in (phase, solute)]
    high, low = halves(jnp.concatenate(flat, axis=1))
    planes = dot(high, picks) + dot(low, picks)
    own[0:SLOTS, 0:TE, :] = planes[:, 0:128].reshape(SLOTS, TE, 128)
    own[SLOTS : 2 * SLOTS, 0:TE, :] = planes[:, 128:256].reshape(SLOTS, TE, 128)
    for face in range(2):
        for number, field in enumerate((phase, solute)):
            for half in range(2):
                row = TE + face * 4 + number * 2 + half
                lanes = slice(half * 128, half * 128 + 128)
                near, far = (0, TE - 1) if face == 0 else (TE - 1, 0)
                own[0:SLOTS, row : row + 1, :] = field[:, far : far + 1, lanes]
                own[SLOTS : 2 * SLOTS, row : row + 1, :] = field[:, near : near + 1, lanes]


def merge_record(source, number):
    side = (iota((TE, 128), 1) % 64) // TE
    out = source[number(2), 0:TE, :]
    for face in range(3, 6):
        out = jnp.where(side == face - 2, source[number(face), 0:TE, :], out)
    edge = jnp.where(
        iota((8, 128), 0) < 4, source[number(0), TE:REC, :], source[number(1), TE:REC, :]
    )
    return out, edge


def pack(own, table, send):
    cap = send[0].shape[0] // REC
    for number, out in enumerate(send):
        for rank in range(cap):
            record = number * cap + rank
            planes, edge = merge_record(own, lambda face: table[face, SLOTS + record])
            out[rank * REC : rank * REC + TE, :] = planes
            out[rank * REC + TE : rank * REC + REC, :] = edge


def first_pack_kernel(table, phase, solute, picks, own, *send):
    write_records(phase[...], solute[...], picks[...], own)
    pack(own, table, send)


def take_heat(cap, table, found, got, spreads, blocks, held, heat):
    parts, deep = block_layout(cap)
    blocks[0] = found[...]
    for number, value in enumerate(got):
        blocks[1 + number] = value[value.shape[0] - deep * CB :, :]
    group = iota((CB, 128), 1) // CB
    for slot in range(SLOTS):
        back, rank = table[6, slot], table[7, slot]
        for x in range(CB):
            row = (x % deep) * CB
            patch = blocks[back, row : row + CB, :]
            held[slot * CB + x] = jnp.where(group == rank * parts + x // deep, patch, 0.0)
    rows = held[...].reshape(SLOTS * CB * CB, 128)
    wide = dot(jnp.concatenate(halves(rows), axis=1), spreads)
    wide = wide.reshape(SLOTS * CB, CB, PLANE)
    keep = iota(wide.shape, 1) == iota(wide.shape, 2) // TE // 2
    coarse = jnp.sum(jnp.where(keep, wide, 0.0), axis=1)
    for half in range(2):
        for odd in range(2):
            heat[half, pl.ds(odd, SLOTS * CB, 2), :] = coarse[:, half * 128 : half * 128 + 128]


def step(table, phase, solute, heat, got, own, stencil, places, all_records, ghosts):
    records = all_records.shape[0] - 2 * SLOTS
    cap = records // len(got)
    for number, value in enumerate(got):
        all_records[number * cap : number * cap + cap] = value[0 : cap * REC, :].reshape(cap, REC, 128)
    all_records[records : records + 2 * SLOTS] = own[...]
    for slot in range(SLOTS):
        out, edge = merge_record(all_records, lambda face: table[face, slot])
        ghosts[slot, 0:TE, :] = out
        ghosts[slot, TE:REC, :] = edge
    beside = jnp.concatenate(halves(ghosts[:, 0:TE, :].reshape(SLOTS * TE, 128)), axis=1)
    beside = dot(beside, places)
    row = iota((SLOTS, TE, PLANE), 1)
    lap = []
    for number, field in enumerate((phase, solute)):
        high, low = halves(field.reshape(SLOTS * TE, PLANE))
        total = dot(high, stencil) + dot(low, stencil)
        total += beside[:, number * PLANE : number * PLANE + PLANE]
        total = total.reshape(SLOTS, TE, PLANE) - 6.0 * field
        sides = []
        for face in range(2):
            at = TE + face * 4 + number * 2
            sides.append(
                jnp.concatenate([ghosts[:, at : at + 1, :], ghosts[:, at + 1 : at + 2, :]], axis=2)
            )
        total += jnp.where(row == 0, sides[0], pltpu.roll(field, 1, 1))
        total += jnp.where(row == TE - 1, sides[1], pltpu.roll(field, TE - 1, 1))
        lap.append(total)
    warm = jnp.concatenate([heat[0], heat[1]], axis=1).reshape(SLOTS, TE, PLANE)
    squared = 1.0 - phase * phase
    new_phase = phase + ORDER_SPEED * (
        lap[0] + phase - phase * phase * phase - COUPLING * (warm + solute) * squared * squared
    )
    new_solute = solute + SOLUTE_RATE * lap[1] + REJECTION * (new_phase - phase)
    return new_phase, new_solute


def first_step_kernel(cap, table, phase, solute, own, picks, stencil, places, spreads, found, *rest):
    others = lax.axis_size("gx") - 1
    got, rest = rest[:others], rest[others:]
    phase_out, solute_out, heat_out, own_out, *rest = rest
    send, (all_records, ghosts, blocks, held) = rest[:others], rest[others:]
    take_heat(cap, table, found, got, spreads[...], blocks, held, heat_out)
    new_phase, new_solute = step(
        table, phase[...], solute[...], heat_out[...], got, own, stencil[...], places[...],
        all_records, ghosts,
    )
    phase_out[...] = new_phase
    solute_out[...] = new_solute
    write_records(new_phase, new_solute, picks[...], own_out)
    pack(own_out, table, send)


def write_out_kernel(value, out, sem):
    copy = pltpu.make_async_copy(value, out, sem)
    copy.start()
    copy.wait()


def middle_step_kernel(table, phase, solute, heat, own, picks, stencil, places, *rest):
    others = lax.axis_size("gx") - 1
    got, (phase_out, solute_out, own_out, *rest) = rest[:others], rest[others:]
    send, (all_records, ghosts) = rest[:others], rest[others:]
    new_phase, new_solute = step(
        table, phase[...], solute[...], heat[...], got, own, stencil[...], places[...],
        all_records, ghosts,
    )
    phase_out[...] = new_phase
    solute_out[...] = new_solute
    write_records(new_phase, new_solute, picks[...], own_out)
    pack(own_out, table, send)


def last_step_kernel(table, phase, solute, heat, own, stencil, places, *rest):
    others = lax.axis_size("gx") - 1
    got, (phase_out, solute_out, all_records, ghosts) = rest[:others], rest[others:]
    new_phase, new_solute = step(
        table, phase[...], solute[...], heat[...], got, own, stencil[...], places[...],
        all_records, ghosts,
    )
    phase_out[...] = new_phase
    solute_out[...] = new_solute


def call(kernel, in_specs, out_shapes, scratch=(), out_specs=None, mib=16):
    return pl.pallas_call(
        kernel,
        out_shape=out_shapes,
        in_specs=in_specs,
        out_specs=out_specs or jax.tree.map(lambda _: VMEM, out_shapes),
        scratch_shapes=list(scratch),
        compiler_params=pltpu.CompilerParams(vmem_limit_bytes=mib * 1024 * 1024),
    )


def shape(*dims):
    return jax.ShapeDtypeStruct(dims, F32)


def local(enthalpy, conductivity, phase, solute, tile_source, tile_block, tile_neighbour):
    count = lax.axis_size("gx")
    sizes = (lax.axis_size("gy"), lax.axis_size("gz"))
    plane_cap = -(-SLOTS // (count - 1))
    block_cap = 2 * SLOTS // count
    others = count - 1
    records = others * plane_cap
    bx, by, bz = enthalpy.shape
    picks, stencil, places, spreads = tables()

    integers = functools.partial(jax.ShapeDtypeStruct, dtype=jnp.int32)
    sides, table, *asked = call(
        functools.partial(sides_kernel, sizes, plane_cap),
        [ANY] * 5,
        [shape(sizes[0] * sizes[1], 3 * bx, 128), integers((8, 128)), *[shape(8, 128)] * count],
        [
            pltpu.VMEM((1, SLOTS), jnp.int32),
            pltpu.VMEM((1, SLOTS), jnp.int32),
            pltpu.VMEM((FACES, 1, SLOTS), jnp.int32),
            pltpu.VMEM((bx, by, bz), F32),
            pltpu.VMEM((bx, by, bz), F32),
            pltpu.SemaphoreType.DMA((2 * bx + 3,)),
        ],
        mib=56,
    )(
        tile_source.reshape(1, SLOTS),
        tile_block.reshape(1, SLOTS),
        jnp.transpose(tile_neighbour, (0, 1, 4, 2, 3)).reshape(FACES, 1, SLOTS),
        enthalpy,
        conductivity,
    )
    sides = lax.all_to_all(sides, ("gy", "gz"), split_axis=0, concat_axis=0, tiled=True)

    def pass_on(value, shift):
        return lax.ppermute(value, "gx", [(i, (i + shift) % count) for i in range(count)])

    def exchange(values):
        return [pass_on(value, shift) for shift, value in enumerate(values, 1)]

    farther = [pass_on(asked[shift], shift) for shift in range(2, others)]

    phase_field = phase.reshape(SLOTS, TE, PLANE)
    solute_field = solute.reshape(SLOTS, TE, PLANE)
    own_shape, send_shapes = shape(2 * SLOTS, REC, 128), [shape(plane_cap * REC, 128)] * others
    own, *packed = call(first_pack_kernel, [SMEM] + [VMEM] * 3, [own_shape, *send_shapes])(
        table, phase_field, solute_field, picks
    )

    layer = shape(3 * by + 8, bz)
    down, up = call(
        functools.partial(layers_kernel, sizes), [VMEM] * 5 + [ANY] * (1 + len(farther)), [layer, layer]
    )(enthalpy, conductivity, sides, asked[1], asked[others], packed[0], *farther)
    from_low, from_high = pass_on(up, 1), pass_on(down, others)
    row = 3 * by + 4
    request = [asked[0][0], from_low[row], *[value[0] for value in farther], from_high[row]]
    request = jnp.stack([value[:block_cap] for value in request]).astype(jnp.int32)
    _, deep = block_layout(block_cap)
    brick = shape(bx, by, bz)
    heated, found, *send = call(
        functools.partial(heat_kernel, block_cap, sizes),
        [SMEM] + [VMEM] * (5 + others),
        [brick, shape(deep * CB, 128)] + [shape(plane_cap * REC + deep * CB, 128)] * others,
        [pltpu.VMEM((bx, by // CB, CB, bz), F32)],
    )(request, enthalpy, conductivity, sides, from_low, from_high, *packed)

    (heat_out,) = call(write_out_kernel, [ANY], [brick], [pltpu.SemaphoreType.DMA], [ANY])(heated)

    got = exchange(send)
    field = shape(SLOTS, TE, PLANE)
    step_scratch = [
        pltpu.VMEM((records + 2 * SLOTS, REC, 128), F32),
        pltpu.VMEM((SLOTS, REC, 128), F32),
    ]
    phase_field, solute_field, heat, own, *send = call(
        functools.partial(first_step_kernel, block_cap),
        [SMEM] + [VMEM] * (8 + others),
        [field, field, shape(2, SLOTS * TE, 128), own_shape, *send_shapes],
        step_scratch
        + [
            pltpu.VMEM((count, deep * CB, 128), F32),
            pltpu.VMEM((SLOTS * CB, CB, 128), F32),
        ],
    )(table, phase_field, solute_field, own, picks, stencil, places, spreads, found, *got)
    for _ in range(PHASE_STEPS - 2):
        got = exchange(send)
        phase_field, solute_field, own, *send = call(
            middle_step_kernel,
            [SMEM] + [VMEM] * (7 + others),
            [field, field, own_shape, *send_shapes],
            step_scratch,
        )(table, phase_field, solute_field, heat, own, picks, stencil, places, *got)
    got = exchange(send)
    phase_field, solute_field = call(
        last_step_kernel, [SMEM] + [VMEM] * (6 + others), [field, field], step_scratch
    )(table, phase_field, solute_field, heat, own, stencil, places, *got)
    return heat_out, phase_field.reshape(phase.shape), solute_field.reshape(solute.shape)


def solution(mesh):
    grid = P("gx", "gy", "gz")
    tiles = P("gx", "gy", "gz", None, None, None)
    return jax.shard_map(
        local,
        mesh=mesh,
        in_specs=(
            grid,
            grid,
            tiles,
            tiles,
            P("gx", "gy", "gz", None, None),
            P("gx", "gy", "gz", None),
            P("gx", "gy", "gz", None, None),
        ),
        out_specs=(grid, tiles, tiles),
        check_vma=False,
    )
```

```python
import functools

import jax
import jax.numpy as jnp
import numpy as np
from jax import lax
from jax.experimental import pallas as pl
from jax.experimental.pallas import tpu as pltpu
from jax.sharding import PartitionSpec as P

CB = 8
TE = 16
PLANE = TE * TE
SLOTS = 16
FACES = 6
PHASE_STEPS = 4
REC = 24

RATE = 0.16
ORDER_SPEED = 0.1
SOLUTE_RATE = 0.15
COUPLING = 0.5
REJECTION = 0.5

F32 = jnp.float32
BF16 = jnp.bfloat16
VMEM = pl.BlockSpec(memory_space=pltpu.VMEM)
SMEM = pl.BlockSpec(memory_space=pltpu.SMEM)
ANY = pl.BlockSpec(memory_space=pl.ANY)


def plane_lane(face):
    j = np.arange(TE)
    return [j, PLANE - TE + j, j * TE, j * TE + TE - 1][face - 2]


def constant_tables():
    pick = np.zeros((2, PLANE, 256), np.float32)
    place = np.zeros((2, 128, PLANE), np.float32)
    for field in range(2):
        for face in range(2, 6):
            at = field * 64 + (face - 2) * TE + np.arange(TE)
            pick[field, plane_lane(face ^ 1), at] = 1.0
            pick[field, plane_lane(face), 128 + at] = 1.0
            place[field, at, plane_lane(face)] = 1.0
    y, z = np.divmod(np.arange(PLANE), TE)
    dy, dz = np.abs(y[:, None] - y[None, :]), np.abs(z[:, None] - z[None, :])
    stencil = ((dy + dz) == 1).astype(np.float32)
    lane = np.arange(128)
    spread = (lane[:, None] % CB == z[None, :] // 2).astype(np.float32)
    return pick, place, stencil, spread


def tables():
    pick, place, stencil, spread = constant_tables()
    place = np.concatenate([place[0], place[1]], axis=1)
    return (
        jnp.asarray(np.concatenate([pick[0], pick[1]], axis=0), BF16),
        jnp.asarray(stencil, BF16),
        jnp.asarray(np.concatenate([place, place], axis=0), BF16),
        jnp.asarray(np.concatenate([spread, spread], axis=0), BF16),
    )


def halves(value):
    high = value.astype(BF16)
    return high, (value - high.astype(F32)).astype(BF16)


def dot(a, b):
    return jnp.dot(a, b, preferred_element_type=F32)


def temperature(h):
    return jnp.minimum(h, 0.0) + jnp.maximum(h - 1.0, 0.0)


def iota(shape, dim):
    return lax.broadcasted_iota(jnp.int32, shape, dim)


def to_lanes(column):
    bx, by, _ = column.shape
    diagonal = iota((bx, by, 128), 1) == iota((bx, by, 128), 2)
    return jnp.sum(jnp.where(diagonal, column, 0.0), axis=1)


def to_column(line, by):
    bx = line.shape[0]
    diagonal = iota((bx, by, 128), 1) == iota((bx, by, 128), 2)
    return jnp.sum(jnp.where(diagonal, line[:, None, :], 0.0), axis=2, keepdims=True)


def conduct(h, k, xlo, xhi, ylo, yhi, zlo, zhi):
    bx, by, bz = h.shape
    t = temperature(h)
    row, lane = iota((bx, by, bz), 1), iota((bx, by, bz), 2)
    if bx > 1:
        total = jnp.concatenate([xlo, t[:-1]], axis=0) + jnp.concatenate([t[1:], xhi], axis=0)
    else:
        total = xlo + xhi
    total += jnp.where(row == 0, ylo[:, None, :], pltpu.roll(t, 1, 1))
    total += jnp.where(row == by - 1, yhi[:, None, :], pltpu.roll(t, by - 1, 1))
    total += jnp.where(lane == 0, to_column(zlo, by), pltpu.roll(t, 1, 2))
    total += jnp.where(lane == bz - 1, to_column(zhi, by), pltpu.roll(t, bz - 1, 2))
    return h + RATE * k * (total - 6.0 * t)


def sublanes(value, y):
    return jnp.concatenate([value[x, y : y + 1, :] for x in range(value.shape[0])], axis=0)


def side_blocks(h, k):
    by, bz = h.shape[1:]
    return [
        (sublanes(h, 0), sublanes(h, 1), sublanes(k, 0)),
        (sublanes(h, by - 1), sublanes(h, by - 2), sublanes(k, by - 1)),
        (to_lanes(h[:, :, 0:1]), to_lanes(h[:, :, 1:2]), to_lanes(k[:, :, 0:1])),
        (to_lanes(h[:, :, bz - 1 : bz]), to_lanes(h[:, :, bz - 2 : bz - 1]), to_lanes(k[:, :, bz - 1 : bz])),
    ]


def column_of(row):
    square = (row.shape[1], row.shape[1])
    return jnp.sum(jnp.where(iota(square, 0) == iota(square, 1), row, 0.0), axis=1, keepdims=True)


def write_tables(plane_cap, source, block, neighbour, asked, table):
    me = lax.axis_index("gx").astype(F32)
    count = len(asked)
    records = (count - 1) * plane_cap
    cap = float(plane_cap)

    def wrapped(shift):
        return jnp.where(shift < 0.0, shift + float(count), shift)

    square = (SLOTS, SLOTS)
    before = iota(square, 0) < iota(square, 1)
    slot = iota((1, SLOTS), 1).astype(F32)
    source_row, block_column = source[...].astype(F32), column_of(block[...].astype(F32))
    source_column = column_of(source_row)
    rank = jnp.sum(
        jnp.where((source_column == source_row) & before, 1.0, 0.0), axis=0, keepdims=True
    )
    rank_column = column_of(rank)
    lane = iota((SLOTS, 128), 1).astype(F32)
    for shift in range(count):
        hit = (wrapped(source_column - me) == float(shift)) & (rank_column == lane)
        row = jnp.sum(jnp.where(hit, block_column, 0.0), axis=0, keepdims=True)
        asked[shift][...] = jnp.broadcast_to(row, asked[shift].shape)
    table[6:7, 0:SLOTS] = wrapped(me - source_row).astype(jnp.int32)
    table[7:8, 0:SLOTS] = rank.astype(jnp.int32)
    slot_column = iota((SLOTS, records), 0).astype(F32)
    for face in range(FACES):
        number = neighbour[face]
        owner_row, number_row = (number >> 4).astype(F32), number.astype(F32)
        owner_column, number_column = column_of(owner_row), column_of(number_row)
        other_row = (number_row >= 0.0) & (owner_row != me)
        alike = (owner_column == owner_row) & (owner_column >= 0.0) & (owner_column != me)
        receive_rank = jnp.sum(
            jnp.where(alike & (number_column < number_row), 1.0, 0.0), axis=0, keepdims=True
        )
        send_rank = jnp.sum(jnp.where(alike & before, 1.0, 0.0), axis=0, keepdims=True)
        here = records + (number_row - owner_row * SLOTS)
        there = (wrapped(me - owner_row) - 1.0) * cap + receive_rank
        receive = jnp.where(owner_row == me, here, there)
        receive = jnp.where(number_row < 0.0, records + SLOTS + slot, receive)
        table[face : face + 1, 0:SLOTS] = receive.astype(jnp.int32)
        key = jnp.where(other_row, (wrapped(owner_row - me) - 1.0) * cap + send_rank, -1.0)
        hit = iota((SLOTS, records), 1).astype(F32) == column_of(key)
        tile = jnp.sum(jnp.where(hit, slot_column, 0.0), axis=0, keepdims=True)
        table[face ^ 1 : (face ^ 1) + 1, SLOTS : SLOTS + records] = tile.astype(jnp.int32)


def sides_kernel(
    sizes, plane_cap, source_far, block_far, neighbour_far, h_far, k_far, send, table, *rest
):
    *asked, source, block, neighbour, h, k, sems = rest
    ny, nz = sizes
    my_y, my_z = lax.axis_index("gy"), lax.axis_index("gz")
    bx = h.shape[0]
    small = [(source_far, source), (block_far, block), (neighbour_far, neighbour)]
    copies = [pltpu.make_async_copy(*pair, sems.at[2 * bx + n]) for n, pair in enumerate(small)]
    large = []
    for x in range(bx):
        large.append(pltpu.make_async_copy(h_far.at[x], h.at[x], sems.at[x]))
        large.append(pltpu.make_async_copy(k_far.at[x], k.at[x], sems.at[bx + x]))
    for copy in copies + large:
        copy.start()
    for copy in copies:
        copy.wait()
    write_tables(plane_cap, source, block, neighbour, asked, table)
    for copy in large:
        copy.wait()
    blocks = side_blocks(h[...], k[...])
    for y in range(ny):
        for z in range(nz):
            for part in range(3):
                ylo, yhi, zlo, zhi = [block[part] for block in blocks]
                chosen = jnp.where(
                    my_y == y, jnp.where(z < my_z, zlo, zhi), jnp.where(y < my_y, ylo, yhi)
                )
                send[y * nz + z, part * bx : part * bx + bx, :] = chosen


def side_reader(sizes, got, bx):
    ny, nz = sizes
    my_y, my_z = lax.axis_index("gy"), lax.axis_index("gz")

    def read(dy, dz, part=0):
        y, z = my_y + dy, my_z + dz
        inside = (y >= 0) & (y < ny) & (z >= 0) & (z < nz)
        at = jnp.where(inside, y * nz + z, 0)
        return jnp.where(inside, got[at, part * bx : part * bx + bx, :], 0.0)

    return read


def layers_kernel(sizes, h, k, got, ask_up, ask_down, *rest):
    down, up = rest[-2:]
    bx, by, bz = h.shape
    read = side_reader(sizes, got, bx)
    around = [read(-1, 0), read(1, 0), read(0, -1), read(0, 1)]
    for out, near, far, ask in ((down, 0, 1, ask_down), (up, bx - 1, bx - 2, ask_up)):
        out[0:by, :] = h[near]
        out[by : 2 * by, :] = h[far]
        out[2 * by : 3 * by, :] = k[near]
        for number, side in enumerate(around):
            out[3 * by + number : 3 * by + number + 1, :] = side[near : near + 1, :]
        out[3 * by + 4 : 3 * by + 8, :] = ask[0:4, :]


def block_layout(cap):
    parts = 128 // CB // cap
    return parts, CB // parts


def flat_step(h, k, inner, outer, first, last, before, after, length):
    bx, lanes = h.shape
    t = temperature(h)
    row, lane = iota(h.shape, 0), iota(h.shape, 1)
    total = temperature(inner) + temperature(outer)
    total += jnp.where(row == 0, temperature(first), pltpu.roll(t, 1, 0))
    total += jnp.where(row == bx - 1, temperature(last), pltpu.roll(t, bx - 1, 0))
    total += jnp.where(lane == 0, temperature(before), pltpu.roll(t, 1, 1))
    total += jnp.where(lane == length - 1, temperature(after), pltpu.roll(t, lanes - 1, 1))
    return h + RATE * k * (total - 6.0 * t)


def heat_kernel(cap, sizes, request, h, k, got, low, high, *rest):
    count = lax.axis_size("gx")
    packed, (out, found, *send, held) = rest[: count - 1], rest[count - 1 :]

    bx, by, bz = h.shape
    h0, k0 = h[...], k[...]
    read = side_reader(sizes, got, bx)
    me = lax.axis_index("gx")
    layers, lines = [], []
    for beside, inside in ((low, me > 0), (high, me < count - 1)):
        beside = jnp.where(inside, beside[...], 0.0)
        layers.append([beside[part * by : part * by + by, :][None] for part in range(3)])
        lines.append([beside[3 * by + n : 3 * by + n + 1, :] for n in range(4)])
    y_sides = [[read(d, 0, part) for part in range(3)] for d in (-1, 1)]
    z_sides = [[read(0, d, part) for part in range(3)] for d in (-1, 1)]
    corner = [[read(dy, dz) for dz in (-1, 1)] for dy in (-1, 1)]
    to_first = [[pltpu.roll(c[0], 1, 1), c[1]] for c in corner]
    y_inner = [sublanes(h0, 0), sublanes(h0, by - 1)]
    z_inner = [to_lanes(h0[:, :, 0:1]), to_lanes(h0[:, :, bz - 1 : bz])]

    sides = [temperature(layers[0][0]), temperature(layers[1][0])]
    sides += [temperature(side[0]) for side in y_sides + z_sides]
    h1 = conduct(h0, k0, *sides)
    next_sides = []
    for side in range(2):
        near, far, near_k = layers[side]
        across = [temperature(far), temperature(h0[0:1])]
        if side:
            across = [temperature(h0[bx - 1 : bx]), temperature(far)]
        next_sides.append(conduct(near, near_k, *across, *[temperature(line) for line in lines[side]]))
    for side in range(2):
        near, far, near_k = y_sides[side]
        ends = [to_first[side][0], pltpu.roll(to_first[side][1], bz - 1, 1)]
        next_sides.append(
            flat_step(near, near_k, y_inner[side], far, lines[0][side], lines[1][side], *ends, bz)
        )
    for side in range(2):
        near, far, near_k = z_sides[side]
        ends = [to_first[0][side], pltpu.roll(to_first[1][side], by - 1, 1)]
        next_sides.append(
            flat_step(near, near_k, z_inner[side], far, lines[0][2 + side], lines[1][2 + side], *ends, by)
        )
    h2 = conduct(h1, k0, *[temperature(side) for side in next_sides])
    out[...] = h2

    held[...] = temperature(h2).reshape(bx, by // CB, CB, bz)
    parts, deep = block_layout(cap)
    nby, nbz = by // CB, bz // CB
    group = iota((deep, CB, bz), 2) // CB
    for shift in range(count):
        total = jnp.zeros((deep, CB, bz), F32)
        for rank in range(cap):
            block = request[(count - shift) % count, rank]
            a, b, c = block // (nby * nbz), (block // nbz) % nby, block % nbz
            for part in range(parts):
                at = rank * parts + part
                patch = held[pl.ds(a * CB + part * deep, deep), b]
                moved = pltpu.roll(patch, (CB * at - CB * c + bz) % bz, 2)
                total = jnp.where(group == at, moved, total)
        total = total.reshape(deep * CB, bz)
        if shift == 0:
            found[...] = total
        else:
            behind = packed[shift - 1].shape[0]
            send[shift - 1][0:behind, :] = packed[shift - 1][...]
            send[shift - 1][behind:, :] = total


def write_records(phase, solute, picks, own):
    flat = [f.reshape(SLOTS * TE, PLANE) for f in (phase, solute)]
    high, low = halves(jnp.concatenate(flat, axis=1))
    planes = dot(high, picks) + dot(low, picks)
    own[0:SLOTS, 0:TE, :] = planes[:, 0:128].reshape(SLOTS, TE, 128)
    own[SLOTS : 2 * SLOTS, 0:TE, :] = planes[:, 128:256].reshape(SLOTS, TE, 128)
    for face in range(2):
        for number, field in enumerate((phase, solute)):
            for half in range(2):
                row = TE + face * 4 + number * 2 + half
                lanes = slice(half * 128, half * 128 + 128)
                near, far = (0, TE - 1) if face == 0 else (TE - 1, 0)
                own[0:SLOTS, row : row + 1, :] = field[:, far : far + 1, lanes]
                own[SLOTS : 2 * SLOTS, row : row + 1, :] = field[:, near : near + 1, lanes]


def merge_record(source, number):
    side = (iota((TE, 128), 1) % 64) // TE
    out = source[number(2), 0:TE, :]
    for face in range(3, 6):
        out = jnp.where(side == face - 2, source[number(face), 0:TE, :], out)
    edge = jnp.where(
        iota((8, 128), 0) < 4, source[number(0), TE:REC, :], source[number(1), TE:REC, :]
    )
    return out, edge


def pack(own, table, send):
    cap = send[0].shape[0] // REC
    for number, out in enumerate(send):
        for rank in range(cap):
            record = number * cap + rank
            planes, edge = merge_record(own, lambda face: table[face, SLOTS + record])
            out[rank * REC : rank * REC + TE, :] = planes
            out[rank * REC + TE : rank * REC + REC, :] = edge


def first_pack_kernel(table, phase, solute, picks, own, *send):
    write_records(phase[...], solute[...], picks[...], own)
    pack(own, table, send)


def take_heat(cap, table, found, got, spreads, blocks, held, heat):
    parts, deep = block_layout(cap)
    blocks[0] = found[...]
    for number, value in enumerate(got):
        blocks[1 + number] = value[value.shape[0] - deep * CB :, :]
    group = iota((CB, 128), 1) // CB
    for slot in range(SLOTS):
        back, rank = table[6, slot], table[7, slot]
        for x in range(CB):
            row = (x % deep) * CB
            patch = blocks[back, row : row + CB, :]
            held[slot * CB + x] = jnp.where(group == rank * parts + x // deep, patch, 0.0)
    rows = held[...].reshape(SLOTS * CB * CB, 128)
    wide = dot(jnp.concatenate(halves(rows), axis=1), spreads)
    wide = wide.reshape(SLOTS * CB, CB, PLANE)
    keep = iota(wide.shape, 1) == iota(wide.shape, 2) // TE // 2
    coarse = jnp.sum(jnp.where(keep, wide, 0.0), axis=1)
    for half in range(2):
        for odd in range(2):
            heat[half, pl.ds(odd, SLOTS * CB, 2), :] = coarse[:, half * 128 : half * 128 + 128]


def inner_step(phase, solute, heat, stencil):
    row = iota((SLOTS, TE, PLANE), 1)
    lap = []
    for field in (phase, solute):
        high, low = halves(field.reshape(SLOTS * TE, PLANE))
        total = (dot(high, stencil) + dot(low, stencil)).reshape(SLOTS, TE, PLANE) - 6.0 * field
        total += jnp.where(row == 0, 0.0, pltpu.roll(field, 1, 1))
        total += jnp.where(row == TE - 1, 0.0, pltpu.roll(field, TE - 1, 1))
        lap.append(total)
    squared = 1.0 - phase * phase
    drive = solute if heat is None else heat + solute
    change = ORDER_SPEED * (
        lap[0] + phase - phase * phase * phase - COUPLING * drive * squared * squared
    )
    return phase + change, solute + SOLUTE_RATE * lap[1] + REJECTION * change


def wide_heat(heat):
    return jnp.concatenate([heat[0], heat[1]], axis=1).reshape(SLOTS, TE, PLANE)


def gather_ghosts(table, got, own, all_records, ghosts):
    records = all_records.shape[0] - 2 * SLOTS
    cap = records // len(got)
    for number, value in enumerate(got):
        all_records[number * cap : number * cap + cap] = value[0 : cap * REC, :].reshape(cap, REC, 128)
    all_records[records : records + 2 * SLOTS] = own[...]
    for slot in range(SLOTS):
        out, edge = merge_record(all_records, lambda face: table[face, slot])
        ghosts[slot, 0:TE, :] = out
        ghosts[slot, TE:REC, :] = edge


def ghost_shares(ghosts, places):
    beside = jnp.concatenate(halves(ghosts[:, 0:TE, :].reshape(SLOTS * TE, 128)), axis=1)
    beside = dot(beside, places)
    row = iota((SLOTS, TE, PLANE), 1)
    shares = []
    for number in range(2):
        share = beside[:, number * PLANE : number * PLANE + PLANE].reshape(SLOTS, TE, PLANE)
        for face, at_row in ((0, 0), (1, TE - 1)):
            at = TE + face * 4 + number * 2
            side = jnp.concatenate([ghosts[:, at : at + 1, :], ghosts[:, at + 1 : at + 2, :]], axis=2)
            share += jnp.where(row == at_row, side, 0.0)
        shares.append(share)
    return shares


def add_shares(phase, solute, shares, heat_share=None):
    change = ORDER_SPEED * shares[0]
    if heat_share is not None:
        change += heat_share
    return phase + change, solute + SOLUTE_RATE * shares[1] + REJECTION * change


def inner_kernel(has_heat, phase, solute, stencil, *rest):
    phase_out, solute_out = rest[-2:]
    heat = wide_heat(rest[0]) if has_heat else None
    phase_out[...], solute_out[...] = inner_step(phase[...], solute[...], heat, stencil[...])


def first_step_kernel(cap, table, old_phase, phase, solute, own, picks, places, spreads, found, *rest):
    others = lax.axis_size("gx") - 1
    got, rest = rest[:others], rest[others:]
    phase_out, solute_out, heat_out, own_out, *rest = rest
    send, (all_records, ghosts, blocks, held) = rest[:others], rest[others:]
    take_heat(cap, table, found, got, spreads[...], blocks, held, heat_out)
    gather_ghosts(table, got, own, all_records, ghosts)
    squared = 1.0 - old_phase[...] * old_phase[...]
    heat_share = (-ORDER_SPEED * COUPLING) * wide_heat(heat_out) * squared * squared
    new_phase, new_solute = add_shares(
        phase[...], solute[...], ghost_shares(ghosts, places[...]), heat_share
    )
    phase_out[...] = new_phase
    solute_out[...] = new_solute
    write_records(new_phase, new_solute, picks[...], own_out)
    pack(own_out, table, send)


def write_out_kernel(value, out, sem):
    copy = pltpu.make_async_copy(value, out, sem)
    copy.start()
    copy.wait()


def middle_step_kernel(table, phase, solute, own, picks, places, *rest):
    others = lax.axis_size("gx") - 1
    got, (phase_out, solute_out, own_out, *rest) = rest[:others], rest[others:]
    send, (all_records, ghosts) = rest[:others], rest[others:]
    gather_ghosts(table, got, own, all_records, ghosts)
    new_phase, new_solute = add_shares(phase[...], solute[...], ghost_shares(ghosts, places[...]))
    phase_out[...] = new_phase
    solute_out[...] = new_solute
    write_records(new_phase, new_solute, picks[...], own_out)
    pack(own_out, table, send)


def last_step_kernel(table, phase, solute, own, places, *rest):
    others = lax.axis_size("gx") - 1
    got, (phase_out, solute_out, all_records, ghosts) = rest[:others], rest[others:]
    gather_ghosts(table, got, own, all_records, ghosts)
    phase_out[...], solute_out[...] = add_shares(
        phase[...], solute[...], ghost_shares(ghosts, places[...])
    )


def call(kernel, in_specs, out_shapes, scratch=(), out_specs=None, mib=16):
    return pl.pallas_call(
        kernel,
        out_shape=out_shapes,
        in_specs=in_specs,
        out_specs=out_specs or jax.tree.map(lambda _: VMEM, out_shapes),
        scratch_shapes=list(scratch),
        compiler_params=pltpu.CompilerParams(vmem_limit_bytes=mib * 1024 * 1024),
    )


def shape(*dims):
    return jax.ShapeDtypeStruct(dims, F32)


def local(enthalpy, conductivity, phase, solute, tile_source, tile_block, tile_neighbour):
    count = lax.axis_size("gx")
    sizes = (lax.axis_size("gy"), lax.axis_size("gz"))
    plane_cap = -(-SLOTS // (count - 1))
    block_cap = 2 * SLOTS // count
    others = count - 1
    records = others * plane_cap
    bx, by, bz = enthalpy.shape
    picks, stencil, places, spreads = tables()

    integers = functools.partial(jax.ShapeDtypeStruct, dtype=jnp.int32)
    sides, table, *asked = call(
        functools.partial(sides_kernel, sizes, plane_cap),
        [ANY] * 5,
        [shape(sizes[0] * sizes[1], 3 * bx, 128), integers((8, 128)), *[shape(8, 128)] * count],
        [
            pltpu.VMEM((1, SLOTS), jnp.int32),
            pltpu.VMEM((1, SLOTS), jnp.int32),
            pltpu.VMEM((FACES, 1, SLOTS), jnp.int32),
            pltpu.VMEM((bx, by, bz), F32),
            pltpu.VMEM((bx, by, bz), F32),
            pltpu.SemaphoreType.DMA((2 * bx + 3,)),
        ],
        mib=56,
    )(
        tile_source.reshape(1, SLOTS),
        tile_block.reshape(1, SLOTS),
        jnp.transpose(tile_neighbour, (0, 1, 4, 2, 3)).reshape(FACES, 1, SLOTS),
        enthalpy,
        conductivity,
    )
    sides = lax.all_to_all(sides, ("gy", "gz"), split_axis=0, concat_axis=0, tiled=True)

    def pass_on(value, shift):
        return lax.ppermute(value, "gx", [(i, (i + shift) % count) for i in range(count)])

    def exchange(values):
        return [pass_on(value, shift) for shift, value in enumerate(values, 1)]

    farther = [pass_on(asked[shift], shift) for shift in range(2, others)]

    phase_field = phase.reshape(SLOTS, TE, PLANE)
    solute_field = solute.reshape(SLOTS, TE, PLANE)
    own_shape, send_shapes = shape(2 * SLOTS, REC, 128), [shape(plane_cap * REC, 128)] * others
    own, *packed = call(first_pack_kernel, [SMEM] + [VMEM] * 3, [own_shape, *send_shapes])(
        table, phase_field, solute_field, picks
    )

    layer = shape(3 * by + 8, bz)
    down, up = call(
        functools.partial(layers_kernel, sizes), [VMEM] * 5 + [ANY] * (1 + len(farther)), [layer, layer]
    )(enthalpy, conductivity, sides, asked[1], asked[others], packed[0], *farther)
    from_low, from_high = pass_on(up, 1), pass_on(down, others)
    row = 3 * by + 4
    request = [asked[0][0], from_low[row], *[value[0] for value in farther], from_high[row]]
    request = jnp.stack([value[:block_cap] for value in request]).astype(jnp.int32)
    _, deep = block_layout(block_cap)
    brick = shape(bx, by, bz)
    heated, found, *send = call(
        functools.partial(heat_kernel, block_cap, sizes),
        [SMEM] + [VMEM] * (5 + others),
        [brick, shape(deep * CB, 128)] + [shape(plane_cap * REC + deep * CB, 128)] * others,
        [pltpu.VMEM((bx, by // CB, CB, bz), F32)],
    )(request, enthalpy, conductivity, sides, from_low, from_high, *packed)

    (heat_out,) = call(write_out_kernel, [ANY], [brick], [pltpu.SemaphoreType.DMA], [ANY])(heated)

    got = exchange(send)
    field = shape(SLOTS, TE, PLANE)
    step_scratch = [
        pltpu.VMEM((records + 2 * SLOTS, REC, 128), F32),
        pltpu.VMEM((SLOTS, REC, 128), F32),
    ]
    def inner(phase_field, solute_field, *heat):
        return call(
            functools.partial(inner_kernel, bool(heat)), [VMEM] * (3 + len(heat)), [field, field]
        )(phase_field, solute_field, stencil, *heat)

    inner_fields = inner(phase_field, solute_field)
    phase_field, solute_field, heat, own, *send = call(
        functools.partial(first_step_kernel, block_cap),
        [SMEM] + [VMEM] * (8 + others),
        [field, field, shape(2, SLOTS * TE, 128), own_shape, *send_shapes],
        step_scratch
        + [
            pltpu.VMEM((count, deep * CB, 128), F32),
            pltpu.VMEM((SLOTS * CB, CB, 128), F32),
        ],
    )(table, phase_field, *inner_fields, own, picks, places, spreads, found, *got)
    for _ in range(PHASE_STEPS - 2):
        got = exchange(send)
        inner_fields = inner(phase_field, solute_field, heat)
        phase_field, solute_field, own, *send = call(
            middle_step_kernel,
            [SMEM] + [VMEM] * (5 + others),
            [field, field, own_shape, *send_shapes],
            step_scratch,
        )(table, *inner_fields, own, picks, places, *got)
    got = exchange(send)
    inner_fields = inner(phase_field, solute_field, heat)
    phase_field, solute_field = call(
        last_step_kernel, [SMEM] + [VMEM] * (4 + others), [field, field], step_scratch
    )(table, *inner_fields, own, places, *got)
    return heat_out, phase_field.reshape(phase.shape), solute_field.reshape(solute.shape)


def solution(mesh):
    grid = P("gx", "gy", "gz")
    tiles = P("gx", "gy", "gz", None, None, None)
    return jax.shard_map(
        local,
        mesh=mesh,
        in_specs=(
            grid,
            grid,
            tiles,
            tiles,
            P("gx", "gy", "gz", None, None),
            P("gx", "gy", "gz", None),
            P("gx", "gy", "gz", None, None),
        ),
        out_specs=(grid, tiles, tiles),
        check_vma=False,
    )
```

```python
import functools

import jax
import jax.numpy as jnp
import numpy as np
from jax import lax
from jax.experimental import pallas as pl
from jax.experimental.pallas import tpu as pltpu
from jax.sharding import PartitionSpec as P

CB = 8
TE = 16
PLANE = TE * TE
SLOTS = 16
FACES = 6
PHASE_STEPS = 4
REC = 24

RATE = 0.16
ORDER_SPEED = 0.1
SOLUTE_RATE = 0.15
COUPLING = 0.5
REJECTION = 0.5

F32 = jnp.float32
BF16 = jnp.bfloat16
VMEM = pl.BlockSpec(memory_space=pltpu.VMEM)
SMEM = pl.BlockSpec(memory_space=pltpu.SMEM)
ANY = pl.BlockSpec(memory_space=pl.ANY)


def plane_lane(face):
    j = np.arange(TE)
    return [j, PLANE - TE + j, j * TE, j * TE + TE - 1][face - 2]


def constant_tables():
    pick = np.zeros((2, PLANE, 256), np.float32)
    place = np.zeros((2, 128, PLANE), np.float32)
    for field in range(2):
        for face in range(2, 6):
            at = field * 64 + (face - 2) * TE + np.arange(TE)
            pick[field, plane_lane(face ^ 1), at] = 1.0
            pick[field, plane_lane(face), 128 + at] = 1.0
            place[field, at, plane_lane(face)] = 1.0
    y, z = np.divmod(np.arange(PLANE), TE)
    dy, dz = np.abs(y[:, None] - y[None, :]), np.abs(z[:, None] - z[None, :])
    stencil = ((dy + dz) == 1).astype(np.float32)
    lane = np.arange(128)
    spread = (lane[:, None] % CB == z[None, :] // 2).astype(np.float32)
    return pick, place, stencil, spread


def tables():
    pick, place, stencil, spread = constant_tables()
    place = np.concatenate([place[0], place[1]], axis=1)
    return (
        jnp.asarray(np.concatenate([pick[0], pick[1]], axis=0), BF16),
        jnp.asarray(stencil, BF16),
        jnp.asarray(np.concatenate([place, place], axis=0), BF16),
        jnp.asarray(np.concatenate([spread, spread], axis=0), BF16),
    )


def halves(value):
    high = value.astype(BF16)
    return high, (value - high.astype(F32)).astype(BF16)


def dot(a, b):
    return jnp.dot(a, b, preferred_element_type=F32)


def temperature(h):
    return jnp.minimum(h, 0.0) + jnp.maximum(h - 1.0, 0.0)


def iota(shape, dim):
    return lax.broadcasted_iota(jnp.int32, shape, dim)


def to_lanes(column):
    bx, by, _ = column.shape
    diagonal = iota((bx, by, 128), 1) == iota((bx, by, 128), 2)
    return jnp.sum(jnp.where(diagonal, column, 0.0), axis=1)


def to_column(line, by):
    bx = line.shape[0]
    diagonal = iota((bx, by, 128), 1) == iota((bx, by, 128), 2)
    return jnp.sum(jnp.where(diagonal, line[:, None, :], 0.0), axis=2, keepdims=True)


def conduct(h, k, xlo, xhi, ylo, yhi, zlo, zhi):
    bx, by, bz = h.shape
    t = temperature(h)
    row, lane = iota((bx, by, bz), 1), iota((bx, by, bz), 2)
    if bx > 1:
        total = jnp.concatenate([xlo, t[:-1]], axis=0) + jnp.concatenate([t[1:], xhi], axis=0)
    else:
        total = xlo + xhi
    total += jnp.where(row == 0, ylo[:, None, :], pltpu.roll(t, 1, 1))
    total += jnp.where(row == by - 1, yhi[:, None, :], pltpu.roll(t, by - 1, 1))
    total += jnp.where(lane == 0, to_column(zlo, by), pltpu.roll(t, 1, 2))
    total += jnp.where(lane == bz - 1, to_column(zhi, by), pltpu.roll(t, bz - 1, 2))
    return h + RATE * k * (total - 6.0 * t)


def sublanes(value, y):
    return jnp.concatenate([value[x, y : y + 1, :] for x in range(value.shape[0])], axis=0)


def side_blocks(h, k):
    by, bz = h.shape[1:]
    return [
        (sublanes(h, 0), sublanes(h, 1), sublanes(k, 0)),
        (sublanes(h, by - 1), sublanes(h, by - 2), sublanes(k, by - 1)),
        (to_lanes(h[:, :, 0:1]), to_lanes(h[:, :, 1:2]), to_lanes(k[:, :, 0:1])),
        (to_lanes(h[:, :, bz - 1 : bz]), to_lanes(h[:, :, bz - 2 : bz - 1]), to_lanes(k[:, :, bz - 1 : bz])),
    ]


def column_of(row):
    square = (row.shape[1], row.shape[1])
    return jnp.sum(jnp.where(iota(square, 0) == iota(square, 1), row, 0.0), axis=1, keepdims=True)


def write_tables(plane_cap, source, block, neighbour, asked, table):
    me = lax.axis_index("gx")
    count = asked.shape[0]
    records = (count - 1) * plane_cap
    cap = float(plane_cap)
    square = (SLOTS, SLOTS)
    before = iota(square, 0) < iota(square, 1)
    slot = iota((1, SLOTS), 1).astype(F32)
    source_row, block_column = (source[...] ^ me).astype(F32), column_of(block[...].astype(F32))
    source_column = column_of(source_row)
    rank = jnp.sum(
        jnp.where((source_column == source_row) & before, 1.0, 0.0), axis=0, keepdims=True
    )
    rank_column = column_of(rank)
    lane = iota((SLOTS, 128), 1).astype(F32)
    for shift in range(count):
        hit = (source_column == float(shift)) & (rank_column == lane)
        row = jnp.sum(jnp.where(hit, block_column, 0.0), axis=0, keepdims=True)
        asked[shift : shift + 1, :] = row
    table[6:7, 0:SLOTS] = source[...] ^ me
    table[7:8, 0:SLOTS] = rank.astype(jnp.int32)
    slot_column = iota((SLOTS, records), 0).astype(F32)
    for face in range(FACES):
        number = neighbour[face]
        shift = jnp.where(number < 0, 0, (number >> 4) ^ me)
        shift_row, number_row = shift.astype(F32), number.astype(F32)
        shift_column, number_column = column_of(shift_row), column_of(number_row)
        alike = (shift_column == shift_row) & (shift_column > 0.0)
        receive_rank = jnp.sum(
            jnp.where(alike & (number_column < number_row), 1.0, 0.0), axis=0, keepdims=True
        )
        send_rank = jnp.sum(jnp.where(alike & before, 1.0, 0.0), axis=0, keepdims=True)
        here = records + (number & (SLOTS - 1)).astype(F32)
        there = (shift_row - 1.0) * cap + receive_rank
        receive = jnp.where(shift_row == 0.0, here, there)
        receive = jnp.where(number_row < 0.0, records + SLOTS + slot, receive)
        table[face : face + 1, 0:SLOTS] = receive.astype(jnp.int32)
        key = jnp.where(shift_row > 0.0, (shift_row - 1.0) * cap + send_rank, -1.0)
        hit = iota((SLOTS, records), 1).astype(F32) == column_of(key)
        tile = jnp.sum(jnp.where(hit, slot_column, 0.0), axis=0, keepdims=True)
        table[face ^ 1 : (face ^ 1) + 1, SLOTS : SLOTS + records] = tile.astype(jnp.int32)


def sides_kernel(
    sizes, plane_cap, source_far, block_far, neighbour_far, h_far, k_far, send, table, asked,
    source, block, neighbour, h, k, sems,
):
    ny, nz = sizes
    my_y, my_z = lax.axis_index("gy"), lax.axis_index("gz")
    bx = h.shape[0]
    small = [(source_far, source), (block_far, block), (neighbour_far, neighbour)]
    copies = [pltpu.make_async_copy(*pair, sems.at[2 * bx + n]) for n, pair in enumerate(small)]
    large = []
    for x in range(bx):
        large.append(pltpu.make_async_copy(h_far.at[x], h.at[x], sems.at[x]))
        large.append(pltpu.make_async_copy(k_far.at[x], k.at[x], sems.at[bx + x]))
    for copy in copies + large:
        copy.start()
    for copy in copies:
        copy.wait()
    write_tables(plane_cap, source, block, neighbour, asked, table)
    for copy in large:
        copy.wait()
    blocks = side_blocks(h[...], k[...])
    for y in range(ny):
        for z in range(nz):
            for part in range(3):
                ylo, yhi, zlo, zhi = [block[part] for block in blocks]
                chosen = jnp.where(
                    my_y == y, jnp.where(z < my_z, zlo, zhi), jnp.where(y < my_y, ylo, yhi)
                )
                send[y * nz + z, part * bx : part * bx + bx, :] = chosen


def side_reader(sizes, got, bx):
    ny, nz = sizes
    my_y, my_z = lax.axis_index("gy"), lax.axis_index("gz")

    def read(dy, dz, part=0):
        y, z = my_y + dy, my_z + dz
        inside = (y >= 0) & (y < ny) & (z >= 0) & (z < nz)
        at = jnp.where(inside, y * nz + z, 0)
        return jnp.where(inside, got[at, part * bx : part * bx + bx, :], 0.0)

    return read


def layers_kernel(sizes, h, k, got, _, first, second):
    bx, by, bz = h.shape
    read = side_reader(sizes, got, bx)
    even = lax.rem(lax.axis_index("gx"), 2) == 0
    around = [read(-1, 0), read(1, 0), read(0, -1), read(0, 1)]
    layers = [(h[bx - 1], h[0]), (h[bx - 2], h[1]), (k[bx - 1], k[0])]
    layers += [(side[bx - 1 : bx, :], side[0:1, :]) for side in around]
    row = 0
    for upper, lower in layers:
        first[row : row + upper.shape[0], :] = jnp.where(even, upper, lower)
        second[row : row + upper.shape[0], :] = jnp.where(even, lower, upper)
        row += upper.shape[0]
    for out in (first, second):
        out[row:, :] = jnp.zeros((out.shape[0] - row, bz), F32)


def block_layout(cap):
    parts = 128 // CB // cap
    return parts, CB // parts


def flat_step(h, k, inner, outer, first, last, before, after, length):
    bx, lanes = h.shape
    t = temperature(h)
    row, lane = iota(h.shape, 0), iota(h.shape, 1)
    total = temperature(inner) + temperature(outer)
    total += jnp.where(row == 0, temperature(first), pltpu.roll(t, 1, 0))
    total += jnp.where(row == bx - 1, temperature(last), pltpu.roll(t, bx - 1, 0))
    total += jnp.where(lane == 0, temperature(before), pltpu.roll(t, 1, 1))
    total += jnp.where(lane == length - 1, temperature(after), pltpu.roll(t, lanes - 1, 1))
    return h + RATE * k * (total - 6.0 * t)


def heat_kernel(cap, sizes, request, h, k, got, first, second, out, found, *rest):
    *send, held = rest
    bx, by, bz = h.shape
    h0, k0 = h[...], k[...]
    read = side_reader(sizes, got, bx)
    me, count = lax.axis_index("gx"), lax.axis_size("gx")
    even = lax.rem(me, 2) == 0
    layers, lines = [], []
    pairs = (first[...], second[...])
    low, high = jnp.where(even, *pairs[::-1]), jnp.where(even, *pairs)
    for beside, inside in ((low, me > 0), (high, me < count - 1)):
        beside = jnp.where(inside, beside, 0.0)
        layers.append([beside[part * by : part * by + by, :][None] for part in range(3)])
        lines.append([beside[3 * by + n : 3 * by + n + 1, :] for n in range(4)])
    y_sides = [[read(d, 0, part) for part in range(3)] for d in (-1, 1)]
    z_sides = [[read(0, d, part) for part in range(3)] for d in (-1, 1)]
    corner = [[read(dy, dz) for dz in (-1, 1)] for dy in (-1, 1)]
    to_first = [[pltpu.roll(c[0], 1, 1), c[1]] for c in corner]
    y_inner = [sublanes(h0, 0), sublanes(h0, by - 1)]
    z_inner = [to_lanes(h0[:, :, 0:1]), to_lanes(h0[:, :, bz - 1 : bz])]

    sides = [temperature(layers[0][0]), temperature(layers[1][0])]
    sides += [temperature(side[0]) for side in y_sides + z_sides]
    h1 = conduct(h0, k0, *sides)
    next_sides = []
    for side in range(2):
        near, far, near_k = layers[side]
        across = [temperature(far), temperature(h0[0:1])]
        if side:
            across = [temperature(h0[bx - 1 : bx]), temperature(far)]
        next_sides.append(conduct(near, near_k, *across, *[temperature(line) for line in lines[side]]))
    for side in range(2):
        near, far, near_k = y_sides[side]
        ends = [to_first[side][0], pltpu.roll(to_first[side][1], bz - 1, 1)]
        next_sides.append(
            flat_step(near, near_k, y_inner[side], far, lines[0][side], lines[1][side], *ends, bz)
        )
    for side in range(2):
        near, far, near_k = z_sides[side]
        ends = [to_first[0][side], pltpu.roll(to_first[1][side], by - 1, 1)]
        next_sides.append(
            flat_step(near, near_k, z_inner[side], far, lines[0][2 + side], lines[1][2 + side], *ends, by)
        )
    h2 = conduct(h1, k0, *[temperature(side) for side in next_sides])
    out[...] = h2

    held[...] = temperature(h2).reshape(bx, by // CB, CB, bz)
    parts, deep = block_layout(cap)
    nby, nbz = by // CB, bz // CB
    group = iota((deep, CB, bz), 2) // CB
    for shift in range(count):
        total = jnp.zeros((deep, CB, bz), F32)
        for rank in range(cap):
            block = request[shift, rank]
            a, b, c = block // (nby * nbz), (block // nbz) % nby, block % nbz
            for part in range(parts):
                at = rank * parts + part
                patch = held[pl.ds(a * CB + part * deep, deep), b]
                moved = pltpu.roll(patch, (CB * at - CB * c + bz) % bz, 2)
                total = jnp.where(group == at, moved, total)
        total = total.reshape(deep * CB, bz)
        (send[shift - 1] if shift else found)[...] = total


def write_records(phase, solute, picks, own):
    flat = [f.reshape(SLOTS * TE, PLANE) for f in (phase, solute)]
    high, low = halves(jnp.concatenate(flat, axis=1))
    planes = dot(high, picks) + dot(low, picks)
    own[0:SLOTS, 0:TE, :] = planes[:, 0:128].reshape(SLOTS, TE, 128)
    own[SLOTS : 2 * SLOTS, 0:TE, :] = planes[:, 128:256].reshape(SLOTS, TE, 128)
    for face in range(2):
        for number, field in enumerate((phase, solute)):
            for half in range(2):
                row = TE + face * 4 + number * 2 + half
                lanes = slice(half * 128, half * 128 + 128)
                near, far = (0, TE - 1) if face == 0 else (TE - 1, 0)
                own[0:SLOTS, row : row + 1, :] = field[:, far : far + 1, lanes]
                own[SLOTS : 2 * SLOTS, row : row + 1, :] = field[:, near : near + 1, lanes]


def merge_record(source, number):
    side = (iota((TE, 128), 1) % 64) // TE
    out = source[number(2), 0:TE, :]
    for face in range(3, 6):
        out = jnp.where(side == face - 2, source[number(face), 0:TE, :], out)
    edge = jnp.where(
        iota((8, 128), 0) < 4, source[number(0), TE:REC, :], source[number(1), TE:REC, :]
    )
    return out, edge


def pack(own, table, send):
    cap = send[0].shape[0] // REC
    for number, out in enumerate(send):
        for rank in range(cap):
            record = number * cap + rank
            planes, edge = merge_record(own, lambda face: table[face, SLOTS + record])
            out[rank * REC : rank * REC + TE, :] = planes
            out[rank * REC + TE : rank * REC + REC, :] = edge


def first_pack_kernel(table, asked, phase, solute, picks, own, *send):
    write_records(phase[...], solute[...], picks[...], own)
    pack(own, table, send)
    for number, out in enumerate(send):
        row = asked[number + 1 : number + 2, :]
        out[out.shape[0] - 8 :, :] = jnp.broadcast_to(row, (8, 128))


def take_heat(cap, table, found, spreads, blocks, held, heat):
    parts, deep = block_layout(cap)
    for number, value in enumerate(found):
        blocks[number] = value[...]
    group = iota((CB, 128), 1) // CB
    for slot in range(SLOTS):
        back, rank = table[6, slot], table[7, slot]
        for x in range(CB):
            row = (x % deep) * CB
            patch = blocks[back, row : row + CB, :]
            held[slot * CB + x] = jnp.where(group == rank * parts + x // deep, patch, 0.0)
    rows = held[...].reshape(SLOTS * CB * CB, 128)
    wide = dot(jnp.concatenate(halves(rows), axis=1), spreads)
    wide = wide.reshape(SLOTS * CB, CB, PLANE)
    keep = iota(wide.shape, 1) == iota(wide.shape, 2) // TE // 2
    coarse = jnp.sum(jnp.where(keep, wide, 0.0), axis=1)
    for half in range(2):
        for odd in range(2):
            heat[half, pl.ds(odd, SLOTS * CB, 2), :] = coarse[:, half * 128 : half * 128 + 128]


def inner_step(phase, solute, heat, stencil):
    row = iota((SLOTS, TE, PLANE), 1)
    lap = []
    for field in (phase, solute):
        high, low = halves(field.reshape(SLOTS * TE, PLANE))
        total = (dot(high, stencil) + dot(low, stencil)).reshape(SLOTS, TE, PLANE) - 6.0 * field
        total += jnp.where(row == 0, 0.0, pltpu.roll(field, 1, 1))
        total += jnp.where(row == TE - 1, 0.0, pltpu.roll(field, TE - 1, 1))
        lap.append(total)
    squared = 1.0 - phase * phase
    drive = solute if heat is None else heat + solute
    change = ORDER_SPEED * (
        lap[0] + phase - phase * phase * phase - COUPLING * drive * squared * squared
    )
    return phase + change, solute + SOLUTE_RATE * lap[1] + REJECTION * change


def wide_heat(heat):
    return jnp.concatenate([heat[0], heat[1]], axis=1).reshape(SLOTS, TE, PLANE)


def gather_ghosts(table, got, own, all_records, ghosts):
    records = all_records.shape[0] - 2 * SLOTS
    cap = records // len(got)
    for number, value in enumerate(got):
        all_records[number * cap : number * cap + cap] = value[0 : cap * REC, :].reshape(cap, REC, 128)
    all_records[records : records + 2 * SLOTS] = own[...]
    for slot in range(SLOTS):
        out, edge = merge_record(all_records, lambda face: table[face, slot])
        ghosts[slot, 0:TE, :] = out
        ghosts[slot, TE:REC, :] = edge


def ghost_shares(ghosts, places):
    beside = jnp.concatenate(halves(ghosts[:, 0:TE, :].reshape(SLOTS * TE, 128)), axis=1)
    beside = dot(beside, places)
    row = iota((SLOTS, TE, PLANE), 1)
    shares = []
    for number in range(2):
        share = beside[:, number * PLANE : number * PLANE + PLANE].reshape(SLOTS, TE, PLANE)
        for face, at_row in ((0, 0), (1, TE - 1)):
            at = TE + face * 4 + number * 2
            side = jnp.concatenate([ghosts[:, at : at + 1, :], ghosts[:, at + 1 : at + 2, :]], axis=2)
            share += jnp.where(row == at_row, side, 0.0)
        shares.append(share)
    return shares


def add_shares(phase, solute, shares, heat_share=None):
    change = ORDER_SPEED * shares[0]
    if heat_share is not None:
        change += heat_share
    return phase + change, solute + SOLUTE_RATE * shares[1] + REJECTION * change


def inner_kernel(has_heat, phase, solute, stencil, *rest):
    phase_out, solute_out = rest[-2:]
    heat = wide_heat(rest[0]) if has_heat else None
    phase_out[...], solute_out[...] = inner_step(phase[...], solute[...], heat, stencil[...])


def first_step_kernel(cap, table, old_phase, phase, solute, own, picks, places, spreads, *rest):
    others = lax.axis_size("gx") - 1
    found, got, rest = rest[: others + 1], rest[others + 1 : 2 * others + 1], rest[2 * others + 1 :]
    phase_out, solute_out, heat_out, own_out, *rest = rest
    send, (all_records, ghosts, blocks, held) = rest[:others], rest[others:]
    take_heat(cap, table, found, spreads[...], blocks, held, heat_out)
    gather_ghosts(table, got, own, all_records, ghosts)
    squared = 1.0 - old_phase[...] * old_phase[...]
    heat_share = (-ORDER_SPEED * COUPLING) * wide_heat(heat_out) * squared * squared
    new_phase, new_solute = add_shares(
        phase[...], solute[...], ghost_shares(ghosts, places[...]), heat_share
    )
    phase_out[...] = new_phase
    solute_out[...] = new_solute
    write_records(new_phase, new_solute, picks[...], own_out)
    pack(own_out, table, send)


def write_out_kernel(value, out, sem):
    copy = pltpu.make_async_copy(value, out, sem)
    copy.start()
    copy.wait()


def middle_step_kernel(table, phase, solute, own, picks, places, *rest):
    others = lax.axis_size("gx") - 1
    got, (phase_out, solute_out, own_out, *rest) = rest[:others], rest[others:]
    send, (all_records, ghosts) = rest[:others], rest[others:]
    gather_ghosts(table, got, own, all_records, ghosts)
    new_phase, new_solute = add_shares(phase[...], solute[...], ghost_shares(ghosts, places[...]))
    phase_out[...] = new_phase
    solute_out[...] = new_solute
    write_records(new_phase, new_solute, picks[...], own_out)
    pack(own_out, table, send)


def last_step_kernel(table, phase, solute, own, places, *rest):
    others = lax.axis_size("gx") - 1
    got, (phase_out, solute_out, all_records, ghosts) = rest[:others], rest[others:]
    gather_ghosts(table, got, own, all_records, ghosts)
    phase_out[...], solute_out[...] = add_shares(
        phase[...], solute[...], ghost_shares(ghosts, places[...])
    )


def call(kernel, in_specs, out_shapes, scratch=(), out_specs=None, mib=16):
    return pl.pallas_call(
        kernel,
        out_shape=out_shapes,
        in_specs=in_specs,
        out_specs=out_specs or jax.tree.map(lambda _: VMEM, out_shapes),
        scratch_shapes=list(scratch),
        compiler_params=pltpu.CompilerParams(vmem_limit_bytes=mib * 1024 * 1024),
    )


def shape(*dims):
    return jax.ShapeDtypeStruct(dims, F32)


def local(enthalpy, conductivity, phase, solute, tile_source, tile_block, tile_neighbour):
    count = lax.axis_size("gx")
    sizes = (lax.axis_size("gy"), lax.axis_size("gz"))
    plane_cap = -(-SLOTS // (count - 1))
    block_cap = 2 * SLOTS // count
    others = count - 1
    records = others * plane_cap
    bx, by, bz = enthalpy.shape
    picks, stencil, places, spreads = tables()

    integers = functools.partial(jax.ShapeDtypeStruct, dtype=jnp.int32)
    sides, table, asked = call(
        functools.partial(sides_kernel, sizes, plane_cap),
        [ANY] * 5,
        [shape(sizes[0] * sizes[1], 3 * bx, 128), integers((8, 128)), shape(count, 128)],
        [
            pltpu.VMEM((1, SLOTS), jnp.int32),
            pltpu.VMEM((1, SLOTS), jnp.int32),
            pltpu.VMEM((FACES, 1, SLOTS), jnp.int32),
            pltpu.VMEM((bx, by, bz), F32),
            pltpu.VMEM((bx, by, bz), F32),
            pltpu.SemaphoreType.DMA((2 * bx + 3,)),
        ],
        mib=56,
    )(
        tile_source.reshape(1, SLOTS),
        tile_block.reshape(1, SLOTS),
        jnp.transpose(tile_neighbour, (0, 1, 4, 2, 3)).reshape(FACES, 1, SLOTS),
        enthalpy,
        conductivity,
    )
    sides = lax.all_to_all(sides, ("gy", "gz"), split_axis=0, concat_axis=0, tiled=True)

    def swap(value, partner):
        return lax.ppermute(value, "gx", [(i, partner(i)) for i in range(count)])

    def exchange(values):
        got = {s: swap(values[s - 1], lambda i, s=s: i ^ s) for s in range(others, 0, -1)}
        return [got[s] for s in range(1, count)]

    phase_field = phase.reshape(SLOTS, TE, PLANE)
    solute_field = solute.reshape(SLOTS, TE, PLANE)
    own_shape, send_shapes = shape(2 * SLOTS, REC, 128), [shape(plane_cap * REC, 128)] * others
    own, *packed = call(
        first_pack_kernel,
        [SMEM] + [VMEM] * 4,
        [own_shape] + [shape(plane_cap * REC + 8, 128)] * others,
    )(table, asked, phase_field, solute_field, picks)
    got = exchange(packed)
    request = jnp.stack([asked[0], *[value[plane_cap * REC] for value in got]])
    request = request[:, :block_cap].astype(jnp.int32)

    layer = shape(3 * by + 8, bz)
    first, second = call(
        functools.partial(layers_kernel, sizes), [VMEM] * 3 + [ANY], [layer, layer]
    )(enthalpy, conductivity, sides, packed[0])
    first = swap(first, lambda i: i ^ 1)
    second = swap(second, lambda i: i if i in (0, others) else ((i + 1) ^ 1) - 1)
    _, deep = block_layout(block_cap)
    brick = shape(bx, by, bz)
    heated, *found = call(
        functools.partial(heat_kernel, block_cap, sizes),
        [SMEM] + [VMEM] * 5,
        [brick] + [shape(deep * CB, 128)] * count,
        [pltpu.VMEM((bx, by // CB, CB, bz), F32)],
    )(request, enthalpy, conductivity, sides, first, second)
    found[1:] = exchange(found[1:])
    (heat_out,) = call(write_out_kernel, [ANY], [brick], [pltpu.SemaphoreType.DMA], [ANY])(heated)

    field = shape(SLOTS, TE, PLANE)
    step_scratch = [
        pltpu.VMEM((records + 2 * SLOTS, REC, 128), F32),
        pltpu.VMEM((SLOTS, REC, 128), F32),
    ]
    def inner(phase_field, solute_field, *heat):
        return call(
            functools.partial(inner_kernel, bool(heat)), [VMEM] * (3 + len(heat)), [field, field]
        )(phase_field, solute_field, stencil, *heat)

    inner_fields = inner(phase_field, solute_field)
    phase_field, solute_field, heat, own, *send = call(
        functools.partial(first_step_kernel, block_cap),
        [SMEM] + [VMEM] * (7 + count + others),
        [field, field, shape(2, SLOTS * TE, 128), own_shape, *send_shapes],
        step_scratch
        + [
            pltpu.VMEM((count, deep * CB, 128), F32),
            pltpu.VMEM((SLOTS * CB, CB, 128), F32),
        ],
    )(table, phase_field, *inner_fields, own, picks, places, spreads, *found, *got)
    for _ in range(PHASE_STEPS - 2):
        got = exchange(send)
        inner_fields = inner(phase_field, solute_field, heat)
        phase_field, solute_field, own, *send = call(
            middle_step_kernel,
            [SMEM] + [VMEM] * (5 + others),
            [field, field, own_shape, *send_shapes],
            step_scratch,
        )(table, *inner_fields, own, picks, places, *got)
    got = exchange(send)
    inner_fields = inner(phase_field, solute_field, heat)
    phase_field, solute_field = call(
        last_step_kernel, [SMEM] + [VMEM] * (4 + others), [field, field], step_scratch
    )(table, *inner_fields, own, places, *got)
    return heat_out, phase_field.reshape(phase.shape), solute_field.reshape(solute.shape)


def solution(mesh):
    grid = P("gx", "gy", "gz")
    tiles = P("gx", "gy", "gz", None, None, None)
    return jax.shard_map(
        local,
        mesh=mesh,
        in_specs=(
            grid,
            grid,
            tiles,
            tiles,
            P("gx", "gy", "gz", None, None),
            P("gx", "gy", "gz", None),
            P("gx", "gy", "gz", None, None),
        ),
        out_specs=(grid, tiles, tiles),
        check_vma=False,
    )
```

```python
import functools

import jax
import jax.numpy as jnp
import numpy as np
from jax import lax
from jax.experimental import pallas as pl
from jax.experimental.pallas import tpu as pltpu
from jax.sharding import PartitionSpec as P

CB = 8
TE = 16
PLANE = TE * TE
SLOTS = 16
FACES = 6
PHASE_STEPS = 4
REC = 24

RATE = 0.16
ORDER_SPEED = 0.1
SOLUTE_RATE = 0.15
COUPLING = 0.5
REJECTION = 0.5

F32 = jnp.float32
BF16 = jnp.bfloat16
VMEM = pl.BlockSpec(memory_space=pltpu.VMEM)
SMEM = pl.BlockSpec(memory_space=pltpu.SMEM)
ANY = pl.BlockSpec(memory_space=pl.ANY)


def plane_lane(face):
    j = np.arange(TE)
    return [j, PLANE - TE + j, j * TE, j * TE + TE - 1][face - 2]


def constant_tables():
    pick = np.zeros((2, PLANE, 256), np.float32)
    place = np.zeros((2, 128, PLANE), np.float32)
    for field in range(2):
        for face in range(2, 6):
            at = field * 64 + (face - 2) * TE + np.arange(TE)
            pick[field, plane_lane(face ^ 1), at] = 1.0
            pick[field, plane_lane(face), 128 + at] = 1.0
            place[field, at, plane_lane(face)] = 1.0
    y, z = np.divmod(np.arange(PLANE), TE)
    dy, dz = np.abs(y[:, None] - y[None, :]), np.abs(z[:, None] - z[None, :])
    stencil = ((dy + dz) == 1).astype(np.float32)
    lane = np.arange(128)
    spread = (lane[:, None] % CB == z[None, :] // 2).astype(np.float32)
    return pick, place, stencil, spread


def tables():
    pick, place, stencil, spread = constant_tables()
    place = np.concatenate([place[0], place[1]], axis=1)
    return (
        jnp.asarray(np.concatenate([pick[0], pick[1]], axis=0), BF16),
        jnp.asarray(stencil, BF16),
        jnp.asarray(np.concatenate([place, place], axis=0), BF16),
        jnp.asarray(np.concatenate([spread, spread], axis=0), BF16),
    )


def halves(value):
    high = value.astype(BF16)
    return high, (value - high.astype(F32)).astype(BF16)


def dot(a, b):
    return jnp.dot(a, b, preferred_element_type=F32)


def temperature(h):
    return jnp.minimum(h, 0.0) + jnp.maximum(h - 1.0, 0.0)


def iota(shape, dim):
    return lax.broadcasted_iota(jnp.int32, shape, dim)


def to_lanes(column):
    bx, by, _ = column.shape
    diagonal = iota((bx, by, 128), 1) == iota((bx, by, 128), 2)
    return jnp.sum(jnp.where(diagonal, column, 0.0), axis=1)


def to_column(line, by):
    bx = line.shape[0]
    diagonal = iota((bx, by, 128), 1) == iota((bx, by, 128), 2)
    return jnp.sum(jnp.where(diagonal, line[:, None, :], 0.0), axis=2, keepdims=True)


def conduct(h, k, xlo, xhi, ylo, yhi, zlo, zhi):
    bx, by, bz = h.shape
    t = temperature(h)
    row, lane = iota((bx, by, bz), 1), iota((bx, by, bz), 2)
    if bx > 1:
        total = jnp.concatenate([xlo, t[:-1]], axis=0) + jnp.concatenate([t[1:], xhi], axis=0)
    else:
        total = xlo + xhi
    total += jnp.where(row == 0, ylo[:, None, :], pltpu.roll(t, 1, 1))
    total += jnp.where(row == by - 1, yhi[:, None, :], pltpu.roll(t, by - 1, 1))
    total += jnp.where(lane == 0, to_column(zlo, by), pltpu.roll(t, 1, 2))
    total += jnp.where(lane == bz - 1, to_column(zhi, by), pltpu.roll(t, bz - 1, 2))
    return h + RATE * k * (total - 6.0 * t)


def sublanes(value, y):
    return jnp.concatenate([value[x, y : y + 1, :] for x in range(value.shape[0])], axis=0)


def side_blocks(h, k):
    by, bz = h.shape[1:]
    return [
        (sublanes(h, 0), sublanes(h, 1), sublanes(k, 0)),
        (sublanes(h, by - 1), sublanes(h, by - 2), sublanes(k, by - 1)),
        (to_lanes(h[:, :, 0:1]), to_lanes(h[:, :, 1:2]), to_lanes(k[:, :, 0:1])),
        (to_lanes(h[:, :, bz - 1 : bz]), to_lanes(h[:, :, bz - 2 : bz - 1]), to_lanes(k[:, :, bz - 1 : bz])),
    ]


def column_of(row):
    square = (row.shape[1], row.shape[1])
    return jnp.sum(jnp.where(iota(square, 0) == iota(square, 1), row, 0.0), axis=1, keepdims=True)


def write_tables(plane_cap, source, block, neighbour, asked, table):
    me = lax.axis_index("gx").astype(F32)
    count = len(asked)
    records = (count - 1) * plane_cap
    cap = float(plane_cap)

    def wrapped(shift):
        return jnp.where(shift < 0.0, shift + float(count), shift)

    square = (SLOTS, SLOTS)
    before = iota(square, 0) < iota(square, 1)
    slot = iota((1, SLOTS), 1).astype(F32)
    source_row, block_column = source[...].astype(F32), column_of(block[...].astype(F32))
    source_column = column_of(source_row)
    rank = jnp.sum(
        jnp.where((source_column == source_row) & before, 1.0, 0.0), axis=0, keepdims=True
    )
    rank_column = column_of(rank)
    lane = iota((SLOTS, 128), 1).astype(F32)
    for shift in range(count):
        hit = (wrapped(source_column - me) == float(shift)) & (rank_column == lane)
        row = jnp.sum(jnp.where(hit, block_column, 0.0), axis=0, keepdims=True)
        asked[shift][...] = jnp.broadcast_to(row, asked[shift].shape)
    table[6:7, 0:SLOTS] = wrapped(me - source_row).astype(jnp.int32)
    table[7:8, 0:SLOTS] = rank.astype(jnp.int32)
    slot_column = iota((SLOTS, records), 0).astype(F32)
    for face in range(FACES):
        number = neighbour[face]
        owner_row, number_row = (number >> 4).astype(F32), number.astype(F32)
        owner_column, number_column = column_of(owner_row), column_of(number_row)
        other_row = (number_row >= 0.0) & (owner_row != me)
        alike = (owner_column == owner_row) & (owner_column >= 0.0) & (owner_column != me)
        receive_rank = jnp.sum(
            jnp.where(alike & (number_column < number_row), 1.0, 0.0), axis=0, keepdims=True
        )
        send_rank = jnp.sum(jnp.where(alike & before, 1.0, 0.0), axis=0, keepdims=True)
        here = records + (number_row - owner_row * SLOTS)
        there = (wrapped(me - owner_row) - 1.0) * cap + receive_rank
        receive = jnp.where(owner_row == me, here, there)
        receive = jnp.where(number_row < 0.0, records + SLOTS + slot, receive)
        table[face : face + 1, 0:SLOTS] = receive.astype(jnp.int32)
        key = jnp.where(other_row, (wrapped(owner_row - me) - 1.0) * cap + send_rank, -1.0)
        hit = iota((SLOTS, records), 1).astype(F32) == column_of(key)
        tile = jnp.sum(jnp.where(hit, slot_column, 0.0), axis=0, keepdims=True)
        table[face ^ 1 : (face ^ 1) + 1, SLOTS : SLOTS + records] = tile.astype(jnp.int32)


def sides_kernel(
    sizes, plane_cap, source_far, block_far, neighbour_far, h_far, k_far, send, table, *rest
):
    *asked, source, block, neighbour, h, k, sems = rest
    ny, nz = sizes
    my_y, my_z = lax.axis_index("gy"), lax.axis_index("gz")
    bx = h.shape[0]
    small = [(source_far, source), (block_far, block), (neighbour_far, neighbour)]
    copies = [pltpu.make_async_copy(*pair, sems.at[2 * bx + n]) for n, pair in enumerate(small)]
    large = []
    for x in range(bx):
        large.append(pltpu.make_async_copy(h_far.at[x], h.at[x], sems.at[x]))
        large.append(pltpu.make_async_copy(k_far.at[x], k.at[x], sems.at[bx + x]))
    for copy in copies + large:
        copy.start()
    for copy in copies:
        copy.wait()
    write_tables(plane_cap, source, block, neighbour, asked, table)
    for copy in large:
        copy.wait()
    blocks = side_blocks(h[...], k[...])
    for y in range(ny):
        for z in range(nz):
            for part in range(3):
                ylo, yhi, zlo, zhi = [block[part] for block in blocks]
                chosen = jnp.where(
                    my_y == y, jnp.where(z < my_z, zlo, zhi), jnp.where(y < my_y, ylo, yhi)
                )
                send[y * nz + z, part * bx : part * bx + bx, :] = chosen


def side_reader(sizes, got, bx):
    ny, nz = sizes
    my_y, my_z = lax.axis_index("gy"), lax.axis_index("gz")

    def read(dy, dz, part=0):
        y, z = my_y + dy, my_z + dz
        inside = (y >= 0) & (y < ny) & (z >= 0) & (z < nz)
        at = jnp.where(inside, y * nz + z, 0)
        return jnp.where(inside, got[at, part * bx : part * bx + bx, :], 0.0)

    return read


def layers_kernel(sizes, h, k, got, ask_up, ask_down, *rest):
    down, up = rest[-2:]
    bx, by, bz = h.shape
    read = side_reader(sizes, got, bx)
    around = [read(-1, 0), read(1, 0), read(0, -1), read(0, 1)]
    for out, near, far, ask in ((down, 0, 1, ask_down), (up, bx - 1, bx - 2, ask_up)):
        out[0:by, :] = h[near]
        out[by : 2 * by, :] = h[far]
        out[2 * by : 3 * by, :] = k[near]
        for number, side in enumerate(around):
            out[3 * by + number : 3 * by + number + 1, :] = side[near : near + 1, :]
        out[3 * by + 4 : 3 * by + 8, :] = ask[0:4, :]


def block_layout(cap):
    parts = 128 // CB // cap
    return parts, CB // parts


def flat_step(h, k, inner, outer, first, last, before, after, length):
    bx, lanes = h.shape
    t = temperature(h)
    row, lane = iota(h.shape, 0), iota(h.shape, 1)
    total = temperature(inner) + temperature(outer)
    total += jnp.where(row == 0, temperature(first), pltpu.roll(t, 1, 0))
    total += jnp.where(row == bx - 1, temperature(last), pltpu.roll(t, bx - 1, 0))
    total += jnp.where(lane == 0, temperature(before), pltpu.roll(t, 1, 1))
    total += jnp.where(lane == length - 1, temperature(after), pltpu.roll(t, lanes - 1, 1))
    return h + RATE * k * (total - 6.0 * t)


def heat_kernel(cap, sizes, request, h, k, got, low, high, out, found, *rest):
    *send, held = rest
    count = lax.axis_size("gx")
    bx, by, bz = h.shape
    h0, k0 = h[...], k[...]
    read = side_reader(sizes, got, bx)
    me = lax.axis_index("gx")
    layers, lines = [], []
    for beside, inside in ((low, me > 0), (high, me < count - 1)):
        beside = jnp.where(inside, beside[...], 0.0)
        layers.append([beside[part * by : part * by + by, :][None] for part in range(3)])
        lines.append([beside[3 * by + n : 3 * by + n + 1, :] for n in range(4)])
    y_sides = [[read(d, 0, part) for part in range(3)] for d in (-1, 1)]
    z_sides = [[read(0, d, part) for part in range(3)] for d in (-1, 1)]
    corner = [[read(dy, dz) for dz in (-1, 1)] for dy in (-1, 1)]
    to_first = [[pltpu.roll(c[0], 1, 1), c[1]] for c in corner]
    y_inner = [sublanes(h0, 0), sublanes(h0, by - 1)]
    z_inner = [to_lanes(h0[:, :, 0:1]), to_lanes(h0[:, :, bz - 1 : bz])]

    sides = [temperature(layers[0][0]), temperature(layers[1][0])]
    sides += [temperature(side[0]) for side in y_sides + z_sides]
    h1 = conduct(h0, k0, *sides)
    next_sides = []
    for side in range(2):
        near, far, near_k = layers[side]
        across = [temperature(far), temperature(h0[0:1])]
        if side:
            across = [temperature(h0[bx - 1 : bx]), temperature(far)]
        next_sides.append(conduct(near, near_k, *across, *[temperature(line) for line in lines[side]]))
    for side in range(2):
        near, far, near_k = y_sides[side]
        ends = [to_first[side][0], pltpu.roll(to_first[side][1], bz - 1, 1)]
        next_sides.append(
            flat_step(near, near_k, y_inner[side], far, lines[0][side], lines[1][side], *ends, bz)
        )
    for side in range(2):
        near, far, near_k = z_sides[side]
        ends = [to_first[0][side], pltpu.roll(to_first[1][side], by - 1, 1)]
        next_sides.append(
            flat_step(near, near_k, z_inner[side], far, lines[0][2 + side], lines[1][2 + side], *ends, by)
        )
    h2 = conduct(h1, k0, *[temperature(side) for side in next_sides])
    out[...] = h2

    held[...] = temperature(h2).reshape(bx, by // CB, CB, bz)
    parts, deep = block_layout(cap)
    nby, nbz = by // CB, bz // CB
    group = iota((deep, CB, bz), 2) // CB
    for shift in range(count):
        total = jnp.zeros((deep, CB, bz), F32)
        for rank in range(cap):
            block = request[(count - shift) % count, rank]
            a, b, c = block // (nby * nbz), (block // nbz) % nby, block % nbz
            for part in range(parts):
                at = rank * parts + part
                patch = held[pl.ds(a * CB + part * deep, deep), b]
                moved = pltpu.roll(patch, (CB * at - CB * c + bz) % bz, 2)
                total = jnp.where(group == at, moved, total)
        total = total.reshape(deep * CB, bz)
        (send[shift - 1] if shift else found)[...] = total


def write_records(phase, solute, picks, own):
    flat = [f.reshape(SLOTS * TE, PLANE) for f in (phase, solute)]
    high, low = halves(jnp.concatenate(flat, axis=1))
    planes = dot(high, picks) + dot(low, picks)
    own[0:SLOTS, 0:TE, :] = planes[:, 0:128].reshape(SLOTS, TE, 128)
    own[SLOTS : 2 * SLOTS, 0:TE, :] = planes[:, 128:256].reshape(SLOTS, TE, 128)
    for face in range(2):
        for number, field in enumerate((phase, solute)):
            for half in range(2):
                row = TE + face * 4 + number * 2 + half
                lanes = slice(half * 128, half * 128 + 128)
                near, far = (0, TE - 1) if face == 0 else (TE - 1, 0)
                own[0:SLOTS, row : row + 1, :] = field[:, far : far + 1, lanes]
                own[SLOTS : 2 * SLOTS, row : row + 1, :] = field[:, near : near + 1, lanes]


def merge_record(source, number):
    side = (iota((TE, 128), 1) % 64) // TE
    out = source[number(2), 0:TE, :]
    for face in range(3, 6):
        out = jnp.where(side == face - 2, source[number(face), 0:TE, :], out)
    edge = jnp.where(
        iota((8, 128), 0) < 4, source[number(0), TE:REC, :], source[number(1), TE:REC, :]
    )
    return out, edge


def pack(own, table, send):
    cap = send[0].shape[0] // REC
    for number, out in enumerate(send):
        for rank in range(cap):
            record = number * cap + rank
            planes, edge = merge_record(own, lambda face: table[face, SLOTS + record])
            out[rank * REC : rank * REC + TE, :] = planes
            out[rank * REC + TE : rank * REC + REC, :] = edge


def first_pack_kernel(table, phase, solute, picks, own, *send):
    write_records(phase[...], solute[...], picks[...], own)
    pack(own, table, send)


def take_heat(cap, table, found, spreads, blocks, held, heat):
    parts, deep = block_layout(cap)
    for number, value in enumerate(found):
        blocks[number] = value[...]
    group = iota((CB, 128), 1) // CB
    for slot in range(SLOTS):
        back, rank = table[6, slot], table[7, slot]
        for x in range(CB):
            row = (x % deep) * CB
            patch = blocks[back, row : row + CB, :]
            held[slot * CB + x] = jnp.where(group == rank * parts + x // deep, patch, 0.0)
    rows = held[...].reshape(SLOTS * CB * CB, 128)
    wide = dot(jnp.concatenate(halves(rows), axis=1), spreads)
    wide = wide.reshape(SLOTS * CB, CB, PLANE)
    keep = iota(wide.shape, 1) == iota(wide.shape, 2) // TE // 2
    coarse = jnp.sum(jnp.where(keep, wide, 0.0), axis=1)
    for half in range(2):
        for odd in range(2):
            heat[half, pl.ds(odd, SLOTS * CB, 2), :] = coarse[:, half * 128 : half * 128 + 128]


def inner_step(phase, solute, heat, stencil):
    row = iota((SLOTS, TE, PLANE), 1)
    lap = []
    for field in (phase, solute):
        high, low = halves(field.reshape(SLOTS * TE, PLANE))
        total = (dot(high, stencil) + dot(low, stencil)).reshape(SLOTS, TE, PLANE) - 6.0 * field
        total += jnp.where(row == 0, 0.0, pltpu.roll(field, 1, 1))
        total += jnp.where(row == TE - 1, 0.0, pltpu.roll(field, TE - 1, 1))
        lap.append(total)
    squared = 1.0 - phase * phase
    drive = solute if heat is None else heat + solute
    change = ORDER_SPEED * (
        lap[0] + phase - phase * phase * phase - COUPLING * drive * squared * squared
    )
    return phase + change, solute + SOLUTE_RATE * lap[1] + REJECTION * change


def wide_heat(heat):
    return jnp.concatenate([heat[0], heat[1]], axis=1).reshape(SLOTS, TE, PLANE)


def gather_ghosts(table, got, own, all_records, ghosts):
    records = all_records.shape[0] - 2 * SLOTS
    cap = records // len(got)
    for number, value in enumerate(got):
        all_records[number * cap : number * cap + cap] = value[0 : cap * REC, :].reshape(cap, REC, 128)
    all_records[records : records + 2 * SLOTS] = own[...]
    for slot in range(SLOTS):
        out, edge = merge_record(all_records, lambda face: table[face, slot])
        ghosts[slot, 0:TE, :] = out
        ghosts[slot, TE:REC, :] = edge


def ghost_shares(ghosts, places):
    beside = jnp.concatenate(halves(ghosts[:, 0:TE, :].reshape(SLOTS * TE, 128)), axis=1)
    beside = dot(beside, places)
    row = iota((SLOTS, TE, PLANE), 1)
    shares = []
    for number in range(2):
        share = beside[:, number * PLANE : number * PLANE + PLANE].reshape(SLOTS, TE, PLANE)
        for face, at_row in ((0, 0), (1, TE - 1)):
            at = TE + face * 4 + number * 2
            side = jnp.concatenate([ghosts[:, at : at + 1, :], ghosts[:, at + 1 : at + 2, :]], axis=2)
            share += jnp.where(row == at_row, side, 0.0)
        shares.append(share)
    return shares


def add_shares(phase, solute, shares, heat_share=None):
    change = ORDER_SPEED * shares[0]
    if heat_share is not None:
        change += heat_share
    return phase + change, solute + SOLUTE_RATE * shares[1] + REJECTION * change


def inner_kernel(has_heat, phase, solute, stencil, *rest):
    phase_out, solute_out = rest[-2:]
    heat = wide_heat(rest[0]) if has_heat else None
    phase_out[...], solute_out[...] = inner_step(phase[...], solute[...], heat, stencil[...])


def first_step_kernel(cap, table, old_phase, phase, solute, own, picks, places, spreads, *rest):
    others = lax.axis_size("gx") - 1
    found, got, rest = rest[: others + 1], rest[others + 1 : 2 * others + 1], rest[2 * others + 1 :]
    phase_out, solute_out, heat_out, own_out, *rest = rest
    send, (all_records, ghosts, blocks, held) = rest[:others], rest[others:]
    take_heat(cap, table, found, spreads[...], blocks, held, heat_out)
    gather_ghosts(table, got, own, all_records, ghosts)
    squared = 1.0 - old_phase[...] * old_phase[...]
    heat_share = (-ORDER_SPEED * COUPLING) * wide_heat(heat_out) * squared * squared
    new_phase, new_solute = add_shares(
        phase[...], solute[...], ghost_shares(ghosts, places[...]), heat_share
    )
    phase_out[...] = new_phase
    solute_out[...] = new_solute
    write_records(new_phase, new_solute, picks[...], own_out)
    pack(own_out, table, send)


def write_out_kernel(value, out, sem):
    copy = pltpu.make_async_copy(value, out, sem)
    copy.start()
    copy.wait()


def middle_step_kernel(table, phase, solute, own, picks, places, *rest):
    others = lax.axis_size("gx") - 1
    got, (phase_out, solute_out, own_out, *rest) = rest[:others], rest[others:]
    send, (all_records, ghosts) = rest[:others], rest[others:]
    gather_ghosts(table, got, own, all_records, ghosts)
    new_phase, new_solute = add_shares(phase[...], solute[...], ghost_shares(ghosts, places[...]))
    phase_out[...] = new_phase
    solute_out[...] = new_solute
    write_records(new_phase, new_solute, picks[...], own_out)
    pack(own_out, table, send)


def last_step_kernel(table, phase, solute, own, places, *rest):
    others = lax.axis_size("gx") - 1
    got, (phase_out, solute_out, all_records, ghosts) = rest[:others], rest[others:]
    gather_ghosts(table, got, own, all_records, ghosts)
    phase_out[...], solute_out[...] = add_shares(
        phase[...], solute[...], ghost_shares(ghosts, places[...])
    )


def call(kernel, in_specs, out_shapes, scratch=(), out_specs=None, mib=16):
    return pl.pallas_call(
        kernel,
        out_shape=out_shapes,
        in_specs=in_specs,
        out_specs=out_specs or jax.tree.map(lambda _: VMEM, out_shapes),
        scratch_shapes=list(scratch),
        compiler_params=pltpu.CompilerParams(vmem_limit_bytes=mib * 1024 * 1024),
    )


def shape(*dims):
    return jax.ShapeDtypeStruct(dims, F32)


def local(enthalpy, conductivity, phase, solute, tile_source, tile_block, tile_neighbour):
    count = lax.axis_size("gx")
    sizes = (lax.axis_size("gy"), lax.axis_size("gz"))
    plane_cap = -(-SLOTS // (count - 1))
    block_cap = 2 * SLOTS // count
    others = count - 1
    records = others * plane_cap
    bx, by, bz = enthalpy.shape
    picks, stencil, places, spreads = tables()

    integers = functools.partial(jax.ShapeDtypeStruct, dtype=jnp.int32)
    sides, table, *asked = call(
        functools.partial(sides_kernel, sizes, plane_cap),
        [ANY] * 5,
        [shape(sizes[0] * sizes[1], 3 * bx, 128), integers((8, 128)), *[shape(8, 128)] * count],
        [
            pltpu.VMEM((1, SLOTS), jnp.int32),
            pltpu.VMEM((1, SLOTS), jnp.int32),
            pltpu.VMEM((FACES, 1, SLOTS), jnp.int32),
            pltpu.VMEM((bx, by, bz), F32),
            pltpu.VMEM((bx, by, bz), F32),
            pltpu.SemaphoreType.DMA((2 * bx + 3,)),
        ],
        mib=56,
    )(
        tile_source.reshape(1, SLOTS),
        tile_block.reshape(1, SLOTS),
        jnp.transpose(tile_neighbour, (0, 1, 4, 2, 3)).reshape(FACES, 1, SLOTS),
        enthalpy,
        conductivity,
    )
    sides = lax.all_to_all(sides, ("gy", "gz"), split_axis=0, concat_axis=0, tiled=True)

    def pass_on(value, shift):
        return lax.ppermute(value, "gx", [(i, (i + shift) % count) for i in range(count)])

    def exchange(values):
        return [pass_on(value, shift) for shift, value in enumerate(values, 1)]

    farther = [pass_on(asked[shift], shift) for shift in range(2, others)]

    phase_field = phase.reshape(SLOTS, TE, PLANE)
    solute_field = solute.reshape(SLOTS, TE, PLANE)
    own_shape, send_shapes = shape(2 * SLOTS, REC, 128), [shape(plane_cap * REC, 128)] * others
    own, *packed = call(first_pack_kernel, [SMEM] + [VMEM] * 3, [own_shape, *send_shapes])(
        table, phase_field, solute_field, picks
    )

    layer = shape(3 * by + 8, bz)
    down, up = call(
        functools.partial(layers_kernel, sizes), [VMEM] * 5 + [ANY] * (1 + len(farther)), [layer, layer]
    )(enthalpy, conductivity, sides, asked[1], asked[others], packed[0], *farther)
    from_low, from_high = pass_on(up, 1), pass_on(down, others)
    row = 3 * by + 4
    request = [asked[0][0], from_low[row], *[value[0] for value in farther], from_high[row]]
    request = jnp.stack([value[:block_cap] for value in request]).astype(jnp.int32)
    _, deep = block_layout(block_cap)
    brick = shape(bx, by, bz)
    got = exchange(packed)
    heated, *found = call(
        functools.partial(heat_kernel, block_cap, sizes),
        [SMEM] + [VMEM] * 5,
        [brick] + [shape(deep * CB, 128)] * count,
        [pltpu.VMEM((bx, by // CB, CB, bz), F32)],
    )(request, enthalpy, conductivity, sides, from_low, from_high)
    found[1:] = exchange(found[1:])
    (heat_out,) = call(write_out_kernel, [ANY], [brick], [pltpu.SemaphoreType.DMA], [ANY])(heated)

    field = shape(SLOTS, TE, PLANE)
    step_scratch = [
        pltpu.VMEM((records + 2 * SLOTS, REC, 128), F32),
        pltpu.VMEM((SLOTS, REC, 128), F32),
    ]
    def inner(phase_field, solute_field, *heat):
        return call(
            functools.partial(inner_kernel, bool(heat)), [VMEM] * (3 + len(heat)), [field, field]
        )(phase_field, solute_field, stencil, *heat)

    inner_fields = inner(phase_field, solute_field)
    phase_field, solute_field, heat, own, *send = call(
        functools.partial(first_step_kernel, block_cap),
        [SMEM] + [VMEM] * (7 + count + others),
        [field, field, shape(2, SLOTS * TE, 128), own_shape, *send_shapes],
        step_scratch
        + [
            pltpu.VMEM((count, deep * CB, 128), F32),
            pltpu.VMEM((SLOTS * CB, CB, 128), F32),
        ],
    )(table, phase_field, *inner_fields, own, picks, places, spreads, *found, *got)
    for _ in range(PHASE_STEPS - 2):
        got = exchange(send)
        inner_fields = inner(phase_field, solute_field, heat)
        phase_field, solute_field, own, *send = call(
            middle_step_kernel,
            [SMEM] + [VMEM] * (5 + others),
            [field, field, own_shape, *send_shapes],
            step_scratch,
        )(table, *inner_fields, own, picks, places, *got)
    got = exchange(send)
    inner_fields = inner(phase_field, solute_field, heat)
    phase_field, solute_field = call(
        last_step_kernel, [SMEM] + [VMEM] * (4 + others), [field, field], step_scratch
    )(table, *inner_fields, own, places, *got)
    return heat_out, phase_field.reshape(phase.shape), solute_field.reshape(solute.shape)


def solution(mesh):
    grid = P("gx", "gy", "gz")
    tiles = P("gx", "gy", "gz", None, None, None)
    return jax.shard_map(
        local,
        mesh=mesh,
        in_specs=(
            grid,
            grid,
            tiles,
            tiles,
            P("gx", "gy", "gz", None, None),
            P("gx", "gy", "gz", None),
            P("gx", "gy", "gz", None, None),
        ),
        out_specs=(grid, tiles, tiles),
        check_vma=False,
    )
```

```python
import functools

import jax
import jax.numpy as jnp
import numpy as np
from jax import lax
from jax.experimental import pallas as pl
from jax.experimental.pallas import tpu as pltpu
from jax.sharding import PartitionSpec as P

CB = 8
TE = 16
PLANE = TE * TE
SLOTS = 16
FACES = 6
PHASE_STEPS = 4
REC = 24

RATE = 0.16
ORDER_SPEED = 0.1
SOLUTE_RATE = 0.15
COUPLING = 0.5
REJECTION = 0.5

F32 = jnp.float32
BF16 = jnp.bfloat16
VMEM = pl.BlockSpec(memory_space=pltpu.VMEM)
SMEM = pl.BlockSpec(memory_space=pltpu.SMEM)
ANY = pl.BlockSpec(memory_space=pl.ANY)


def plane_lane(face):
    j = np.arange(TE)
    return [j, PLANE - TE + j, j * TE, j * TE + TE - 1][face - 2]


def constant_tables():
    pick = np.zeros((2, PLANE, 256), np.float32)
    place = np.zeros((2, 128, PLANE), np.float32)
    for field in range(2):
        for face in range(2, 6):
            at = field * 64 + (face - 2) * TE + np.arange(TE)
            pick[field, plane_lane(face ^ 1), at] = 1.0
            pick[field, plane_lane(face), 128 + at] = 1.0
            place[field, at, plane_lane(face)] = 1.0
    y, z = np.divmod(np.arange(PLANE), TE)
    dy, dz = np.abs(y[:, None] - y[None, :]), np.abs(z[:, None] - z[None, :])
    stencil = ((dy + dz) == 1).astype(np.float32)
    lane = np.arange(128)
    spread = (lane[:, None] % CB == z[None, :] // 2).astype(np.float32)
    return pick, place, stencil, spread


def tables():
    pick, place, stencil, spread = constant_tables()
    place = np.concatenate([place[0], place[1]], axis=1)
    return (
        jnp.asarray(np.concatenate([pick[0], pick[1]], axis=0), BF16),
        jnp.asarray(stencil, BF16),
        jnp.asarray(np.concatenate([place, place], axis=0), BF16),
        jnp.asarray(np.concatenate([spread, spread], axis=0), BF16),
    )


def halves(value):
    high = value.astype(BF16)
    return high, (value - high.astype(F32)).astype(BF16)


def dot(a, b):
    return jnp.dot(a, b, preferred_element_type=F32)


def temperature(h):
    return jnp.minimum(h, 0.0) + jnp.maximum(h - 1.0, 0.0)


def iota(shape, dim):
    return lax.broadcasted_iota(jnp.int32, shape, dim)


def to_lanes(column):
    bx, by, _ = column.shape
    diagonal = iota((bx, by, 128), 1) == iota((bx, by, 128), 2)
    return jnp.sum(jnp.where(diagonal, column, 0.0), axis=1)


def to_column(line, by):
    bx = line.shape[0]
    diagonal = iota((bx, by, 128), 1) == iota((bx, by, 128), 2)
    return jnp.sum(jnp.where(diagonal, line[:, None, :], 0.0), axis=2, keepdims=True)


def conduct(h, k, xlo, xhi, ylo, yhi, zlo, zhi):
    bx, by, bz = h.shape
    t = temperature(h)
    row, lane = iota((bx, by, bz), 1), iota((bx, by, bz), 2)
    if bx > 1:
        total = jnp.concatenate([xlo, t[:-1]], axis=0) + jnp.concatenate([t[1:], xhi], axis=0)
    else:
        total = xlo + xhi
    total += jnp.where(row == 0, ylo[:, None, :], pltpu.roll(t, 1, 1))
    total += jnp.where(row == by - 1, yhi[:, None, :], pltpu.roll(t, by - 1, 1))
    total += jnp.where(lane == 0, to_column(zlo, by), pltpu.roll(t, 1, 2))
    total += jnp.where(lane == bz - 1, to_column(zhi, by), pltpu.roll(t, bz - 1, 2))
    return h + RATE * k * (total - 6.0 * t)


def sublanes(value, y):
    return jnp.concatenate([value[x, y : y + 1, :] for x in range(value.shape[0])], axis=0)


def side_blocks(h, k):
    by, bz = h.shape[1:]
    return [
        (sublanes(h, 0), sublanes(h, 1), sublanes(k, 0)),
        (sublanes(h, by - 1), sublanes(h, by - 2), sublanes(k, by - 1)),
        (to_lanes(h[:, :, 0:1]), to_lanes(h[:, :, 1:2]), to_lanes(k[:, :, 0:1])),
        (to_lanes(h[:, :, bz - 1 : bz]), to_lanes(h[:, :, bz - 2 : bz - 1]), to_lanes(k[:, :, bz - 1 : bz])),
    ]


def column_of(row):
    square = (row.shape[1], row.shape[1])
    return jnp.sum(jnp.where(iota(square, 0) == iota(square, 1), row, 0.0), axis=1, keepdims=True)


def write_tables(plane_cap, source, block, neighbour, table, farther):
    me = lax.axis_index("gx").astype(F32)
    count = lax.axis_size("gx")
    records = (count - 1) * plane_cap
    cap = float(plane_cap)

    def wrapped(shift):
        return jnp.where(shift < 0.0, shift + float(count), shift)

    square = (SLOTS, SLOTS)
    before = iota(square, 0) < iota(square, 1)
    slot = iota((1, SLOTS), 1).astype(F32)
    source_row, block_column = source[...].astype(F32), column_of(block[...].astype(F32))
    source_column = column_of(source_row)
    rank = jnp.sum(
        jnp.where((source_column == source_row) & before, 1.0, 0.0), axis=0, keepdims=True
    )
    rank_column = column_of(rank)
    lane = iota((SLOTS, 128), 1).astype(F32)
    for shift in range(count):
        hit = (wrapped(source_column - me) == float(shift)) & (rank_column == lane)
        row = jnp.sum(jnp.where(hit, block_column, 0.0), axis=0, keepdims=True)
        table[8 + shift : 9 + shift, :] = row.astype(jnp.int32)
        if 2 <= shift < count - 1:
            farther[shift - 2][...] = jnp.broadcast_to(row, (8, 128))
    table[6:7, 0:SLOTS] = wrapped(me - source_row).astype(jnp.int32)
    table[7:8, 0:SLOTS] = rank.astype(jnp.int32)
    slot_column = iota((SLOTS, records), 0).astype(F32)
    for face in range(FACES):
        number = neighbour[face]
        owner_row, number_row = (number >> 4).astype(F32), number.astype(F32)
        owner_column, number_column = column_of(owner_row), column_of(number_row)
        other_row = (number_row >= 0.0) & (owner_row != me)
        alike = (owner_column == owner_row) & (owner_column >= 0.0) & (owner_column != me)
        receive_rank = jnp.sum(
            jnp.where(alike & (number_column < number_row), 1.0, 0.0), axis=0, keepdims=True
        )
        send_rank = jnp.sum(jnp.where(alike & before, 1.0, 0.0), axis=0, keepdims=True)
        here = records + (number_row - owner_row * SLOTS)
        there = (wrapped(me - owner_row) - 1.0) * cap + receive_rank
        receive = jnp.where(owner_row == me, here, there)
        receive = jnp.where(number_row < 0.0, records + SLOTS + slot, receive)
        table[face : face + 1, 0:SLOTS] = receive.astype(jnp.int32)
        key = jnp.where(other_row, (wrapped(owner_row - me) - 1.0) * cap + send_rank, -1.0)
        hit = iota((SLOTS, records), 1).astype(F32) == column_of(key)
        tile = jnp.sum(jnp.where(hit, slot_column, 0.0), axis=0, keepdims=True)
        table[face ^ 1 : (face ^ 1) + 1, SLOTS : SLOTS + records] = tile.astype(jnp.int32)


def sides_kernel(
    sizes, plane_cap, source_far, block_far, neighbour_far, h_far, k_far, send_far, table, *rest
):
    *farther, source, block, neighbour, h, k, send, sems = rest
    ny, nz = sizes
    my_y, my_z = lax.axis_index("gy"), lax.axis_index("gz")
    bx = h.shape[0]
    small = [(source_far, source), (block_far, block), (neighbour_far, neighbour)]
    copies = [pltpu.make_async_copy(*pair, sems.at[2 * bx + n]) for n, pair in enumerate(small)]
    out = pltpu.make_async_copy(send, send_far, sems.at[2 * bx + 3])
    large = []
    for x in range(bx):
        large.append(pltpu.make_async_copy(h_far.at[x], h.at[x], sems.at[x]))
        large.append(pltpu.make_async_copy(k_far.at[x], k.at[x], sems.at[bx + x]))
    for copy in copies + large:
        copy.start()
    for copy in large:
        copy.wait()
    blocks = side_blocks(h[...], k[...])
    for y in range(ny):
        for z in range(nz):
            for part in range(3):
                ylo, yhi, zlo, zhi = [block[part] for block in blocks]
                chosen = jnp.where(
                    my_y == y, jnp.where(z < my_z, zlo, zhi), jnp.where(y < my_y, ylo, yhi)
                )
                send[y * nz + z, part * bx : part * bx + bx, :] = chosen
    out.start()
    for copy in copies:
        copy.wait()
    write_tables(plane_cap, source, block, neighbour, table, farther)
    out.wait()


def side_reader(sizes, got, bx):
    ny, nz = sizes
    my_y, my_z = lax.axis_index("gy"), lax.axis_index("gz")

    def read(dy, dz, part=0):
        y, z = my_y + dy, my_z + dz
        inside = (y >= 0) & (y < ny) & (z >= 0) & (z < nz)
        at = jnp.where(inside, y * nz + z, 0)
        return jnp.where(inside, got[at, part * bx : part * bx + bx, :], 0.0)

    return read


def layers_kernel(sizes, h, k, got, table, *rest):
    down, up = rest[-2:]
    bx, by, bz = h.shape
    read = side_reader(sizes, got, bx)
    around = [read(-1, 0), read(1, 0), read(0, -1), read(0, 1)]
    down_ask = 7 + lax.axis_size("gx")
    for out, near, far, ask in ((down, 0, 1, down_ask), (up, bx - 1, bx - 2, 9)):
        out[0:by, :] = h[near]
        out[by : 2 * by, :] = h[far]
        out[2 * by : 3 * by, :] = k[near]
        for number, side in enumerate(around):
            out[3 * by + number : 3 * by + number + 1, :] = side[near : near + 1, :]
        row = table[ask : ask + 1, :].astype(F32)
        out[3 * by + 4 : 3 * by + 8, :] = jnp.broadcast_to(row, (4, bz))


def block_layout(cap):
    parts = 128 // CB // cap
    return parts, CB // parts


def flat_step(h, k, inner, outer, first, last, before, after, length):
    bx, lanes = h.shape
    t = temperature(h)
    row, lane = iota(h.shape, 0), iota(h.shape, 1)
    total = temperature(inner) + temperature(outer)
    total += jnp.where(row == 0, temperature(first), pltpu.roll(t, 1, 0))
    total += jnp.where(row == bx - 1, temperature(last), pltpu.roll(t, bx - 1, 0))
    total += jnp.where(lane == 0, temperature(before), pltpu.roll(t, 1, 1))
    total += jnp.where(lane == length - 1, temperature(after), pltpu.roll(t, lanes - 1, 1))
    return h + RATE * k * (total - 6.0 * t)


def heat_kernel(cap, sizes, table, request, h, k, got, low, high, out, found, *rest):
    *send, held = rest
    count = lax.axis_size("gx")
    bx, by, bz = h.shape
    h0, k0 = h[...], k[...]
    read = side_reader(sizes, got, bx)
    me = lax.axis_index("gx")
    layers, lines = [], []
    for beside, inside in ((low, me > 0), (high, me < count - 1)):
        beside = jnp.where(inside, beside[...], 0.0)
        layers.append([beside[part * by : part * by + by, :][None] for part in range(3)])
        lines.append([beside[3 * by + n : 3 * by + n + 1, :] for n in range(4)])
    y_sides = [[read(d, 0, part) for part in range(3)] for d in (-1, 1)]
    z_sides = [[read(0, d, part) for part in range(3)] for d in (-1, 1)]
    corner = [[read(dy, dz) for dz in (-1, 1)] for dy in (-1, 1)]
    to_first = [[pltpu.roll(c[0], 1, 1), c[1]] for c in corner]
    y_inner = [sublanes(h0, 0), sublanes(h0, by - 1)]
    z_inner = [to_lanes(h0[:, :, 0:1]), to_lanes(h0[:, :, bz - 1 : bz])]

    sides = [temperature(layers[0][0]), temperature(layers[1][0])]
    sides += [temperature(side[0]) for side in y_sides + z_sides]
    h1 = conduct(h0, k0, *sides)
    next_sides = []
    for side in range(2):
        near, far, near_k = layers[side]
        across = [temperature(far), temperature(h0[0:1])]
        if side:
            across = [temperature(h0[bx - 1 : bx]), temperature(far)]
        next_sides.append(conduct(near, near_k, *across, *[temperature(line) for line in lines[side]]))
    for side in range(2):
        near, far, near_k = y_sides[side]
        ends = [to_first[side][0], pltpu.roll(to_first[side][1], bz - 1, 1)]
        next_sides.append(
            flat_step(near, near_k, y_inner[side], far, lines[0][side], lines[1][side], *ends, bz)
        )
    for side in range(2):
        near, far, near_k = z_sides[side]
        ends = [to_first[0][side], pltpu.roll(to_first[1][side], by - 1, 1)]
        next_sides.append(
            flat_step(near, near_k, z_inner[side], far, lines[0][2 + side], lines[1][2 + side], *ends, by)
        )
    h2 = conduct(h1, k0, *[temperature(side) for side in next_sides])
    out[...] = h2

    held[...] = temperature(h2).reshape(bx, by // CB, CB, bz)
    parts, deep = block_layout(cap)
    nby, nbz = by // CB, bz // CB
    group = iota((deep, CB, bz), 2) // CB
    for shift in range(count):
        total = jnp.zeros((deep, CB, bz), F32)
        for rank in range(cap):
            block = request[count - shift - 1, rank] if shift else table[8, rank]
            a, b, c = block // (nby * nbz), (block // nbz) % nby, block % nbz
            for part in range(parts):
                at = rank * parts + part
                patch = held[pl.ds(a * CB + part * deep, deep), b]
                moved = pltpu.roll(patch, (CB * at - CB * c + bz) % bz, 2)
                total = jnp.where(group == at, moved, total)
        total = total.reshape(deep * CB, bz)
        (send[shift - 1] if shift else found)[...] = total


def write_records(phase, solute, picks, own):
    flat = [f.reshape(SLOTS * TE, PLANE) for f in (phase, solute)]
    high, low = halves(jnp.concatenate(flat, axis=1))
    planes = dot(high, picks) + dot(low, picks)
    own[0:SLOTS, 0:TE, :] = planes[:, 0:128].reshape(SLOTS, TE, 128)
    own[SLOTS : 2 * SLOTS, 0:TE, :] = planes[:, 128:256].reshape(SLOTS, TE, 128)
    for face in range(2):
        for number, field in enumerate((phase, solute)):
            for half in range(2):
                row = TE + face * 4 + number * 2 + half
                lanes = slice(half * 128, half * 128 + 128)
                near, far = (0, TE - 1) if face == 0 else (TE - 1, 0)
                own[0:SLOTS, row : row + 1, :] = field[:, far : far + 1, lanes]
                own[SLOTS : 2 * SLOTS, row : row + 1, :] = field[:, near : near + 1, lanes]


def merge_record(source, number):
    side = (iota((TE, 128), 1) % 64) // TE
    out = source[number(2), 0:TE, :]
    for face in range(3, 6):
        out = jnp.where(side == face - 2, source[number(face), 0:TE, :], out)
    edge = jnp.where(
        iota((8, 128), 0) < 4, source[number(0), TE:REC, :], source[number(1), TE:REC, :]
    )
    return out, edge


def pack(own, table, send):
    cap = send[0].shape[0] // REC
    for number, out in enumerate(send):
        for rank in range(cap):
            record = number * cap + rank
            planes, edge = merge_record(own, lambda face: table[face, SLOTS + record])
            out[rank * REC : rank * REC + TE, :] = planes
            out[rank * REC + TE : rank * REC + REC, :] = edge


def first_pack_kernel(table, phase, solute, picks, own, *send):
    write_records(phase[...], solute[...], picks[...], own)
    pack(own, table, send)


def take_heat(cap, table, found, spreads, blocks, held, heat):
    parts, deep = block_layout(cap)
    for number, value in enumerate(found):
        blocks[number] = value[...]
    group = iota((CB, 128), 1) // CB
    for slot in range(SLOTS):
        back, rank = table[6, slot], table[7, slot]
        for x in range(CB):
            row = (x % deep) * CB
            patch = blocks[back, row : row + CB, :]
            held[slot * CB + x] = jnp.where(group == rank * parts + x // deep, patch, 0.0)
    rows = held[...].reshape(SLOTS * CB * CB, 128)
    wide = dot(jnp.concatenate(halves(rows), axis=1), spreads)
    wide = wide.reshape(SLOTS * CB, CB, PLANE)
    keep = iota(wide.shape, 1) == iota(wide.shape, 2) // TE // 2
    coarse = jnp.sum(jnp.where(keep, wide, 0.0), axis=1)
    for half in range(2):
        for odd in range(2):
            heat[half, pl.ds(odd, SLOTS * CB, 2), :] = coarse[:, half * 128 : half * 128 + 128]


def inner_step(phase, solute, heat, stencil):
    row = iota((SLOTS, TE, PLANE), 1)
    lap = []
    for field in (phase, solute):
        high, low = halves(field.reshape(SLOTS * TE, PLANE))
        total = (dot(high, stencil) + dot(low, stencil)).reshape(SLOTS, TE, PLANE) - 6.0 * field
        total += jnp.where(row == 0, 0.0, pltpu.roll(field, 1, 1))
        total += jnp.where(row == TE - 1, 0.0, pltpu.roll(field, TE - 1, 1))
        lap.append(total)
    squared = 1.0 - phase * phase
    drive = solute if heat is None else heat + solute
    change = ORDER_SPEED * (
        lap[0] + phase - phase * phase * phase - COUPLING * drive * squared * squared
    )
    return phase + change, solute + SOLUTE_RATE * lap[1] + REJECTION * change


def wide_heat(heat):
    return jnp.concatenate([heat[0], heat[1]], axis=1).reshape(SLOTS, TE, PLANE)


def gather_ghosts(table, got, own, all_records, ghosts):
    records = all_records.shape[0] - 2 * SLOTS
    cap = records // len(got)
    for number, value in enumerate(got):
        all_records[number * cap : number * cap + cap] = value[0 : cap * REC, :].reshape(cap, REC, 128)
    all_records[records : records + 2 * SLOTS] = own[...]
    for slot in range(SLOTS):
        out, edge = merge_record(all_records, lambda face: table[face, slot])
        ghosts[slot, 0:TE, :] = out
        ghosts[slot, TE:REC, :] = edge


def ghost_shares(ghosts, places):
    beside = jnp.concatenate(halves(ghosts[:, 0:TE, :].reshape(SLOTS * TE, 128)), axis=1)
    beside = dot(beside, places)
    row = iota((SLOTS, TE, PLANE), 1)
    shares = []
    for number in range(2):
        share = beside[:, number * PLANE : number * PLANE + PLANE].reshape(SLOTS, TE, PLANE)
        for face, at_row in ((0, 0), (1, TE - 1)):
            at = TE + face * 4 + number * 2
            side = jnp.concatenate([ghosts[:, at : at + 1, :], ghosts[:, at + 1 : at + 2, :]], axis=2)
            share += jnp.where(row == at_row, side, 0.0)
        shares.append(share)
    return shares


def add_shares(phase, solute, shares, heat_share=None):
    change = ORDER_SPEED * shares[0]
    if heat_share is not None:
        change += heat_share
    return phase + change, solute + SOLUTE_RATE * shares[1] + REJECTION * change


def inner_kernel(has_heat, phase, solute, stencil, *rest):
    phase_out, solute_out = rest[-2:]
    heat = wide_heat(rest[0]) if has_heat else None
    phase_out[...], solute_out[...] = inner_step(phase[...], solute[...], heat, stencil[...])


def first_step_kernel(cap, table, old_phase, phase, solute, own, picks, places, spreads, *rest):
    others = lax.axis_size("gx") - 1
    found, got, rest = rest[: others + 1], rest[others + 1 : 2 * others + 1], rest[2 * others + 1 :]
    phase_out, solute_out, heat_out, own_out, *rest = rest
    send, (all_records, ghosts, blocks, held) = rest[:others], rest[others:]
    take_heat(cap, table, found, spreads[...], blocks, held, heat_out)
    gather_ghosts(table, got, own, all_records, ghosts)
    squared = 1.0 - old_phase[...] * old_phase[...]
    heat_share = (-ORDER_SPEED * COUPLING) * wide_heat(heat_out) * squared * squared
    new_phase, new_solute = add_shares(
        phase[...], solute[...], ghost_shares(ghosts, places[...]), heat_share
    )
    phase_out[...] = new_phase
    solute_out[...] = new_solute
    write_records(new_phase, new_solute, picks[...], own_out)
    pack(own_out, table, send)


def write_out_kernel(value, out, sem):
    copy = pltpu.make_async_copy(value, out, sem)
    copy.start()
    copy.wait()


def middle_step_kernel(table, phase, solute, own, picks, places, *rest):
    others = lax.axis_size("gx") - 1
    got, (phase_out, solute_out, own_out, *rest) = rest[:others], rest[others:]
    send, (all_records, ghosts) = rest[:others], rest[others:]
    gather_ghosts(table, got, own, all_records, ghosts)
    new_phase, new_solute = add_shares(phase[...], solute[...], ghost_shares(ghosts, places[...]))
    phase_out[...] = new_phase
    solute_out[...] = new_solute
    write_records(new_phase, new_solute, picks[...], own_out)
    pack(own_out, table, send)


def last_step_kernel(table, phase, solute, own, places, *rest):
    others = lax.axis_size("gx") - 1
    got, (phase_far, solute_far, all_records, ghosts, phase_out, solute_out, sems) = (
        rest[:others], rest[others:]
    )
    gather_ghosts(table, got, own, all_records, ghosts)
    shares = ghost_shares(ghosts, places[...])
    copies = []
    for piece in range(4):
        at = pl.ds(piece * SLOTS // 4, SLOTS // 4)
        part = slice(piece * SLOTS // 4, (piece + 1) * SLOTS // 4)
        phase_out[at], solute_out[at] = add_shares(
            phase[at], solute[at], [share[part] for share in shares]
        )
        for number, (out, far) in enumerate(((phase_out, phase_far), (solute_out, solute_far))):
            copy = pltpu.make_async_copy(out.at[at], far.at[at], sems.at[2 * piece + number])
            copy.start()
            copies.append(copy)
    for copy in copies:
        copy.wait()


def call(kernel, in_specs, out_shapes, scratch=(), out_specs=None, mib=16):
    return pl.pallas_call(
        kernel,
        out_shape=out_shapes,
        in_specs=in_specs,
        out_specs=out_specs or jax.tree.map(lambda _: VMEM, out_shapes),
        scratch_shapes=list(scratch),
        compiler_params=pltpu.CompilerParams(vmem_limit_bytes=mib * 1024 * 1024),
    )


def shape(*dims):
    return jax.ShapeDtypeStruct(dims, F32)


def local(enthalpy, conductivity, phase, solute, tile_source, tile_block, tile_neighbour):
    count = lax.axis_size("gx")
    sizes = (lax.axis_size("gy"), lax.axis_size("gz"))
    plane_cap = -(-SLOTS // (count - 1))
    block_cap = 2 * SLOTS // count
    others = count - 1
    records = others * plane_cap
    bx, by, bz = enthalpy.shape
    picks, stencil, places, spreads = tables()

    integers = functools.partial(jax.ShapeDtypeStruct, dtype=jnp.int32)
    sides, table, *farther = call(
        functools.partial(sides_kernel, sizes, plane_cap),
        [ANY] * 5,
        [shape(sizes[0] * sizes[1], 3 * bx, 128), integers((8 + -(-count // 8) * 8, 128)), *[shape(8, 128)] * (count - 3)],
        [
            pltpu.VMEM((1, SLOTS), jnp.int32),
            pltpu.VMEM((1, SLOTS), jnp.int32),
            pltpu.VMEM((FACES, 1, SLOTS), jnp.int32),
            pltpu.VMEM((bx, by, bz), F32),
            pltpu.VMEM((bx, by, bz), F32),
            pltpu.VMEM((sizes[0] * sizes[1], 3 * bx, 128), F32),
            pltpu.SemaphoreType.DMA((2 * bx + 4,)),
        ],
        [ANY] + [VMEM] * (count - 2),
        mib=56,
    )(
        tile_source.reshape(1, SLOTS),
        tile_block.reshape(1, SLOTS),
        jnp.transpose(tile_neighbour, (0, 1, 4, 2, 3)).reshape(FACES, 1, SLOTS),
        enthalpy,
        conductivity,
    )
    sides = lax.all_to_all(sides, ("gy", "gz"), split_axis=0, concat_axis=0, tiled=True)

    def pass_on(value, shift):
        return lax.ppermute(value, "gx", [(i, (i + shift) % count) for i in range(count)])

    def exchange(values):
        return [pass_on(value, shift) for shift, value in enumerate(values, 1)]

    farther = [pass_on(value, shift) for shift, value in enumerate(farther, 2)]

    phase_field = phase.reshape(SLOTS, TE, PLANE)
    solute_field = solute.reshape(SLOTS, TE, PLANE)
    own_shape, send_shapes = shape(2 * SLOTS, REC, 128), [shape(plane_cap * REC, 128)] * others
    own, *packed = call(first_pack_kernel, [SMEM] + [VMEM] * 3, [own_shape, *send_shapes])(
        table, phase_field, solute_field, picks
    )

    layer = shape(3 * by + 8, bz)
    down, up = call(
        functools.partial(layers_kernel, sizes), [VMEM] * 4 + [ANY] * (1 + len(farther)), [layer, layer]
    )(enthalpy, conductivity, sides, table, packed[0], *farther)
    from_low, from_high = pass_on(up, 1), pass_on(down, others)
    row = 3 * by + 4
    request = [from_low[row], *[value[0] for value in farther], from_high[row]]
    request = jnp.stack([value[:block_cap] for value in request]).astype(jnp.int32)
    _, deep = block_layout(block_cap)
    brick = shape(bx, by, bz)
    got = exchange(packed)
    heated, *found = call(
        functools.partial(heat_kernel, block_cap, sizes),
        [SMEM] * 2 + [VMEM] * 5,
        [brick] + [shape(deep * CB, 128)] * count,
        [pltpu.VMEM((bx, by // CB, CB, bz), F32)],
    )(table, request, enthalpy, conductivity, sides, from_low, from_high)
    found[1:] = exchange(found[1:])
    (heat_out,) = call(write_out_kernel, [ANY], [brick], [pltpu.SemaphoreType.DMA], [ANY])(heated)

    field = shape(SLOTS, TE, PLANE)
    step_scratch = [
        pltpu.VMEM((records + 2 * SLOTS, REC, 128), F32),
        pltpu.VMEM((SLOTS, REC, 128), F32),
    ]
    def inner(phase_field, solute_field, *heat):
        return call(
            functools.partial(inner_kernel, bool(heat)), [VMEM] * (3 + len(heat)), [field, field]
        )(phase_field, solute_field, stencil, *heat)

    inner_fields = inner(phase_field, solute_field)
    phase_field, solute_field, heat, own, *send = call(
        functools.partial(first_step_kernel, block_cap),
        [SMEM] + [VMEM] * (7 + count + others),
        [field, field, shape(2, SLOTS * TE, 128), own_shape, *send_shapes],
        step_scratch
        + [
            pltpu.VMEM((count, deep * CB, 128), F32),
            pltpu.VMEM((SLOTS * CB, CB, 128), F32),
        ],
    )(table, phase_field, *inner_fields, own, picks, places, spreads, *found, *got)
    for _ in range(PHASE_STEPS - 2):
        got = exchange(send)
        inner_fields = inner(phase_field, solute_field, heat)
        phase_field, solute_field, own, *send = call(
            middle_step_kernel,
            [SMEM] + [VMEM] * (5 + others),
            [field, field, own_shape, *send_shapes],
            step_scratch,
        )(table, *inner_fields, own, picks, places, *got)
    got = exchange(send)
    inner_fields = inner(phase_field, solute_field, heat)
    phase_field, solute_field = call(
        last_step_kernel,
        [SMEM] + [VMEM] * (4 + others),
        [field, field],
        step_scratch + [pltpu.VMEM(field.shape, F32)] * 2 + [pltpu.SemaphoreType.DMA((8,))],
        [ANY] * 2,
    )(table, *inner_fields, own, places, *got)
    return heat_out, phase_field.reshape(phase.shape), solute_field.reshape(solute.shape)


def solution(mesh):
    grid = P("gx", "gy", "gz")
    tiles = P("gx", "gy", "gz", None, None, None)
    return jax.shard_map(
        local,
        mesh=mesh,
        in_specs=(
            grid,
            grid,
            tiles,
            tiles,
            P("gx", "gy", "gz", None, None),
            P("gx", "gy", "gz", None),
            P("gx", "gy", "gz", None, None),
        ),
        out_specs=(grid, tiles, tiles),
        check_vma=False,
    )
```

```python
import functools

import jax
import jax.numpy as jnp
import numpy as np
from jax import lax
from jax.experimental import pallas as pl
from jax.experimental.pallas import tpu as pltpu
from jax.sharding import PartitionSpec as P

CB = 8
TE = 16
PLANE = TE * TE
SLOTS = 16
FACES = 6
PHASE_STEPS = 4
REC = 24

RATE = 0.16
ORDER_SPEED = 0.1
SOLUTE_RATE = 0.15
COUPLING = 0.5
REJECTION = 0.5

F32 = jnp.float32
BF16 = jnp.bfloat16
VMEM = pl.BlockSpec(memory_space=pltpu.VMEM)
SMEM = pl.BlockSpec(memory_space=pltpu.SMEM)
ANY = pl.BlockSpec(memory_space=pl.ANY)


def plane_lane(face):
    j = np.arange(TE)
    return [j, PLANE - TE + j, j * TE, j * TE + TE - 1][face - 2]


def constant_tables():
    pick = np.zeros((2, PLANE, 256), np.float32)
    place = np.zeros((2, 128, PLANE), np.float32)
    for field in range(2):
        for face in range(2, 6):
            at = field * 64 + (face - 2) * TE + np.arange(TE)
            pick[field, plane_lane(face ^ 1), at] = 1.0
            pick[field, plane_lane(face), 128 + at] = 1.0
            place[field, at, plane_lane(face)] = 1.0
    y, z = np.divmod(np.arange(PLANE), TE)
    dy, dz = np.abs(y[:, None] - y[None, :]), np.abs(z[:, None] - z[None, :])
    stencil = ((dy + dz) == 1).astype(np.float32)
    lane = np.arange(128)
    spread = (lane[:, None] % CB == z[None, :] // 2).astype(np.float32)
    return pick, place, stencil, spread


def tables():
    pick, place, stencil, spread = constant_tables()
    place = np.concatenate([place[0], place[1]], axis=1)
    return (
        jnp.asarray(np.concatenate([pick[0], pick[1]], axis=0), BF16),
        jnp.asarray(stencil, BF16),
        jnp.asarray(np.concatenate([place, place], axis=0), BF16),
        jnp.asarray(np.concatenate([spread, spread], axis=0), BF16),
    )


def halves(value):
    high = value.astype(BF16)
    return high, (value - high.astype(F32)).astype(BF16)


def dot(a, b):
    return jnp.dot(a, b, preferred_element_type=F32)


def temperature(h):
    return jnp.minimum(h, 0.0) + jnp.maximum(h - 1.0, 0.0)


def iota(shape, dim):
    return lax.broadcasted_iota(jnp.int32, shape, dim)


def to_lanes(column):
    bx, by, _ = column.shape
    diagonal = iota((bx, by, 128), 1) == iota((bx, by, 128), 2)
    return jnp.sum(jnp.where(diagonal, column, 0.0), axis=1)


def to_column(line, by):
    bx = line.shape[0]
    diagonal = iota((bx, by, 128), 1) == iota((bx, by, 128), 2)
    return jnp.sum(jnp.where(diagonal, line[:, None, :], 0.0), axis=2, keepdims=True)


def conduct(h, k, xlo, xhi, ylo, yhi, zlo, zhi):
    bx, by, bz = h.shape
    t = temperature(h)
    row, lane = iota((bx, by, bz), 1), iota((bx, by, bz), 2)
    if bx > 1:
        total = jnp.concatenate([xlo, t[:-1]], axis=0) + jnp.concatenate([t[1:], xhi], axis=0)
    else:
        total = xlo + xhi
    total += jnp.where(row == 0, ylo[:, None, :], pltpu.roll(t, 1, 1))
    total += jnp.where(row == by - 1, yhi[:, None, :], pltpu.roll(t, by - 1, 1))
    total += jnp.where(lane == 0, to_column(zlo, by), pltpu.roll(t, 1, 2))
    total += jnp.where(lane == bz - 1, to_column(zhi, by), pltpu.roll(t, bz - 1, 2))
    return h + RATE * k * (total - 6.0 * t)


def sublanes(value, y):
    return jnp.concatenate([value[x, y : y + 1, :] for x in range(value.shape[0])], axis=0)


def side_blocks(h, k):
    by, bz = h.shape[1:]
    return [
        (sublanes(h, 0), sublanes(h, 1), sublanes(k, 0)),
        (sublanes(h, by - 1), sublanes(h, by - 2), sublanes(k, by - 1)),
        (to_lanes(h[:, :, 0:1]), to_lanes(h[:, :, 1:2]), to_lanes(k[:, :, 0:1])),
        (to_lanes(h[:, :, bz - 1 : bz]), to_lanes(h[:, :, bz - 2 : bz - 1]), to_lanes(k[:, :, bz - 1 : bz])),
    ]


def column_of(row):
    square = (row.shape[1], row.shape[1])
    return jnp.sum(jnp.where(iota(square, 0) == iota(square, 1), row, 0.0), axis=1, keepdims=True)


def table_sizes(count, plane_cap):
    records = (count - 1) * plane_cap
    faces = min(FACES, 128 // records)
    return records, faces, 1 + -(-FACES // faces)


def place_of(table, slot):
    return table[0, FACES * SLOTS + slot], table[0, FACES * SLOTS + SLOTS + slot]


def write_tables(plane_cap, source, block, neighbour, asked, farther, table):
    me = lax.axis_index("gx").astype(F32)
    count = lax.axis_size("gx")
    records, faces, _ = table_sizes(count, plane_cap)
    cap = float(plane_cap)

    def wrapped(shift):
        return jnp.where(shift < 0.0, shift + float(count), shift)

    square = (SLOTS, SLOTS)
    before = iota(square, 0) < iota(square, 1)
    slot = iota((1, SLOTS), 1).astype(F32)
    source_row, block_column = source[...].astype(F32), column_of(block[...].astype(F32))
    source_column = column_of(source_row)
    rank = jnp.sum(
        jnp.where((source_column == source_row) & before, 1.0, 0.0), axis=0, keepdims=True
    )
    rank_column = column_of(rank)
    lane = iota((SLOTS, 128), 1).astype(F32)
    for shift in range(count):
        hit = (wrapped(source_column - me) == float(shift)) & (rank_column == lane)
        row = jnp.sum(jnp.where(hit, block_column, 0.0), axis=0, keepdims=True)
        asked[shift : shift + 1, :] = row
        if 2 <= shift < count - 1:
            farther[shift - 2][...] = jnp.broadcast_to(row, (8, 128))
    at = FACES * SLOTS
    table[0:1, at : at + SLOTS] = wrapped(me - source_row).astype(jnp.int32)
    table[0:1, at + SLOTS : at + 2 * SLOTS] = rank.astype(jnp.int32)
    slot_column = iota((SLOTS, records), 0).astype(F32)
    for face in range(FACES):
        number = neighbour[face]
        owner_row, number_row = (number >> 4).astype(F32), number.astype(F32)
        owner_column, number_column = column_of(owner_row), column_of(number_row)
        other_row = (number_row >= 0.0) & (owner_row != me)
        alike = (owner_column == owner_row) & (owner_column >= 0.0) & (owner_column != me)
        receive_rank = jnp.sum(
            jnp.where(alike & (number_column < number_row), 1.0, 0.0), axis=0, keepdims=True
        )
        send_rank = jnp.sum(jnp.where(alike & before, 1.0, 0.0), axis=0, keepdims=True)
        here = records + (number_row - owner_row * SLOTS)
        there = (wrapped(me - owner_row) - 1.0) * cap + receive_rank
        receive = jnp.where(owner_row == me, here, there)
        receive = jnp.where(number_row < 0.0, records + SLOTS + slot, receive)
        table[0:1, face * SLOTS : face * SLOTS + SLOTS] = receive.astype(jnp.int32)
        key = jnp.where(other_row, (wrapped(owner_row - me) - 1.0) * cap + send_rank, -1.0)
        hit = iota((SLOTS, records), 1).astype(F32) == column_of(key)
        tile = jnp.sum(jnp.where(hit, slot_column, 0.0), axis=0, keepdims=True)
        row, at = 1 + (face ^ 1) // faces, (face ^ 1) % faces * records
        table[row : row + 1, at : at + records] = tile.astype(jnp.int32)


def sides_kernel(
    sizes, plane_cap, source_far, block_far, neighbour_far, h_far, k_far, send, table, *rest
):
    asked, *farther, source, block, neighbour, h, k, sems = rest
    ny, nz = sizes
    my_y, my_z = lax.axis_index("gy"), lax.axis_index("gz")
    bx = h.shape[0]
    small = [(source_far, source), (block_far, block), (neighbour_far, neighbour)]
    copies = [pltpu.make_async_copy(*pair, sems.at[2 * bx + n]) for n, pair in enumerate(small)]
    large = []
    for x in range(bx):
        large.append(pltpu.make_async_copy(h_far.at[x], h.at[x], sems.at[x]))
        large.append(pltpu.make_async_copy(k_far.at[x], k.at[x], sems.at[bx + x]))
    for copy in copies + large:
        copy.start()
    for copy in copies:
        copy.wait()
    write_tables(plane_cap, source, block, neighbour, asked, farther, table)
    for copy in large:
        copy.wait()
    blocks = side_blocks(h[...], k[...])
    for y in range(ny):
        for z in range(nz):
            for part in range(3):
                ylo, yhi, zlo, zhi = [block[part] for block in blocks]
                chosen = jnp.where(
                    my_y == y, jnp.where(z < my_z, zlo, zhi), jnp.where(y < my_y, ylo, yhi)
                )
                send[y * nz + z, part * bx : part * bx + bx, :] = chosen


def side_reader(sizes, got, bx):
    ny, nz = sizes
    my_y, my_z = lax.axis_index("gy"), lax.axis_index("gz")

    def read(dy, dz, part=0):
        y, z = my_y + dy, my_z + dz
        inside = (y >= 0) & (y < ny) & (z >= 0) & (z < nz)
        at = jnp.where(inside, y * nz + z, 0)
        return jnp.where(inside, got[at, part * bx : part * bx + bx, :], 0.0)

    return read


def layers_kernel(sizes, h, k, got, asked, *rest):
    down, up = rest[-2:]
    bx, by, bz = h.shape
    read = side_reader(sizes, got, bx)
    around = [read(-1, 0), read(1, 0), read(0, -1), read(0, 1)]
    last = asked.shape[0] - 1
    for out, near, far, ask in ((down, 0, 1, last), (up, bx - 1, bx - 2, 1)):
        out[0:by, :] = h[near]
        out[by : 2 * by, :] = h[far]
        out[2 * by : 3 * by, :] = k[near]
        for number, side in enumerate(around):
            out[3 * by + number : 3 * by + number + 1, :] = side[near : near + 1, :]
        out[3 * by + 4 : 3 * by + 8, :] = jnp.broadcast_to(asked[ask : ask + 1, :], (4, bz))


def block_layout(cap):
    parts = 128 // CB // cap
    return parts, CB // parts


def flat_step(h, k, inner, outer, first, last, before, after, length):
    bx, lanes = h.shape
    t = temperature(h)
    row, lane = iota(h.shape, 0), iota(h.shape, 1)
    total = temperature(inner) + temperature(outer)
    total += jnp.where(row == 0, temperature(first), pltpu.roll(t, 1, 0))
    total += jnp.where(row == bx - 1, temperature(last), pltpu.roll(t, bx - 1, 0))
    total += jnp.where(lane == 0, temperature(before), pltpu.roll(t, 1, 1))
    total += jnp.where(lane == length - 1, temperature(after), pltpu.roll(t, lanes - 1, 1))
    return h + RATE * k * (total - 6.0 * t)


def heat_kernel(cap, sizes, request, h, k, got, low, high, out, found, *rest):
    *send, held = rest
    count = lax.axis_size("gx")
    bx, by, bz = h.shape
    h0, k0 = h[...], k[...]
    read = side_reader(sizes, got, bx)
    me = lax.axis_index("gx")
    layers, lines = [], []
    for beside, inside in ((low, me > 0), (high, me < count - 1)):
        beside = jnp.where(inside, beside[...], 0.0)
        layers.append([beside[part * by : part * by + by, :][None] for part in range(3)])
        lines.append([beside[3 * by + n : 3 * by + n + 1, :] for n in range(4)])
    y_sides = [[read(d, 0, part) for part in range(3)] for d in (-1, 1)]
    z_sides = [[read(0, d, part) for part in range(3)] for d in (-1, 1)]
    corner = [[read(dy, dz) for dz in (-1, 1)] for dy in (-1, 1)]
    to_first = [[pltpu.roll(c[0], 1, 1), c[1]] for c in corner]
    y_inner = [sublanes(h0, 0), sublanes(h0, by - 1)]
    z_inner = [to_lanes(h0[:, :, 0:1]), to_lanes(h0[:, :, bz - 1 : bz])]

    sides = [temperature(layers[0][0]), temperature(layers[1][0])]
    sides += [temperature(side[0]) for side in y_sides + z_sides]
    h1 = conduct(h0, k0, *sides)
    next_sides = []
    for side in range(2):
        near, far, near_k = layers[side]
        across = [temperature(far), temperature(h0[0:1])]
        if side:
            across = [temperature(h0[bx - 1 : bx]), temperature(far)]
        next_sides.append(conduct(near, near_k, *across, *[temperature(line) for line in lines[side]]))
    for side in range(2):
        near, far, near_k = y_sides[side]
        ends = [to_first[side][0], pltpu.roll(to_first[side][1], bz - 1, 1)]
        next_sides.append(
            flat_step(near, near_k, y_inner[side], far, lines[0][side], lines[1][side], *ends, bz)
        )
    for side in range(2):
        near, far, near_k = z_sides[side]
        ends = [to_first[0][side], pltpu.roll(to_first[1][side], by - 1, 1)]
        next_sides.append(
            flat_step(near, near_k, z_inner[side], far, lines[0][2 + side], lines[1][2 + side], *ends, by)
        )
    h2 = conduct(h1, k0, *[temperature(side) for side in next_sides])
    out[...] = h2

    held[...] = temperature(h2).reshape(bx, by // CB, CB, bz)
    parts, deep = block_layout(cap)
    nby, nbz = by // CB, bz // CB
    group = iota((deep, CB, bz), 2) // CB
    for shift in range(count):
        total = jnp.zeros((deep, CB, bz), F32)
        for rank in range(cap):
            block = request[(count - shift) % count, rank]
            a, b, c = block // (nby * nbz), (block // nbz) % nby, block % nbz
            for part in range(parts):
                at = rank * parts + part
                patch = held[pl.ds(a * CB + part * deep, deep), b]
                moved = pltpu.roll(patch, (CB * at - CB * c + bz) % bz, 2)
                total = jnp.where(group == at, moved, total)
        total = total.reshape(deep * CB, bz)
        (send[shift - 1] if shift else found)[...] = total


def write_records(phase, solute, picks, own, own_edges, rows):
    flat = [f.reshape(SLOTS * TE, PLANE) for f in (phase, solute)]
    high, low = halves(jnp.concatenate(flat, axis=1))
    planes = dot(high, picks) + dot(low, picks)
    own[0:SLOTS] = planes[:, 0:128].reshape(SLOTS, TE, 128)
    own[SLOTS : 2 * SLOTS] = planes[:, 128:256].reshape(SLOTS, TE, 128)
    for part in range(4):
        rows[part] = flat[part // 2][:, part % 2 * 128 : part % 2 * 128 + 128]
    for part in range(4):
        low_face = rows[part, pl.ds(0, SLOTS, TE), :]
        high_face = rows[part, pl.ds(TE - 1, SLOTS, TE), :]
        for at, value in ((0, high_face), (4, low_face)):
            own_edges[pl.ds(at + part, SLOTS, 8), :] = value
            own_edges[pl.ds(8 * SLOTS + 4 - at + part, SLOTS, 8), :] = value


def merge_record(planes, edges, number):
    side = (iota((TE, 128), 1) % 64) // TE
    out = planes[number(2)]
    for face in range(3, 6):
        out = jnp.where(side == face - 2, planes[number(face)], out)
    first, second = [edges[pl.ds(pl.multiple_of(number(face) * 8, 8), 8), :] for face in range(2)]
    return out, jnp.where(iota((8, 128), 0) < 4, first, second)


def pack(own, own_edges, table, send):
    cap = send[0].shape[0] // REC
    records, faces, _ = table_sizes(len(send) + 1, cap)
    for record in range(records):
        out, row = send[record // cap], record % cap * REC
        planes, edge = merge_record(
            own, own_edges, lambda face: table[1 + face // faces, face % faces * records + record]
        )
        out[row : row + TE, :] = planes
        out[row + TE : row + REC, :] = edge


def first_pack_kernel(table, asked, phase, solute, picks, own, own_edges, asked_out, *rest):
    *send, rows = rest
    write_records(phase[...], solute[...], picks[...], own, own_edges, rows)
    pack(own, own_edges, table, send)
    asked_out[...] = asked[...]


def take_heat(cap, table, found, spreads, blocks, held, heat):
    parts, deep = block_layout(cap)
    for number, value in enumerate(found):
        blocks[number] = value[...]
    group = iota((CB, 128), 1) // CB
    for slot in range(SLOTS):
        back, rank = place_of(table, slot)
        for x in range(CB):
            row = (x % deep) * CB
            patch = blocks[back, row : row + CB, :]
            held[slot * CB + x] = jnp.where(group == rank * parts + x // deep, patch, 0.0)
    rows = held[...].reshape(SLOTS * CB * CB, 128)
    wide = dot(jnp.concatenate(halves(rows), axis=1), spreads)
    wide = wide.reshape(SLOTS * CB, CB, PLANE)
    keep = iota(wide.shape, 1) == iota(wide.shape, 2) // TE // 2
    coarse = jnp.sum(jnp.where(keep, wide, 0.0), axis=1)
    for half in range(2):
        for odd in range(2):
            heat[half, pl.ds(odd, SLOTS * CB, 2), :] = coarse[:, half * 128 : half * 128 + 128]


def inner_step(phase, solute, heat, stencil):
    row = iota((SLOTS, TE, PLANE), 1)
    lap = []
    for field in (phase, solute):
        high, low = halves(field.reshape(SLOTS * TE, PLANE))
        total = (dot(high, stencil) + dot(low, stencil)).reshape(SLOTS, TE, PLANE) - 6.0 * field
        total += jnp.where(row == 0, 0.0, pltpu.roll(field, 1, 1))
        total += jnp.where(row == TE - 1, 0.0, pltpu.roll(field, TE - 1, 1))
        lap.append(total)
    squared = 1.0 - phase * phase
    drive = solute if heat is None else heat + solute
    change = ORDER_SPEED * (
        lap[0] + phase - phase * phase * phase - COUPLING * drive * squared * squared
    )
    return phase + change, solute + SOLUTE_RATE * lap[1] + REJECTION * change


def wide_heat(heat):
    return jnp.concatenate([heat[0], heat[1]], axis=1).reshape(SLOTS, TE, PLANE)


def gather_ghosts(table, got, own, own_edges, planes, edges, ghosts, ghost_edges):
    records = planes.shape[0] - 2 * SLOTS
    cap = records // len(got)
    for record in range(records):
        value, row = got[record // cap], record % cap * REC
        planes[record] = value[row : row + TE, :]
        edges[record * 8 : record * 8 + 8, :] = value[row + TE : row + REC, :]
    planes[records:] = own[...]
    edges[records * 8 :, :] = own_edges[...]
    for slot in range(SLOTS):
        out, edge = merge_record(planes, edges, lambda face: table[0, face * SLOTS + slot])
        ghosts[slot] = out
        ghost_edges[slot] = edge


def ghost_shares(ghosts, ghost_edges, places):
    beside = jnp.concatenate(halves(ghosts[...].reshape(SLOTS * TE, 128)), axis=1)
    beside = dot(beside, places)
    rows = iota((SLOTS, TE, PLANE), 1)
    shares = []
    for number in range(2):
        share = beside[:, number * PLANE : number * PLANE + PLANE].reshape(SLOTS, TE, PLANE)
        for face, at_row in ((0, 0), (1, TE - 1)):
            at = face * 4 + number * 2
            side = [ghost_edges[:, row : row + 1, :] for row in (at, at + 1)]
            side = jnp.concatenate(side, axis=2)
            share += jnp.where(rows == at_row, side, 0.0)
        shares.append(share)
    return shares


def add_shares(phase, solute, shares, heat_share=None):
    change = ORDER_SPEED * shares[0]
    if heat_share is not None:
        change += heat_share
    return phase + change, solute + SOLUTE_RATE * shares[1] + REJECTION * change


def inner_kernel(has_heat, phase, solute, stencil, *rest):
    phase_out, solute_out = rest[-2:]
    heat = wide_heat(rest[0]) if has_heat else None
    phase_out[...], solute_out[...] = inner_step(phase[...], solute[...], heat, stencil[...])


def first_step_kernel(cap, table, old_phase, phase, solute, own, own_edges, picks, places, spreads, *rest):
    others = lax.axis_size("gx") - 1
    found, got, rest = rest[: others + 1], rest[others + 1 : 2 * others + 1], rest[2 * others + 1 :]
    phase_out, solute_out, heat_out, own_out, edges_out, *rest = rest
    send, (*records, ghosts, ghost_edges, rows, blocks, held) = rest[:others], rest[others:]
    take_heat(cap, table, found, spreads[...], blocks, held, heat_out)
    gather_ghosts(table, got, own, own_edges, *records, ghosts, ghost_edges)
    squared = 1.0 - old_phase[...] * old_phase[...]
    heat_share = (-ORDER_SPEED * COUPLING) * wide_heat(heat_out) * squared * squared
    new_phase, new_solute = add_shares(
        phase[...], solute[...], ghost_shares(ghosts, ghost_edges, places[...]), heat_share
    )
    phase_out[...] = new_phase
    solute_out[...] = new_solute
    write_records(new_phase, new_solute, picks[...], own_out, edges_out, rows)
    pack(own_out, edges_out, table, send)


def write_out_kernel(value, out, sem):
    copy = pltpu.make_async_copy(value, out, sem)
    copy.start()
    copy.wait()


def middle_step_kernel(table, phase, solute, own, own_edges, picks, places, *rest):
    others = lax.axis_size("gx") - 1
    got, (phase_out, solute_out, own_out, edges_out, *rest) = rest[:others], rest[others:]
    send, (*records, ghosts, ghost_edges, rows) = rest[:others], rest[others:]
    gather_ghosts(table, got, own, own_edges, *records, ghosts, ghost_edges)
    new_phase, new_solute = add_shares(phase[...], solute[...], ghost_shares(ghosts, ghost_edges, places[...]))
    phase_out[...] = new_phase
    solute_out[...] = new_solute
    write_records(new_phase, new_solute, picks[...], own_out, edges_out, rows)
    pack(own_out, edges_out, table, send)


def last_step_kernel(table, phase, solute, own, own_edges, places, *rest):
    others = lax.axis_size("gx") - 1
    got, (phase_out, solute_out, *records, ghosts, ghost_edges, _) = rest[:others], rest[others:]
    gather_ghosts(table, got, own, own_edges, *records, ghosts, ghost_edges)
    phase_out[...], solute_out[...] = add_shares(
        phase[...], solute[...], ghost_shares(ghosts, ghost_edges, places[...])
    )


def call(kernel, in_specs, out_shapes, scratch=(), out_specs=None, mib=16):
    return pl.pallas_call(
        kernel,
        out_shape=out_shapes,
        in_specs=in_specs,
        out_specs=out_specs or jax.tree.map(lambda _: VMEM, out_shapes),
        scratch_shapes=list(scratch),
        compiler_params=pltpu.CompilerParams(vmem_limit_bytes=mib * 1024 * 1024),
    )


def shape(*dims):
    return jax.ShapeDtypeStruct(dims, F32)


def local(enthalpy, conductivity, phase, solute, tile_source, tile_block, tile_neighbour):
    count = lax.axis_size("gx")
    sizes = (lax.axis_size("gy"), lax.axis_size("gz"))
    plane_cap = -(-SLOTS // (count - 1))
    block_cap = 2 * SLOTS // count
    others = count - 1
    records = others * plane_cap
    bx, by, bz = enthalpy.shape
    picks, stencil, places, spreads = tables()

    integers = functools.partial(jax.ShapeDtypeStruct, dtype=jnp.int32)
    sides, table, asked, *farther = call(
        functools.partial(sides_kernel, sizes, plane_cap),
        [ANY] * 5,
        [
            shape(sizes[0] * sizes[1], 3 * bx, 128),
            integers((table_sizes(count, plane_cap)[2], 128)),
            shape(count, 128),
            *[shape(8, 128)] * (count - 3),
        ],
        [
            pltpu.VMEM((1, SLOTS), jnp.int32),
            pltpu.VMEM((1, SLOTS), jnp.int32),
            pltpu.VMEM((FACES, 1, SLOTS), jnp.int32),
            pltpu.VMEM((bx, by, bz), F32),
            pltpu.VMEM((bx, by, bz), F32),
            pltpu.SemaphoreType.DMA((2 * bx + 3,)),
        ],
        mib=56,
    )(
        tile_source.reshape(1, SLOTS),
        tile_block.reshape(1, SLOTS),
        jnp.transpose(tile_neighbour, (0, 1, 4, 2, 3)).reshape(FACES, 1, SLOTS),
        enthalpy,
        conductivity,
    )
    sides = lax.all_to_all(sides, ("gy", "gz"), split_axis=0, concat_axis=0, tiled=True)

    def pass_on(value, shift):
        return lax.ppermute(value, "gx", [(i, (i + shift) % count) for i in range(count)])

    def exchange(values):
        return [pass_on(value, shift) for shift, value in enumerate(values, 1)]

    farther = [pass_on(value, shift) for shift, value in enumerate(farther, 2)]

    phase_field = phase.reshape(SLOTS, TE, PLANE)
    solute_field = solute.reshape(SLOTS, TE, PLANE)
    own_shapes = [shape(2 * SLOTS, TE, 128), shape(2 * SLOTS * 8, 128)]
    send_shapes = [shape(plane_cap * REC, 128)] * others
    rows_scratch = pltpu.VMEM((4, SLOTS * TE, 128), F32)
    packed = call(
        first_pack_kernel,
        [SMEM] + [VMEM] * 4,
        [*own_shapes, shape(count, 128), *send_shapes],
        [rows_scratch],
    )(table, asked, phase_field, solute_field, picks)
    own, asked, packed = packed[:2], packed[2], packed[3:]

    layer = shape(3 * by + 8, bz)
    down, up = call(
        functools.partial(layers_kernel, sizes), [VMEM] * 4 + [ANY] * len(farther), [layer, layer]
    )(enthalpy, conductivity, sides, asked, *farther)
    from_low, from_high = pass_on(up, 1), pass_on(down, others)
    row = 3 * by + 4
    request = [asked[0], from_low[row], *[value[0] for value in farther], from_high[row]]
    request = jnp.stack([value[:block_cap] for value in request]).astype(jnp.int32)
    _, deep = block_layout(block_cap)
    brick = shape(bx, by, bz)
    got = exchange(packed)
    heated, *found = call(
        functools.partial(heat_kernel, block_cap, sizes),
        [SMEM] + [VMEM] * 5,
        [brick] + [shape(deep * CB, 128)] * count,
        [pltpu.VMEM((bx, by // CB, CB, bz), F32)],
    )(request, enthalpy, conductivity, sides, from_low, from_high)
    found[1:] = exchange(found[1:])
    (heat_out,) = call(write_out_kernel, [ANY], [brick], [pltpu.SemaphoreType.DMA], [ANY])(heated)

    field = shape(SLOTS, TE, PLANE)
    step_scratch = [
        pltpu.VMEM((records + 2 * SLOTS, TE, 128), F32),
        pltpu.VMEM(((records + 2 * SLOTS) * 8, 128), F32),
        pltpu.VMEM((SLOTS, TE, 128), F32),
        pltpu.VMEM((SLOTS, 8, 128), F32),
        rows_scratch,
    ]
    def inner(phase_field, solute_field, *heat):
        return call(
            functools.partial(inner_kernel, bool(heat)), [VMEM] * (3 + len(heat)), [field, field]
        )(phase_field, solute_field, stencil, *heat)

    inner_fields = inner(phase_field, solute_field)
    phase_field, solute_field, heat, *rest = call(
        functools.partial(first_step_kernel, block_cap),
        [SMEM] + [VMEM] * (8 + count + others),
        [field, field, shape(2, SLOTS * TE, 128), *own_shapes, *send_shapes],
        step_scratch
        + [
            pltpu.VMEM((count, deep * CB, 128), F32),
            pltpu.VMEM((SLOTS * CB, CB, 128), F32),
        ],
    )(table, phase_field, *inner_fields, *own, picks, places, spreads, *found, *got)
    own, send = rest[:2], rest[2:]
    for _ in range(PHASE_STEPS - 2):
        got = exchange(send)
        inner_fields = inner(phase_field, solute_field, heat)
        phase_field, solute_field, *rest = call(
            middle_step_kernel,
            [SMEM] + [VMEM] * (6 + others),
            [field, field, *own_shapes, *send_shapes],
            step_scratch,
        )(table, *inner_fields, *own, picks, places, *got)
        own, send = rest[:2], rest[2:]
    got = exchange(send)
    inner_fields = inner(phase_field, solute_field, heat)
    phase_field, solute_field = call(
        last_step_kernel, [SMEM] + [VMEM] * (5 + others), [field, field], step_scratch
    )(table, *inner_fields, *own, places, *got)
    return heat_out, phase_field.reshape(phase.shape), solute_field.reshape(solute.shape)


def solution(mesh):
    grid = P("gx", "gy", "gz")
    tiles = P("gx", "gy", "gz", None, None, None)
    return jax.shard_map(
        local,
        mesh=mesh,
        in_specs=(
            grid,
            grid,
            tiles,
            tiles,
            P("gx", "gy", "gz", None, None),
            P("gx", "gy", "gz", None),
            P("gx", "gy", "gz", None, None),
        ),
        out_specs=(grid, tiles, tiles),
        check_vma=False,
    )
```

```python
import functools

import jax
import jax.numpy as jnp
import numpy as np
from jax import lax
from jax.experimental import pallas as pl
from jax.experimental.pallas import tpu as pltpu
from jax.sharding import PartitionSpec as P

CB = 8
TE = 16
PLANE = TE * TE
SLOTS = 16
FACES = 6
PHASE_STEPS = 4
REC = 24

RATE = 0.16
ORDER_SPEED = 0.1
SOLUTE_RATE = 0.15
COUPLING = 0.5
REJECTION = 0.5

F32 = jnp.float32
BF16 = jnp.bfloat16
VMEM = pl.BlockSpec(memory_space=pltpu.VMEM)
SMEM = pl.BlockSpec(memory_space=pltpu.SMEM)
ANY = pl.BlockSpec(memory_space=pl.ANY)


def plane_lane(face):
    j = np.arange(TE)
    return [j, PLANE - TE + j, j * TE, j * TE + TE - 1][face - 2]


def constant_tables():
    pick = np.zeros((2, PLANE, 256), np.float32)
    place = np.zeros((2, 128, PLANE), np.float32)
    for field in range(2):
        for face in range(2, 6):
            at = field * 64 + (face - 2) * TE + np.arange(TE)
            pick[field, plane_lane(face ^ 1), at] = 1.0
            pick[field, plane_lane(face), 128 + at] = 1.0
            place[field, at, plane_lane(face)] = 1.0
    y, z = np.divmod(np.arange(PLANE), TE)
    dy, dz = np.abs(y[:, None] - y[None, :]), np.abs(z[:, None] - z[None, :])
    stencil = ((dy + dz) == 1).astype(np.float32)
    lane = np.arange(128)
    spread = (lane[:, None] % CB == z[None, :] // 2).astype(np.float32)
    return pick, place, stencil, spread


def tables():
    pick, place, stencil, spread = constant_tables()
    place = np.concatenate([place[0], place[1]], axis=1)
    return (
        jnp.asarray(np.concatenate([pick[0], pick[1]], axis=0), BF16),
        jnp.asarray(stencil, BF16),
        jnp.asarray(np.concatenate([place, place], axis=0), BF16),
        jnp.asarray(np.concatenate([spread, spread], axis=0), BF16),
    )


def halves(value):
    high = value.astype(BF16)
    return high, (value - high.astype(F32)).astype(BF16)


def dot(a, b):
    return jnp.dot(a, b, preferred_element_type=F32)


def temperature(h):
    return jnp.minimum(h, 0.0) + jnp.maximum(h - 1.0, 0.0)


def iota(shape, dim):
    return lax.broadcasted_iota(jnp.int32, shape, dim)


def to_lanes(column):
    bx, by, _ = column.shape
    diagonal = iota((bx, by, 128), 1) == iota((bx, by, 128), 2)
    return jnp.sum(jnp.where(diagonal, column, 0.0), axis=1)


def to_column(line, by):
    bx = line.shape[0]
    diagonal = iota((bx, by, 128), 1) == iota((bx, by, 128), 2)
    return jnp.sum(jnp.where(diagonal, line[:, None, :], 0.0), axis=2, keepdims=True)


def conduct(h, k, xlo, xhi, ylo, yhi, zlo, zhi):
    bx, by, bz = h.shape
    t = temperature(h)
    row, lane = iota((bx, by, bz), 1), iota((bx, by, bz), 2)
    if bx > 1:
        total = jnp.concatenate([xlo, t[:-1]], axis=0) + jnp.concatenate([t[1:], xhi], axis=0)
    else:
        total = xlo + xhi
    total += jnp.where(row == 0, ylo[:, None, :], pltpu.roll(t, 1, 1))
    total += jnp.where(row == by - 1, yhi[:, None, :], pltpu.roll(t, by - 1, 1))
    total += jnp.where(lane == 0, to_column(zlo, by), pltpu.roll(t, 1, 2))
    total += jnp.where(lane == bz - 1, to_column(zhi, by), pltpu.roll(t, bz - 1, 2))
    return h + RATE * k * (total - 6.0 * t)


def sublanes(value, y):
    return jnp.concatenate([value[x, y : y + 1, :] for x in range(value.shape[0])], axis=0)


def side_blocks(h, k):
    by, bz = h.shape[1:]
    return [
        (sublanes(h, 0), sublanes(h, 1), sublanes(k, 0)),
        (sublanes(h, by - 1), sublanes(h, by - 2), sublanes(k, by - 1)),
        (to_lanes(h[:, :, 0:1]), to_lanes(h[:, :, 1:2]), to_lanes(k[:, :, 0:1])),
        (to_lanes(h[:, :, bz - 1 : bz]), to_lanes(h[:, :, bz - 2 : bz - 1]), to_lanes(k[:, :, bz - 1 : bz])),
    ]


def column_of(row):
    square = (row.shape[1], row.shape[1])
    return jnp.sum(jnp.where(iota(square, 0) == iota(square, 1), row, 0.0), axis=1, keepdims=True)


def table_sizes(count, plane_cap):
    records = (count - 1) * plane_cap
    faces = min(FACES, 128 // records)
    return records, faces, 1 + -(-FACES // faces)


def place_of(table, slot):
    return table[0, FACES * SLOTS + slot], table[0, FACES * SLOTS + SLOTS + slot]


def write_tables(plane_cap, source, block, neighbour, asked, farther, table):
    me = lax.axis_index("gx").astype(F32)
    count = lax.axis_size("gx")
    records, faces, _ = table_sizes(count, plane_cap)
    cap = float(plane_cap)

    def wrapped(shift):
        return jnp.where(shift < 0.0, shift + float(count), shift)

    square = (SLOTS, SLOTS)
    before = iota(square, 0) < iota(square, 1)
    slot = iota((1, SLOTS), 1).astype(F32)
    source_row, block_column = source[...].astype(F32), column_of(block[...].astype(F32))
    source_column = column_of(source_row)
    rank = jnp.sum(
        jnp.where((source_column == source_row) & before, 1.0, 0.0), axis=0, keepdims=True
    )
    rank_column = column_of(rank)
    lane = iota((SLOTS, 128), 1).astype(F32)
    for shift in range(count):
        hit = (wrapped(source_column - me) == float(shift)) & (rank_column == lane)
        row = jnp.sum(jnp.where(hit, block_column, 0.0), axis=0, keepdims=True)
        asked[shift : shift + 1, :] = row
        if 2 <= shift < count - 1:
            farther[shift - 2][...] = jnp.broadcast_to(row, (8, 128))
    at = FACES * SLOTS
    table[0:1, at : at + SLOTS] = wrapped(me - source_row).astype(jnp.int32)
    table[0:1, at + SLOTS : at + 2 * SLOTS] = rank.astype(jnp.int32)
    slot_column = iota((SLOTS, records), 0).astype(F32)
    for face in range(FACES):
        number = neighbour[face]
        owner_row, number_row = (number >> 4).astype(F32), number.astype(F32)
        owner_column, number_column = column_of(owner_row), column_of(number_row)
        other_row = (number_row >= 0.0) & (owner_row != me)
        alike = (owner_column == owner_row) & (owner_column >= 0.0) & (owner_column != me)
        receive_rank = jnp.sum(
            jnp.where(alike & (number_column < number_row), 1.0, 0.0), axis=0, keepdims=True
        )
        send_rank = jnp.sum(jnp.where(alike & before, 1.0, 0.0), axis=0, keepdims=True)
        here = records + (number_row - owner_row * SLOTS)
        there = (wrapped(me - owner_row) - 1.0) * cap + receive_rank
        receive = jnp.where(owner_row == me, here, there)
        receive = jnp.where(number_row < 0.0, records + SLOTS + slot, receive)
        table[0:1, face * SLOTS : face * SLOTS + SLOTS] = receive.astype(jnp.int32)
        key = jnp.where(other_row, (wrapped(owner_row - me) - 1.0) * cap + send_rank, -1.0)
        hit = iota((SLOTS, records), 1).astype(F32) == column_of(key)
        tile = jnp.sum(jnp.where(hit, slot_column, 0.0), axis=0, keepdims=True)
        row, at = 1 + (face ^ 1) // faces, (face ^ 1) % faces * records
        table[row : row + 1, at : at + records] = tile.astype(jnp.int32)


def sides_kernel(
    sizes, plane_cap, source_far, block_far, neighbour_far, h_far, k_far, send, table, *rest
):
    asked, *farther, source, block, neighbour, h, k, sems = rest
    ny, nz = sizes
    my_y, my_z = lax.axis_index("gy"), lax.axis_index("gz")
    bx = h.shape[0]
    small = [(source_far, source), (block_far, block), (neighbour_far, neighbour)]
    copies = [pltpu.make_async_copy(*pair, sems.at[2 * bx + n]) for n, pair in enumerate(small)]
    large = []
    for x in range(bx):
        large.append(pltpu.make_async_copy(h_far.at[x], h.at[x], sems.at[x]))
        large.append(pltpu.make_async_copy(k_far.at[x], k.at[x], sems.at[bx + x]))
    for copy in copies + large:
        copy.start()
    for copy in copies:
        copy.wait()
    write_tables(plane_cap, source, block, neighbour, asked, farther, table)
    for copy in large:
        copy.wait()
    blocks = side_blocks(h[...], k[...])
    for y in range(ny):
        for z in range(nz):
            for part in range(3):
                ylo, yhi, zlo, zhi = [block[part] for block in blocks]
                chosen = jnp.where(
                    my_y == y, jnp.where(z < my_z, zlo, zhi), jnp.where(y < my_y, ylo, yhi)
                )
                send[y * nz + z, part * bx : part * bx + bx, :] = chosen


def side_reader(sizes, got, bx):
    ny, nz = sizes
    my_y, my_z = lax.axis_index("gy"), lax.axis_index("gz")

    def read(dy, dz, part=0):
        y, z = my_y + dy, my_z + dz
        inside = (y >= 0) & (y < ny) & (z >= 0) & (z < nz)
        at = jnp.where(inside, y * nz + z, 0)
        return jnp.where(inside, got[at, part * bx : part * bx + bx, :], 0.0)

    return read


def layers_kernel(sizes, h, k, got, asked, *rest):
    down, up = rest[-2:]
    bx, by, bz = h.shape
    read = side_reader(sizes, got, bx)
    around = [read(-1, 0), read(1, 0), read(0, -1), read(0, 1)]
    last = asked.shape[0] - 1
    for out, near, far, ask in ((down, 0, 1, last), (up, bx - 1, bx - 2, 1)):
        out[0:by, :] = h[near]
        out[by : 2 * by, :] = h[far]
        out[2 * by : 3 * by, :] = k[near]
        for number, side in enumerate(around):
            out[3 * by + number : 3 * by + number + 1, :] = side[near : near + 1, :]
        out[3 * by + 4 : 3 * by + 8, :] = jnp.broadcast_to(asked[ask : ask + 1, :], (4, bz))


def block_layout(cap):
    parts = 128 // CB // cap
    return parts, CB // parts


def flat_step(h, k, inner, outer, first, last, before, after, length):
    bx, lanes = h.shape
    t = temperature(h)
    row, lane = iota(h.shape, 0), iota(h.shape, 1)
    total = temperature(inner) + temperature(outer)
    total += jnp.where(row == 0, temperature(first), pltpu.roll(t, 1, 0))
    total += jnp.where(row == bx - 1, temperature(last), pltpu.roll(t, bx - 1, 0))
    total += jnp.where(lane == 0, temperature(before), pltpu.roll(t, 1, 1))
    total += jnp.where(lane == length - 1, temperature(after), pltpu.roll(t, lanes - 1, 1))
    return h + RATE * k * (total - 6.0 * t)


def heat_kernel(cap, sizes, request, h, k, got, low, high, out, found, *rest):
    *send, held = rest
    count = lax.axis_size("gx")
    bx, by, bz = h.shape
    h0, k0 = h[...], k[...]
    read = side_reader(sizes, got, bx)
    me = lax.axis_index("gx")
    layers, lines = [], []
    for beside, inside in ((low, me > 0), (high, me < count - 1)):
        beside = jnp.where(inside, beside[...], 0.0)
        layers.append([beside[part * by : part * by + by, :][None] for part in range(3)])
        lines.append([beside[3 * by + n : 3 * by + n + 1, :] for n in range(4)])
    y_sides = [[read(d, 0, part) for part in range(3)] for d in (-1, 1)]
    z_sides = [[read(0, d, part) for part in range(3)] for d in (-1, 1)]
    corner = [[read(dy, dz) for dz in (-1, 1)] for dy in (-1, 1)]
    to_first = [[pltpu.roll(c[0], 1, 1), c[1]] for c in corner]
    y_inner = [sublanes(h0, 0), sublanes(h0, by - 1)]
    z_inner = [to_lanes(h0[:, :, 0:1]), to_lanes(h0[:, :, bz - 1 : bz])]

    sides = [temperature(layers[0][0]), temperature(layers[1][0])]
    sides += [temperature(side[0]) for side in y_sides + z_sides]
    h1 = conduct(h0, k0, *sides)
    next_sides = []
    for side in range(2):
        near, far, near_k = layers[side]
        across = [temperature(far), temperature(h0[0:1])]
        if side:
            across = [temperature(h0[bx - 1 : bx]), temperature(far)]
        next_sides.append(conduct(near, near_k, *across, *[temperature(line) for line in lines[side]]))
    for side in range(2):
        near, far, near_k = y_sides[side]
        ends = [to_first[side][0], pltpu.roll(to_first[side][1], bz - 1, 1)]
        next_sides.append(
            flat_step(near, near_k, y_inner[side], far, lines[0][side], lines[1][side], *ends, bz)
        )
    for side in range(2):
        near, far, near_k = z_sides[side]
        ends = [to_first[0][side], pltpu.roll(to_first[1][side], by - 1, 1)]
        next_sides.append(
            flat_step(near, near_k, z_inner[side], far, lines[0][2 + side], lines[1][2 + side], *ends, by)
        )
    h2 = conduct(h1, k0, *[temperature(side) for side in next_sides])
    out[...] = h2

    held[...] = temperature(h2).reshape(bx, by // CB, CB, bz)
    parts, deep = block_layout(cap)
    nby, nbz = by // CB, bz // CB
    group = iota((deep, CB, bz), 2) // CB
    for shift in range(count):
        total = jnp.zeros((deep, CB, bz), F32)
        for rank in range(cap):
            block = request[(count - shift) % count, rank]
            a, b, c = block // (nby * nbz), (block // nbz) % nby, block % nbz
            for part in range(parts):
                at = rank * parts + part
                patch = held[pl.ds(a * CB + part * deep, deep), b]
                moved = pltpu.roll(patch, (CB * at - CB * c + bz) % bz, 2)
                total = jnp.where(group == at, moved, total)
        total = total.reshape(deep * CB, bz)
        (send[shift - 1] if shift else found)[...] = total


def write_records(phase, solute, picks, own, own_edges, rows):
    flat = [f.reshape(SLOTS * TE, PLANE) for f in (phase, solute)]
    high, low = halves(jnp.concatenate(flat, axis=1))
    planes = dot(high, picks) + dot(low, picks)
    own[0:SLOTS] = planes[:, 0:128].reshape(SLOTS, TE, 128)
    own[SLOTS : 2 * SLOTS] = planes[:, 128:256].reshape(SLOTS, TE, 128)
    for part in range(4):
        rows[part] = flat[part // 2][:, part % 2 * 128 : part % 2 * 128 + 128]
    for part in range(4):
        low_face = rows[part, pl.ds(0, SLOTS, TE), :]
        high_face = rows[part, pl.ds(TE - 1, SLOTS, TE), :]
        for at, value in ((0, high_face), (4, low_face)):
            own_edges[pl.ds(at + part, SLOTS, 8), :] = value
            own_edges[pl.ds(8 * SLOTS + 4 - at + part, SLOTS, 8), :] = value


def merge_record(planes, edges, number):
    side = (iota((TE, 128), 1) % 64) // TE
    out = planes[number(2)]
    for face in range(3, 6):
        out = jnp.where(side == face - 2, planes[number(face)], out)
    first, second = [edges[pl.ds(pl.multiple_of(number(face) * 8, 8), 8), :] for face in range(2)]
    return out, jnp.where(iota((8, 128), 0) < 4, first, second)


def pack(own, own_edges, table, send):
    cap = send[0].shape[0] // REC
    records, faces, _ = table_sizes(len(send) + 1, cap)
    for record in range(records):
        out, row = send[record // cap], record % cap * REC
        planes, edge = merge_record(
            own, own_edges, lambda face: table[1 + face // faces, face % faces * records + record]
        )
        out[row : row + TE, :] = planes
        out[row + TE : row + REC, :] = edge


def first_pack_kernel(table, asked, phase, solute, picks, own, own_edges, asked_out, *rest):
    *send, rows = rest
    write_records(phase[...], solute[...], picks[...], own, own_edges, rows)
    pack(own, own_edges, table, send)
    asked_out[...] = asked[...]


def take_heat(cap, table, found, spreads, blocks, held, heat):
    parts, deep = block_layout(cap)
    for number, value in enumerate(found):
        blocks[number] = value[...]
    group = iota((CB, 128), 1) // CB
    for slot in range(SLOTS):
        back, rank = place_of(table, slot)
        for x in range(CB):
            row = (x % deep) * CB
            patch = blocks[back, row : row + CB, :]
            held[slot * CB + x] = jnp.where(group == rank * parts + x // deep, patch, 0.0)
    rows = held[...].reshape(SLOTS * CB * CB, 128)
    wide = dot(jnp.concatenate(halves(rows), axis=1), spreads)
    wide = wide.reshape(SLOTS * CB, CB, PLANE)
    keep = iota(wide.shape, 1) == iota(wide.shape, 2) // TE // 2
    coarse = jnp.sum(jnp.where(keep, wide, 0.0), axis=1)
    for half in range(2):
        for odd in range(2):
            heat[half, pl.ds(odd, SLOTS * CB, 2), :] = coarse[:, half * 128 : half * 128 + 128]


def inner_step(phase, solute, heat, stencil):
    row = iota((SLOTS, TE, PLANE), 1)
    lap = []
    for field in (phase, solute):
        high, low = halves(field.reshape(SLOTS * TE, PLANE))
        total = (dot(high, stencil) + dot(low, stencil)).reshape(SLOTS, TE, PLANE) - 6.0 * field
        total += jnp.where(row == 0, 0.0, pltpu.roll(field, 1, 1))
        total += jnp.where(row == TE - 1, 0.0, pltpu.roll(field, TE - 1, 1))
        lap.append(total)
    squared = 1.0 - phase * phase
    drive = solute if heat is None else heat + solute
    change = ORDER_SPEED * (
        lap[0] + phase - phase * phase * phase - COUPLING * drive * squared * squared
    )
    return phase + change, solute + SOLUTE_RATE * lap[1] + REJECTION * change


def wide_heat(heat):
    return jnp.concatenate([heat[0], heat[1]], axis=1).reshape(SLOTS, TE, PLANE)


def hold_records(got, own, own_edges, planes, edges):
    records = planes.shape[0] - 2 * SLOTS
    cap = records // len(got)
    for record in range(records):
        value, row = got[record // cap], record % cap * REC
        planes[record] = value[row : row + TE, :]
        edges[record * 8 : record * 8 + 8, :] = value[row + TE : row + REC, :]
    planes[records:] = own[...]
    edges[records * 8 :, :] = own_edges[...]


def place_ghosts(table, planes, edges, ghosts, ghost_edges, tiles):
    for slot in tiles:
        out, edge = merge_record(planes, edges, lambda face: table[0, face * SLOTS + slot])
        ghosts[slot] = out
        ghost_edges[slot] = edge


def gather_ghosts(table, got, own, own_edges, planes, edges, ghosts, ghost_edges):
    hold_records(got, own, own_edges, planes, edges)
    place_ghosts(table, planes, edges, ghosts, ghost_edges, range(SLOTS))


def ghost_shares(ghosts, ghost_edges, places):
    tiles = ghosts.shape[0]
    beside = jnp.concatenate(halves(ghosts[...].reshape(tiles * TE, 128)), axis=1)
    beside = dot(beside, places)
    rows = iota((tiles, TE, PLANE), 1)
    shares = []
    for number in range(2):
        share = beside[:, number * PLANE : number * PLANE + PLANE].reshape(tiles, TE, PLANE)
        for face, at_row in ((0, 0), (1, TE - 1)):
            at = face * 4 + number * 2
            side = [ghost_edges[:, row : row + 1, :] for row in (at, at + 1)]
            side = jnp.concatenate(side, axis=2)
            share += jnp.where(rows == at_row, side, 0.0)
        shares.append(share)
    return shares


def add_shares(phase, solute, shares, heat_share=None):
    change = ORDER_SPEED * shares[0]
    if heat_share is not None:
        change += heat_share
    return phase + change, solute + SOLUTE_RATE * shares[1] + REJECTION * change


def inner_kernel(has_heat, phase, solute, stencil, *rest):
    phase_out, solute_out = rest[-2:]
    heat = wide_heat(rest[0]) if has_heat else None
    phase_out[...], solute_out[...] = inner_step(phase[...], solute[...], heat, stencil[...])


def first_step_kernel(cap, table, old_phase, phase, solute, own, own_edges, picks, places, spreads, *rest):
    others = lax.axis_size("gx") - 1
    found, got, rest = rest[: others + 1], rest[others + 1 : 2 * others + 1], rest[2 * others + 1 :]
    phase_out, solute_out, heat_out, own_out, edges_out, *rest = rest
    send, (*records, ghosts, ghost_edges, rows, blocks, held) = rest[:others], rest[others:]
    take_heat(cap, table, found, spreads[...], blocks, held, heat_out)
    gather_ghosts(table, got, own, own_edges, *records, ghosts, ghost_edges)
    squared = 1.0 - old_phase[...] * old_phase[...]
    heat_share = (-ORDER_SPEED * COUPLING) * wide_heat(heat_out) * squared * squared
    new_phase, new_solute = add_shares(
        phase[...], solute[...], ghost_shares(ghosts, ghost_edges, places[...]), heat_share
    )
    phase_out[...] = new_phase
    solute_out[...] = new_solute
    write_records(new_phase, new_solute, picks[...], own_out, edges_out, rows)
    pack(own_out, edges_out, table, send)


def write_out_kernel(value, out, sem):
    copy = pltpu.make_async_copy(value, out, sem)
    copy.start()
    copy.wait()


def middle_step_kernel(table, phase, solute, own, own_edges, picks, places, *rest):
    others = lax.axis_size("gx") - 1
    got, (phase_out, solute_out, own_out, edges_out, *rest) = rest[:others], rest[others:]
    send, (*records, ghosts, ghost_edges, rows) = rest[:others], rest[others:]
    gather_ghosts(table, got, own, own_edges, *records, ghosts, ghost_edges)
    new_phase, new_solute = add_shares(phase[...], solute[...], ghost_shares(ghosts, ghost_edges, places[...]))
    phase_out[...] = new_phase
    solute_out[...] = new_solute
    write_records(new_phase, new_solute, picks[...], own_out, edges_out, rows)
    pack(own_out, edges_out, table, send)


def last_step_kernel(table, phase, solute, own, own_edges, places, *rest):
    others = lax.axis_size("gx") - 1
    got, (phase_far, solute_far, planes, edges, ghosts, ghost_edges, phase_out, solute_out, sems) = (
        rest[:others], rest[others:]
    )
    hold_records(got, own, own_edges, planes, edges)
    copies = []
    step = 4
    for first in range(0, SLOTS, step):
        at = pl.ds(first, step)
        place_ghosts(table, planes, edges, ghosts, ghost_edges, range(first, first + step))
        shares = ghost_shares(ghosts.at[at], ghost_edges.at[at], places[...])
        phase_out[at], solute_out[at] = add_shares(phase[at], solute[at], shares)
        for out, far in ((phase_out, phase_far), (solute_out, solute_far)):
            copy = pltpu.make_async_copy(out.at[at], far.at[at], sems.at[len(copies)])
            copy.start()
            copies.append(copy)
    for copy in copies:
        copy.wait()


def call(kernel, in_specs, out_shapes, scratch=(), out_specs=None, mib=16):
    return pl.pallas_call(
        kernel,
        out_shape=out_shapes,
        in_specs=in_specs,
        out_specs=out_specs or jax.tree.map(lambda _: VMEM, out_shapes),
        scratch_shapes=list(scratch),
        compiler_params=pltpu.CompilerParams(vmem_limit_bytes=mib * 1024 * 1024),
    )


def shape(*dims):
    return jax.ShapeDtypeStruct(dims, F32)


def local(enthalpy, conductivity, phase, solute, tile_source, tile_block, tile_neighbour):
    count = lax.axis_size("gx")
    sizes = (lax.axis_size("gy"), lax.axis_size("gz"))
    plane_cap = -(-SLOTS // (count - 1))
    block_cap = 2 * SLOTS // count
    others = count - 1
    records = others * plane_cap
    bx, by, bz = enthalpy.shape
    picks, stencil, places, spreads = tables()

    integers = functools.partial(jax.ShapeDtypeStruct, dtype=jnp.int32)
    sides, table, asked, *farther = call(
        functools.partial(sides_kernel, sizes, plane_cap),
        [ANY] * 5,
        [
            shape(sizes[0] * sizes[1], 3 * bx, 128),
            integers((table_sizes(count, plane_cap)[2], 128)),
            shape(count, 128),
            *[shape(8, 128)] * (count - 3),
        ],
        [
            pltpu.VMEM((1, SLOTS), jnp.int32),
            pltpu.VMEM((1, SLOTS), jnp.int32),
            pltpu.VMEM((FACES, 1, SLOTS), jnp.int32),
            pltpu.VMEM((bx, by, bz), F32),
            pltpu.VMEM((bx, by, bz), F32),
            pltpu.SemaphoreType.DMA((2 * bx + 3,)),
        ],
        mib=56,
    )(
        tile_source.reshape(1, SLOTS),
        tile_block.reshape(1, SLOTS),
        jnp.transpose(tile_neighbour, (0, 1, 4, 2, 3)).reshape(FACES, 1, SLOTS),
        enthalpy,
        conductivity,
    )
    sides = lax.all_to_all(sides, ("gy", "gz"), split_axis=0, concat_axis=0, tiled=True)

    def pass_on(value, shift):
        return lax.ppermute(value, "gx", [(i, (i + shift) % count) for i in range(count)])

    def exchange(values):
        order = sorted(range(1, count), key=lambda shift: (-min(shift, count - shift), shift))
        got = {shift: pass_on(values[shift - 1], shift) for shift in order}
        return [got[shift] for shift in range(1, count)]

    farther = [pass_on(value, shift) for shift, value in enumerate(farther, 2)]

    phase_field = phase.reshape(SLOTS, TE, PLANE)
    solute_field = solute.reshape(SLOTS, TE, PLANE)
    own_shapes = [shape(2 * SLOTS, TE, 128), shape(2 * SLOTS * 8, 128)]
    send_shapes = [shape(plane_cap * REC, 128)] * others
    rows_scratch = pltpu.VMEM((4, SLOTS * TE, 128), F32)
    packed = call(
        first_pack_kernel,
        [SMEM] + [VMEM] * 4,
        [*own_shapes, shape(count, 128), *send_shapes],
        [rows_scratch],
    )(table, asked, phase_field, solute_field, picks)
    own, asked, packed = packed[:2], packed[2], packed[3:]

    layer = shape(3 * by + 8, bz)
    down, up = call(
        functools.partial(layers_kernel, sizes), [VMEM] * 4 + [ANY] * len(farther), [layer, layer]
    )(enthalpy, conductivity, sides, asked, *farther)
    from_low, from_high = pass_on(up, 1), pass_on(down, others)
    row = 3 * by + 4
    request = [asked[0], from_low[row], *[value[0] for value in farther], from_high[row]]
    request = jnp.stack([value[:block_cap] for value in request]).astype(jnp.int32)
    _, deep = block_layout(block_cap)
    brick = shape(bx, by, bz)
    got = exchange(packed)
    heated, *found = call(
        functools.partial(heat_kernel, block_cap, sizes),
        [SMEM] + [VMEM] * 5,
        [brick] + [shape(deep * CB, 128)] * count,
        [pltpu.VMEM((bx, by // CB, CB, bz), F32)],
    )(request, enthalpy, conductivity, sides, from_low, from_high)
    found[1:] = exchange(found[1:])
    (heat_out,) = call(write_out_kernel, [ANY], [brick], [pltpu.SemaphoreType.DMA], [ANY])(heated)

    field = shape(SLOTS, TE, PLANE)
    step_scratch = [
        pltpu.VMEM((records + 2 * SLOTS, TE, 128), F32),
        pltpu.VMEM(((records + 2 * SLOTS) * 8, 128), F32),
        pltpu.VMEM((SLOTS, TE, 128), F32),
        pltpu.VMEM((SLOTS, 8, 128), F32),
        rows_scratch,
    ]
    def inner(phase_field, solute_field, *heat):
        return call(
            functools.partial(inner_kernel, bool(heat)), [VMEM] * (3 + len(heat)), [field, field]
        )(phase_field, solute_field, stencil, *heat)

    inner_fields = inner(phase_field, solute_field)
    phase_field, solute_field, heat, *rest = call(
        functools.partial(first_step_kernel, block_cap),
        [SMEM] + [VMEM] * (8 + count + others),
        [field, field, shape(2, SLOTS * TE, 128), *own_shapes, *send_shapes],
        step_scratch
        + [
            pltpu.VMEM((count, deep * CB, 128), F32),
            pltpu.VMEM((SLOTS * CB, CB, 128), F32),
        ],
    )(table, phase_field, *inner_fields, *own, picks, places, spreads, *found, *got)
    own, send = rest[:2], rest[2:]
    for _ in range(PHASE_STEPS - 2):
        got = exchange(send)
        inner_fields = inner(phase_field, solute_field, heat)
        phase_field, solute_field, *rest = call(
            middle_step_kernel,
            [SMEM] + [VMEM] * (6 + others),
            [field, field, *own_shapes, *send_shapes],
            step_scratch,
        )(table, *inner_fields, *own, picks, places, *got)
        own, send = rest[:2], rest[2:]
    got = exchange(send)
    inner_fields = inner(phase_field, solute_field, heat)
    phase_field, solute_field = call(
        last_step_kernel,
        [SMEM] + [VMEM] * (5 + others),
        [field, field],
        step_scratch[:4] + [pltpu.VMEM(field.shape, F32)] * 2 + [pltpu.SemaphoreType.DMA((8,))],
        [ANY] * 2,
    )(table, *inner_fields, *own, places, *got)
    return heat_out, phase_field.reshape(phase.shape), solute_field.reshape(solute.shape)


def solution(mesh):
    grid = P("gx", "gy", "gz")
    tiles = P("gx", "gy", "gz", None, None, None)
    return jax.shard_map(
        local,
        mesh=mesh,
        in_specs=(
            grid,
            grid,
            tiles,
            tiles,
            P("gx", "gy", "gz", None, None),
            P("gx", "gy", "gz", None),
            P("gx", "gy", "gz", None, None),
        ),
        out_specs=(grid, tiles, tiles),
        check_vma=False,
    )
```

```python
import functools

import jax
import jax.numpy as jnp
import numpy as np
from jax import lax
from jax.experimental import pallas as pl
from jax.experimental.pallas import tpu as pltpu
from jax.sharding import PartitionSpec as P

CB = 8
TE = 16
PLANE = TE * TE
SLOTS = 16
FACES = 6
PHASE_STEPS = 4
REC = 24

RATE = 0.16
ORDER_SPEED = 0.1
SOLUTE_RATE = 0.15
COUPLING = 0.5
REJECTION = 0.5

F32 = jnp.float32
BF16 = jnp.bfloat16
VMEM = pl.BlockSpec(memory_space=pltpu.VMEM)
SMEM = pl.BlockSpec(memory_space=pltpu.SMEM)
ANY = pl.BlockSpec(memory_space=pl.ANY)


def plane_lane(face):
    j = np.arange(TE)
    return [j, PLANE - TE + j, j * TE, j * TE + TE - 1][face - 2]


def constant_tables():
    pick = np.zeros((2, PLANE, 256), np.float32)
    place = np.zeros((2, 128, PLANE), np.float32)
    for field in range(2):
        for face in range(2, 6):
            at = field * 64 + (face - 2) * TE + np.arange(TE)
            pick[field, plane_lane(face ^ 1), at] = 1.0
            pick[field, plane_lane(face), 128 + at] = 1.0
            place[field, at, plane_lane(face)] = 1.0
    y, z = np.divmod(np.arange(PLANE), TE)
    dy, dz = np.abs(y[:, None] - y[None, :]), np.abs(z[:, None] - z[None, :])
    stencil = ((dy + dz) == 1).astype(np.float32)
    lane = np.arange(128)
    spread = (lane[:, None] % CB == z[None, :] // 2).astype(np.float32)
    return pick, place, stencil, spread


def tables():
    pick, place, stencil, spread = constant_tables()
    place = np.concatenate([place[0], place[1]], axis=1)
    return (
        jnp.asarray(np.concatenate([pick[0], pick[1]], axis=0), BF16),
        jnp.asarray(stencil, BF16),
        jnp.asarray(np.concatenate([place, place], axis=0), BF16),
        jnp.asarray(np.concatenate([spread, spread], axis=0), BF16),
    )


def halves(value):
    high = value.astype(BF16)
    return high, (value - high.astype(F32)).astype(BF16)


def dot(a, b):
    return jnp.dot(a, b, preferred_element_type=F32)


def temperature(h):
    return jnp.minimum(h, 0.0) + jnp.maximum(h - 1.0, 0.0)


def iota(shape, dim):
    return lax.broadcasted_iota(jnp.int32, shape, dim)


def to_lanes(column):
    bx, by, _ = column.shape
    diagonal = iota((bx, by, 128), 1) == iota((bx, by, 128), 2)
    return jnp.sum(jnp.where(diagonal, column, 0.0), axis=1)


def to_column(line, by):
    bx = line.shape[0]
    diagonal = iota((bx, by, 128), 1) == iota((bx, by, 128), 2)
    return jnp.sum(jnp.where(diagonal, line[:, None, :], 0.0), axis=2, keepdims=True)


def conduct(h, k, xlo, xhi, ylo, yhi, zlo, zhi):
    bx, by, bz = h.shape
    t = temperature(h)
    row, lane = iota((bx, by, bz), 1), iota((bx, by, bz), 2)
    if bx > 1:
        total = jnp.concatenate([xlo, t[:-1]], axis=0) + jnp.concatenate([t[1:], xhi], axis=0)
    else:
        total = xlo + xhi
    total += jnp.where(row == 0, ylo[:, None, :], pltpu.roll(t, 1, 1))
    total += jnp.where(row == by - 1, yhi[:, None, :], pltpu.roll(t, by - 1, 1))
    total += jnp.where(lane == 0, to_column(zlo, by), pltpu.roll(t, 1, 2))
    total += jnp.where(lane == bz - 1, to_column(zhi, by), pltpu.roll(t, bz - 1, 2))
    return h + RATE * k * (total - 6.0 * t)


def sublanes(value, y):
    return jnp.concatenate([value[x, y : y + 1, :] for x in range(value.shape[0])], axis=0)


def side_blocks(h, k):
    by, bz = h.shape[1:]
    return [
        (sublanes(h, 0), sublanes(h, 1), sublanes(k, 0)),
        (sublanes(h, by - 1), sublanes(h, by - 2), sublanes(k, by - 1)),
        (to_lanes(h[:, :, 0:1]), to_lanes(h[:, :, 1:2]), to_lanes(k[:, :, 0:1])),
        (to_lanes(h[:, :, bz - 1 : bz]), to_lanes(h[:, :, bz - 2 : bz - 1]), to_lanes(k[:, :, bz - 1 : bz])),
    ]


def column_of(row):
    square = (row.shape[1], row.shape[1])
    return jnp.sum(jnp.where(iota(square, 0) == iota(square, 1), row, 0.0), axis=1, keepdims=True)


def table_sizes(count, plane_cap):
    records = (count - 1) * plane_cap
    faces = min(FACES, 128 // records)
    return records, faces, 1 + -(-FACES // faces)


def swap_order(count):
    return sorted(range(1, count), key=lambda s: (-s.bit_length(), s))


def place_of(table, slot):
    return table[0, FACES * SLOTS + slot], table[0, FACES * SLOTS + SLOTS + slot]


def write_tables(plane_cap, source, block, neighbour, asked, farther, table):
    here = lax.axis_index("gx")
    me = here.astype(F32)
    count = lax.axis_size("gx")
    records, faces, _ = table_sizes(count, plane_cap)
    cap = float(plane_cap)

    def wrapped(shift):
        return jnp.where(shift < 0.0, shift + float(count), shift)

    square = (SLOTS, SLOTS)
    before = iota(square, 0) < iota(square, 1)
    slot = iota((1, SLOTS), 1).astype(F32)
    source_row, block_column = source[...].astype(F32), column_of(block[...].astype(F32))
    source_column = column_of(source_row)
    rank = jnp.sum(
        jnp.where((source_column == source_row) & before, 1.0, 0.0), axis=0, keepdims=True
    )
    rank_column = column_of(rank)
    lane = iota((SLOTS, 128), 1).astype(F32)
    for shift in range(count):
        hit = (wrapped(source_column - me) == float(shift)) & (rank_column == lane)
        row = jnp.sum(jnp.where(hit, block_column, 0.0), axis=0, keepdims=True)
        asked[shift : shift + 1, :] = row
        if 2 <= shift < count - 1:
            farther[shift - 2][...] = jnp.broadcast_to(row, (8, 128))
    at = FACES * SLOTS
    table[0:1, at : at + SLOTS] = wrapped(me - source_row).astype(jnp.int32)
    table[0:1, at + SLOTS : at + 2 * SLOTS] = rank.astype(jnp.int32)
    slot_column = iota((SLOTS, records), 0).astype(F32)
    for face in range(FACES):
        number = neighbour[face]
        owner_row, number_row = (number >> 4).astype(F32), number.astype(F32)
        owner_column, number_column = column_of(owner_row), column_of(number_row)
        other_row = (number_row >= 0.0) & (owner_row != me)
        alike = (owner_column == owner_row) & (owner_column >= 0.0) & (owner_column != me)
        receive_rank = jnp.sum(
            jnp.where(alike & (number_column < number_row), 1.0, 0.0), axis=0, keepdims=True
        )
        send_rank = jnp.sum(jnp.where(alike & before, 1.0, 0.0), axis=0, keepdims=True)
        swap = jnp.where(number < 0, 0, (number >> 4) ^ here)
        position = jnp.zeros(swap.shape, F32)
        for at, other in enumerate(swap_order(count)):
            position = jnp.where(swap == other, float(at), position)
        mine = records + (number_row - owner_row * SLOTS)
        there = position * cap + receive_rank
        receive = jnp.where(owner_row == me, mine, there)
        receive = jnp.where(number_row < 0.0, records + SLOTS + slot, receive)
        table[0:1, face * SLOTS : face * SLOTS + SLOTS] = receive.astype(jnp.int32)
        key = jnp.where(other_row, position * cap + send_rank, -1.0)
        hit = iota((SLOTS, records), 1).astype(F32) == column_of(key)
        tile = jnp.sum(jnp.where(hit, slot_column, 0.0), axis=0, keepdims=True)
        row, at = 1 + (face ^ 1) // faces, (face ^ 1) % faces * records
        table[row : row + 1, at : at + records] = tile.astype(jnp.int32)


def sides_kernel(
    sizes, plane_cap, source_far, block_far, neighbour_far, h_far, k_far, send, table, *rest
):
    asked, *farther, source, block, neighbour, h, k, sems = rest
    ny, nz = sizes
    my_y, my_z = lax.axis_index("gy"), lax.axis_index("gz")
    bx = h.shape[0]
    small = [(source_far, source), (block_far, block), (neighbour_far, neighbour)]
    copies = [pltpu.make_async_copy(*pair, sems.at[2 * bx + n]) for n, pair in enumerate(small)]
    large = []
    for x in range(bx):
        large.append(pltpu.make_async_copy(h_far.at[x], h.at[x], sems.at[x]))
        large.append(pltpu.make_async_copy(k_far.at[x], k.at[x], sems.at[bx + x]))
    for copy in copies + large:
        copy.start()
    for copy in copies:
        copy.wait()
    write_tables(plane_cap, source, block, neighbour, asked, farther, table)
    for copy in large:
        copy.wait()
    blocks = side_blocks(h[...], k[...])
    for y in range(ny):
        for z in range(nz):
            for part in range(3):
                ylo, yhi, zlo, zhi = [block[part] for block in blocks]
                chosen = jnp.where(
                    my_y == y, jnp.where(z < my_z, zlo, zhi), jnp.where(y < my_y, ylo, yhi)
                )
                send[y * nz + z, part * bx : part * bx + bx, :] = chosen


def side_reader(sizes, got, bx):
    ny, nz = sizes
    my_y, my_z = lax.axis_index("gy"), lax.axis_index("gz")

    def read(dy, dz, part=0):
        y, z = my_y + dy, my_z + dz
        inside = (y >= 0) & (y < ny) & (z >= 0) & (z < nz)
        at = jnp.where(inside, y * nz + z, 0)
        return jnp.where(inside, got[at, part * bx : part * bx + bx, :], 0.0)

    return read


def layers_kernel(sizes, h, k, got, asked, *rest):
    down, up = rest[-2:]
    bx, by, bz = h.shape
    read = side_reader(sizes, got, bx)
    around = [read(-1, 0), read(1, 0), read(0, -1), read(0, 1)]
    last = asked.shape[0] - 1
    for out, near, far, ask in ((down, 0, 1, last), (up, bx - 1, bx - 2, 1)):
        out[0:by, :] = h[near]
        out[by : 2 * by, :] = h[far]
        out[2 * by : 3 * by, :] = k[near]
        for number, side in enumerate(around):
            out[3 * by + number : 3 * by + number + 1, :] = side[near : near + 1, :]
        out[3 * by + 4 : 3 * by + 8, :] = jnp.broadcast_to(asked[ask : ask + 1, :], (4, bz))


def block_layout(cap):
    parts = 128 // CB // cap
    return parts, CB // parts


def flat_step(h, k, inner, outer, first, last, before, after, length):
    bx, lanes = h.shape
    t = temperature(h)
    row, lane = iota(h.shape, 0), iota(h.shape, 1)
    total = temperature(inner) + temperature(outer)
    total += jnp.where(row == 0, temperature(first), pltpu.roll(t, 1, 0))
    total += jnp.where(row == bx - 1, temperature(last), pltpu.roll(t, bx - 1, 0))
    total += jnp.where(lane == 0, temperature(before), pltpu.roll(t, 1, 1))
    total += jnp.where(lane == length - 1, temperature(after), pltpu.roll(t, lanes - 1, 1))
    return h + RATE * k * (total - 6.0 * t)


def heat_kernel(cap, sizes, request, h, k, got, low, high, out, found, *rest):
    *send, held = rest
    count = lax.axis_size("gx")
    bx, by, bz = h.shape
    h0, k0 = h[...], k[...]
    read = side_reader(sizes, got, bx)
    me = lax.axis_index("gx")
    layers, lines = [], []
    for beside, inside in ((low, me > 0), (high, me < count - 1)):
        beside = jnp.where(inside, beside[...], 0.0)
        layers.append([beside[part * by : part * by + by, :][None] for part in range(3)])
        lines.append([beside[3 * by + n : 3 * by + n + 1, :] for n in range(4)])
    y_sides = [[read(d, 0, part) for part in range(3)] for d in (-1, 1)]
    z_sides = [[read(0, d, part) for part in range(3)] for d in (-1, 1)]
    corner = [[read(dy, dz) for dz in (-1, 1)] for dy in (-1, 1)]
    to_first = [[pltpu.roll(c[0], 1, 1), c[1]] for c in corner]
    y_inner = [sublanes(h0, 0), sublanes(h0, by - 1)]
    z_inner = [to_lanes(h0[:, :, 0:1]), to_lanes(h0[:, :, bz - 1 : bz])]

    sides = [temperature(layers[0][0]), temperature(layers[1][0])]
    sides += [temperature(side[0]) for side in y_sides + z_sides]
    h1 = conduct(h0, k0, *sides)
    next_sides = []
    for side in range(2):
        near, far, near_k = layers[side]
        across = [temperature(far), temperature(h0[0:1])]
        if side:
            across = [temperature(h0[bx - 1 : bx]), temperature(far)]
        next_sides.append(conduct(near, near_k, *across, *[temperature(line) for line in lines[side]]))
    for side in range(2):
        near, far, near_k = y_sides[side]
        ends = [to_first[side][0], pltpu.roll(to_first[side][1], bz - 1, 1)]
        next_sides.append(
            flat_step(near, near_k, y_inner[side], far, lines[0][side], lines[1][side], *ends, bz)
        )
    for side in range(2):
        near, far, near_k = z_sides[side]
        ends = [to_first[0][side], pltpu.roll(to_first[1][side], by - 1, 1)]
        next_sides.append(
            flat_step(near, near_k, z_inner[side], far, lines[0][2 + side], lines[1][2 + side], *ends, by)
        )
    h2 = conduct(h1, k0, *[temperature(side) for side in next_sides])
    out[...] = h2

    held[...] = temperature(h2).reshape(bx, by // CB, CB, bz)
    parts, deep = block_layout(cap)
    nby, nbz = by // CB, bz // CB
    group = iota((deep, CB, bz), 2) // CB
    for shift in range(count):
        total = jnp.zeros((deep, CB, bz), F32)
        for rank in range(cap):
            block = request[(count - shift) % count, rank]
            a, b, c = block // (nby * nbz), (block // nbz) % nby, block % nbz
            for part in range(parts):
                at = rank * parts + part
                patch = held[pl.ds(a * CB + part * deep, deep), b]
                moved = pltpu.roll(patch, (CB * at - CB * c + bz) % bz, 2)
                total = jnp.where(group == at, moved, total)
        total = total.reshape(deep * CB, bz)
        (send[shift - 1] if shift else found)[...] = total


def write_records(phase, solute, picks, own, own_edges, rows):
    flat = [f.reshape(SLOTS * TE, PLANE) for f in (phase, solute)]
    high, low = halves(jnp.concatenate(flat, axis=1))
    planes = dot(high, picks) + dot(low, picks)
    own[0:SLOTS] = planes[:, 0:128].reshape(SLOTS, TE, 128)
    own[SLOTS : 2 * SLOTS] = planes[:, 128:256].reshape(SLOTS, TE, 128)
    for part in range(4):
        rows[part] = flat[part // 2][:, part % 2 * 128 : part % 2 * 128 + 128]
    for part in range(4):
        low_face = rows[part, pl.ds(0, SLOTS, TE), :]
        high_face = rows[part, pl.ds(TE - 1, SLOTS, TE), :]
        for at, value in ((0, high_face), (4, low_face)):
            own_edges[pl.ds(at + part, SLOTS, 8), :] = value
            own_edges[pl.ds(8 * SLOTS + 4 - at + part, SLOTS, 8), :] = value


def merge_record(planes, edges, number):
    side = (iota((TE, 128), 1) % 64) // TE
    out = planes[number(2)]
    for face in range(3, 6):
        out = jnp.where(side == face - 2, planes[number(face)], out)
    first, second = [edges[pl.ds(pl.multiple_of(number(face) * 8, 8), 8), :] for face in range(2)]
    return out, jnp.where(iota((8, 128), 0) < 4, first, second)


def pack(own, own_edges, table, send):
    cap = send[0].shape[0] // REC
    records, faces, _ = table_sizes(len(send) + 1, cap)
    for record in range(records):
        out, row = send[record // cap], record % cap * REC
        planes, edge = merge_record(
            own, own_edges, lambda face: table[1 + face // faces, face % faces * records + record]
        )
        out[row : row + TE, :] = planes
        out[row + TE : row + REC, :] = edge


def first_pack_kernel(table, asked, phase, solute, picks, own, own_edges, asked_out, *rest):
    *send, rows = rest
    write_records(phase[...], solute[...], picks[...], own, own_edges, rows)
    pack(own, own_edges, table, send)
    asked_out[...] = asked[...]


def take_heat(cap, table, found, spreads, blocks, held, heat):
    parts, deep = block_layout(cap)
    for number, value in enumerate(found):
        blocks[number] = value[...]
    group = iota((CB, 128), 1) // CB
    for slot in range(SLOTS):
        back, rank = place_of(table, slot)
        for x in range(CB):
            row = (x % deep) * CB
            patch = blocks[back, row : row + CB, :]
            held[slot * CB + x] = jnp.where(group == rank * parts + x // deep, patch, 0.0)
    rows = held[...].reshape(SLOTS * CB * CB, 128)
    wide = dot(jnp.concatenate(halves(rows), axis=1), spreads)
    wide = wide.reshape(SLOTS * CB, CB, PLANE)
    keep = iota(wide.shape, 1) == iota(wide.shape, 2) // TE // 2
    coarse = jnp.sum(jnp.where(keep, wide, 0.0), axis=1)
    for half in range(2):
        for odd in range(2):
            heat[half, pl.ds(odd, SLOTS * CB, 2), :] = coarse[:, half * 128 : half * 128 + 128]


def inner_step(phase, solute, heat, stencil):
    row = iota((SLOTS, TE, PLANE), 1)
    lap = []
    for field in (phase, solute):
        high, low = halves(field.reshape(SLOTS * TE, PLANE))
        total = (dot(high, stencil) + dot(low, stencil)).reshape(SLOTS, TE, PLANE) - 6.0 * field
        total += jnp.where(row == 0, 0.0, pltpu.roll(field, 1, 1))
        total += jnp.where(row == TE - 1, 0.0, pltpu.roll(field, TE - 1, 1))
        lap.append(total)
    squared = 1.0 - phase * phase
    drive = solute if heat is None else heat + solute
    change = ORDER_SPEED * (
        lap[0] + phase - phase * phase * phase - COUPLING * drive * squared * squared
    )
    return phase + change, solute + SOLUTE_RATE * lap[1] + REJECTION * change


def wide_heat(heat):
    return jnp.concatenate([heat[0], heat[1]], axis=1).reshape(SLOTS, TE, PLANE)


def gather_ghosts(table, got, own, own_edges, planes, edges, ghosts, ghost_edges):
    records = planes.shape[0] - 2 * SLOTS
    cap = records // len(got)
    for record in range(records):
        value, row = got[record // cap], record % cap * REC
        planes[record] = value[row : row + TE, :]
        edges[record * 8 : record * 8 + 8, :] = value[row + TE : row + REC, :]
    planes[records:] = own[...]
    edges[records * 8 :, :] = own_edges[...]
    for slot in range(SLOTS):
        out, edge = merge_record(planes, edges, lambda face: table[0, face * SLOTS + slot])
        ghosts[slot] = out
        ghost_edges[slot] = edge


def ghost_shares(ghosts, ghost_edges, places):
    beside = jnp.concatenate(halves(ghosts[...].reshape(SLOTS * TE, 128)), axis=1)
    beside = dot(beside, places)
    rows = iota((SLOTS, TE, PLANE), 1)
    shares = []
    for number in range(2):
        share = beside[:, number * PLANE : number * PLANE + PLANE].reshape(SLOTS, TE, PLANE)
        for face, at_row in ((0, 0), (1, TE - 1)):
            at = face * 4 + number * 2
            side = [ghost_edges[:, row : row + 1, :] for row in (at, at + 1)]
            side = jnp.concatenate(side, axis=2)
            share += jnp.where(rows == at_row, side, 0.0)
        shares.append(share)
    return shares


def add_shares(phase, solute, shares, heat_share=None):
    change = ORDER_SPEED * shares[0]
    if heat_share is not None:
        change += heat_share
    return phase + change, solute + SOLUTE_RATE * shares[1] + REJECTION * change


def inner_kernel(has_heat, phase, solute, stencil, *rest):
    phase_out, solute_out = rest[-2:]
    heat = wide_heat(rest[0]) if has_heat else None
    phase_out[...], solute_out[...] = inner_step(phase[...], solute[...], heat, stencil[...])


def first_step_kernel(cap, table, old_phase, phase, solute, own, own_edges, picks, places, spreads, *rest):
    others = lax.axis_size("gx") - 1
    found, got, rest = rest[: others + 1], rest[others + 1 : 2 * others + 1], rest[2 * others + 1 :]
    phase_out, solute_out, heat_out, own_out, edges_out, *rest = rest
    send, (*records, ghosts, ghost_edges, rows, blocks, held) = rest[:others], rest[others:]
    take_heat(cap, table, found, spreads[...], blocks, held, heat_out)
    gather_ghosts(table, got, own, own_edges, *records, ghosts, ghost_edges)
    squared = 1.0 - old_phase[...] * old_phase[...]
    heat_share = (-ORDER_SPEED * COUPLING) * wide_heat(heat_out) * squared * squared
    new_phase, new_solute = add_shares(
        phase[...], solute[...], ghost_shares(ghosts, ghost_edges, places[...]), heat_share
    )
    phase_out[...] = new_phase
    solute_out[...] = new_solute
    write_records(new_phase, new_solute, picks[...], own_out, edges_out, rows)
    pack(own_out, edges_out, table, send)


def write_out_kernel(value, out, sem):
    copy = pltpu.make_async_copy(value, out, sem)
    copy.start()
    copy.wait()


def middle_step_kernel(table, phase, solute, own, own_edges, picks, places, *rest):
    others = lax.axis_size("gx") - 1
    got, (phase_out, solute_out, own_out, edges_out, *rest) = rest[:others], rest[others:]
    send, (*records, ghosts, ghost_edges, rows) = rest[:others], rest[others:]
    gather_ghosts(table, got, own, own_edges, *records, ghosts, ghost_edges)
    new_phase, new_solute = add_shares(phase[...], solute[...], ghost_shares(ghosts, ghost_edges, places[...]))
    phase_out[...] = new_phase
    solute_out[...] = new_solute
    write_records(new_phase, new_solute, picks[...], own_out, edges_out, rows)
    pack(own_out, edges_out, table, send)


def last_step_kernel(table, phase, solute, own, own_edges, places, *rest):
    others = lax.axis_size("gx") - 1
    got, (phase_out, solute_out, *records, ghosts, ghost_edges, _) = rest[:others], rest[others:]
    gather_ghosts(table, got, own, own_edges, *records, ghosts, ghost_edges)
    phase_out[...], solute_out[...] = add_shares(
        phase[...], solute[...], ghost_shares(ghosts, ghost_edges, places[...])
    )


def call(kernel, in_specs, out_shapes, scratch=(), out_specs=None, mib=16):
    return pl.pallas_call(
        kernel,
        out_shape=out_shapes,
        in_specs=in_specs,
        out_specs=out_specs or jax.tree.map(lambda _: VMEM, out_shapes),
        scratch_shapes=list(scratch),
        compiler_params=pltpu.CompilerParams(vmem_limit_bytes=mib * 1024 * 1024),
    )


def shape(*dims):
    return jax.ShapeDtypeStruct(dims, F32)


def local(enthalpy, conductivity, phase, solute, tile_source, tile_block, tile_neighbour):
    count = lax.axis_size("gx")
    sizes = (lax.axis_size("gy"), lax.axis_size("gz"))
    plane_cap = -(-SLOTS // (count - 1))
    block_cap = 2 * SLOTS // count
    others = count - 1
    records = others * plane_cap
    bx, by, bz = enthalpy.shape
    picks, stencil, places, spreads = tables()

    integers = functools.partial(jax.ShapeDtypeStruct, dtype=jnp.int32)
    sides, table, asked, *farther = call(
        functools.partial(sides_kernel, sizes, plane_cap),
        [ANY] * 5,
        [
            shape(sizes[0] * sizes[1], 3 * bx, 128),
            integers((table_sizes(count, plane_cap)[2], 128)),
            shape(count, 128),
            *[shape(8, 128)] * (count - 3),
        ],
        [
            pltpu.VMEM((1, SLOTS), jnp.int32),
            pltpu.VMEM((1, SLOTS), jnp.int32),
            pltpu.VMEM((FACES, 1, SLOTS), jnp.int32),
            pltpu.VMEM((bx, by, bz), F32),
            pltpu.VMEM((bx, by, bz), F32),
            pltpu.SemaphoreType.DMA((2 * bx + 3,)),
        ],
        mib=56,
    )(
        tile_source.reshape(1, SLOTS),
        tile_block.reshape(1, SLOTS),
        jnp.transpose(tile_neighbour, (0, 1, 4, 2, 3)).reshape(FACES, 1, SLOTS),
        enthalpy,
        conductivity,
    )
    sides = lax.all_to_all(sides, ("gy", "gz"), split_axis=0, concat_axis=0, tiled=True)

    def pass_on(value, shift):
        return lax.ppermute(value, "gx", [(i, (i + shift) % count) for i in range(count)])

    def exchange(values):
        return [pass_on(value, shift) for shift, value in enumerate(values, 1)]

    def swap_all(values):
        return [
            lax.ppermute(value, "gx", [(i, i ^ swap) for i in range(count)])
            for swap, value in zip(swap_order(count), values)
        ]

    farther = [pass_on(value, shift) for shift, value in enumerate(farther, 2)]

    phase_field = phase.reshape(SLOTS, TE, PLANE)
    solute_field = solute.reshape(SLOTS, TE, PLANE)
    own_shapes = [shape(2 * SLOTS, TE, 128), shape(2 * SLOTS * 8, 128)]
    send_shapes = [shape(plane_cap * REC, 128)] * others
    rows_scratch = pltpu.VMEM((4, SLOTS * TE, 128), F32)
    packed = call(
        first_pack_kernel,
        [SMEM] + [VMEM] * 4,
        [*own_shapes, shape(count, 128), *send_shapes],
        [rows_scratch],
    )(table, asked, phase_field, solute_field, picks)
    own, asked, packed = packed[:2], packed[2], packed[3:]

    layer = shape(3 * by + 8, bz)
    down, up = call(
        functools.partial(layers_kernel, sizes), [VMEM] * 4 + [ANY] * len(farther), [layer, layer]
    )(enthalpy, conductivity, sides, asked, *farther)
    from_low, from_high = pass_on(up, 1), pass_on(down, others)
    row = 3 * by + 4
    request = [asked[0], from_low[row], *[value[0] for value in farther], from_high[row]]
    request = jnp.stack([value[:block_cap] for value in request]).astype(jnp.int32)
    _, deep = block_layout(block_cap)
    brick = shape(bx, by, bz)
    got = swap_all(packed)
    heated, *found = call(
        functools.partial(heat_kernel, block_cap, sizes),
        [SMEM] + [VMEM] * 5,
        [brick] + [shape(deep * CB, 128)] * count,
        [pltpu.VMEM((bx, by // CB, CB, bz), F32)],
    )(request, enthalpy, conductivity, sides, from_low, from_high)
    found[1:] = exchange(found[1:])
    (heat_out,) = call(write_out_kernel, [ANY], [brick], [pltpu.SemaphoreType.DMA], [ANY])(heated)

    field = shape(SLOTS, TE, PLANE)
    step_scratch = [
        pltpu.VMEM((records + 2 * SLOTS, TE, 128), F32),
        pltpu.VMEM(((records + 2 * SLOTS) * 8, 128), F32),
        pltpu.VMEM((SLOTS, TE, 128), F32),
        pltpu.VMEM((SLOTS, 8, 128), F32),
        rows_scratch,
    ]
    def inner(phase_field, solute_field, *heat):
        return call(
            functools.partial(inner_kernel, bool(heat)), [VMEM] * (3 + len(heat)), [field, field]
        )(phase_field, solute_field, stencil, *heat)

    inner_fields = inner(phase_field, solute_field)
    phase_field, solute_field, heat, *rest = call(
        functools.partial(first_step_kernel, block_cap),
        [SMEM] + [VMEM] * (8 + count + others),
        [field, field, shape(2, SLOTS * TE, 128), *own_shapes, *send_shapes],
        step_scratch
        + [
            pltpu.VMEM((count, deep * CB, 128), F32),
            pltpu.VMEM((SLOTS * CB, CB, 128), F32),
        ],
    )(table, phase_field, *inner_fields, *own, picks, places, spreads, *found, *got)
    own, send = rest[:2], rest[2:]
    for _ in range(PHASE_STEPS - 2):
        got = swap_all(send)
        inner_fields = inner(phase_field, solute_field, heat)
        phase_field, solute_field, *rest = call(
            middle_step_kernel,
            [SMEM] + [VMEM] * (6 + others),
            [field, field, *own_shapes, *send_shapes],
            step_scratch,
        )(table, *inner_fields, *own, picks, places, *got)
        own, send = rest[:2], rest[2:]
    got = swap_all(send)
    inner_fields = inner(phase_field, solute_field, heat)
    phase_field, solute_field = call(
        last_step_kernel, [SMEM] + [VMEM] * (5 + others), [field, field], step_scratch
    )(table, *inner_fields, *own, places, *got)
    return heat_out, phase_field.reshape(phase.shape), solute_field.reshape(solute.shape)


def solution(mesh):
    grid = P("gx", "gy", "gz")
    tiles = P("gx", "gy", "gz", None, None, None)
    return jax.shard_map(
        local,
        mesh=mesh,
        in_specs=(
            grid,
            grid,
            tiles,
            tiles,
            P("gx", "gy", "gz", None, None),
            P("gx", "gy", "gz", None),
            P("gx", "gy", "gz", None, None),
        ),
        out_specs=(grid, tiles, tiles),
        check_vma=False,
    )
```

```python
import functools

import jax
import jax.numpy as jnp
import numpy as np
from jax import lax
from jax.experimental import pallas as pl
from jax.experimental.pallas import tpu as pltpu
from jax.sharding import PartitionSpec as P

CB = 8
TE = 16
PLANE = TE * TE
SLOTS = 16
FACES = 6
PHASE_STEPS = 4
REC = 24

RATE = 0.16
ORDER_SPEED = 0.1
SOLUTE_RATE = 0.15
COUPLING = 0.5
REJECTION = 0.5

F32 = jnp.float32
BF16 = jnp.bfloat16
VMEM = pl.BlockSpec(memory_space=pltpu.VMEM)
SMEM = pl.BlockSpec(memory_space=pltpu.SMEM)
ANY = pl.BlockSpec(memory_space=pl.ANY)


def plane_lane(face):
    j = np.arange(TE)
    return [j, PLANE - TE + j, j * TE, j * TE + TE - 1][face - 2]


def constant_tables():
    pick = np.zeros((2, PLANE, 256), np.float32)
    place = np.zeros((2, 128, PLANE), np.float32)
    for field in range(2):
        for face in range(2, 6):
            at = field * 64 + (face - 2) * TE + np.arange(TE)
            pick[field, plane_lane(face ^ 1), at] = 1.0
            pick[field, plane_lane(face), 128 + at] = 1.0
            place[field, at, plane_lane(face)] = 1.0
    y, z = np.divmod(np.arange(PLANE), TE)
    dy, dz = np.abs(y[:, None] - y[None, :]), np.abs(z[:, None] - z[None, :])
    stencil = ((dy + dz) == 1).astype(np.float32)
    lane = np.arange(128)
    spread = (lane[:, None] % CB == z[None, :] // 2).astype(np.float32)
    return pick, place, stencil, spread


def tables():
    pick, place, stencil, spread = constant_tables()
    place = np.concatenate([place[0], place[1]], axis=1)
    return (
        jnp.asarray(np.concatenate([pick[0], pick[1]], axis=0), BF16),
        jnp.asarray(stencil, BF16),
        jnp.asarray(np.concatenate([place, place], axis=0), BF16),
        jnp.asarray(np.concatenate([spread, spread], axis=0), BF16),
    )


def halves(value):
    high = value.astype(BF16)
    return high, (value - high.astype(F32)).astype(BF16)


def dot(a, b):
    return jnp.dot(a, b, preferred_element_type=F32)


def temperature(h):
    return jnp.minimum(h, 0.0) + jnp.maximum(h - 1.0, 0.0)


def iota(shape, dim):
    return lax.broadcasted_iota(jnp.int32, shape, dim)


def to_lanes(column):
    bx, by, _ = column.shape
    diagonal = iota((bx, by, 128), 1) == iota((bx, by, 128), 2)
    return jnp.sum(jnp.where(diagonal, column, 0.0), axis=1)


def to_column(line, by):
    bx = line.shape[0]
    diagonal = iota((bx, by, 128), 1) == iota((bx, by, 128), 2)
    return jnp.sum(jnp.where(diagonal, line[:, None, :], 0.0), axis=2, keepdims=True)


def conduct(h, k, xlo, xhi, ylo, yhi, zlo, zhi):
    bx, by, bz = h.shape
    t = temperature(h)
    row, lane = iota((bx, by, bz), 1), iota((bx, by, bz), 2)
    if bx > 1:
        total = jnp.concatenate([xlo, t[:-1]], axis=0) + jnp.concatenate([t[1:], xhi], axis=0)
    else:
        total = xlo + xhi
    total += jnp.where(row == 0, ylo[:, None, :], pltpu.roll(t, 1, 1))
    total += jnp.where(row == by - 1, yhi[:, None, :], pltpu.roll(t, by - 1, 1))
    total += jnp.where(lane == 0, to_column(zlo, by), pltpu.roll(t, 1, 2))
    total += jnp.where(lane == bz - 1, to_column(zhi, by), pltpu.roll(t, bz - 1, 2))
    return h + RATE * k * (total - 6.0 * t)


def sublanes(value, y):
    return jnp.concatenate([value[x, y : y + 1, :] for x in range(value.shape[0])], axis=0)


def side_blocks(h, k):
    by, bz = h.shape[1:]
    return [
        (sublanes(h, 0), sublanes(h, 1), sublanes(k, 0)),
        (sublanes(h, by - 1), sublanes(h, by - 2), sublanes(k, by - 1)),
        (to_lanes(h[:, :, 0:1]), to_lanes(h[:, :, 1:2]), to_lanes(k[:, :, 0:1])),
        (to_lanes(h[:, :, bz - 1 : bz]), to_lanes(h[:, :, bz - 2 : bz - 1]), to_lanes(k[:, :, bz - 1 : bz])),
    ]


def column_of(row):
    square = (row.shape[1], row.shape[1])
    return jnp.sum(jnp.where(iota(square, 0) == iota(square, 1), row, 0.0), axis=1, keepdims=True)


def table_sizes(count, plane_cap):
    records = (count - 1) * plane_cap
    faces = min(FACES, 128 // records)
    return records, faces, 1 + -(-FACES // faces)


def swap_order(count):
    return sorted(range(1, count), key=lambda s: (-s.bit_length(), s))


def place_of(table, slot):
    return table[0, FACES * SLOTS + slot], table[0, FACES * SLOTS + SLOTS + slot]


def write_tables(plane_cap, source, block, neighbour, asked, farther, table):
    here = lax.axis_index("gx")
    me = here.astype(F32)
    count = lax.axis_size("gx")
    records, faces, _ = table_sizes(count, plane_cap)
    cap = float(plane_cap)

    def position_of(swap):
        position = jnp.zeros(swap.shape, F32)
        for at, other in enumerate(swap_order(count)):
            position = jnp.where(swap == other, float(at), position)
        return position

    def wrapped(shift):
        return jnp.where(shift < 0.0, shift + float(count), shift)

    square = (SLOTS, SLOTS)
    before = iota(square, 0) < iota(square, 1)
    slot = iota((1, SLOTS), 1).astype(F32)
    source_row, block_column = source[...].astype(F32), column_of(block[...].astype(F32))
    source_column = column_of(source_row)
    rank = jnp.sum(
        jnp.where((source_column == source_row) & before, 1.0, 0.0), axis=0, keepdims=True
    )
    rank_column = column_of(rank)
    lane = iota((SLOTS, 128), 1).astype(F32)
    for shift in range(count):
        hit = (wrapped(source_column - me) == float(shift)) & (rank_column == lane)
        row = jnp.sum(jnp.where(hit, block_column, 0.0), axis=0, keepdims=True)
        asked[shift : shift + 1, :] = row
        if 2 <= shift < count - 1:
            farther[shift - 2][...] = jnp.broadcast_to(row, (8, 128))
    at = FACES * SLOTS
    swap = source[...] ^ here
    found = jnp.where(swap == 0, 0.0, 1.0 + position_of(swap))
    table[0:1, at : at + SLOTS] = found.astype(jnp.int32)
    table[0:1, at + SLOTS : at + 2 * SLOTS] = rank.astype(jnp.int32)
    slot_column = iota((SLOTS, records), 0).astype(F32)
    for face in range(FACES):
        number = neighbour[face]
        owner_row, number_row = (number >> 4).astype(F32), number.astype(F32)
        owner_column, number_column = column_of(owner_row), column_of(number_row)
        other_row = (number_row >= 0.0) & (owner_row != me)
        alike = (owner_column == owner_row) & (owner_column >= 0.0) & (owner_column != me)
        receive_rank = jnp.sum(
            jnp.where(alike & (number_column < number_row), 1.0, 0.0), axis=0, keepdims=True
        )
        send_rank = jnp.sum(jnp.where(alike & before, 1.0, 0.0), axis=0, keepdims=True)
        position = position_of(jnp.where(number < 0, 0, (number >> 4) ^ here))
        mine = records + (number_row - owner_row * SLOTS)
        there = position * cap + receive_rank
        receive = jnp.where(owner_row == me, mine, there)
        receive = jnp.where(number_row < 0.0, records + SLOTS + slot, receive)
        table[0:1, face * SLOTS : face * SLOTS + SLOTS] = receive.astype(jnp.int32)
        key = jnp.where(other_row, position * cap + send_rank, -1.0)
        hit = iota((SLOTS, records), 1).astype(F32) == column_of(key)
        tile = jnp.sum(jnp.where(hit, slot_column, 0.0), axis=0, keepdims=True)
        row, at = 1 + (face ^ 1) // faces, (face ^ 1) % faces * records
        table[row : row + 1, at : at + records] = tile.astype(jnp.int32)


def sides_kernel(
    sizes, plane_cap, source_far, block_far, neighbour_far, h_far, k_far, send, table, *rest
):
    asked, *farther, source, block, neighbour, h, k, sems = rest
    ny, nz = sizes
    my_y, my_z = lax.axis_index("gy"), lax.axis_index("gz")
    bx = h.shape[0]
    small = [(source_far, source), (block_far, block), (neighbour_far, neighbour)]
    copies = [pltpu.make_async_copy(*pair, sems.at[2 * bx + n]) for n, pair in enumerate(small)]
    large = []
    for x in range(bx):
        large.append(pltpu.make_async_copy(h_far.at[x], h.at[x], sems.at[x]))
        large.append(pltpu.make_async_copy(k_far.at[x], k.at[x], sems.at[bx + x]))
    for copy in copies + large:
        copy.start()
    for copy in copies:
        copy.wait()
    write_tables(plane_cap, source, block, neighbour, asked, farther, table)
    for copy in large:
        copy.wait()
    blocks = side_blocks(h[...], k[...])
    for y in range(ny):
        for z in range(nz):
            for part in range(3):
                ylo, yhi, zlo, zhi = [block[part] for block in blocks]
                chosen = jnp.where(
                    my_y == y, jnp.where(z < my_z, zlo, zhi), jnp.where(y < my_y, ylo, yhi)
                )
                send[y * nz + z, part * bx : part * bx + bx, :] = chosen


def side_reader(sizes, got, bx):
    ny, nz = sizes
    my_y, my_z = lax.axis_index("gy"), lax.axis_index("gz")

    def read(dy, dz, part=0):
        y, z = my_y + dy, my_z + dz
        inside = (y >= 0) & (y < ny) & (z >= 0) & (z < nz)
        at = jnp.where(inside, y * nz + z, 0)
        return jnp.where(inside, got[at, part * bx : part * bx + bx, :], 0.0)

    return read


def layers_kernel(sizes, h, k, got, asked, *rest):
    down, up = rest[-2:]
    bx, by, bz = h.shape
    read = side_reader(sizes, got, bx)
    around = [read(-1, 0), read(1, 0), read(0, -1), read(0, 1)]
    last = asked.shape[0] - 1
    for out, near, far, ask in ((down, 0, 1, last), (up, bx - 1, bx - 2, 1)):
        out[0:by, :] = h[near]
        out[by : 2 * by, :] = h[far]
        out[2 * by : 3 * by, :] = k[near]
        for number, side in enumerate(around):
            out[3 * by + number : 3 * by + number + 1, :] = side[near : near + 1, :]
        out[3 * by + 4 : 3 * by + 8, :] = jnp.broadcast_to(asked[ask : ask + 1, :], (4, bz))


def block_layout(cap):
    parts = 128 // CB // cap
    return parts, CB // parts


def flat_step(h, k, inner, outer, first, last, before, after, length):
    bx, lanes = h.shape
    t = temperature(h)
    row, lane = iota(h.shape, 0), iota(h.shape, 1)
    total = temperature(inner) + temperature(outer)
    total += jnp.where(row == 0, temperature(first), pltpu.roll(t, 1, 0))
    total += jnp.where(row == bx - 1, temperature(last), pltpu.roll(t, bx - 1, 0))
    total += jnp.where(lane == 0, temperature(before), pltpu.roll(t, 1, 1))
    total += jnp.where(lane == length - 1, temperature(after), pltpu.roll(t, lanes - 1, 1))
    return h + RATE * k * (total - 6.0 * t)


def heat_kernel(cap, sizes, request, h, k, got, low, high, out, found, *rest):
    *send, held = rest
    count = lax.axis_size("gx")
    bx, by, bz = h.shape
    h0, k0 = h[...], k[...]
    read = side_reader(sizes, got, bx)
    me = lax.axis_index("gx")
    layers, lines = [], []
    for beside, inside in ((low, me > 0), (high, me < count - 1)):
        beside = jnp.where(inside, beside[...], 0.0)
        layers.append([beside[part * by : part * by + by, :][None] for part in range(3)])
        lines.append([beside[3 * by + n : 3 * by + n + 1, :] for n in range(4)])
    y_sides = [[read(d, 0, part) for part in range(3)] for d in (-1, 1)]
    z_sides = [[read(0, d, part) for part in range(3)] for d in (-1, 1)]
    corner = [[read(dy, dz) for dz in (-1, 1)] for dy in (-1, 1)]
    to_first = [[pltpu.roll(c[0], 1, 1), c[1]] for c in corner]
    y_inner = [sublanes(h0, 0), sublanes(h0, by - 1)]
    z_inner = [to_lanes(h0[:, :, 0:1]), to_lanes(h0[:, :, bz - 1 : bz])]

    sides = [temperature(layers[0][0]), temperature(layers[1][0])]
    sides += [temperature(side[0]) for side in y_sides + z_sides]
    h1 = conduct(h0, k0, *sides)
    next_sides = []
    for side in range(2):
        near, far, near_k = layers[side]
        across = [temperature(far), temperature(h0[0:1])]
        if side:
            across = [temperature(h0[bx - 1 : bx]), temperature(far)]
        next_sides.append(conduct(near, near_k, *across, *[temperature(line) for line in lines[side]]))
    for side in range(2):
        near, far, near_k = y_sides[side]
        ends = [to_first[side][0], pltpu.roll(to_first[side][1], bz - 1, 1)]
        next_sides.append(
            flat_step(near, near_k, y_inner[side], far, lines[0][side], lines[1][side], *ends, bz)
        )
    for side in range(2):
        near, far, near_k = z_sides[side]
        ends = [to_first[0][side], pltpu.roll(to_first[1][side], by - 1, 1)]
        next_sides.append(
            flat_step(near, near_k, z_inner[side], far, lines[0][2 + side], lines[1][2 + side], *ends, by)
        )
    h2 = conduct(h1, k0, *[temperature(side) for side in next_sides])
    out[...] = h2

    held[...] = temperature(h2).reshape(bx, by // CB, CB, bz)
    parts, deep = block_layout(cap)
    nby, nbz = by // CB, bz // CB
    group = iota((deep, CB, bz), 2) // CB
    for out, swap in zip((found, *send), (0, *swap_order(count))):
        back = lax.rem(me - (me ^ swap) + count, count)
        total = jnp.zeros((deep, CB, bz), F32)
        for rank in range(cap):
            block = request[back, rank]
            a, b, c = block // (nby * nbz), (block // nbz) % nby, block % nbz
            for part in range(parts):
                at = rank * parts + part
                patch = held[pl.ds(a * CB + part * deep, deep), b]
                moved = pltpu.roll(patch, (CB * at - CB * c + bz) % bz, 2)
                total = jnp.where(group == at, moved, total)
        out[...] = total.reshape(deep * CB, bz)


def write_records(phase, solute, picks, own, own_edges, rows):
    flat = [f.reshape(SLOTS * TE, PLANE) for f in (phase, solute)]
    high, low = halves(jnp.concatenate(flat, axis=1))
    planes = dot(high, picks) + dot(low, picks)
    own[0:SLOTS] = planes[:, 0:128].reshape(SLOTS, TE, 128)
    own[SLOTS : 2 * SLOTS] = planes[:, 128:256].reshape(SLOTS, TE, 128)
    for part in range(4):
        rows[part] = flat[part // 2][:, part % 2 * 128 : part % 2 * 128 + 128]
    for part in range(4):
        low_face = rows[part, pl.ds(0, SLOTS, TE), :]
        high_face = rows[part, pl.ds(TE - 1, SLOTS, TE), :]
        for at, value in ((0, high_face), (4, low_face)):
            own_edges[pl.ds(at + part, SLOTS, 8), :] = value
            own_edges[pl.ds(8 * SLOTS + 4 - at + part, SLOTS, 8), :] = value


def merge_record(planes, edges, number):
    side = (iota((TE, 128), 1) % 64) // TE
    out = planes[number(2)]
    for face in range(3, 6):
        out = jnp.where(side == face - 2, planes[number(face)], out)
    first, second = [edges[pl.ds(pl.multiple_of(number(face) * 8, 8), 8), :] for face in range(2)]
    return out, jnp.where(iota((8, 128), 0) < 4, first, second)


def pack(own, own_edges, table, send):
    cap = send[0].shape[0] // REC
    records, faces, _ = table_sizes(len(send) + 1, cap)
    for record in range(records):
        out, row = send[record // cap], record % cap * REC
        planes, edge = merge_record(
            own, own_edges, lambda face: table[1 + face // faces, face % faces * records + record]
        )
        out[row : row + TE, :] = planes
        out[row + TE : row + REC, :] = edge


def first_pack_kernel(table, asked, phase, solute, picks, own, own_edges, asked_out, *rest):
    *send, rows = rest
    write_records(phase[...], solute[...], picks[...], own, own_edges, rows)
    pack(own, own_edges, table, send)
    asked_out[...] = asked[...]


def take_heat(cap, table, found, spreads, blocks, held, heat):
    parts, deep = block_layout(cap)
    for number, value in enumerate(found):
        blocks[number] = value[...]
    group = iota((CB, 128), 1) // CB
    for slot in range(SLOTS):
        back, rank = place_of(table, slot)
        for x in range(CB):
            row = (x % deep) * CB
            patch = blocks[back, row : row + CB, :]
            held[slot * CB + x] = jnp.where(group == rank * parts + x // deep, patch, 0.0)
    rows = held[...].reshape(SLOTS * CB * CB, 128)
    wide = dot(jnp.concatenate(halves(rows), axis=1), spreads)
    wide = wide.reshape(SLOTS * CB, CB, PLANE)
    keep = iota(wide.shape, 1) == iota(wide.shape, 2) // TE // 2
    coarse = jnp.sum(jnp.where(keep, wide, 0.0), axis=1)
    for half in range(2):
        for odd in range(2):
            heat[half, pl.ds(odd, SLOTS * CB, 2), :] = coarse[:, half * 128 : half * 128 + 128]


def inner_step(phase, solute, heat, stencil):
    row = iota((SLOTS, TE, PLANE), 1)
    lap = []
    for field in (phase, solute):
        high, low = halves(field.reshape(SLOTS * TE, PLANE))
        total = (dot(high, stencil) + dot(low, stencil)).reshape(SLOTS, TE, PLANE) - 6.0 * field
        total += jnp.where(row == 0, 0.0, pltpu.roll(field, 1, 1))
        total += jnp.where(row == TE - 1, 0.0, pltpu.roll(field, TE - 1, 1))
        lap.append(total)
    squared = 1.0 - phase * phase
    drive = solute if heat is None else heat + solute
    change = ORDER_SPEED * (
        lap[0] + phase - phase * phase * phase - COUPLING * drive * squared * squared
    )
    return phase + change, solute + SOLUTE_RATE * lap[1] + REJECTION * change


def wide_heat(heat):
    return jnp.concatenate([heat[0], heat[1]], axis=1).reshape(SLOTS, TE, PLANE)


def gather_ghosts(table, got, own, own_edges, planes, edges, ghosts, ghost_edges):
    records = planes.shape[0] - 2 * SLOTS
    cap = records // len(got)
    for record in range(records):
        value, row = got[record // cap], record % cap * REC
        planes[record] = value[row : row + TE, :]
        edges[record * 8 : record * 8 + 8, :] = value[row + TE : row + REC, :]
    planes[records:] = own[...]
    edges[records * 8 :, :] = own_edges[...]
    for slot in range(SLOTS):
        out, edge = merge_record(planes, edges, lambda face: table[0, face * SLOTS + slot])
        ghosts[slot] = out
        ghost_edges[slot] = edge


def ghost_shares(ghosts, ghost_edges, places):
    beside = jnp.concatenate(halves(ghosts[...].reshape(SLOTS * TE, 128)), axis=1)
    beside = dot(beside, places)
    rows = iota((SLOTS, TE, PLANE), 1)
    shares = []
    for number in range(2):
        share = beside[:, number * PLANE : number * PLANE + PLANE].reshape(SLOTS, TE, PLANE)
        for face, at_row in ((0, 0), (1, TE - 1)):
            at = face * 4 + number * 2
            side = [ghost_edges[:, row : row + 1, :] for row in (at, at + 1)]
            side = jnp.concatenate(side, axis=2)
            share += jnp.where(rows == at_row, side, 0.0)
        shares.append(share)
    return shares


def add_shares(phase, solute, shares, heat_share=None):
    change = ORDER_SPEED * shares[0]
    if heat_share is not None:
        change += heat_share
    return phase + change, solute + SOLUTE_RATE * shares[1] + REJECTION * change


def inner_kernel(has_heat, phase, solute, stencil, *rest):
    phase_out, solute_out = rest[-2:]
    heat = wide_heat(rest[0]) if has_heat else None
    phase_out[...], solute_out[...] = inner_step(phase[...], solute[...], heat, stencil[...])


def first_step_kernel(cap, table, old_phase, phase, solute, own, own_edges, picks, places, spreads, *rest):
    others = lax.axis_size("gx") - 1
    found, got, rest = rest[: others + 1], rest[others + 1 : 2 * others + 1], rest[2 * others + 1 :]
    phase_out, solute_out, heat_out, own_out, edges_out, *rest = rest
    send, (*records, ghosts, ghost_edges, rows, blocks, held) = rest[:others], rest[others:]
    take_heat(cap, table, found, spreads[...], blocks, held, heat_out)
    gather_ghosts(table, got, own, own_edges, *records, ghosts, ghost_edges)
    squared = 1.0 - old_phase[...] * old_phase[...]
    heat_share = (-ORDER_SPEED * COUPLING) * wide_heat(heat_out) * squared * squared
    new_phase, new_solute = add_shares(
        phase[...], solute[...], ghost_shares(ghosts, ghost_edges, places[...]), heat_share
    )
    phase_out[...] = new_phase
    solute_out[...] = new_solute
    write_records(new_phase, new_solute, picks[...], own_out, edges_out, rows)
    pack(own_out, edges_out, table, send)


def write_out_kernel(value, out, sem):
    copy = pltpu.make_async_copy(value, out, sem)
    copy.start()
    copy.wait()


def middle_step_kernel(table, phase, solute, own, own_edges, picks, places, *rest):
    others = lax.axis_size("gx") - 1
    got, (phase_out, solute_out, own_out, edges_out, *rest) = rest[:others], rest[others:]
    send, (*records, ghosts, ghost_edges, rows) = rest[:others], rest[others:]
    gather_ghosts(table, got, own, own_edges, *records, ghosts, ghost_edges)
    new_phase, new_solute = add_shares(phase[...], solute[...], ghost_shares(ghosts, ghost_edges, places[...]))
    phase_out[...] = new_phase
    solute_out[...] = new_solute
    write_records(new_phase, new_solute, picks[...], own_out, edges_out, rows)
    pack(own_out, edges_out, table, send)


def last_step_kernel(table, phase, solute, own, own_edges, places, *rest):
    others = lax.axis_size("gx") - 1
    got, (phase_out, solute_out, *records, ghosts, ghost_edges, _) = rest[:others], rest[others:]
    gather_ghosts(table, got, own, own_edges, *records, ghosts, ghost_edges)
    phase_out[...], solute_out[...] = add_shares(
        phase[...], solute[...], ghost_shares(ghosts, ghost_edges, places[...])
    )


def call(kernel, in_specs, out_shapes, scratch=(), out_specs=None, mib=16):
    return pl.pallas_call(
        kernel,
        out_shape=out_shapes,
        in_specs=in_specs,
        out_specs=out_specs or jax.tree.map(lambda _: VMEM, out_shapes),
        scratch_shapes=list(scratch),
        compiler_params=pltpu.CompilerParams(vmem_limit_bytes=mib * 1024 * 1024),
    )


def shape(*dims):
    return jax.ShapeDtypeStruct(dims, F32)


def local(enthalpy, conductivity, phase, solute, tile_source, tile_block, tile_neighbour):
    count = lax.axis_size("gx")
    sizes = (lax.axis_size("gy"), lax.axis_size("gz"))
    plane_cap = -(-SLOTS // (count - 1))
    block_cap = 2 * SLOTS // count
    others = count - 1
    records = others * plane_cap
    bx, by, bz = enthalpy.shape
    picks, stencil, places, spreads = tables()

    integers = functools.partial(jax.ShapeDtypeStruct, dtype=jnp.int32)
    sides, table, asked, *farther = call(
        functools.partial(sides_kernel, sizes, plane_cap),
        [ANY] * 5,
        [
            shape(sizes[0] * sizes[1], 3 * bx, 128),
            integers((table_sizes(count, plane_cap)[2], 128)),
            shape(count, 128),
            *[shape(8, 128)] * (count - 3),
        ],
        [
            pltpu.VMEM((1, SLOTS), jnp.int32),
            pltpu.VMEM((1, SLOTS), jnp.int32),
            pltpu.VMEM((FACES, 1, SLOTS), jnp.int32),
            pltpu.VMEM((bx, by, bz), F32),
            pltpu.VMEM((bx, by, bz), F32),
            pltpu.SemaphoreType.DMA((2 * bx + 3,)),
        ],
        mib=56,
    )(
        tile_source.reshape(1, SLOTS),
        tile_block.reshape(1, SLOTS),
        jnp.transpose(tile_neighbour, (0, 1, 4, 2, 3)).reshape(FACES, 1, SLOTS),
        enthalpy,
        conductivity,
    )
    sides = lax.all_to_all(sides, ("gy", "gz"), split_axis=0, concat_axis=0, tiled=True)

    def pass_on(value, shift):
        return lax.ppermute(value, "gx", [(i, (i + shift) % count) for i in range(count)])

    def swap_all(values):
        return [
            lax.ppermute(value, "gx", [(i, i ^ swap) for i in range(count)])
            for swap, value in zip(swap_order(count), values)
        ]

    farther = [pass_on(value, shift) for shift, value in enumerate(farther, 2)]

    phase_field = phase.reshape(SLOTS, TE, PLANE)
    solute_field = solute.reshape(SLOTS, TE, PLANE)
    own_shapes = [shape(2 * SLOTS, TE, 128), shape(2 * SLOTS * 8, 128)]
    send_shapes = [shape(plane_cap * REC, 128)] * others
    rows_scratch = pltpu.VMEM((4, SLOTS * TE, 128), F32)
    packed = call(
        first_pack_kernel,
        [SMEM] + [VMEM] * 4,
        [*own_shapes, shape(count, 128), *send_shapes],
        [rows_scratch],
    )(table, asked, phase_field, solute_field, picks)
    own, asked, packed = packed[:2], packed[2], packed[3:]

    layer = shape(3 * by + 8, bz)
    down, up = call(
        functools.partial(layers_kernel, sizes), [VMEM] * 4 + [ANY] * len(farther), [layer, layer]
    )(enthalpy, conductivity, sides, asked, *farther)
    from_low, from_high = pass_on(up, 1), pass_on(down, others)
    row = 3 * by + 4
    request = [asked[0], from_low[row], *[value[0] for value in farther], from_high[row]]
    request = jnp.stack([value[:block_cap] for value in request]).astype(jnp.int32)
    _, deep = block_layout(block_cap)
    brick = shape(bx, by, bz)
    got = swap_all(packed)
    heated, *found = call(
        functools.partial(heat_kernel, block_cap, sizes),
        [SMEM] + [VMEM] * 5,
        [brick] + [shape(deep * CB, 128)] * count,
        [pltpu.VMEM((bx, by // CB, CB, bz), F32)],
    )(request, enthalpy, conductivity, sides, from_low, from_high)
    found[1:] = swap_all(found[1:])
    (heat_out,) = call(write_out_kernel, [ANY], [brick], [pltpu.SemaphoreType.DMA], [ANY])(heated)

    field = shape(SLOTS, TE, PLANE)
    step_scratch = [
        pltpu.VMEM((records + 2 * SLOTS, TE, 128), F32),
        pltpu.VMEM(((records + 2 * SLOTS) * 8, 128), F32),
        pltpu.VMEM((SLOTS, TE, 128), F32),
        pltpu.VMEM((SLOTS, 8, 128), F32),
        rows_scratch,
    ]
    def inner(phase_field, solute_field, *heat):
        return call(
            functools.partial(inner_kernel, bool(heat)), [VMEM] * (3 + len(heat)), [field, field]
        )(phase_field, solute_field, stencil, *heat)

    inner_fields = inner(phase_field, solute_field)
    phase_field, solute_field, heat, *rest = call(
        functools.partial(first_step_kernel, block_cap),
        [SMEM] + [VMEM] * (8 + count + others),
        [field, field, shape(2, SLOTS * TE, 128), *own_shapes, *send_shapes],
        step_scratch
        + [
            pltpu.VMEM((count, deep * CB, 128), F32),
            pltpu.VMEM((SLOTS * CB, CB, 128), F32),
        ],
    )(table, phase_field, *inner_fields, *own, picks, places, spreads, *found, *got)
    own, send = rest[:2], rest[2:]
    for _ in range(PHASE_STEPS - 2):
        got = swap_all(send)
        inner_fields = inner(phase_field, solute_field, heat)
        phase_field, solute_field, *rest = call(
            middle_step_kernel,
            [SMEM] + [VMEM] * (6 + others),
            [field, field, *own_shapes, *send_shapes],
            step_scratch,
        )(table, *inner_fields, *own, picks, places, *got)
        own, send = rest[:2], rest[2:]
    got = swap_all(send)
    inner_fields = inner(phase_field, solute_field, heat)
    phase_field, solute_field = call(
        last_step_kernel, [SMEM] + [VMEM] * (5 + others), [field, field], step_scratch
    )(table, *inner_fields, *own, places, *got)
    return heat_out, phase_field.reshape(phase.shape), solute_field.reshape(solute.shape)


def solution(mesh):
    grid = P("gx", "gy", "gz")
    tiles = P("gx", "gy", "gz", None, None, None)
    return jax.shard_map(
        local,
        mesh=mesh,
        in_specs=(
            grid,
            grid,
            tiles,
            tiles,
            P("gx", "gy", "gz", None, None),
            P("gx", "gy", "gz", None),
            P("gx", "gy", "gz", None, None),
        ),
        out_specs=(grid, tiles, tiles),
        check_vma=False,
    )
```

```python
import functools

import jax
import jax.numpy as jnp
import numpy as np
from jax import lax
from jax.experimental import pallas as pl
from jax.experimental.pallas import tpu as pltpu
from jax.sharding import PartitionSpec as P

CB = 8
TE = 16
PLANE = TE * TE
SLOTS = 16
FACES = 6
PHASE_STEPS = 4
REC = 24

RATE = 0.16
ORDER_SPEED = 0.1
SOLUTE_RATE = 0.15
COUPLING = 0.5
REJECTION = 0.5

F32 = jnp.float32
BF16 = jnp.bfloat16
VMEM = pl.BlockSpec(memory_space=pltpu.VMEM)
SMEM = pl.BlockSpec(memory_space=pltpu.SMEM)
ANY = pl.BlockSpec(memory_space=pl.ANY)


def plane_lane(face):
    j = np.arange(TE)
    return [j, PLANE - TE + j, j * TE, j * TE + TE - 1][face - 2]


def constant_tables():
    pick = np.zeros((2, PLANE, 256), np.float32)
    place = np.zeros((2, 128, PLANE), np.float32)
    for field in range(2):
        for face in range(2, 6):
            at = field * 64 + (face - 2) * TE + np.arange(TE)
            pick[field, plane_lane(face ^ 1), at] = 1.0
            pick[field, plane_lane(face), 128 + at] = 1.0
            place[field, at, plane_lane(face)] = 1.0
    y, z = np.divmod(np.arange(PLANE), TE)
    dy, dz = np.abs(y[:, None] - y[None, :]), np.abs(z[:, None] - z[None, :])
    stencil = ((dy + dz) == 1).astype(np.float32)
    lane = np.arange(128)
    spread = (lane[:, None] % CB == z[None, :] // 2).astype(np.float32)
    return pick, place, stencil, spread


def tables():
    pick, place, stencil, spread = constant_tables()
    place = np.concatenate([place[0], place[1]], axis=1)
    return (
        jnp.asarray(np.concatenate([pick[0], pick[1]], axis=0), BF16),
        jnp.asarray(stencil, BF16),
        jnp.asarray(np.concatenate([place, place], axis=0), BF16),
        jnp.asarray(np.concatenate([spread, spread], axis=0), BF16),
    )


def halves(value):
    high = value.astype(BF16)
    return high, (value - high.astype(F32)).astype(BF16)


def dot(a, b):
    return jnp.dot(a, b, preferred_element_type=F32)


def temperature(h):
    return jnp.minimum(h, 0.0) + jnp.maximum(h - 1.0, 0.0)


def iota(shape, dim):
    return lax.broadcasted_iota(jnp.int32, shape, dim)


def to_lanes(column):
    bx, by, _ = column.shape
    diagonal = iota((bx, by, 128), 1) == iota((bx, by, 128), 2)
    return jnp.sum(jnp.where(diagonal, column, 0.0), axis=1)


def to_column(line, by):
    bx = line.shape[0]
    diagonal = iota((bx, by, 128), 1) == iota((bx, by, 128), 2)
    return jnp.sum(jnp.where(diagonal, line[:, None, :], 0.0), axis=2, keepdims=True)


def conduct(h, k, xlo, xhi, ylo, yhi, zlo, zhi):
    bx, by, bz = h.shape
    t = temperature(h)
    row, lane = iota((bx, by, bz), 1), iota((bx, by, bz), 2)
    if bx > 1:
        total = jnp.concatenate([xlo, t[:-1]], axis=0) + jnp.concatenate([t[1:], xhi], axis=0)
    else:
        total = xlo + xhi
    total += jnp.where(row == 0, ylo[:, None, :], pltpu.roll(t, 1, 1))
    total += jnp.where(row == by - 1, yhi[:, None, :], pltpu.roll(t, by - 1, 1))
    total += jnp.where(lane == 0, to_column(zlo, by), pltpu.roll(t, 1, 2))
    total += jnp.where(lane == bz - 1, to_column(zhi, by), pltpu.roll(t, bz - 1, 2))
    return h + RATE * k * (total - 6.0 * t)


def sublanes(value, y):
    return jnp.concatenate([value[x, y : y + 1, :] for x in range(value.shape[0])], axis=0)


def side_blocks(h, k):
    by, bz = h.shape[1:]
    return [
        (sublanes(h, 0), sublanes(h, 1), sublanes(k, 0)),
        (sublanes(h, by - 1), sublanes(h, by - 2), sublanes(k, by - 1)),
        (to_lanes(h[:, :, 0:1]), to_lanes(h[:, :, 1:2]), to_lanes(k[:, :, 0:1])),
        (to_lanes(h[:, :, bz - 1 : bz]), to_lanes(h[:, :, bz - 2 : bz - 1]), to_lanes(k[:, :, bz - 1 : bz])),
    ]


def column_of(row):
    square = (row.shape[1], row.shape[1])
    return jnp.sum(jnp.where(iota(square, 0) == iota(square, 1), row, 0.0), axis=1, keepdims=True)


def table_sizes(count, plane_cap):
    records = (count - 1) * plane_cap
    faces = min(FACES, 128 // records)
    return records, faces, 1 + -(-FACES // faces)


def swap_order(count):
    return sorted(range(1, count), key=lambda s: (-s.bit_length(), s))


def place_of(table, slot):
    return table[0, FACES * SLOTS + slot], table[0, FACES * SLOTS + SLOTS + slot]


def write_tables(plane_cap, source, block, neighbour, asked, farther, table):
    here = lax.axis_index("gx")
    me = here.astype(F32)
    count = lax.axis_size("gx")
    records, faces, _ = table_sizes(count, plane_cap)
    cap = float(plane_cap)

    def position_of(swap):
        position = jnp.zeros(swap.shape, F32)
        for at, other in enumerate(swap_order(count)):
            position = jnp.where(swap == other, float(at), position)
        return position

    square = (SLOTS, SLOTS)
    before = iota(square, 0) < iota(square, 1)
    slot = iota((1, SLOTS), 1).astype(F32)
    source_row, block_column = source[...].astype(F32), column_of(block[...].astype(F32))
    source_column = column_of(source_row)
    rank = jnp.sum(
        jnp.where((source_column == source_row) & before, 1.0, 0.0), axis=0, keepdims=True
    )
    rank_column = column_of(rank)
    lane = iota((SLOTS, 128), 1).astype(F32)
    swap = source[...] ^ here
    swap_column = column_of(swap.astype(F32))
    for shift in range(count):
        hit = (swap_column == float(shift)) & (rank_column == lane)
        row = jnp.sum(jnp.where(hit, block_column, 0.0), axis=0, keepdims=True)
        asked[shift : shift + 1, :] = row
        if shift > 1:
            farther[shift - 2][...] = jnp.broadcast_to(row, (8, 128))
    at = FACES * SLOTS
    found = jnp.where(swap == 0, 0.0, 1.0 + position_of(swap))
    table[0:1, at : at + SLOTS] = found.astype(jnp.int32)
    table[0:1, at + SLOTS : at + 2 * SLOTS] = rank.astype(jnp.int32)
    slot_column = iota((SLOTS, records), 0).astype(F32)
    for face in range(FACES):
        number = neighbour[face]
        owner_row, number_row = (number >> 4).astype(F32), number.astype(F32)
        owner_column, number_column = column_of(owner_row), column_of(number_row)
        other_row = (number_row >= 0.0) & (owner_row != me)
        alike = (owner_column == owner_row) & (owner_column >= 0.0) & (owner_column != me)
        receive_rank = jnp.sum(
            jnp.where(alike & (number_column < number_row), 1.0, 0.0), axis=0, keepdims=True
        )
        send_rank = jnp.sum(jnp.where(alike & before, 1.0, 0.0), axis=0, keepdims=True)
        position = position_of(jnp.where(number < 0, 0, (number >> 4) ^ here))
        mine = records + (number_row - owner_row * SLOTS)
        there = position * cap + receive_rank
        receive = jnp.where(owner_row == me, mine, there)
        receive = jnp.where(number_row < 0.0, records + SLOTS + slot, receive)
        table[0:1, face * SLOTS : face * SLOTS + SLOTS] = receive.astype(jnp.int32)
        key = jnp.where(other_row, position * cap + send_rank, -1.0)
        hit = iota((SLOTS, records), 1).astype(F32) == column_of(key)
        tile = jnp.sum(jnp.where(hit, slot_column, 0.0), axis=0, keepdims=True)
        row, at = 1 + (face ^ 1) // faces, (face ^ 1) % faces * records
        table[row : row + 1, at : at + records] = tile.astype(jnp.int32)


def sides_kernel(
    sizes, plane_cap, source_far, block_far, neighbour_far, h_far, k_far, send, table, *rest
):
    asked, *farther, source, block, neighbour, h, k, sems = rest
    ny, nz = sizes
    my_y, my_z = lax.axis_index("gy"), lax.axis_index("gz")
    bx = h.shape[0]
    small = [(source_far, source), (block_far, block), (neighbour_far, neighbour)]
    copies = [pltpu.make_async_copy(*pair, sems.at[2 * bx + n]) for n, pair in enumerate(small)]
    large = []
    for x in range(bx):
        large.append(pltpu.make_async_copy(h_far.at[x], h.at[x], sems.at[x]))
        large.append(pltpu.make_async_copy(k_far.at[x], k.at[x], sems.at[bx + x]))
    for copy in copies + large:
        copy.start()
    for copy in copies:
        copy.wait()
    write_tables(plane_cap, source, block, neighbour, asked, farther, table)
    for copy in large:
        copy.wait()
    blocks = side_blocks(h[...], k[...])
    for y in range(ny):
        for z in range(nz):
            for part in range(3):
                ylo, yhi, zlo, zhi = [block[part] for block in blocks]
                chosen = jnp.where(
                    my_y == y, jnp.where(z < my_z, zlo, zhi), jnp.where(y < my_y, ylo, yhi)
                )
                send[y * nz + z, part * bx : part * bx + bx, :] = chosen


def side_reader(sizes, got, bx):
    ny, nz = sizes
    my_y, my_z = lax.axis_index("gy"), lax.axis_index("gz")

    def read(dy, dz, part=0):
        y, z = my_y + dy, my_z + dz
        inside = (y >= 0) & (y < ny) & (z >= 0) & (z < nz)
        at = jnp.where(inside, y * nz + z, 0)
        return jnp.where(inside, got[at, part * bx : part * bx + bx, :], 0.0)

    return read


def layers_kernel(sizes, h, k, got, asked, *rest):
    first, second = rest[-2:]
    bx, by, bz = h.shape
    read = side_reader(sizes, got, bx)
    even = lax.rem(lax.axis_index("gx"), 2) == 0
    around = [read(-1, 0), read(1, 0), read(0, -1), read(0, 1)]
    layers = [(h[bx - 1], h[0]), (h[bx - 2], h[1]), (k[bx - 1], k[0])]
    layers += [(side[bx - 1 : bx, :], side[0:1, :]) for side in around]
    row = 0
    for upper, lower in layers:
        first[row : row + upper.shape[0], :] = jnp.where(even, upper, lower)
        second[row : row + upper.shape[0], :] = jnp.where(even, lower, upper)
        row += upper.shape[0]
    for out in (first, second):
        out[row:, :] = jnp.broadcast_to(asked[1:2, :], (out.shape[0] - row, bz))


def block_layout(cap):
    parts = 128 // CB // cap
    return parts, CB // parts


def flat_step(h, k, inner, outer, first, last, before, after, length):
    bx, lanes = h.shape
    t = temperature(h)
    row, lane = iota(h.shape, 0), iota(h.shape, 1)
    total = temperature(inner) + temperature(outer)
    total += jnp.where(row == 0, temperature(first), pltpu.roll(t, 1, 0))
    total += jnp.where(row == bx - 1, temperature(last), pltpu.roll(t, bx - 1, 0))
    total += jnp.where(lane == 0, temperature(before), pltpu.roll(t, 1, 1))
    total += jnp.where(lane == length - 1, temperature(after), pltpu.roll(t, lanes - 1, 1))
    return h + RATE * k * (total - 6.0 * t)


def heat_kernel(cap, sizes, request, h, k, got, first, second, out, found, *rest):
    *send, held = rest
    count = lax.axis_size("gx")
    bx, by, bz = h.shape
    h0, k0 = h[...], k[...]
    read = side_reader(sizes, got, bx)
    me = lax.axis_index("gx")
    layers, lines = [], []
    even = lax.rem(me, 2) == 0
    pairs = (first[...], second[...])
    low, high = jnp.where(even, *pairs[::-1]), jnp.where(even, *pairs)
    for beside, inside in ((low, me > 0), (high, me < count - 1)):
        beside = jnp.where(inside, beside, 0.0)
        layers.append([beside[part * by : part * by + by, :][None] for part in range(3)])
        lines.append([beside[3 * by + n : 3 * by + n + 1, :] for n in range(4)])
    y_sides = [[read(d, 0, part) for part in range(3)] for d in (-1, 1)]
    z_sides = [[read(0, d, part) for part in range(3)] for d in (-1, 1)]
    corner = [[read(dy, dz) for dz in (-1, 1)] for dy in (-1, 1)]
    to_first = [[pltpu.roll(c[0], 1, 1), c[1]] for c in corner]
    y_inner = [sublanes(h0, 0), sublanes(h0, by - 1)]
    z_inner = [to_lanes(h0[:, :, 0:1]), to_lanes(h0[:, :, bz - 1 : bz])]

    sides = [temperature(layers[0][0]), temperature(layers[1][0])]
    sides += [temperature(side[0]) for side in y_sides + z_sides]
    h1 = conduct(h0, k0, *sides)
    next_sides = []
    for side in range(2):
        near, far, near_k = layers[side]
        across = [temperature(far), temperature(h0[0:1])]
        if side:
            across = [temperature(h0[bx - 1 : bx]), temperature(far)]
        next_sides.append(conduct(near, near_k, *across, *[temperature(line) for line in lines[side]]))
    for side in range(2):
        near, far, near_k = y_sides[side]
        ends = [to_first[side][0], pltpu.roll(to_first[side][1], bz - 1, 1)]
        next_sides.append(
            flat_step(near, near_k, y_inner[side], far, lines[0][side], lines[1][side], *ends, bz)
        )
    for side in range(2):
        near, far, near_k = z_sides[side]
        ends = [to_first[0][side], pltpu.roll(to_first[1][side], by - 1, 1)]
        next_sides.append(
            flat_step(near, near_k, z_inner[side], far, lines[0][2 + side], lines[1][2 + side], *ends, by)
        )
    h2 = conduct(h1, k0, *[temperature(side) for side in next_sides])
    out[...] = h2

    held[...] = temperature(h2).reshape(bx, by // CB, CB, bz)
    parts, deep = block_layout(cap)
    nby, nbz = by // CB, bz // CB
    group = iota((deep, CB, bz), 2) // CB
    for out, swap in zip((found, *send), (0, *swap_order(count))):
        total = jnp.zeros((deep, CB, bz), F32)
        for rank in range(cap):
            block = request[swap, rank]
            a, b, c = block // (nby * nbz), (block // nbz) % nby, block % nbz
            for part in range(parts):
                at = rank * parts + part
                patch = held[pl.ds(a * CB + part * deep, deep), b]
                moved = pltpu.roll(patch, (CB * at - CB * c + bz) % bz, 2)
                total = jnp.where(group == at, moved, total)
        out[...] = total.reshape(deep * CB, bz)


def write_records(phase, solute, picks, own, own_edges, rows):
    flat = [f.reshape(SLOTS * TE, PLANE) for f in (phase, solute)]
    high, low = halves(jnp.concatenate(flat, axis=1))
    planes = dot(high, picks) + dot(low, picks)
    own[0:SLOTS] = planes[:, 0:128].reshape(SLOTS, TE, 128)
    own[SLOTS : 2 * SLOTS] = planes[:, 128:256].reshape(SLOTS, TE, 128)
    for part in range(4):
        rows[part] = flat[part // 2][:, part % 2 * 128 : part % 2 * 128 + 128]
    for part in range(4):
        low_face = rows[part, pl.ds(0, SLOTS, TE), :]
        high_face = rows[part, pl.ds(TE - 1, SLOTS, TE), :]
        for at, value in ((0, high_face), (4, low_face)):
            own_edges[pl.ds(at + part, SLOTS, 8), :] = value
            own_edges[pl.ds(8 * SLOTS + 4 - at + part, SLOTS, 8), :] = value


def merge_record(planes, edges, number):
    side = (iota((TE, 128), 1) % 64) // TE
    out = planes[number(2)]
    for face in range(3, 6):
        out = jnp.where(side == face - 2, planes[number(face)], out)
    first, second = [edges[pl.ds(pl.multiple_of(number(face) * 8, 8), 8), :] for face in range(2)]
    return out, jnp.where(iota((8, 128), 0) < 4, first, second)


def pack(own, own_edges, table, send):
    cap = send[0].shape[0] // REC
    records, faces, _ = table_sizes(len(send) + 1, cap)
    for record in range(records):
        out, row = send[record // cap], record % cap * REC
        planes, edge = merge_record(
            own, own_edges, lambda face: table[1 + face // faces, face % faces * records + record]
        )
        out[row : row + TE, :] = planes
        out[row + TE : row + REC, :] = edge


def first_pack_kernel(table, asked, phase, solute, picks, own, own_edges, asked_out, *rest):
    *send, rows = rest
    write_records(phase[...], solute[...], picks[...], own, own_edges, rows)
    pack(own, own_edges, table, send)
    asked_out[...] = asked[...]


def take_heat(cap, table, found, spreads, blocks, held, heat):
    parts, deep = block_layout(cap)
    for number, value in enumerate(found):
        blocks[number] = value[...]
    group = iota((CB, 128), 1) // CB
    for slot in range(SLOTS):
        back, rank = place_of(table, slot)
        for x in range(CB):
            row = (x % deep) * CB
            patch = blocks[back, row : row + CB, :]
            held[slot * CB + x] = jnp.where(group == rank * parts + x // deep, patch, 0.0)
    rows = held[...].reshape(SLOTS * CB * CB, 128)
    wide = dot(jnp.concatenate(halves(rows), axis=1), spreads)
    wide = wide.reshape(SLOTS * CB, CB, PLANE)
    keep = iota(wide.shape, 1) == iota(wide.shape, 2) // TE // 2
    coarse = jnp.sum(jnp.where(keep, wide, 0.0), axis=1)
    for half in range(2):
        for odd in range(2):
            heat[half, pl.ds(odd, SLOTS * CB, 2), :] = coarse[:, half * 128 : half * 128 + 128]


def inner_step(phase, solute, heat, stencil):
    row = iota((SLOTS, TE, PLANE), 1)
    lap = []
    for field in (phase, solute):
        high, low = halves(field.reshape(SLOTS * TE, PLANE))
        total = (dot(high, stencil) + dot(low, stencil)).reshape(SLOTS, TE, PLANE) - 6.0 * field
        total += jnp.where(row == 0, 0.0, pltpu.roll(field, 1, 1))
        total += jnp.where(row == TE - 1, 0.0, pltpu.roll(field, TE - 1, 1))
        lap.append(total)
    squared = 1.0 - phase * phase
    drive = solute if heat is None else heat + solute
    change = ORDER_SPEED * (
        lap[0] + phase - phase * phase * phase - COUPLING * drive * squared * squared
    )
    return phase + change, solute + SOLUTE_RATE * lap[1] + REJECTION * change


def wide_heat(heat):
    return jnp.concatenate([heat[0], heat[1]], axis=1).reshape(SLOTS, TE, PLANE)


def gather_ghosts(table, got, own, own_edges, planes, edges, ghosts, ghost_edges):
    records = planes.shape[0] - 2 * SLOTS
    cap = records // len(got)
    for record in range(records):
        value, row = got[record // cap], record % cap * REC
        planes[record] = value[row : row + TE, :]
        edges[record * 8 : record * 8 + 8, :] = value[row + TE : row + REC, :]
    planes[records:] = own[...]
    edges[records * 8 :, :] = own_edges[...]
    for slot in range(SLOTS):
        out, edge = merge_record(planes, edges, lambda face: table[0, face * SLOTS + slot])
        ghosts[slot] = out
        ghost_edges[slot] = edge


def ghost_shares(ghosts, ghost_edges, places):
    beside = jnp.concatenate(halves(ghosts[...].reshape(SLOTS * TE, 128)), axis=1)
    beside = dot(beside, places)
    rows = iota((SLOTS, TE, PLANE), 1)
    shares = []
    for number in range(2):
        share = beside[:, number * PLANE : number * PLANE + PLANE].reshape(SLOTS, TE, PLANE)
        for face, at_row in ((0, 0), (1, TE - 1)):
            at = face * 4 + number * 2
            side = [ghost_edges[:, row : row + 1, :] for row in (at, at + 1)]
            side = jnp.concatenate(side, axis=2)
            share += jnp.where(rows == at_row, side, 0.0)
        shares.append(share)
    return shares


def add_shares(phase, solute, shares, heat_share=None):
    change = ORDER_SPEED * shares[0]
    if heat_share is not None:
        change += heat_share
    return phase + change, solute + SOLUTE_RATE * shares[1] + REJECTION * change


def inner_kernel(has_heat, phase, solute, stencil, *rest):
    phase_out, solute_out = rest[-2:]
    heat = wide_heat(rest[0]) if has_heat else None
    phase_out[...], solute_out[...] = inner_step(phase[...], solute[...], heat, stencil[...])


def first_step_kernel(cap, table, old_phase, phase, solute, own, own_edges, picks, places, spreads, *rest):
    others = lax.axis_size("gx") - 1
    found, got, rest = rest[: others + 1], rest[others + 1 : 2 * others + 1], rest[2 * others + 1 :]
    phase_out, solute_out, heat_out, own_out, edges_out, *rest = rest
    send, (*records, ghosts, ghost_edges, rows, blocks, held) = rest[:others], rest[others:]
    take_heat(cap, table, found, spreads[...], blocks, held, heat_out)
    gather_ghosts(table, got, own, own_edges, *records, ghosts, ghost_edges)
    squared = 1.0 - old_phase[...] * old_phase[...]
    heat_share = (-ORDER_SPEED * COUPLING) * wide_heat(heat_out) * squared * squared
    new_phase, new_solute = add_shares(
        phase[...], solute[...], ghost_shares(ghosts, ghost_edges, places[...]), heat_share
    )
    phase_out[...] = new_phase
    solute_out[...] = new_solute
    write_records(new_phase, new_solute, picks[...], own_out, edges_out, rows)
    pack(own_out, edges_out, table, send)


def write_out_kernel(value, out, sem):
    copy = pltpu.make_async_copy(value, out, sem)
    copy.start()
    copy.wait()


def middle_step_kernel(table, phase, solute, own, own_edges, picks, places, *rest):
    others = lax.axis_size("gx") - 1
    got, (phase_out, solute_out, own_out, edges_out, *rest) = rest[:others], rest[others:]
    send, (*records, ghosts, ghost_edges, rows) = rest[:others], rest[others:]
    gather_ghosts(table, got, own, own_edges, *records, ghosts, ghost_edges)
    new_phase, new_solute = add_shares(phase[...], solute[...], ghost_shares(ghosts, ghost_edges, places[...]))
    phase_out[...] = new_phase
    solute_out[...] = new_solute
    write_records(new_phase, new_solute, picks[...], own_out, edges_out, rows)
    pack(own_out, edges_out, table, send)


def last_step_kernel(table, phase, solute, own, own_edges, places, *rest):
    others = lax.axis_size("gx") - 1
    got, (phase_out, solute_out, *records, ghosts, ghost_edges, _) = rest[:others], rest[others:]
    gather_ghosts(table, got, own, own_edges, *records, ghosts, ghost_edges)
    phase_out[...], solute_out[...] = add_shares(
        phase[...], solute[...], ghost_shares(ghosts, ghost_edges, places[...])
    )


def call(kernel, in_specs, out_shapes, scratch=(), out_specs=None, mib=16):
    return pl.pallas_call(
        kernel,
        out_shape=out_shapes,
        in_specs=in_specs,
        out_specs=out_specs or jax.tree.map(lambda _: VMEM, out_shapes),
        scratch_shapes=list(scratch),
        compiler_params=pltpu.CompilerParams(vmem_limit_bytes=mib * 1024 * 1024),
    )


def shape(*dims):
    return jax.ShapeDtypeStruct(dims, F32)


def local(enthalpy, conductivity, phase, solute, tile_source, tile_block, tile_neighbour):
    count = lax.axis_size("gx")
    sizes = (lax.axis_size("gy"), lax.axis_size("gz"))
    plane_cap = -(-SLOTS // (count - 1))
    block_cap = 2 * SLOTS // count
    others = count - 1
    records = others * plane_cap
    bx, by, bz = enthalpy.shape
    picks, stencil, places, spreads = tables()

    integers = functools.partial(jax.ShapeDtypeStruct, dtype=jnp.int32)
    sides, table, asked, *farther = call(
        functools.partial(sides_kernel, sizes, plane_cap),
        [ANY] * 5,
        [
            shape(sizes[0] * sizes[1], 3 * bx, 128),
            integers((table_sizes(count, plane_cap)[2], 128)),
            shape(count, 128),
            *[shape(8, 128)] * (count - 2),
        ],
        [
            pltpu.VMEM((1, SLOTS), jnp.int32),
            pltpu.VMEM((1, SLOTS), jnp.int32),
            pltpu.VMEM((FACES, 1, SLOTS), jnp.int32),
            pltpu.VMEM((bx, by, bz), F32),
            pltpu.VMEM((bx, by, bz), F32),
            pltpu.SemaphoreType.DMA((2 * bx + 3,)),
        ],
        mib=56,
    )(
        tile_source.reshape(1, SLOTS),
        tile_block.reshape(1, SLOTS),
        jnp.transpose(tile_neighbour, (0, 1, 4, 2, 3)).reshape(FACES, 1, SLOTS),
        enthalpy,
        conductivity,
    )
    sides = lax.all_to_all(sides, ("gy", "gz"), split_axis=0, concat_axis=0, tiled=True)

    def swap_with(value, partner):
        return lax.ppermute(value, "gx", [(i, partner(i)) for i in range(count)])

    def swap_all(values):
        return [
            swap_with(value, lambda i, swap=swap: i ^ swap)
            for swap, value in zip(swap_order(count), values)
        ]

    farther = [swap_with(value, lambda i, s=s: i ^ s) for s, value in enumerate(farther, 2)]

    phase_field = phase.reshape(SLOTS, TE, PLANE)
    solute_field = solute.reshape(SLOTS, TE, PLANE)
    own_shapes = [shape(2 * SLOTS, TE, 128), shape(2 * SLOTS * 8, 128)]
    send_shapes = [shape(plane_cap * REC, 128)] * others
    rows_scratch = pltpu.VMEM((4, SLOTS * TE, 128), F32)
    packed = call(
        first_pack_kernel,
        [SMEM] + [VMEM] * 4,
        [*own_shapes, shape(count, 128), *send_shapes],
        [rows_scratch],
    )(table, asked, phase_field, solute_field, picks)
    own, asked, packed = packed[:2], packed[2], packed[3:]

    layer = shape(3 * by + 8, bz)
    first, second = call(
        functools.partial(layers_kernel, sizes), [VMEM] * 4 + [ANY] * len(farther), [layer, layer]
    )(enthalpy, conductivity, sides, asked, *farther)
    first = swap_with(first, lambda i: i ^ 1)
    second = swap_with(second, lambda i: i if i in (0, others) else ((i + 1) ^ 1) - 1)
    row = 3 * by + 4
    request = [asked[0], first[row], *[value[0] for value in farther]]
    request = jnp.stack([value[:block_cap] for value in request]).astype(jnp.int32)
    _, deep = block_layout(block_cap)
    brick = shape(bx, by, bz)
    got = swap_all(packed)
    heated, *found = call(
        functools.partial(heat_kernel, block_cap, sizes),
        [SMEM] + [VMEM] * 5,
        [brick] + [shape(deep * CB, 128)] * count,
        [pltpu.VMEM((bx, by // CB, CB, bz), F32)],
    )(request, enthalpy, conductivity, sides, first, second)
    found[1:] = swap_all(found[1:])
    (heat_out,) = call(write_out_kernel, [ANY], [brick], [pltpu.SemaphoreType.DMA], [ANY])(heated)

    field = shape(SLOTS, TE, PLANE)
    step_scratch = [
        pltpu.VMEM((records + 2 * SLOTS, TE, 128), F32),
        pltpu.VMEM(((records + 2 * SLOTS) * 8, 128), F32),
        pltpu.VMEM((SLOTS, TE, 128), F32),
        pltpu.VMEM((SLOTS, 8, 128), F32),
        rows_scratch,
    ]
    def inner(phase_field, solute_field, *heat):
        return call(
            functools.partial(inner_kernel, bool(heat)), [VMEM] * (3 + len(heat)), [field, field]
        )(phase_field, solute_field, stencil, *heat)

    inner_fields = inner(phase_field, solute_field)
    phase_field, solute_field, heat, *rest = call(
        functools.partial(first_step_kernel, block_cap),
        [SMEM] + [VMEM] * (8 + count + others),
        [field, field, shape(2, SLOTS * TE, 128), *own_shapes, *send_shapes],
        step_scratch
        + [
            pltpu.VMEM((count, deep * CB, 128), F32),
            pltpu.VMEM((SLOTS * CB, CB, 128), F32),
        ],
    )(table, phase_field, *inner_fields, *own, picks, places, spreads, *found, *got)
    own, send = rest[:2], rest[2:]
    for _ in range(PHASE_STEPS - 2):
        got = swap_all(send)
        inner_fields = inner(phase_field, solute_field, heat)
        phase_field, solute_field, *rest = call(
            middle_step_kernel,
            [SMEM] + [VMEM] * (6 + others),
            [field, field, *own_shapes, *send_shapes],
            step_scratch,
        )(table, *inner_fields, *own, picks, places, *got)
        own, send = rest[:2], rest[2:]
    got = swap_all(send)
    inner_fields = inner(phase_field, solute_field, heat)
    phase_field, solute_field = call(
        last_step_kernel, [SMEM] + [VMEM] * (5 + others), [field, field], step_scratch
    )(table, *inner_fields, *own, places, *got)
    return heat_out, phase_field.reshape(phase.shape), solute_field.reshape(solute.shape)


def solution(mesh):
    grid = P("gx", "gy", "gz")
    tiles = P("gx", "gy", "gz", None, None, None)
    return jax.shard_map(
        local,
        mesh=mesh,
        in_specs=(
            grid,
            grid,
            tiles,
            tiles,
            P("gx", "gy", "gz", None, None),
            P("gx", "gy", "gz", None),
            P("gx", "gy", "gz", None, None),
        ),
        out_specs=(grid, tiles, tiles),
        check_vma=False,
    )
```

```python
import functools

import jax
import jax.numpy as jnp
import numpy as np
from jax import lax
from jax.experimental import pallas as pl
from jax.experimental.pallas import tpu as pltpu
from jax.sharding import PartitionSpec as P

CB = 8
TE = 16
PLANE = TE * TE
SLOTS = 16
FACES = 6
PHASE_STEPS = 4
REC = 24

RATE = 0.16
ORDER_SPEED = 0.1
SOLUTE_RATE = 0.15
COUPLING = 0.5
REJECTION = 0.5

F32 = jnp.float32
BF16 = jnp.bfloat16
VMEM = pl.BlockSpec(memory_space=pltpu.VMEM)
SMEM = pl.BlockSpec(memory_space=pltpu.SMEM)
ANY = pl.BlockSpec(memory_space=pl.ANY)


def plane_lane(face):
    j = np.arange(TE)
    return [j, PLANE - TE + j, j * TE, j * TE + TE - 1][face - 2]


def constant_tables():
    pick = np.zeros((2, PLANE, 256), np.float32)
    place = np.zeros((2, 128, PLANE), np.float32)
    for field in range(2):
        for face in range(2, 6):
            at = field * 64 + (face - 2) * TE + np.arange(TE)
            pick[field, plane_lane(face ^ 1), at] = 1.0
            pick[field, plane_lane(face), 128 + at] = 1.0
            place[field, at, plane_lane(face)] = 1.0
    y, z = np.divmod(np.arange(PLANE), TE)
    dy, dz = np.abs(y[:, None] - y[None, :]), np.abs(z[:, None] - z[None, :])
    stencil = ((dy + dz) == 1).astype(np.float32)
    lane = np.arange(128)
    spread = (lane[:, None] % CB == z[None, :] // 2).astype(np.float32)
    return pick, place, stencil, spread


def tables():
    pick, place, stencil, spread = constant_tables()
    place = np.concatenate([place[0], place[1]], axis=1)
    return (
        jnp.asarray(np.concatenate([pick[0], pick[1]], axis=0), BF16),
        jnp.asarray(stencil, BF16),
        jnp.asarray(np.concatenate([place, place], axis=0), BF16),
        jnp.asarray(np.concatenate([spread, spread], axis=0), BF16),
    )


def halves(value):
    high = value.astype(BF16)
    return high, (value - high.astype(F32)).astype(BF16)


def dot(a, b):
    return jnp.dot(a, b, preferred_element_type=F32)


def temperature(h):
    return jnp.minimum(h, 0.0) + jnp.maximum(h - 1.0, 0.0)


def iota(shape, dim):
    return lax.broadcasted_iota(jnp.int32, shape, dim)


def to_lanes(column):
    bx, by, _ = column.shape
    diagonal = iota((bx, by, 128), 1) == iota((bx, by, 128), 2)
    return jnp.sum(jnp.where(diagonal, column, 0.0), axis=1)


def to_column(line, by):
    bx = line.shape[0]
    diagonal = iota((bx, by, 128), 1) == iota((bx, by, 128), 2)
    return jnp.sum(jnp.where(diagonal, line[:, None, :], 0.0), axis=2, keepdims=True)


def conduct(h, k, xlo, xhi, ylo, yhi, zlo, zhi):
    bx, by, bz = h.shape
    t = temperature(h)
    row, lane = iota((bx, by, bz), 1), iota((bx, by, bz), 2)
    if bx > 1:
        total = jnp.concatenate([xlo, t[:-1]], axis=0) + jnp.concatenate([t[1:], xhi], axis=0)
    else:
        total = xlo + xhi
    total += jnp.where(row == 0, ylo[:, None, :], pltpu.roll(t, 1, 1))
    total += jnp.where(row == by - 1, yhi[:, None, :], pltpu.roll(t, by - 1, 1))
    total += jnp.where(lane == 0, to_column(zlo, by), pltpu.roll(t, 1, 2))
    total += jnp.where(lane == bz - 1, to_column(zhi, by), pltpu.roll(t, bz - 1, 2))
    return h + RATE * k * (total - 6.0 * t)


def sublanes(value, y):
    return jnp.concatenate([value[x, y : y + 1, :] for x in range(value.shape[0])], axis=0)


def side_blocks(h, k):
    by, bz = h.shape[1:]
    return [
        (sublanes(h, 0), sublanes(h, 1), sublanes(k, 0)),
        (sublanes(h, by - 1), sublanes(h, by - 2), sublanes(k, by - 1)),
        (to_lanes(h[:, :, 0:1]), to_lanes(h[:, :, 1:2]), to_lanes(k[:, :, 0:1])),
        (to_lanes(h[:, :, bz - 1 : bz]), to_lanes(h[:, :, bz - 2 : bz - 1]), to_lanes(k[:, :, bz - 1 : bz])),
    ]


def column_of(row):
    square = (row.shape[1], row.shape[1])
    return jnp.sum(jnp.where(iota(square, 0) == iota(square, 1), row, 0.0), axis=1, keepdims=True)


def table_sizes(count, plane_cap):
    records = (count - 1) * plane_cap
    faces = min(FACES, 128 // records)
    return records, faces, 1 + -(-FACES // faces)


def swap_order(count):
    return sorted(range(1, count), key=lambda s: (-s.bit_length(), s))


def place_of(table, slot):
    return table[0, FACES * SLOTS + slot], table[0, FACES * SLOTS + SLOTS + slot]


def write_tables(plane_cap, source, block, neighbour, asked, farther, table):
    here = lax.axis_index("gx")
    me = here.astype(F32)
    count = lax.axis_size("gx")
    records, faces, _ = table_sizes(count, plane_cap)
    cap = float(plane_cap)

    def wrapped(shift):
        return jnp.where(shift < 0.0, shift + float(count), shift)

    square = (SLOTS, SLOTS)
    before = iota(square, 0) < iota(square, 1)
    slot = iota((1, SLOTS), 1).astype(F32)
    source_row, block_column = source[...].astype(F32), column_of(block[...].astype(F32))
    source_column = column_of(source_row)
    rank = jnp.sum(
        jnp.where((source_column == source_row) & before, 1.0, 0.0), axis=0, keepdims=True
    )
    rank_column = column_of(rank)
    lane = iota((SLOTS, 128), 1).astype(F32)
    for shift in range(count):
        hit = (wrapped(source_column - me) == float(shift)) & (rank_column == lane)
        row = jnp.sum(jnp.where(hit, block_column, 0.0), axis=0, keepdims=True)
        asked[shift : shift + 1, :] = row
        if 2 <= shift < count - 1:
            farther[shift - 2][...] = jnp.broadcast_to(row, (8, 128))
    at = FACES * SLOTS
    table[0:1, at : at + SLOTS] = wrapped(me - source_row).astype(jnp.int32)
    table[0:1, at + SLOTS : at + 2 * SLOTS] = rank.astype(jnp.int32)
    slot_column = iota((SLOTS, records), 0).astype(F32)
    for face in range(FACES):
        number = neighbour[face]
        owner_row, number_row = (number >> 4).astype(F32), number.astype(F32)
        owner_column, number_column = column_of(owner_row), column_of(number_row)
        other_row = (number_row >= 0.0) & (owner_row != me)
        alike = (owner_column == owner_row) & (owner_column >= 0.0) & (owner_column != me)
        receive_rank = jnp.sum(
            jnp.where(alike & (number_column < number_row), 1.0, 0.0), axis=0, keepdims=True
        )
        send_rank = jnp.sum(jnp.where(alike & before, 1.0, 0.0), axis=0, keepdims=True)
        swap = jnp.where(number < 0, 0, (number >> 4) ^ here)
        position = jnp.zeros(swap.shape, F32)
        for at, other in enumerate(swap_order(count)):
            position = jnp.where(swap == other, float(at), position)
        mine = records + (number_row - owner_row * SLOTS)
        there = position * cap + receive_rank
        receive = jnp.where(owner_row == me, mine, there)
        receive = jnp.where(number_row < 0.0, records + SLOTS + slot, receive)
        table[0:1, face * SLOTS : face * SLOTS + SLOTS] = receive.astype(jnp.int32)
        key = jnp.where(other_row, position * cap + send_rank, -1.0)
        hit = iota((SLOTS, records), 1).astype(F32) == column_of(key)
        tile = jnp.sum(jnp.where(hit, slot_column, 0.0), axis=0, keepdims=True)
        row, at = 1 + (face ^ 1) // faces, (face ^ 1) % faces * records
        table[row : row + 1, at : at + records] = tile.astype(jnp.int32)


def sides_kernel(
    sizes, plane_cap, source_far, block_far, neighbour_far, h_far, k_far, send, table, *rest
):
    asked, *farther, source, block, neighbour, h, k, sems = rest
    ny, nz = sizes
    my_y, my_z = lax.axis_index("gy"), lax.axis_index("gz")
    bx = h.shape[0]
    small = [(source_far, source), (block_far, block), (neighbour_far, neighbour)]
    copies = [pltpu.make_async_copy(*pair, sems.at[2 * bx + n]) for n, pair in enumerate(small)]
    large = []
    for x in range(bx):
        large.append(pltpu.make_async_copy(h_far.at[x], h.at[x], sems.at[x]))
        large.append(pltpu.make_async_copy(k_far.at[x], k.at[x], sems.at[bx + x]))
    for copy in copies + large:
        copy.start()
    for copy in copies:
        copy.wait()
    write_tables(plane_cap, source, block, neighbour, asked, farther, table)
    for copy in large:
        copy.wait()
    blocks = side_blocks(h[...], k[...])
    for y in range(ny):
        for z in range(nz):
            for part in range(3):
                ylo, yhi, zlo, zhi = [block[part] for block in blocks]
                chosen = jnp.where(
                    my_y == y, jnp.where(z < my_z, zlo, zhi), jnp.where(y < my_y, ylo, yhi)
                )
                send[y * nz + z, part * bx : part * bx + bx, :] = chosen


def side_reader(sizes, got, bx):
    ny, nz = sizes
    my_y, my_z = lax.axis_index("gy"), lax.axis_index("gz")

    def read(dy, dz, part=0):
        y, z = my_y + dy, my_z + dz
        inside = (y >= 0) & (y < ny) & (z >= 0) & (z < nz)
        at = jnp.where(inside, y * nz + z, 0)
        return jnp.where(inside, got[at, part * bx : part * bx + bx, :], 0.0)

    return read


def layers_kernel(sizes, h, k, got, asked, *rest):
    down, up = rest[-2:]
    bx, by, bz = h.shape
    read = side_reader(sizes, got, bx)
    around = [read(-1, 0), read(1, 0), read(0, -1), read(0, 1)]
    last = asked.shape[0] - 1
    for out, near, far, ask in ((down, 0, 1, last), (up, bx - 1, bx - 2, 1)):
        out[0:by, :] = h[near]
        out[by : 2 * by, :] = h[far]
        out[2 * by : 3 * by, :] = k[near]
        for number, side in enumerate(around):
            out[3 * by + number : 3 * by + number + 1, :] = side[near : near + 1, :]
        out[3 * by + 4 : 3 * by + 8, :] = jnp.broadcast_to(asked[ask : ask + 1, :], (4, bz))


def block_layout(cap):
    parts = 128 // CB // cap
    return parts, CB // parts


def flat_step(h, k, inner, outer, first, last, before, after, length):
    bx, lanes = h.shape
    t = temperature(h)
    row, lane = iota(h.shape, 0), iota(h.shape, 1)
    total = temperature(inner) + temperature(outer)
    total += jnp.where(row == 0, temperature(first), pltpu.roll(t, 1, 0))
    total += jnp.where(row == bx - 1, temperature(last), pltpu.roll(t, bx - 1, 0))
    total += jnp.where(lane == 0, temperature(before), pltpu.roll(t, 1, 1))
    total += jnp.where(lane == length - 1, temperature(after), pltpu.roll(t, lanes - 1, 1))
    return h + RATE * k * (total - 6.0 * t)


def heat_kernel(cap, sizes, request, h, k, got, low, high, out, found, *rest):
    *send, held = rest
    count = lax.axis_size("gx")
    bx, by, bz = h.shape
    h0, k0 = h[...], k[...]
    read = side_reader(sizes, got, bx)
    me = lax.axis_index("gx")
    layers, lines = [], []
    for beside, inside in ((low, me > 0), (high, me < count - 1)):
        beside = jnp.where(inside, beside[...], 0.0)
        layers.append([beside[part * by : part * by + by, :][None] for part in range(3)])
        lines.append([beside[3 * by + n : 3 * by + n + 1, :] for n in range(4)])
    y_sides = [[read(d, 0, part) for part in range(3)] for d in (-1, 1)]
    z_sides = [[read(0, d, part) for part in range(3)] for d in (-1, 1)]
    corner = [[read(dy, dz) for dz in (-1, 1)] for dy in (-1, 1)]
    to_first = [[pltpu.roll(c[0], 1, 1), c[1]] for c in corner]
    y_inner = [sublanes(h0, 0), sublanes(h0, by - 1)]
    z_inner = [to_lanes(h0[:, :, 0:1]), to_lanes(h0[:, :, bz - 1 : bz])]

    sides = [temperature(layers[0][0]), temperature(layers[1][0])]
    sides += [temperature(side[0]) for side in y_sides + z_sides]
    h1 = conduct(h0, k0, *sides)
    next_sides = []
    for side in range(2):
        near, far, near_k = layers[side]
        across = [temperature(far), temperature(h0[0:1])]
        if side:
            across = [temperature(h0[bx - 1 : bx]), temperature(far)]
        next_sides.append(conduct(near, near_k, *across, *[temperature(line) for line in lines[side]]))
    for side in range(2):
        near, far, near_k = y_sides[side]
        ends = [to_first[side][0], pltpu.roll(to_first[side][1], bz - 1, 1)]
        next_sides.append(
            flat_step(near, near_k, y_inner[side], far, lines[0][side], lines[1][side], *ends, bz)
        )
    for side in range(2):
        near, far, near_k = z_sides[side]
        ends = [to_first[0][side], pltpu.roll(to_first[1][side], by - 1, 1)]
        next_sides.append(
            flat_step(near, near_k, z_inner[side], far, lines[0][2 + side], lines[1][2 + side], *ends, by)
        )
    h2 = conduct(h1, k0, *[temperature(side) for side in next_sides])
    out[...] = h2

    held[...] = temperature(h2).reshape(bx, by // CB, CB, bz)
    parts, deep = block_layout(cap)
    nby, nbz = by // CB, bz // CB
    group = iota((deep, CB, bz), 2) // CB
    for shift in range(count):
        total = jnp.zeros((deep, CB, bz), F32)
        for rank in range(cap):
            block = request[(count - shift) % count, rank]
            a, b, c = block // (nby * nbz), (block // nbz) % nby, block % nbz
            for part in range(parts):
                at = rank * parts + part
                patch = held[pl.ds(a * CB + part * deep, deep), b]
                moved = pltpu.roll(patch, (CB * at - CB * c + bz) % bz, 2)
                total = jnp.where(group == at, moved, total)
        total = total.reshape(deep * CB, bz)
        (send[shift - 1] if shift else found)[...] = total


def write_records(phase, solute, picks, own, own_edges, rows):
    flat = [f.reshape(SLOTS * TE, PLANE) for f in (phase, solute)]
    high, low = halves(jnp.concatenate(flat, axis=1))
    planes = dot(high, picks) + dot(low, picks)
    own[0:SLOTS] = planes[:, 0:128].reshape(SLOTS, TE, 128)
    own[SLOTS : 2 * SLOTS] = planes[:, 128:256].reshape(SLOTS, TE, 128)
    for part in range(4):
        rows[part] = flat[part // 2][:, part % 2 * 128 : part % 2 * 128 + 128]
    for part in range(4):
        low_face = rows[part, pl.ds(0, SLOTS, TE), :]
        high_face = rows[part, pl.ds(TE - 1, SLOTS, TE), :]
        for at, value in ((0, high_face), (4, low_face)):
            own_edges[pl.ds(at + part, SLOTS, 8), :] = value
            own_edges[pl.ds(8 * SLOTS + 4 - at + part, SLOTS, 8), :] = value


def merge_record(planes, edges, number):
    side = (iota((TE, 128), 1) % 64) // TE
    out = planes[number(2)]
    for face in range(3, 6):
        out = jnp.where(side == face - 2, planes[number(face)], out)
    first, second = [edges[pl.ds(pl.multiple_of(number(face) * 8, 8), 8), :] for face in range(2)]
    return out, jnp.where(iota((8, 128), 0) < 4, first, second)


def pack(own, own_edges, table, send):
    cap = send[0].shape[0] // REC
    records, faces, _ = table_sizes(len(send) + 1, cap)
    for record in range(records):
        out, row = send[record // cap], record % cap * REC
        planes, edge = merge_record(
            own, own_edges, lambda face: table[1 + face // faces, face % faces * records + record]
        )
        out[row : row + TE, :] = planes
        out[row + TE : row + REC, :] = edge


def first_pack_kernel(table, asked, phase, solute, picks, own, own_edges, asked_out, *rest):
    *send, rows = rest
    write_records(phase[...], solute[...], picks[...], own, own_edges, rows)
    pack(own, own_edges, table, send)
    asked_out[...] = asked[...]


def take_heat(cap, table, found, spreads, blocks, held, heat):
    parts, deep = block_layout(cap)
    for number, value in enumerate(found):
        blocks[number] = value[...]
    group = iota((CB, 128), 1) // CB
    for slot in range(SLOTS):
        back, rank = place_of(table, slot)
        for x in range(CB):
            row = (x % deep) * CB
            patch = blocks[back, row : row + CB, :]
            held[slot * CB + x] = jnp.where(group == rank * parts + x // deep, patch, 0.0)
    rows = held[...].reshape(SLOTS * CB * CB, 128)
    wide = dot(jnp.concatenate(halves(rows), axis=1), spreads)
    wide = wide.reshape(SLOTS * CB, CB, PLANE)
    keep = iota(wide.shape, 1) == iota(wide.shape, 2) // TE // 2
    coarse = jnp.sum(jnp.where(keep, wide, 0.0), axis=1)
    for half in range(2):
        for odd in range(2):
            heat[half, pl.ds(odd, SLOTS * CB, 2), :] = coarse[:, half * 128 : half * 128 + 128]


def inner_step(phase, solute, heat, stencil):
    row = iota((SLOTS, TE, PLANE), 1)
    lap = []
    for field in (phase, solute):
        high, low = halves(field.reshape(SLOTS * TE, PLANE))
        total = (dot(high, stencil) + dot(low, stencil)).reshape(SLOTS, TE, PLANE) - 6.0 * field
        total += jnp.where(row == 0, 0.0, pltpu.roll(field, 1, 1))
        total += jnp.where(row == TE - 1, 0.0, pltpu.roll(field, TE - 1, 1))
        lap.append(total)
    squared = 1.0 - phase * phase
    drive = solute if heat is None else heat + solute
    change = ORDER_SPEED * (
        lap[0] + phase - phase * phase * phase - COUPLING * drive * squared * squared
    )
    return phase + change, solute + SOLUTE_RATE * lap[1] + REJECTION * change


def wide_heat(heat):
    return jnp.concatenate([heat[0], heat[1]], axis=1).reshape(SLOTS, TE, PLANE)


def gather_ghosts(table, got, own, own_edges, planes, edges, ghosts, ghost_edges):
    records = planes.shape[0] - 2 * SLOTS
    cap = records // len(got)
    for record in range(records):
        value, row = got[record // cap], record % cap * REC
        planes[record] = value[row : row + TE, :]
        edges[record * 8 : record * 8 + 8, :] = value[row + TE : row + REC, :]
    planes[records:] = own[...]
    edges[records * 8 :, :] = own_edges[...]
    for slot in range(SLOTS):
        out, edge = merge_record(planes, edges, lambda face: table[0, face * SLOTS + slot])
        ghosts[slot] = out
        ghost_edges[slot] = edge


def ghost_shares(ghosts, ghost_edges, places):
    beside = jnp.concatenate(halves(ghosts[...].reshape(SLOTS * TE, 128)), axis=1)
    beside = dot(beside, places)
    half = TE // 2
    rows = iota((SLOTS, half, PLANE), 1)
    shares = []
    for number in range(2):
        share = beside[:, number * PLANE : number * PLANE + PLANE].reshape(SLOTS, TE, PLANE)
        parts = []
        for face, at_row in ((0, 0), (1, half - 1)):
            at = face * 4 + number * 2
            side = [ghost_edges[:, row : row + 1, :] for row in (at, at + 1)]
            side = jnp.where(rows == at_row, jnp.concatenate(side, axis=2), 0.0)
            parts.append(share[:, face * half : face * half + half] + side)
        shares.append(jnp.concatenate(parts, axis=1))
    return shares


def add_shares(phase, solute, shares, heat_share=None):
    change = ORDER_SPEED * shares[0]
    if heat_share is not None:
        change += heat_share
    return phase + change, solute + SOLUTE_RATE * shares[1] + REJECTION * change


def inner_kernel(has_heat, phase, solute, stencil, *rest):
    phase_out, solute_out = rest[-2:]
    heat = wide_heat(rest[0]) if has_heat else None
    phase_out[...], solute_out[...] = inner_step(phase[...], solute[...], heat, stencil[...])


def first_step_kernel(cap, table, old_phase, phase, solute, own, own_edges, picks, places, spreads, *rest):
    others = lax.axis_size("gx") - 1
    found, got, rest = rest[: others + 1], rest[others + 1 : 2 * others + 1], rest[2 * others + 1 :]
    phase_out, solute_out, heat_out, own_out, edges_out, *rest = rest
    send, (*records, ghosts, ghost_edges, rows, blocks, held) = rest[:others], rest[others:]
    take_heat(cap, table, found, spreads[...], blocks, held, heat_out)
    gather_ghosts(table, got, own, own_edges, *records, ghosts, ghost_edges)
    squared = 1.0 - old_phase[...] * old_phase[...]
    heat_share = (-ORDER_SPEED * COUPLING) * wide_heat(heat_out) * squared * squared
    new_phase, new_solute = add_shares(
        phase[...], solute[...], ghost_shares(ghosts, ghost_edges, places[...]), heat_share
    )
    phase_out[...] = new_phase
    solute_out[...] = new_solute
    write_records(new_phase, new_solute, picks[...], own_out, edges_out, rows)
    pack(own_out, edges_out, table, send)


def write_out_kernel(value, out, sem):
    copy = pltpu.make_async_copy(value, out, sem)
    copy.start()
    copy.wait()


def middle_step_kernel(table, phase, solute, own, own_edges, picks, places, *rest):
    others = lax.axis_size("gx") - 1
    got, (phase_out, solute_out, own_out, edges_out, *rest) = rest[:others], rest[others:]
    send, (*records, ghosts, ghost_edges, rows) = rest[:others], rest[others:]
    gather_ghosts(table, got, own, own_edges, *records, ghosts, ghost_edges)
    new_phase, new_solute = add_shares(phase[...], solute[...], ghost_shares(ghosts, ghost_edges, places[...]))
    phase_out[...] = new_phase
    solute_out[...] = new_solute
    write_records(new_phase, new_solute, picks[...], own_out, edges_out, rows)
    pack(own_out, edges_out, table, send)


def last_step_kernel(table, phase, solute, own, own_edges, places, *rest):
    others = lax.axis_size("gx") - 1
    got, (phase_out, solute_out, *records, ghosts, ghost_edges, _) = rest[:others], rest[others:]
    gather_ghosts(table, got, own, own_edges, *records, ghosts, ghost_edges)
    phase_out[...], solute_out[...] = add_shares(
        phase[...], solute[...], ghost_shares(ghosts, ghost_edges, places[...])
    )


def call(kernel, in_specs, out_shapes, scratch=(), out_specs=None, mib=16):
    return pl.pallas_call(
        kernel,
        out_shape=out_shapes,
        in_specs=in_specs,
        out_specs=out_specs or jax.tree.map(lambda _: VMEM, out_shapes),
        scratch_shapes=list(scratch),
        compiler_params=pltpu.CompilerParams(vmem_limit_bytes=mib * 1024 * 1024),
    )


def shape(*dims):
    return jax.ShapeDtypeStruct(dims, F32)


def local(enthalpy, conductivity, phase, solute, tile_source, tile_block, tile_neighbour):
    count = lax.axis_size("gx")
    sizes = (lax.axis_size("gy"), lax.axis_size("gz"))
    plane_cap = -(-SLOTS // (count - 1))
    block_cap = 2 * SLOTS // count
    others = count - 1
    records = others * plane_cap
    bx, by, bz = enthalpy.shape
    picks, stencil, places, spreads = tables()

    integers = functools.partial(jax.ShapeDtypeStruct, dtype=jnp.int32)
    sides, table, asked, *farther = call(
        functools.partial(sides_kernel, sizes, plane_cap),
        [ANY] * 5,
        [
            shape(sizes[0] * sizes[1], 3 * bx, 128),
            integers((table_sizes(count, plane_cap)[2], 128)),
            shape(count, 128),
            *[shape(8, 128)] * (count - 3),
        ],
        [
            pltpu.VMEM((1, SLOTS), jnp.int32),
            pltpu.VMEM((1, SLOTS), jnp.int32),
            pltpu.VMEM((FACES, 1, SLOTS), jnp.int32),
            pltpu.VMEM((bx, by, bz), F32),
            pltpu.VMEM((bx, by, bz), F32),
            pltpu.SemaphoreType.DMA((2 * bx + 3,)),
        ],
        mib=56,
    )(
        tile_source.reshape(1, SLOTS),
        tile_block.reshape(1, SLOTS),
        jnp.transpose(tile_neighbour, (0, 1, 4, 2, 3)).reshape(FACES, 1, SLOTS),
        enthalpy,
        conductivity,
    )
    sides = lax.all_to_all(sides, ("gy", "gz"), split_axis=0, concat_axis=0, tiled=True)

    def pass_on(value, shift):
        return lax.ppermute(value, "gx", [(i, (i + shift) % count) for i in range(count)])

    def exchange(values):
        return [pass_on(value, shift) for shift, value in enumerate(values, 1)]

    def swap_all(values):
        return [
            lax.ppermute(value, "gx", [(i, i ^ swap) for i in range(count)])
            for swap, value in zip(swap_order(count), values)
        ]

    farther = [pass_on(value, shift) for shift, value in enumerate(farther, 2)]

    phase_field = phase.reshape(SLOTS, TE, PLANE)
    solute_field = solute.reshape(SLOTS, TE, PLANE)
    own_shapes = [shape(2 * SLOTS, TE, 128), shape(2 * SLOTS * 8, 128)]
    send_shapes = [shape(plane_cap * REC, 128)] * others
    rows_scratch = pltpu.VMEM((4, SLOTS * TE, 128), F32)
    packed = call(
        first_pack_kernel,
        [SMEM] + [VMEM] * 4,
        [*own_shapes, shape(count, 128), *send_shapes],
        [rows_scratch],
    )(table, asked, phase_field, solute_field, picks)
    own, asked, packed = packed[:2], packed[2], packed[3:]

    layer = shape(3 * by + 8, bz)
    down, up = call(
        functools.partial(layers_kernel, sizes), [VMEM] * 4 + [ANY] * len(farther), [layer, layer]
    )(enthalpy, conductivity, sides, asked, *farther)
    from_low, from_high = pass_on(up, 1), pass_on(down, others)
    row = 3 * by + 4
    request = [asked[0], from_low[row], *[value[0] for value in farther], from_high[row]]
    request = jnp.stack([value[:block_cap] for value in request]).astype(jnp.int32)
    _, deep = block_layout(block_cap)
    brick = shape(bx, by, bz)
    got = swap_all(packed)
    heated, *found = call(
        functools.partial(heat_kernel, block_cap, sizes),
        [SMEM] + [VMEM] * 5,
        [brick] + [shape(deep * CB, 128)] * count,
        [pltpu.VMEM((bx, by // CB, CB, bz), F32)],
    )(request, enthalpy, conductivity, sides, from_low, from_high)
    found[1:] = exchange(found[1:])
    (heat_out,) = call(write_out_kernel, [ANY], [brick], [pltpu.SemaphoreType.DMA], [ANY])(heated)

    field = shape(SLOTS, TE, PLANE)
    step_scratch = [
        pltpu.VMEM((records + 2 * SLOTS, TE, 128), F32),
        pltpu.VMEM(((records + 2 * SLOTS) * 8, 128), F32),
        pltpu.VMEM((SLOTS, TE, 128), F32),
        pltpu.VMEM((SLOTS, 8, 128), F32),
        rows_scratch,
    ]
    def inner(phase_field, solute_field, *heat):
        return call(
            functools.partial(inner_kernel, bool(heat)), [VMEM] * (3 + len(heat)), [field, field]
        )(phase_field, solute_field, stencil, *heat)

    inner_fields = inner(phase_field, solute_field)
    phase_field, solute_field, heat, *rest = call(
        functools.partial(first_step_kernel, block_cap),
        [SMEM] + [VMEM] * (8 + count + others),
        [field, field, shape(2, SLOTS * TE, 128), *own_shapes, *send_shapes],
        step_scratch
        + [
            pltpu.VMEM((count, deep * CB, 128), F32),
            pltpu.VMEM((SLOTS * CB, CB, 128), F32),
        ],
    )(table, phase_field, *inner_fields, *own, picks, places, spreads, *found, *got)
    own, send = rest[:2], rest[2:]
    for _ in range(PHASE_STEPS - 2):
        got = swap_all(send)
        inner_fields = inner(phase_field, solute_field, heat)
        phase_field, solute_field, *rest = call(
            middle_step_kernel,
            [SMEM] + [VMEM] * (6 + others),
            [field, field, *own_shapes, *send_shapes],
            step_scratch,
        )(table, *inner_fields, *own, picks, places, *got)
        own, send = rest[:2], rest[2:]
    got = swap_all(send)
    inner_fields = inner(phase_field, solute_field, heat)
    phase_field, solute_field = call(
        last_step_kernel, [SMEM] + [VMEM] * (5 + others), [field, field], step_scratch
    )(table, *inner_fields, *own, places, *got)
    return heat_out, phase_field.reshape(phase.shape), solute_field.reshape(solute.shape)


def solution(mesh):
    grid = P("gx", "gy", "gz")
    tiles = P("gx", "gy", "gz", None, None, None)
    return jax.shard_map(
        local,
        mesh=mesh,
        in_specs=(
            grid,
            grid,
            tiles,
            tiles,
            P("gx", "gy", "gz", None, None),
            P("gx", "gy", "gz", None),
            P("gx", "gy", "gz", None, None),
        ),
        out_specs=(grid, tiles, tiles),
        check_vma=False,
    )
```

```python
import functools

import jax
import jax.numpy as jnp
import numpy as np
from jax import lax
from jax.experimental import pallas as pl
from jax.experimental.pallas import tpu as pltpu
from jax.sharding import PartitionSpec as P

CB = 8
TE = 16
PLANE = TE * TE
SLOTS = 16
FACES = 6
PHASE_STEPS = 4
REC = 24

RATE = 0.16
ORDER_SPEED = 0.1
SOLUTE_RATE = 0.15
COUPLING = 0.5
REJECTION = 0.5

F32 = jnp.float32
BF16 = jnp.bfloat16
VMEM = pl.BlockSpec(memory_space=pltpu.VMEM)
SMEM = pl.BlockSpec(memory_space=pltpu.SMEM)
ANY = pl.BlockSpec(memory_space=pl.ANY)


def plane_lane(face):
    j = np.arange(TE)
    return [j, PLANE - TE + j, j * TE, j * TE + TE - 1][face - 2]


def constant_tables():
    pick = np.zeros((2, PLANE, 256), np.float32)
    place = np.zeros((2, 128, PLANE), np.float32)
    for field in range(2):
        for face in range(2, 6):
            at = field * 64 + (face - 2) * TE + np.arange(TE)
            pick[field, plane_lane(face ^ 1), at] = 1.0
            pick[field, plane_lane(face), 128 + at] = 1.0
            place[field, at, plane_lane(face)] = 1.0
    y, z = np.divmod(np.arange(PLANE), TE)
    dy, dz = np.abs(y[:, None] - y[None, :]), np.abs(z[:, None] - z[None, :])
    stencil = ((dy + dz) == 1).astype(np.float32)
    lane = np.arange(128)
    spread = (lane[:, None] % CB == z[None, :] // 2).astype(np.float32)
    return pick, place, stencil, spread


def tables():
    pick, place, stencil, spread = constant_tables()
    place = np.concatenate([place[0], place[1]], axis=1)
    return (
        jnp.asarray(np.concatenate([pick[0], pick[1]], axis=0), BF16),
        jnp.asarray(stencil, BF16),
        jnp.asarray(np.concatenate([place, place], axis=0), BF16),
        jnp.asarray(np.concatenate([spread, spread], axis=0), BF16),
    )


def halves(value):
    high = value.astype(BF16)
    return high, (value - high.astype(F32)).astype(BF16)


def dot(a, b):
    return jnp.dot(a, b, preferred_element_type=F32)


def temperature(h):
    return jnp.minimum(h, 0.0) + jnp.maximum(h - 1.0, 0.0)


def iota(shape, dim):
    return lax.broadcasted_iota(jnp.int32, shape, dim)


def to_lanes(column):
    bx, by, _ = column.shape
    diagonal = iota((bx, by, 128), 1) == iota((bx, by, 128), 2)
    return jnp.sum(jnp.where(diagonal, column, 0.0), axis=1)


def to_column(line, by):
    bx = line.shape[0]
    diagonal = iota((bx, by, 128), 1) == iota((bx, by, 128), 2)
    return jnp.sum(jnp.where(diagonal, line[:, None, :], 0.0), axis=2, keepdims=True)


def conduct(h, k, xlo, xhi, ylo, yhi, zlo, zhi):
    bx, by, bz = h.shape
    t = temperature(h)
    row, lane = iota((bx, by, bz), 1), iota((bx, by, bz), 2)
    if bx > 1:
        total = jnp.concatenate([xlo, t[:-1]], axis=0) + jnp.concatenate([t[1:], xhi], axis=0)
    else:
        total = xlo + xhi
    total += jnp.where(row == 0, ylo[:, None, :], pltpu.roll(t, 1, 1))
    total += jnp.where(row == by - 1, yhi[:, None, :], pltpu.roll(t, by - 1, 1))
    total += jnp.where(lane == 0, to_column(zlo, by), pltpu.roll(t, 1, 2))
    total += jnp.where(lane == bz - 1, to_column(zhi, by), pltpu.roll(t, bz - 1, 2))
    return h + RATE * k * (total - 6.0 * t)


def sublanes(value, y):
    return jnp.concatenate([value[x, y : y + 1, :] for x in range(value.shape[0])], axis=0)


def side_blocks(h, k):
    by, bz = h.shape[1:]
    return [
        (sublanes(h, 0), sublanes(h, 1), sublanes(k, 0)),
        (sublanes(h, by - 1), sublanes(h, by - 2), sublanes(k, by - 1)),
        (to_lanes(h[:, :, 0:1]), to_lanes(h[:, :, 1:2]), to_lanes(k[:, :, 0:1])),
        (to_lanes(h[:, :, bz - 1 : bz]), to_lanes(h[:, :, bz - 2 : bz - 1]), to_lanes(k[:, :, bz - 1 : bz])),
    ]


def column_of(row):
    square = (row.shape[1], row.shape[1])
    return jnp.sum(jnp.where(iota(square, 0) == iota(square, 1), row, 0.0), axis=1, keepdims=True)


def table_sizes(count, plane_cap):
    records = (count - 1) * plane_cap
    faces = min(FACES, 128 // records)
    return records, faces, 1 + -(-FACES // faces)


def swap_order(count):
    return list(range(count - 1, 0, -1))


def place_of(table, slot):
    return table[0, FACES * SLOTS + slot], table[0, FACES * SLOTS + SLOTS + slot]


def write_tables(plane_cap, source, block, neighbour, asked, farther, table):
    here = lax.axis_index("gx")
    me = here.astype(F32)
    count = lax.axis_size("gx")
    records, faces, _ = table_sizes(count, plane_cap)
    cap = float(plane_cap)

    def wrapped(shift):
        return jnp.where(shift < 0.0, shift + float(count), shift)

    square = (SLOTS, SLOTS)
    before = iota(square, 0) < iota(square, 1)
    slot = iota((1, SLOTS), 1).astype(F32)
    source_row, block_column = source[...].astype(F32), column_of(block[...].astype(F32))
    source_column = column_of(source_row)
    rank = jnp.sum(
        jnp.where((source_column == source_row) & before, 1.0, 0.0), axis=0, keepdims=True
    )
    rank_column = column_of(rank)
    lane = iota((SLOTS, 128), 1).astype(F32)
    for shift in range(count):
        hit = (wrapped(source_column - me) == float(shift)) & (rank_column == lane)
        row = jnp.sum(jnp.where(hit, block_column, 0.0), axis=0, keepdims=True)
        asked[shift : shift + 1, :] = row
        if 2 <= shift < count - 1:
            farther[shift - 2][...] = jnp.broadcast_to(row, (8, 128))
    at = FACES * SLOTS
    table[0:1, at : at + SLOTS] = wrapped(me - source_row).astype(jnp.int32)
    table[0:1, at + SLOTS : at + 2 * SLOTS] = rank.astype(jnp.int32)
    slot_column = iota((SLOTS, records), 0).astype(F32)
    for face in range(FACES):
        number = neighbour[face]
        owner_row, number_row = (number >> 4).astype(F32), number.astype(F32)
        owner_column, number_column = column_of(owner_row), column_of(number_row)
        other_row = (number_row >= 0.0) & (owner_row != me)
        alike = (owner_column == owner_row) & (owner_column >= 0.0) & (owner_column != me)
        receive_rank = jnp.sum(
            jnp.where(alike & (number_column < number_row), 1.0, 0.0), axis=0, keepdims=True
        )
        send_rank = jnp.sum(jnp.where(alike & before, 1.0, 0.0), axis=0, keepdims=True)
        swap = jnp.where(number < 0, 0, (number >> 4) ^ here)
        position = jnp.zeros(swap.shape, F32)
        for at, other in enumerate(swap_order(count)):
            position = jnp.where(swap == other, float(at), position)
        mine = records + (number_row - owner_row * SLOTS)
        there = position * cap + receive_rank
        receive = jnp.where(owner_row == me, mine, there)
        receive = jnp.where(number_row < 0.0, records + SLOTS + slot, receive)
        table[0:1, face * SLOTS : face * SLOTS + SLOTS] = receive.astype(jnp.int32)
        key = jnp.where(other_row, position * cap + send_rank, -1.0)
        hit = iota((SLOTS, records), 1).astype(F32) == column_of(key)
        tile = jnp.sum(jnp.where(hit, slot_column, 0.0), axis=0, keepdims=True)
        row, at = 1 + (face ^ 1) // faces, (face ^ 1) % faces * records
        table[row : row + 1, at : at + records] = tile.astype(jnp.int32)


def sides_kernel(
    sizes, plane_cap, source_far, block_far, neighbour_far, h_far, k_far, send, table, *rest
):
    asked, *farther, source, block, neighbour, h, k, sems = rest
    ny, nz = sizes
    my_y, my_z = lax.axis_index("gy"), lax.axis_index("gz")
    bx = h.shape[0]
    small = [(source_far, source), (block_far, block), (neighbour_far, neighbour)]
    copies = [pltpu.make_async_copy(*pair, sems.at[2 * bx + n]) for n, pair in enumerate(small)]
    large = []
    for x in range(bx):
        large.append(pltpu.make_async_copy(h_far.at[x], h.at[x], sems.at[x]))
        large.append(pltpu.make_async_copy(k_far.at[x], k.at[x], sems.at[bx + x]))
    for copy in copies + large:
        copy.start()
    for copy in copies:
        copy.wait()
    write_tables(plane_cap, source, block, neighbour, asked, farther, table)
    for copy in large:
        copy.wait()
    blocks = side_blocks(h[...], k[...])
    for y in range(ny):
        for z in range(nz):
            for part in range(3):
                ylo, yhi, zlo, zhi = [block[part] for block in blocks]
                chosen = jnp.where(
                    my_y == y, jnp.where(z < my_z, zlo, zhi), jnp.where(y < my_y, ylo, yhi)
                )
                send[y * nz + z, part * bx : part * bx + bx, :] = chosen


def side_reader(sizes, got, bx):
    ny, nz = sizes
    my_y, my_z = lax.axis_index("gy"), lax.axis_index("gz")

    def read(dy, dz, part=0):
        y, z = my_y + dy, my_z + dz
        inside = (y >= 0) & (y < ny) & (z >= 0) & (z < nz)
        at = jnp.where(inside, y * nz + z, 0)
        return jnp.where(inside, got[at, part * bx : part * bx + bx, :], 0.0)

    return read


def layers_kernel(sizes, h, k, got, asked, *rest):
    down, up = rest[-2:]
    bx, by, bz = h.shape
    read = side_reader(sizes, got, bx)
    around = [read(-1, 0), read(1, 0), read(0, -1), read(0, 1)]
    last = asked.shape[0] - 1
    for out, near, far, ask in ((down, 0, 1, last), (up, bx - 1, bx - 2, 1)):
        out[0:by, :] = h[near]
        out[by : 2 * by, :] = h[far]
        out[2 * by : 3 * by, :] = k[near]
        for number, side in enumerate(around):
            out[3 * by + number : 3 * by + number + 1, :] = side[near : near + 1, :]
        out[3 * by + 4 : 3 * by + 8, :] = jnp.broadcast_to(asked[ask : ask + 1, :], (4, bz))


def block_layout(cap):
    parts = 128 // CB // cap
    return parts, CB // parts


def flat_step(h, k, inner, outer, first, last, before, after, length):
    bx, lanes = h.shape
    t = temperature(h)
    row, lane = iota(h.shape, 0), iota(h.shape, 1)
    total = temperature(inner) + temperature(outer)
    total += jnp.where(row == 0, temperature(first), pltpu.roll(t, 1, 0))
    total += jnp.where(row == bx - 1, temperature(last), pltpu.roll(t, bx - 1, 0))
    total += jnp.where(lane == 0, temperature(before), pltpu.roll(t, 1, 1))
    total += jnp.where(lane == length - 1, temperature(after), pltpu.roll(t, lanes - 1, 1))
    return h + RATE * k * (total - 6.0 * t)


def heat_kernel(cap, sizes, request, h, k, got, low, high, out, found, *rest):
    *send, held = rest
    count = lax.axis_size("gx")
    bx, by, bz = h.shape
    h0, k0 = h[...], k[...]
    read = side_reader(sizes, got, bx)
    me = lax.axis_index("gx")
    layers, lines = [], []
    for beside, inside in ((low, me > 0), (high, me < count - 1)):
        beside = jnp.where(inside, beside[...], 0.0)
        layers.append([beside[part * by : part * by + by, :][None] for part in range(3)])
        lines.append([beside[3 * by + n : 3 * by + n + 1, :] for n in range(4)])
    y_sides = [[read(d, 0, part) for part in range(3)] for d in (-1, 1)]
    z_sides = [[read(0, d, part) for part in range(3)] for d in (-1, 1)]
    corner = [[read(dy, dz) for dz in (-1, 1)] for dy in (-1, 1)]
    to_first = [[pltpu.roll(c[0], 1, 1), c[1]] for c in corner]
    y_inner = [sublanes(h0, 0), sublanes(h0, by - 1)]
    z_inner = [to_lanes(h0[:, :, 0:1]), to_lanes(h0[:, :, bz - 1 : bz])]

    sides = [temperature(layers[0][0]), temperature(layers[1][0])]
    sides += [temperature(side[0]) for side in y_sides + z_sides]
    h1 = conduct(h0, k0, *sides)
    next_sides = []
    for side in range(2):
        near, far, near_k = layers[side]
        across = [temperature(far), temperature(h0[0:1])]
        if side:
            across = [temperature(h0[bx - 1 : bx]), temperature(far)]
        next_sides.append(conduct(near, near_k, *across, *[temperature(line) for line in lines[side]]))
    for side in range(2):
        near, far, near_k = y_sides[side]
        ends = [to_first[side][0], pltpu.roll(to_first[side][1], bz - 1, 1)]
        next_sides.append(
            flat_step(near, near_k, y_inner[side], far, lines[0][side], lines[1][side], *ends, bz)
        )
    for side in range(2):
        near, far, near_k = z_sides[side]
        ends = [to_first[0][side], pltpu.roll(to_first[1][side], by - 1, 1)]
        next_sides.append(
            flat_step(near, near_k, z_inner[side], far, lines[0][2 + side], lines[1][2 + side], *ends, by)
        )
    h2 = conduct(h1, k0, *[temperature(side) for side in next_sides])
    out[...] = h2

    held[...] = temperature(h2).reshape(bx, by // CB, CB, bz)
    parts, deep = block_layout(cap)
    nby, nbz = by // CB, bz // CB
    group = iota((deep, CB, bz), 2) // CB
    for shift in range(count):
        total = jnp.zeros((deep, CB, bz), F32)
        for rank in range(cap):
            block = request[(count - shift) % count, rank]
            a, b, c = block // (nby * nbz), (block // nbz) % nby, block % nbz
            for part in range(parts):
                at = rank * parts + part
                patch = held[pl.ds(a * CB + part * deep, deep), b]
                moved = pltpu.roll(patch, (CB * at - CB * c + bz) % bz, 2)
                total = jnp.where(group == at, moved, total)
        total = total.reshape(deep * CB, bz)
        (send[shift - 1] if shift else found)[...] = total


def write_records(phase, solute, picks, own, own_edges, rows):
    flat = [f.reshape(SLOTS * TE, PLANE) for f in (phase, solute)]
    high, low = halves(jnp.concatenate(flat, axis=1))
    planes = dot(high, picks) + dot(low, picks)
    own[0:SLOTS] = planes[:, 0:128].reshape(SLOTS, TE, 128)
    own[SLOTS : 2 * SLOTS] = planes[:, 128:256].reshape(SLOTS, TE, 128)
    for part in range(4):
        rows[part] = flat[part // 2][:, part % 2 * 128 : part % 2 * 128 + 128]
    for part in range(4):
        low_face = rows[part, pl.ds(0, SLOTS, TE), :]
        high_face = rows[part, pl.ds(TE - 1, SLOTS, TE), :]
        for at, value in ((0, high_face), (4, low_face)):
            own_edges[pl.ds(at + part, SLOTS, 8), :] = value
            own_edges[pl.ds(8 * SLOTS + 4 - at + part, SLOTS, 8), :] = value


def merge_record(planes, edges, number):
    side = (iota((TE, 128), 1) % 64) // TE
    out = planes[number(2)]
    for face in range(3, 6):
        out = jnp.where(side == face - 2, planes[number(face)], out)
    first, second = [edges[pl.ds(pl.multiple_of(number(face) * 8, 8), 8), :] for face in range(2)]
    return out, jnp.where(iota((8, 128), 0) < 4, first, second)


def pack(own, own_edges, table, send):
    cap = send[0].shape[0] // REC
    records, faces, _ = table_sizes(len(send) + 1, cap)
    for record in range(records):
        out, row = send[record // cap], record % cap * REC
        planes, edge = merge_record(
            own, own_edges, lambda face: table[1 + face // faces, face % faces * records + record]
        )
        out[row : row + TE, :] = planes
        out[row + TE : row + REC, :] = edge


def first_pack_kernel(table, asked, phase, solute, picks, own, own_edges, asked_out, *rest):
    *send, rows = rest
    write_records(phase[...], solute[...], picks[...], own, own_edges, rows)
    pack(own, own_edges, table, send)
    asked_out[...] = asked[...]


def take_heat(cap, table, found, spreads, blocks, held, heat):
    parts, deep = block_layout(cap)
    for number, value in enumerate(found):
        blocks[number] = value[...]
    group = iota((CB, 128), 1) // CB
    for slot in range(SLOTS):
        back, rank = place_of(table, slot)
        for x in range(CB):
            row = (x % deep) * CB
            patch = blocks[back, row : row + CB, :]
            held[slot * CB + x] = jnp.where(group == rank * parts + x // deep, patch, 0.0)
    rows = held[...].reshape(SLOTS * CB * CB, 128)
    wide = dot(jnp.concatenate(halves(rows), axis=1), spreads)
    wide = wide.reshape(SLOTS * CB, CB, PLANE)
    keep = iota(wide.shape, 1) == iota(wide.shape, 2) // TE // 2
    coarse = jnp.sum(jnp.where(keep, wide, 0.0), axis=1)
    for half in range(2):
        for odd in range(2):
            heat[half, pl.ds(odd, SLOTS * CB, 2), :] = coarse[:, half * 128 : half * 128 + 128]


def inner_step(phase, solute, heat, stencil):
    row = iota((SLOTS, TE, PLANE), 1)
    lap = []
    for field in (phase, solute):
        high, low = halves(field.reshape(SLOTS * TE, PLANE))
        total = (dot(high, stencil) + dot(low, stencil)).reshape(SLOTS, TE, PLANE) - 6.0 * field
        total += jnp.where(row == 0, 0.0, pltpu.roll(field, 1, 1))
        total += jnp.where(row == TE - 1, 0.0, pltpu.roll(field, TE - 1, 1))
        lap.append(total)
    squared = 1.0 - phase * phase
    drive = solute if heat is None else heat + solute
    change = ORDER_SPEED * (
        lap[0] + phase - phase * phase * phase - COUPLING * drive * squared * squared
    )
    return phase + change, solute + SOLUTE_RATE * lap[1] + REJECTION * change


def wide_heat(heat):
    return jnp.concatenate([heat[0], heat[1]], axis=1).reshape(SLOTS, TE, PLANE)


def gather_ghosts(table, got, own, own_edges, planes, edges, ghosts, ghost_edges):
    records = planes.shape[0] - 2 * SLOTS
    cap = records // len(got)
    for record in range(records):
        value, row = got[record // cap], record % cap * REC
        planes[record] = value[row : row + TE, :]
        edges[record * 8 : record * 8 + 8, :] = value[row + TE : row + REC, :]
    planes[records:] = own[...]
    edges[records * 8 :, :] = own_edges[...]
    for slot in range(SLOTS):
        out, edge = merge_record(planes, edges, lambda face: table[0, face * SLOTS + slot])
        ghosts[slot] = out
        ghost_edges[slot] = edge


def ghost_shares(ghosts, ghost_edges, places):
    beside = jnp.concatenate(halves(ghosts[...].reshape(SLOTS * TE, 128)), axis=1)
    beside = dot(beside, places)
    rows = iota((SLOTS, TE, PLANE), 1)
    shares = []
    for number in range(2):
        share = beside[:, number * PLANE : number * PLANE + PLANE].reshape(SLOTS, TE, PLANE)
        for face, at_row in ((0, 0), (1, TE - 1)):
            at = face * 4 + number * 2
            side = [ghost_edges[:, row : row + 1, :] for row in (at, at + 1)]
            side = jnp.concatenate(side, axis=2)
            share += jnp.where(rows == at_row, side, 0.0)
        shares.append(share)
    return shares


def add_shares(phase, solute, shares, heat_share=None):
    change = ORDER_SPEED * shares[0]
    if heat_share is not None:
        change += heat_share
    return phase + change, solute + SOLUTE_RATE * shares[1] + REJECTION * change


def inner_kernel(has_heat, phase, solute, stencil, *rest):
    phase_out, solute_out = rest[-2:]
    heat = wide_heat(rest[0]) if has_heat else None
    phase_out[...], solute_out[...] = inner_step(phase[...], solute[...], heat, stencil[...])


def first_step_kernel(cap, table, old_phase, phase, solute, own, own_edges, picks, places, spreads, *rest):
    others = lax.axis_size("gx") - 1
    found, got, rest = rest[: others + 1], rest[others + 1 : 2 * others + 1], rest[2 * others + 1 :]
    phase_out, solute_out, heat_out, own_out, edges_out, *rest = rest
    send, (*records, ghosts, ghost_edges, rows, blocks, held) = rest[:others], rest[others:]
    take_heat(cap, table, found, spreads[...], blocks, held, heat_out)
    gather_ghosts(table, got, own, own_edges, *records, ghosts, ghost_edges)
    squared = 1.0 - old_phase[...] * old_phase[...]
    heat_share = (-ORDER_SPEED * COUPLING) * wide_heat(heat_out) * squared * squared
    new_phase, new_solute = add_shares(
        phase[...], solute[...], ghost_shares(ghosts, ghost_edges, places[...]), heat_share
    )
    phase_out[...] = new_phase
    solute_out[...] = new_solute
    write_records(new_phase, new_solute, picks[...], own_out, edges_out, rows)
    pack(own_out, edges_out, table, send)


def write_out_kernel(value, out, sem):
    copy = pltpu.make_async_copy(value, out, sem)
    copy.start()
    copy.wait()


def middle_step_kernel(table, phase, solute, own, own_edges, picks, places, *rest):
    others = lax.axis_size("gx") - 1
    got, (phase_out, solute_out, own_out, edges_out, *rest) = rest[:others], rest[others:]
    send, (*records, ghosts, ghost_edges, rows) = rest[:others], rest[others:]
    gather_ghosts(table, got, own, own_edges, *records, ghosts, ghost_edges)
    new_phase, new_solute = add_shares(phase[...], solute[...], ghost_shares(ghosts, ghost_edges, places[...]))
    phase_out[...] = new_phase
    solute_out[...] = new_solute
    write_records(new_phase, new_solute, picks[...], own_out, edges_out, rows)
    pack(own_out, edges_out, table, send)


def last_step_kernel(table, phase, solute, own, own_edges, places, *rest):
    others = lax.axis_size("gx") - 1
    got, (phase_out, solute_out, *records, ghosts, ghost_edges, _) = rest[:others], rest[others:]
    gather_ghosts(table, got, own, own_edges, *records, ghosts, ghost_edges)
    phase_out[...], solute_out[...] = add_shares(
        phase[...], solute[...], ghost_shares(ghosts, ghost_edges, places[...])
    )


def call(kernel, in_specs, out_shapes, scratch=(), out_specs=None, mib=16):
    return pl.pallas_call(
        kernel,
        out_shape=out_shapes,
        in_specs=in_specs,
        out_specs=out_specs or jax.tree.map(lambda _: VMEM, out_shapes),
        scratch_shapes=list(scratch),
        compiler_params=pltpu.CompilerParams(vmem_limit_bytes=mib * 1024 * 1024),
    )


def shape(*dims):
    return jax.ShapeDtypeStruct(dims, F32)


def local(enthalpy, conductivity, phase, solute, tile_source, tile_block, tile_neighbour):
    count = lax.axis_size("gx")
    sizes = (lax.axis_size("gy"), lax.axis_size("gz"))
    plane_cap = -(-SLOTS // (count - 1))
    block_cap = 2 * SLOTS // count
    others = count - 1
    records = others * plane_cap
    bx, by, bz = enthalpy.shape
    picks, stencil, places, spreads = tables()

    integers = functools.partial(jax.ShapeDtypeStruct, dtype=jnp.int32)
    sides, table, asked, *farther = call(
        functools.partial(sides_kernel, sizes, plane_cap),
        [ANY] * 5,
        [
            shape(sizes[0] * sizes[1], 3 * bx, 128),
            integers((table_sizes(count, plane_cap)[2], 128)),
            shape(count, 128),
            *[shape(8, 128)] * (count - 3),
        ],
        [
            pltpu.VMEM((1, SLOTS), jnp.int32),
            pltpu.VMEM((1, SLOTS), jnp.int32),
            pltpu.VMEM((FACES, 1, SLOTS), jnp.int32),
            pltpu.VMEM((bx, by, bz), F32),
            pltpu.VMEM((bx, by, bz), F32),
            pltpu.SemaphoreType.DMA((2 * bx + 3,)),
        ],
        mib=56,
    )(
        tile_source.reshape(1, SLOTS),
        tile_block.reshape(1, SLOTS),
        jnp.transpose(tile_neighbour, (0, 1, 4, 2, 3)).reshape(FACES, 1, SLOTS),
        enthalpy,
        conductivity,
    )
    sides = lax.all_to_all(sides, ("gy", "gz"), split_axis=0, concat_axis=0, tiled=True)

    def pass_on(value, shift):
        return lax.ppermute(value, "gx", [(i, (i + shift) % count) for i in range(count)])

    def exchange(values):
        return [pass_on(value, shift) for shift, value in enumerate(values, 1)]

    def swap_all(values):
        return [
            lax.ppermute(value, "gx", [(i, i ^ swap) for i in range(count)])
            for swap, value in zip(swap_order(count), values)
        ]

    farther = [pass_on(value, shift) for shift, value in enumerate(farther, 2)]

    phase_field = phase.reshape(SLOTS, TE, PLANE)
    solute_field = solute.reshape(SLOTS, TE, PLANE)
    own_shapes = [shape(2 * SLOTS, TE, 128), shape(2 * SLOTS * 8, 128)]
    send_shapes = [shape(plane_cap * REC, 128)] * others
    rows_scratch = pltpu.VMEM((4, SLOTS * TE, 128), F32)
    packed = call(
        first_pack_kernel,
        [SMEM] + [VMEM] * 4,
        [*own_shapes, shape(count, 128), *send_shapes],
        [rows_scratch],
    )(table, asked, phase_field, solute_field, picks)
    own, asked, packed = packed[:2], packed[2], packed[3:]

    layer = shape(3 * by + 8, bz)
    down, up = call(
        functools.partial(layers_kernel, sizes), [VMEM] * 4 + [ANY] * len(farther), [layer, layer]
    )(enthalpy, conductivity, sides, asked, *farther)
    from_low, from_high = pass_on(up, 1), pass_on(down, others)
    row = 3 * by + 4
    request = [asked[0], from_low[row], *[value[0] for value in farther], from_high[row]]
    request = jnp.stack([value[:block_cap] for value in request]).astype(jnp.int32)
    _, deep = block_layout(block_cap)
    brick = shape(bx, by, bz)
    got = swap_all(packed)
    heated, *found = call(
        functools.partial(heat_kernel, block_cap, sizes),
        [SMEM] + [VMEM] * 5,
        [brick] + [shape(deep * CB, 128)] * count,
        [pltpu.VMEM((bx, by // CB, CB, bz), F32)],
    )(request, enthalpy, conductivity, sides, from_low, from_high)
    found[1:] = exchange(found[1:])
    (heat_out,) = call(write_out_kernel, [ANY], [brick], [pltpu.SemaphoreType.DMA], [ANY])(heated)

    field = shape(SLOTS, TE, PLANE)
    step_scratch = [
        pltpu.VMEM((records + 2 * SLOTS, TE, 128), F32),
        pltpu.VMEM(((records + 2 * SLOTS) * 8, 128), F32),
        pltpu.VMEM((SLOTS, TE, 128), F32),
        pltpu.VMEM((SLOTS, 8, 128), F32),
        rows_scratch,
    ]
    def inner(phase_field, solute_field, *heat):
        return call(
            functools.partial(inner_kernel, bool(heat)), [VMEM] * (3 + len(heat)), [field, field]
        )(phase_field, solute_field, stencil, *heat)

    inner_fields = inner(phase_field, solute_field)
    phase_field, solute_field, heat, *rest = call(
        functools.partial(first_step_kernel, block_cap),
        [SMEM] + [VMEM] * (8 + count + others),
        [field, field, shape(2, SLOTS * TE, 128), *own_shapes, *send_shapes],
        step_scratch
        + [
            pltpu.VMEM((count, deep * CB, 128), F32),
            pltpu.VMEM((SLOTS * CB, CB, 128), F32),
        ],
    )(table, phase_field, *inner_fields, *own, picks, places, spreads, *found, *got)
    own, send = rest[:2], rest[2:]
    for _ in range(PHASE_STEPS - 2):
        got = swap_all(send)
        inner_fields = inner(phase_field, solute_field, heat)
        phase_field, solute_field, *rest = call(
            middle_step_kernel,
            [SMEM] + [VMEM] * (6 + others),
            [field, field, *own_shapes, *send_shapes],
            step_scratch,
        )(table, *inner_fields, *own, picks, places, *got)
        own, send = rest[:2], rest[2:]
    got = swap_all(send)
    inner_fields = inner(phase_field, solute_field, heat)
    phase_field, solute_field = call(
        last_step_kernel, [SMEM] + [VMEM] * (5 + others), [field, field], step_scratch
    )(table, *inner_fields, *own, places, *got)
    return heat_out, phase_field.reshape(phase.shape), solute_field.reshape(solute.shape)


def solution(mesh):
    grid = P("gx", "gy", "gz")
    tiles = P("gx", "gy", "gz", None, None, None)
    return jax.shard_map(
        local,
        mesh=mesh,
        in_specs=(
            grid,
            grid,
            tiles,
            tiles,
            P("gx", "gy", "gz", None, None),
            P("gx", "gy", "gz", None),
            P("gx", "gy", "gz", None, None),
        ),
        out_specs=(grid, tiles, tiles),
        check_vma=False,
    )
```

```python
import functools

import jax
import jax.numpy as jnp
import numpy as np
from jax import lax
from jax.experimental import pallas as pl
from jax.experimental.pallas import tpu as pltpu
from jax.sharding import PartitionSpec as P

CB = 8
TE = 16
PLANE = TE * TE
SLOTS = 16
FACES = 6
PHASE_STEPS = 4
REC = 24

RATE = 0.16
ORDER_SPEED = 0.1
SOLUTE_RATE = 0.15
COUPLING = 0.5
REJECTION = 0.5

F32 = jnp.float32
BF16 = jnp.bfloat16
VMEM = pl.BlockSpec(memory_space=pltpu.VMEM)
SMEM = pl.BlockSpec(memory_space=pltpu.SMEM)
ANY = pl.BlockSpec(memory_space=pl.ANY)


def plane_lane(face):
    j = np.arange(TE)
    return [j, PLANE - TE + j, j * TE, j * TE + TE - 1][face - 2]


def constant_tables():
    pick = np.zeros((2, PLANE, 256), np.float32)
    place = np.zeros((2, 128, PLANE), np.float32)
    for field in range(2):
        for face in range(2, 6):
            at = field * 64 + (face - 2) * TE + np.arange(TE)
            pick[field, plane_lane(face ^ 1), at] = 1.0
            pick[field, plane_lane(face), 128 + at] = 1.0
            place[field, at, plane_lane(face)] = 1.0
    y, z = np.divmod(np.arange(PLANE), TE)
    dy, dz = np.abs(y[:, None] - y[None, :]), np.abs(z[:, None] - z[None, :])
    stencil = ((dy + dz) == 1).astype(np.float32)
    lane = np.arange(128)
    spread = (lane[:, None] % CB == z[None, :] // 2).astype(np.float32)
    return pick, place, stencil, spread


def tables():
    pick, place, stencil, spread = constant_tables()
    place = np.concatenate([place[0], place[1]], axis=1)
    return (
        jnp.asarray(np.concatenate([pick[0], pick[1]], axis=0), BF16),
        jnp.asarray(stencil, BF16),
        jnp.asarray(np.concatenate([place, place], axis=0), BF16),
        jnp.asarray(np.concatenate([spread, spread], axis=0), BF16),
    )


def halves(value):
    high = value.astype(BF16)
    return high, (value - high.astype(F32)).astype(BF16)


def dot(a, b):
    return jnp.dot(a, b, preferred_element_type=F32)


def temperature(h):
    return jnp.minimum(h, 0.0) + jnp.maximum(h - 1.0, 0.0)


def iota(shape, dim):
    return lax.broadcasted_iota(jnp.int32, shape, dim)


def to_lanes(column):
    bx, by, _ = column.shape
    diagonal = iota((bx, by, 128), 1) == iota((bx, by, 128), 2)
    return jnp.sum(jnp.where(diagonal, column, 0.0), axis=1)


def to_column(line, by):
    bx = line.shape[0]
    diagonal = iota((bx, by, 128), 1) == iota((bx, by, 128), 2)
    return jnp.sum(jnp.where(diagonal, line[:, None, :], 0.0), axis=2, keepdims=True)


def conduct(h, k, xlo, xhi, ylo, yhi, zlo, zhi):
    bx, by, bz = h.shape
    t = temperature(h)
    row, lane = iota((bx, by, bz), 1), iota((bx, by, bz), 2)
    if bx > 1:
        total = jnp.concatenate([xlo, t[:-1]], axis=0) + jnp.concatenate([t[1:], xhi], axis=0)
    else:
        total = xlo + xhi
    total += jnp.where(row == 0, ylo[:, None, :], pltpu.roll(t, 1, 1))
    total += jnp.where(row == by - 1, yhi[:, None, :], pltpu.roll(t, by - 1, 1))
    total += jnp.where(lane == 0, to_column(zlo, by), pltpu.roll(t, 1, 2))
    total += jnp.where(lane == bz - 1, to_column(zhi, by), pltpu.roll(t, bz - 1, 2))
    return h + RATE * k * (total - 6.0 * t)


def sublanes(value, y):
    return jnp.concatenate([value[x, y : y + 1, :] for x in range(value.shape[0])], axis=0)


def side_blocks(h, k):
    by, bz = h.shape[1:]
    return [
        (sublanes(h, 0), sublanes(h, 1), sublanes(k, 0)),
        (sublanes(h, by - 1), sublanes(h, by - 2), sublanes(k, by - 1)),
        (to_lanes(h[:, :, 0:1]), to_lanes(h[:, :, 1:2]), to_lanes(k[:, :, 0:1])),
        (to_lanes(h[:, :, bz - 1 : bz]), to_lanes(h[:, :, bz - 2 : bz - 1]), to_lanes(k[:, :, bz - 1 : bz])),
    ]


def column_of(row):
    square = (row.shape[1], row.shape[1])
    return jnp.sum(jnp.where(iota(square, 0) == iota(square, 1), row, 0.0), axis=1, keepdims=True)


def table_sizes(count, plane_cap):
    records = (count - 1) * plane_cap
    faces = min(FACES, 128 // records)
    return records, faces, 1 + -(-FACES // faces)


def swap_order(count):
    return sorted(range(1, count), key=lambda s: (-s.bit_length(), s))


def farther_swaps(count):
    return [s for s in range(2, count) if count != 4 or s != 3]


def place_of(table, slot):
    return table[0, FACES * SLOTS + slot], table[0, FACES * SLOTS + SLOTS + slot]


def write_tables(plane_cap, source, block, neighbour, asked, farther, table):
    here = lax.axis_index("gx")
    me = here.astype(F32)
    count = lax.axis_size("gx")
    records, faces, _ = table_sizes(count, plane_cap)
    cap = float(plane_cap)

    def position_of(swap):
        position = jnp.zeros(swap.shape, F32)
        for at, other in enumerate(swap_order(count)):
            position = jnp.where(swap == other, float(at), position)
        return position

    square = (SLOTS, SLOTS)
    before = iota(square, 0) < iota(square, 1)
    slot = iota((1, SLOTS), 1).astype(F32)
    source_row, block_column = source[...].astype(F32), column_of(block[...].astype(F32))
    source_column = column_of(source_row)
    rank = jnp.sum(
        jnp.where((source_column == source_row) & before, 1.0, 0.0), axis=0, keepdims=True
    )
    rank_column = column_of(rank)
    lane = iota((SLOTS, 128), 1).astype(F32)
    swap = source[...] ^ here
    swap_column = column_of(swap.astype(F32))
    for shift in range(count):
        hit = (swap_column == float(shift)) & (rank_column == lane)
        row = jnp.sum(jnp.where(hit, block_column, 0.0), axis=0, keepdims=True)
        asked[shift : shift + 1, :] = row
        if shift in farther_swaps(count):
            farther[farther_swaps(count).index(shift)][...] = jnp.broadcast_to(row, (8, 128))
    at = FACES * SLOTS
    found = jnp.where(swap == 0, 0.0, 1.0 + position_of(swap))
    table[0:1, at : at + SLOTS] = found.astype(jnp.int32)
    table[0:1, at + SLOTS : at + 2 * SLOTS] = rank.astype(jnp.int32)
    slot_column = iota((SLOTS, records), 0).astype(F32)
    for face in range(FACES):
        number = neighbour[face]
        owner_row, number_row = (number >> 4).astype(F32), number.astype(F32)
        owner_column, number_column = column_of(owner_row), column_of(number_row)
        other_row = (number_row >= 0.0) & (owner_row != me)
        alike = (owner_column == owner_row) & (owner_column >= 0.0) & (owner_column != me)
        receive_rank = jnp.sum(
            jnp.where(alike & (number_column < number_row), 1.0, 0.0), axis=0, keepdims=True
        )
        send_rank = jnp.sum(jnp.where(alike & before, 1.0, 0.0), axis=0, keepdims=True)
        position = position_of(jnp.where(number < 0, 0, (number >> 4) ^ here))
        mine = records + (number_row - owner_row * SLOTS)
        there = position * cap + receive_rank
        receive = jnp.where(owner_row == me, mine, there)
        receive = jnp.where(number_row < 0.0, records + SLOTS + slot, receive)
        table[0:1, face * SLOTS : face * SLOTS + SLOTS] = receive.astype(jnp.int32)
        key = jnp.where(other_row, position * cap + send_rank, -1.0)
        hit = iota((SLOTS, records), 1).astype(F32) == column_of(key)
        tile = jnp.sum(jnp.where(hit, slot_column, 0.0), axis=0, keepdims=True)
        row, at = 1 + (face ^ 1) // faces, (face ^ 1) % faces * records
        table[row : row + 1, at : at + records] = tile.astype(jnp.int32)


def sides_kernel(
    sizes, plane_cap, source_far, block_far, neighbour_far, h_far, k_far, send, table, *rest
):
    asked, *farther, source, block, neighbour, h, k, sems = rest
    ny, nz = sizes
    my_y, my_z = lax.axis_index("gy"), lax.axis_index("gz")
    bx = h.shape[0]
    small = [(source_far, source), (block_far, block), (neighbour_far, neighbour)]
    copies = [pltpu.make_async_copy(*pair, sems.at[2 * bx + n]) for n, pair in enumerate(small)]
    large = []
    for x in range(bx):
        large.append(pltpu.make_async_copy(h_far.at[x], h.at[x], sems.at[x]))
        large.append(pltpu.make_async_copy(k_far.at[x], k.at[x], sems.at[bx + x]))
    for copy in copies + large:
        copy.start()
    for copy in copies:
        copy.wait()
    write_tables(plane_cap, source, block, neighbour, asked, farther, table)
    for copy in large:
        copy.wait()
    blocks = side_blocks(h[...], k[...])
    for y in range(ny):
        for z in range(nz):
            for part in range(3):
                ylo, yhi, zlo, zhi = [block[part] for block in blocks]
                chosen = jnp.where(
                    my_y == y, jnp.where(z < my_z, zlo, zhi), jnp.where(y < my_y, ylo, yhi)
                )
                send[y * nz + z, part * bx : part * bx + bx, :] = chosen


def side_reader(sizes, got, bx):
    ny, nz = sizes
    my_y, my_z = lax.axis_index("gy"), lax.axis_index("gz")

    def read(dy, dz, part=0):
        y, z = my_y + dy, my_z + dz
        inside = (y >= 0) & (y < ny) & (z >= 0) & (z < nz)
        at = jnp.where(inside, y * nz + z, 0)
        return jnp.where(inside, got[at, part * bx : part * bx + bx, :], 0.0)

    return read


def layers_kernel(sizes, h, k, got, asked, *rest):
    first, second = rest[-2:]
    bx, by, bz = h.shape
    read = side_reader(sizes, got, bx)
    even = lax.rem(lax.axis_index("gx"), 2) == 0
    around = [read(-1, 0), read(1, 0), read(0, -1), read(0, 1)]
    layers = [(h[bx - 1], h[0]), (h[bx - 2], h[1]), (k[bx - 1], k[0])]
    layers += [(side[bx - 1 : bx, :], side[0:1, :]) for side in around]
    row = 0
    for upper, lower in layers:
        first[row : row + upper.shape[0], :] = jnp.where(even, upper, lower)
        second[row : row + upper.shape[0], :] = jnp.where(even, lower, upper)
        row += upper.shape[0]
    last = asked.shape[0] - 1
    for out, ask in ((first, 1), (second, last)):
        out[row:, :] = jnp.broadcast_to(asked[ask : ask + 1, :], (out.shape[0] - row, bz))


def block_layout(cap):
    parts = 128 // CB // cap
    return parts, CB // parts


def flat_step(h, k, inner, outer, first, last, before, after, length):
    bx, lanes = h.shape
    t = temperature(h)
    row, lane = iota(h.shape, 0), iota(h.shape, 1)
    total = temperature(inner) + temperature(outer)
    total += jnp.where(row == 0, temperature(first), pltpu.roll(t, 1, 0))
    total += jnp.where(row == bx - 1, temperature(last), pltpu.roll(t, bx - 1, 0))
    total += jnp.where(lane == 0, temperature(before), pltpu.roll(t, 1, 1))
    total += jnp.where(lane == length - 1, temperature(after), pltpu.roll(t, lanes - 1, 1))
    return h + RATE * k * (total - 6.0 * t)


def heat_kernel(cap, sizes, request, h, k, got, first, second, out, found, *rest):
    *send, held = rest
    count = lax.axis_size("gx")
    bx, by, bz = h.shape
    h0, k0 = h[...], k[...]
    read = side_reader(sizes, got, bx)
    me = lax.axis_index("gx")
    layers, lines = [], []
    even = lax.rem(me, 2) == 0
    pairs = (first[...], second[...])
    low, high = jnp.where(even, *pairs[::-1]), jnp.where(even, *pairs)
    for beside, inside in ((low, me > 0), (high, me < count - 1)):
        beside = jnp.where(inside, beside, 0.0)
        layers.append([beside[part * by : part * by + by, :][None] for part in range(3)])
        lines.append([beside[3 * by + n : 3 * by + n + 1, :] for n in range(4)])
    y_sides = [[read(d, 0, part) for part in range(3)] for d in (-1, 1)]
    z_sides = [[read(0, d, part) for part in range(3)] for d in (-1, 1)]
    corner = [[read(dy, dz) for dz in (-1, 1)] for dy in (-1, 1)]
    to_first = [[pltpu.roll(c[0], 1, 1), c[1]] for c in corner]
    y_inner = [sublanes(h0, 0), sublanes(h0, by - 1)]
    z_inner = [to_lanes(h0[:, :, 0:1]), to_lanes(h0[:, :, bz - 1 : bz])]

    sides = [temperature(layers[0][0]), temperature(layers[1][0])]
    sides += [temperature(side[0]) for side in y_sides + z_sides]
    h1 = conduct(h0, k0, *sides)
    next_sides = []
    for side in range(2):
        near, far, near_k = layers[side]
        across = [temperature(far), temperature(h0[0:1])]
        if side:
            across = [temperature(h0[bx - 1 : bx]), temperature(far)]
        next_sides.append(conduct(near, near_k, *across, *[temperature(line) for line in lines[side]]))
    for side in range(2):
        near, far, near_k = y_sides[side]
        ends = [to_first[side][0], pltpu.roll(to_first[side][1], bz - 1, 1)]
        next_sides.append(
            flat_step(near, near_k, y_inner[side], far, lines[0][side], lines[1][side], *ends, bz)
        )
    for side in range(2):
        near, far, near_k = z_sides[side]
        ends = [to_first[0][side], pltpu.roll(to_first[1][side], by - 1, 1)]
        next_sides.append(
            flat_step(near, near_k, z_inner[side], far, lines[0][2 + side], lines[1][2 + side], *ends, by)
        )
    h2 = conduct(h1, k0, *[temperature(side) for side in next_sides])
    out[...] = h2

    held[...] = temperature(h2).reshape(bx, by // CB, CB, bz)
    parts, deep = block_layout(cap)
    nby, nbz = by // CB, bz // CB
    group = iota((deep, CB, bz), 2) // CB
    for out, swap in zip((found, *send), (0, *swap_order(count))):
        total = jnp.zeros((deep, CB, bz), F32)
        for rank in range(cap):
            block = request[swap, rank]
            a, b, c = block // (nby * nbz), (block // nbz) % nby, block % nbz
            for part in range(parts):
                at = rank * parts + part
                patch = held[pl.ds(a * CB + part * deep, deep), b]
                moved = pltpu.roll(patch, (CB * at - CB * c + bz) % bz, 2)
                total = jnp.where(group == at, moved, total)
        out[...] = total.reshape(deep * CB, bz)


def write_records(phase, solute, picks, own, own_edges, rows):
    flat = [f.reshape(SLOTS * TE, PLANE) for f in (phase, solute)]
    high, low = halves(jnp.concatenate(flat, axis=1))
    planes = dot(high, picks) + dot(low, picks)
    own[0:SLOTS] = planes[:, 0:128].reshape(SLOTS, TE, 128)
    own[SLOTS : 2 * SLOTS] = planes[:, 128:256].reshape(SLOTS, TE, 128)
    for part in range(4):
        rows[part] = flat[part // 2][:, part % 2 * 128 : part % 2 * 128 + 128]
    for part in range(4):
        low_face = rows[part, pl.ds(0, SLOTS, TE), :]
        high_face = rows[part, pl.ds(TE - 1, SLOTS, TE), :]
        for at, value in ((0, high_face), (4, low_face)):
            own_edges[pl.ds(at + part, SLOTS, 8), :] = value
            own_edges[pl.ds(8 * SLOTS + 4 - at + part, SLOTS, 8), :] = value


def merge_record(planes, edges, number):
    side = (iota((TE, 128), 1) % 64) // TE
    out = planes[number(2)]
    for face in range(3, 6):
        out = jnp.where(side == face - 2, planes[number(face)], out)
    first, second = [edges[pl.ds(pl.multiple_of(number(face) * 8, 8), 8), :] for face in range(2)]
    return out, jnp.where(iota((8, 128), 0) < 4, first, second)


def pack(own, own_edges, table, send):
    cap = send[0].shape[0] // REC
    records, faces, _ = table_sizes(len(send) + 1, cap)
    for record in range(records):
        out, row = send[record // cap], record % cap * REC
        planes, edge = merge_record(
            own, own_edges, lambda face: table[1 + face // faces, face % faces * records + record]
        )
        out[row : row + TE, :] = planes
        out[row + TE : row + REC, :] = edge


def first_pack_kernel(table, asked, phase, solute, picks, own, own_edges, asked_out, *rest):
    *send, rows = rest
    write_records(phase[...], solute[...], picks[...], own, own_edges, rows)
    pack(own, own_edges, table, send)
    asked_out[...] = asked[...]


def take_heat(cap, table, found, spreads, blocks, held, heat):
    parts, deep = block_layout(cap)
    for number, value in enumerate(found):
        blocks[number] = value[...]
    group = iota((CB, 128), 1) // CB
    for slot in range(SLOTS):
        back, rank = place_of(table, slot)
        for x in range(CB):
            row = (x % deep) * CB
            patch = blocks[back, row : row + CB, :]
            held[slot * CB + x] = jnp.where(group == rank * parts + x // deep, patch, 0.0)
    rows = held[...].reshape(SLOTS * CB * CB, 128)
    wide = dot(jnp.concatenate(halves(rows), axis=1), spreads)
    wide = wide.reshape(SLOTS * CB, CB, PLANE)
    keep = iota(wide.shape, 1) == iota(wide.shape, 2) // TE // 2
    coarse = jnp.sum(jnp.where(keep, wide, 0.0), axis=1)
    for half in range(2):
        for odd in range(2):
            heat[half, pl.ds(odd, SLOTS * CB, 2), :] = coarse[:, half * 128 : half * 128 + 128]


def inner_step(phase, solute, heat, stencil):
    row = iota((SLOTS, TE, PLANE), 1)
    lap = []
    for field in (phase, solute):
        high, low = halves(field.reshape(SLOTS * TE, PLANE))
        total = (dot(high, stencil) + dot(low, stencil)).reshape(SLOTS, TE, PLANE) - 6.0 * field
        total += jnp.where(row == 0, 0.0, pltpu.roll(field, 1, 1))
        total += jnp.where(row == TE - 1, 0.0, pltpu.roll(field, TE - 1, 1))
        lap.append(total)
    squared = 1.0 - phase * phase
    drive = solute if heat is None else heat + solute
    change = ORDER_SPEED * (
        lap[0] + phase - phase * phase * phase - COUPLING * drive * squared * squared
    )
    return phase + change, solute + SOLUTE_RATE * lap[1] + REJECTION * change


def wide_heat(heat):
    return jnp.concatenate([heat[0], heat[1]], axis=1).reshape(SLOTS, TE, PLANE)


def gather_ghosts(table, got, own, own_edges, planes, edges, ghosts, ghost_edges):
    records = planes.shape[0] - 2 * SLOTS
    cap = records // len(got)
    for record in range(records):
        value, row = got[record // cap], record % cap * REC
        planes[record] = value[row : row + TE, :]
        edges[record * 8 : record * 8 + 8, :] = value[row + TE : row + REC, :]
    planes[records:] = own[...]
    edges[records * 8 :, :] = own_edges[...]
    for slot in range(SLOTS):
        out, edge = merge_record(planes, edges, lambda face: table[0, face * SLOTS + slot])
        ghosts[slot] = out
        ghost_edges[slot] = edge


def ghost_shares(ghosts, ghost_edges, places):
    beside = jnp.concatenate(halves(ghosts[...].reshape(SLOTS * TE, 128)), axis=1)
    beside = dot(beside, places)
    rows = iota((SLOTS, TE, PLANE), 1)
    shares = []
    for number in range(2):
        share = beside[:, number * PLANE : number * PLANE + PLANE].reshape(SLOTS, TE, PLANE)
        for face, at_row in ((0, 0), (1, TE - 1)):
            at = face * 4 + number * 2
            side = [ghost_edges[:, row : row + 1, :] for row in (at, at + 1)]
            side = jnp.concatenate(side, axis=2)
            share += jnp.where(rows == at_row, side, 0.0)
        shares.append(share)
    return shares


def add_shares(phase, solute, shares, heat_share=None):
    change = ORDER_SPEED * shares[0]
    if heat_share is not None:
        change += heat_share
    return phase + change, solute + SOLUTE_RATE * shares[1] + REJECTION * change


def inner_kernel(has_heat, phase, solute, stencil, *rest):
    phase_out, solute_out = rest[-2:]
    heat = wide_heat(rest[0]) if has_heat else None
    phase_out[...], solute_out[...] = inner_step(phase[...], solute[...], heat, stencil[...])


def first_step_kernel(cap, table, old_phase, phase, solute, own, own_edges, picks, places, spreads, *rest):
    others = lax.axis_size("gx") - 1
    found, got, rest = rest[: others + 1], rest[others + 1 : 2 * others + 1], rest[2 * others + 1 :]
    phase_out, solute_out, heat_out, own_out, edges_out, *rest = rest
    send, (*records, ghosts, ghost_edges, rows, blocks, held) = rest[:others], rest[others:]
    take_heat(cap, table, found, spreads[...], blocks, held, heat_out)
    gather_ghosts(table, got, own, own_edges, *records, ghosts, ghost_edges)
    squared = 1.0 - old_phase[...] * old_phase[...]
    heat_share = (-ORDER_SPEED * COUPLING) * wide_heat(heat_out) * squared * squared
    new_phase, new_solute = add_shares(
        phase[...], solute[...], ghost_shares(ghosts, ghost_edges, places[...]), heat_share
    )
    phase_out[...] = new_phase
    solute_out[...] = new_solute
    write_records(new_phase, new_solute, picks[...], own_out, edges_out, rows)
    pack(own_out, edges_out, table, send)


def write_out_kernel(value, out, sem):
    copy = pltpu.make_async_copy(value, out, sem)
    copy.start()
    copy.wait()


def middle_step_kernel(table, phase, solute, own, own_edges, picks, places, *rest):
    others = lax.axis_size("gx") - 1
    got, (phase_out, solute_out, own_out, edges_out, *rest) = rest[:others], rest[others:]
    send, (*records, ghosts, ghost_edges, rows) = rest[:others], rest[others:]
    gather_ghosts(table, got, own, own_edges, *records, ghosts, ghost_edges)
    new_phase, new_solute = add_shares(phase[...], solute[...], ghost_shares(ghosts, ghost_edges, places[...]))
    phase_out[...] = new_phase
    solute_out[...] = new_solute
    write_records(new_phase, new_solute, picks[...], own_out, edges_out, rows)
    pack(own_out, edges_out, table, send)


def last_step_kernel(table, phase, solute, own, own_edges, places, *rest):
    others = lax.axis_size("gx") - 1
    got, (phase_out, solute_out, *records, ghosts, ghost_edges, _) = rest[:others], rest[others:]
    gather_ghosts(table, got, own, own_edges, *records, ghosts, ghost_edges)
    phase_out[...], solute_out[...] = add_shares(
        phase[...], solute[...], ghost_shares(ghosts, ghost_edges, places[...])
    )


def call(kernel, in_specs, out_shapes, scratch=(), out_specs=None, mib=16):
    return pl.pallas_call(
        kernel,
        out_shape=out_shapes,
        in_specs=in_specs,
        out_specs=out_specs or jax.tree.map(lambda _: VMEM, out_shapes),
        scratch_shapes=list(scratch),
        compiler_params=pltpu.CompilerParams(vmem_limit_bytes=mib * 1024 * 1024),
    )


def shape(*dims):
    return jax.ShapeDtypeStruct(dims, F32)


def local(enthalpy, conductivity, phase, solute, tile_source, tile_block, tile_neighbour):
    count = lax.axis_size("gx")
    sizes = (lax.axis_size("gy"), lax.axis_size("gz"))
    plane_cap = -(-SLOTS // (count - 1))
    block_cap = 2 * SLOTS // count
    others = count - 1
    records = others * plane_cap
    bx, by, bz = enthalpy.shape
    picks, stencil, places, spreads = tables()

    integers = functools.partial(jax.ShapeDtypeStruct, dtype=jnp.int32)
    sides, table, asked, *farther = call(
        functools.partial(sides_kernel, sizes, plane_cap),
        [ANY] * 5,
        [
            shape(sizes[0] * sizes[1], 3 * bx, 128),
            integers((table_sizes(count, plane_cap)[2], 128)),
            shape(count, 128),
            *[shape(8, 128)] * len(farther_swaps(count)),
        ],
        [
            pltpu.VMEM((1, SLOTS), jnp.int32),
            pltpu.VMEM((1, SLOTS), jnp.int32),
            pltpu.VMEM((FACES, 1, SLOTS), jnp.int32),
            pltpu.VMEM((bx, by, bz), F32),
            pltpu.VMEM((bx, by, bz), F32),
            pltpu.SemaphoreType.DMA((2 * bx + 3,)),
        ],
        mib=56,
    )(
        tile_source.reshape(1, SLOTS),
        tile_block.reshape(1, SLOTS),
        jnp.transpose(tile_neighbour, (0, 1, 4, 2, 3)).reshape(FACES, 1, SLOTS),
        enthalpy,
        conductivity,
    )
    sides = lax.all_to_all(sides, ("gy", "gz"), split_axis=0, concat_axis=0, tiled=True)

    def swap_with(value, partner):
        return lax.ppermute(value, "gx", [(i, partner(i)) for i in range(count)])

    def swap_all(values):
        return [
            swap_with(value, lambda i, swap=swap: i ^ swap)
            for swap, value in zip(swap_order(count), values)
        ]

    farther = [
        swap_with(value, lambda i, s=s: i ^ s) for s, value in zip(farther_swaps(count), farther)
    ]

    phase_field = phase.reshape(SLOTS, TE, PLANE)
    solute_field = solute.reshape(SLOTS, TE, PLANE)
    own_shapes = [shape(2 * SLOTS, TE, 128), shape(2 * SLOTS * 8, 128)]
    send_shapes = [shape(plane_cap * REC, 128)] * others
    rows_scratch = pltpu.VMEM((4, SLOTS * TE, 128), F32)
    packed = call(
        first_pack_kernel,
        [SMEM] + [VMEM] * 4,
        [*own_shapes, shape(count, 128), *send_shapes],
        [rows_scratch],
    )(table, asked, phase_field, solute_field, picks)
    own, asked, packed = packed[:2], packed[2], packed[3:]

    layer = shape(3 * by + 8, bz)
    first, second = call(
        functools.partial(layers_kernel, sizes), [VMEM] * 4 + [ANY] * len(farther), [layer, layer]
    )(enthalpy, conductivity, sides, asked, *farther)
    first = swap_with(first, lambda i: i ^ 1)
    if count == 4:
        second = swap_with(second, lambda i: i ^ 3)
    else:
        second = swap_with(second, lambda i: i if i in (0, others) else ((i + 1) ^ 1) - 1)
    row = 3 * by + 4
    request = [asked[0], first[row], *[value[0] for value in farther]]
    if count == 4:
        request.append(second[row])
    request = jnp.stack([value[:block_cap] for value in request]).astype(jnp.int32)
    _, deep = block_layout(block_cap)
    brick = shape(bx, by, bz)
    got = swap_all(packed)
    heated, *found = call(
        functools.partial(heat_kernel, block_cap, sizes),
        [SMEM] + [VMEM] * 5,
        [brick] + [shape(deep * CB, 128)] * count,
        [pltpu.VMEM((bx, by // CB, CB, bz), F32)],
    )(request, enthalpy, conductivity, sides, first, second)
    found[1:] = swap_all(found[1:])
    (heat_out,) = call(write_out_kernel, [ANY], [brick], [pltpu.SemaphoreType.DMA], [ANY])(heated)

    field = shape(SLOTS, TE, PLANE)
    step_scratch = [
        pltpu.VMEM((records + 2 * SLOTS, TE, 128), F32),
        pltpu.VMEM(((records + 2 * SLOTS) * 8, 128), F32),
        pltpu.VMEM((SLOTS, TE, 128), F32),
        pltpu.VMEM((SLOTS, 8, 128), F32),
        rows_scratch,
    ]
    def inner(phase_field, solute_field, *heat):
        return call(
            functools.partial(inner_kernel, bool(heat)), [VMEM] * (3 + len(heat)), [field, field]
        )(phase_field, solute_field, stencil, *heat)

    inner_fields = inner(phase_field, solute_field)
    phase_field, solute_field, heat, *rest = call(
        functools.partial(first_step_kernel, block_cap),
        [SMEM] + [VMEM] * (8 + count + others),
        [field, field, shape(2, SLOTS * TE, 128), *own_shapes, *send_shapes],
        step_scratch
        + [
            pltpu.VMEM((count, deep * CB, 128), F32),
            pltpu.VMEM((SLOTS * CB, CB, 128), F32),
        ],
    )(table, phase_field, *inner_fields, *own, picks, places, spreads, *found, *got)
    own, send = rest[:2], rest[2:]
    for _ in range(PHASE_STEPS - 2):
        got = swap_all(send)
        inner_fields = inner(phase_field, solute_field, heat)
        phase_field, solute_field, *rest = call(
            middle_step_kernel,
            [SMEM] + [VMEM] * (6 + others),
            [field, field, *own_shapes, *send_shapes],
            step_scratch,
        )(table, *inner_fields, *own, picks, places, *got)
        own, send = rest[:2], rest[2:]
    got = swap_all(send)
    inner_fields = inner(phase_field, solute_field, heat)
    phase_field, solute_field = call(
        last_step_kernel, [SMEM] + [VMEM] * (5 + others), [field, field], step_scratch
    )(table, *inner_fields, *own, places, *got)
    return heat_out, phase_field.reshape(phase.shape), solute_field.reshape(solute.shape)


def solution(mesh):
    grid = P("gx", "gy", "gz")
    tiles = P("gx", "gy", "gz", None, None, None)
    return jax.shard_map(
        local,
        mesh=mesh,
        in_specs=(
            grid,
            grid,
            tiles,
            tiles,
            P("gx", "gy", "gz", None, None),
            P("gx", "gy", "gz", None),
            P("gx", "gy", "gz", None, None),
        ),
        out_specs=(grid, tiles, tiles),
        check_vma=False,
    )
```

```python
import functools

import jax
import jax.numpy as jnp
import numpy as np
from jax import lax
from jax.experimental import pallas as pl
from jax.experimental.pallas import tpu as pltpu
from jax.sharding import PartitionSpec as P

CB = 8
TE = 16
PLANE = TE * TE
SLOTS = 16
FACES = 6
PHASE_STEPS = 4
REC = 24

RATE = 0.16
ORDER_SPEED = 0.1
SOLUTE_RATE = 0.15
COUPLING = 0.5
REJECTION = 0.5

F32 = jnp.float32
BF16 = jnp.bfloat16
VMEM = pl.BlockSpec(memory_space=pltpu.VMEM)
SMEM = pl.BlockSpec(memory_space=pltpu.SMEM)
ANY = pl.BlockSpec(memory_space=pl.ANY)


def plane_lane(face):
    j = np.arange(TE)
    return [j, PLANE - TE + j, j * TE, j * TE + TE - 1][face - 2]


def constant_tables():
    pick = np.zeros((2, PLANE, 256), np.float32)
    place = np.zeros((2, 128, PLANE), np.float32)
    for field in range(2):
        for face in range(2, 6):
            at = field * 64 + (face - 2) * TE + np.arange(TE)
            pick[field, plane_lane(face ^ 1), at] = 1.0
            pick[field, plane_lane(face), 128 + at] = 1.0
            place[field, at, plane_lane(face)] = 1.0
    y, z = np.divmod(np.arange(PLANE), TE)
    dy, dz = np.abs(y[:, None] - y[None, :]), np.abs(z[:, None] - z[None, :])
    stencil = ((dy + dz) == 1).astype(np.float32)
    lane = np.arange(128)
    spread = (lane[:, None] % CB == z[None, :] // 2).astype(np.float32)
    return pick, place, stencil, spread


def tables():
    pick, place, stencil, spread = constant_tables()
    place = np.concatenate([place[0], place[1]], axis=1)
    return (
        jnp.asarray(np.concatenate([pick[0], pick[1]], axis=0), BF16),
        jnp.asarray(stencil, BF16),
        jnp.asarray(np.concatenate([place, place], axis=0), BF16),
        jnp.asarray(np.concatenate([spread, spread], axis=0), BF16),
    )


def halves(value):
    high = value.astype(BF16)
    return high, (value - high.astype(F32)).astype(BF16)


def dot(a, b):
    return jnp.dot(a, b, preferred_element_type=F32)


def temperature(h):
    return jnp.minimum(h, 0.0) + jnp.maximum(h - 1.0, 0.0)


def iota(shape, dim):
    return lax.broadcasted_iota(jnp.int32, shape, dim)


def to_lanes(column):
    bx, by, _ = column.shape
    diagonal = iota((bx, by, 128), 1) == iota((bx, by, 128), 2)
    return jnp.sum(jnp.where(diagonal, column, 0.0), axis=1)


def to_column(line, by):
    bx = line.shape[0]
    diagonal = iota((bx, by, 128), 1) == iota((bx, by, 128), 2)
    return jnp.sum(jnp.where(diagonal, line[:, None, :], 0.0), axis=2, keepdims=True)


def conduct(h, k, xlo, xhi, ylo, yhi, zlo, zhi):
    bx, by, bz = h.shape
    t = temperature(h)
    row, lane = iota((bx, by, bz), 1), iota((bx, by, bz), 2)
    if bx > 1:
        total = jnp.concatenate([xlo, t[:-1]], axis=0) + jnp.concatenate([t[1:], xhi], axis=0)
    else:
        total = xlo + xhi
    total += jnp.where(row == 0, ylo[:, None, :], pltpu.roll(t, 1, 1))
    total += jnp.where(row == by - 1, yhi[:, None, :], pltpu.roll(t, by - 1, 1))
    total += jnp.where(lane == 0, to_column(zlo, by), pltpu.roll(t, 1, 2))
    total += jnp.where(lane == bz - 1, to_column(zhi, by), pltpu.roll(t, bz - 1, 2))
    return h + RATE * k * (total - 6.0 * t)


def sublanes(value, y):
    return jnp.concatenate([value[x, y : y + 1, :] for x in range(value.shape[0])], axis=0)


def side_blocks(h, k):
    by, bz = h.shape[1:]
    return [
        (sublanes(h, 0), sublanes(h, 1), sublanes(k, 0)),
        (sublanes(h, by - 1), sublanes(h, by - 2), sublanes(k, by - 1)),
        (to_lanes(h[:, :, 0:1]), to_lanes(h[:, :, 1:2]), to_lanes(k[:, :, 0:1])),
        (to_lanes(h[:, :, bz - 1 : bz]), to_lanes(h[:, :, bz - 2 : bz - 1]), to_lanes(k[:, :, bz - 1 : bz])),
    ]


def column_of(row):
    square = (row.shape[1], row.shape[1])
    return jnp.sum(jnp.where(iota(square, 0) == iota(square, 1), row, 0.0), axis=1, keepdims=True)


def table_sizes(count, plane_cap):
    records = (count - 1) * plane_cap
    faces = min(FACES, 128 // records)
    return records, faces, 1 + -(-FACES // faces)


def swap_order(count):
    return sorted(range(1, count), key=lambda s: (-s.bit_length(), s))


def place_of(table, slot):
    return table[0, FACES * SLOTS + slot], table[0, FACES * SLOTS + SLOTS + slot]


def write_tables(plane_cap, source, block, neighbour, asked, farther, table):
    here = lax.axis_index("gx")
    me = here.astype(F32)
    count = lax.axis_size("gx")
    records, faces, _ = table_sizes(count, plane_cap)
    cap = float(plane_cap)

    def wrapped(shift):
        return jnp.where(shift < 0.0, shift + float(count), shift)

    square = (SLOTS, SLOTS)
    before = iota(square, 0) < iota(square, 1)
    slot = iota((1, SLOTS), 1).astype(F32)
    source_row, block_column = source[...].astype(F32), column_of(block[...].astype(F32))
    source_column = column_of(source_row)
    rank = jnp.sum(
        jnp.where((source_column == source_row) & before, 1.0, 0.0), axis=0, keepdims=True
    )
    rank_column = column_of(rank)
    lane = iota((SLOTS, 128), 1).astype(F32)
    for shift in range(count):
        hit = (wrapped(source_column - me) == float(shift)) & (rank_column == lane)
        row = jnp.sum(jnp.where(hit, block_column, 0.0), axis=0, keepdims=True)
        asked[shift : shift + 1, :] = row
        if 2 <= shift < count - 1:
            farther[shift - 2][...] = jnp.broadcast_to(row, (8, 128))
    at = FACES * SLOTS
    table[0:1, at : at + SLOTS] = wrapped(me - source_row).astype(jnp.int32)
    table[0:1, at + SLOTS : at + 2 * SLOTS] = rank.astype(jnp.int32)
    slot_column = iota((SLOTS, records), 0).astype(F32)
    for face in range(FACES):
        number = neighbour[face]
        owner_row, number_row = (number >> 4).astype(F32), number.astype(F32)
        owner_column, number_column = column_of(owner_row), column_of(number_row)
        other_row = (number_row >= 0.0) & (owner_row != me)
        alike = (owner_column == owner_row) & (owner_column >= 0.0) & (owner_column != me)
        receive_rank = jnp.sum(
            jnp.where(alike & (number_column < number_row), 1.0, 0.0), axis=0, keepdims=True
        )
        send_rank = jnp.sum(jnp.where(alike & before, 1.0, 0.0), axis=0, keepdims=True)
        swap = jnp.where(number < 0, 0, (number >> 4) ^ here)
        position = jnp.zeros(swap.shape, F32)
        for at, other in enumerate(swap_order(count)):
            position = jnp.where(swap == other, float(at), position)
        mine = records + (number_row - owner_row * SLOTS)
        there = position * cap + receive_rank
        receive = jnp.where(owner_row == me, mine, there)
        receive = jnp.where(number_row < 0.0, records + SLOTS + slot, receive)
        table[0:1, face * SLOTS : face * SLOTS + SLOTS] = receive.astype(jnp.int32)
        key = jnp.where(other_row, position * cap + send_rank, -1.0)
        hit = iota((SLOTS, records), 1).astype(F32) == column_of(key)
        tile = jnp.sum(jnp.where(hit, slot_column, 0.0), axis=0, keepdims=True)
        row, at = 1 + (face ^ 1) // faces, (face ^ 1) % faces * records
        table[row : row + 1, at : at + records] = tile.astype(jnp.int32)


def sides_kernel(
    sizes, plane_cap, source_far, block_far, neighbour_far, h_far, k_far, send, table, *rest
):
    asked, *farther, source, block, neighbour, h, k, sems = rest
    ny, nz = sizes
    my_y, my_z = lax.axis_index("gy"), lax.axis_index("gz")
    bx = h.shape[0]
    small = [(source_far, source), (block_far, block), (neighbour_far, neighbour)]
    copies = [pltpu.make_async_copy(*pair, sems.at[2 * bx + n]) for n, pair in enumerate(small)]
    large = []
    for x in range(bx):
        large.append(pltpu.make_async_copy(h_far.at[x], h.at[x], sems.at[x]))
        large.append(pltpu.make_async_copy(k_far.at[x], k.at[x], sems.at[bx + x]))
    for copy in copies + large:
        copy.start()
    for copy in copies:
        copy.wait()
    write_tables(plane_cap, source, block, neighbour, asked, farther, table)
    for copy in large:
        copy.wait()
    blocks = side_blocks(h[...], k[...])
    for y in range(ny):
        for z in range(nz):
            for part in range(3):
                ylo, yhi, zlo, zhi = [block[part] for block in blocks]
                chosen = jnp.where(
                    my_y == y, jnp.where(z < my_z, zlo, zhi), jnp.where(y < my_y, ylo, yhi)
                )
                send[y * nz + z, part * bx : part * bx + bx, :] = chosen


def side_reader(sizes, got, bx):
    ny, nz = sizes
    my_y, my_z = lax.axis_index("gy"), lax.axis_index("gz")

    def read(dy, dz, part=0):
        y, z = my_y + dy, my_z + dz
        inside = (y >= 0) & (y < ny) & (z >= 0) & (z < nz)
        at = jnp.where(inside, y * nz + z, 0)
        return jnp.where(inside, got[at, part * bx : part * bx + bx, :], 0.0)

    return read


def layers_kernel(sizes, h, k, got, asked, *rest):
    down, up = rest[-2:]
    bx, by, bz = h.shape
    read = side_reader(sizes, got, bx)
    around = [read(-1, 0), read(1, 0), read(0, -1), read(0, 1)]
    last = asked.shape[0] - 1
    for out, near, far, ask in ((down, 0, 1, last), (up, bx - 1, bx - 2, 1)):
        out[0:by, :] = h[near]
        out[by : 2 * by, :] = h[far]
        out[2 * by : 3 * by, :] = k[near]
        for number, side in enumerate(around):
            out[3 * by + number : 3 * by + number + 1, :] = side[near : near + 1, :]
        out[3 * by + 4 : 3 * by + 8, :] = jnp.broadcast_to(asked[ask : ask + 1, :], (4, bz))


def block_layout(cap):
    parts = 128 // CB // cap
    return parts, CB // parts


def flat_step(h, k, inner, outer, first, last, before, after, length):
    bx, lanes = h.shape
    t = temperature(h)
    row, lane = iota(h.shape, 0), iota(h.shape, 1)
    total = temperature(inner) + temperature(outer)
    total += jnp.where(row == 0, temperature(first), pltpu.roll(t, 1, 0))
    total += jnp.where(row == bx - 1, temperature(last), pltpu.roll(t, bx - 1, 0))
    total += jnp.where(lane == 0, temperature(before), pltpu.roll(t, 1, 1))
    total += jnp.where(lane == length - 1, temperature(after), pltpu.roll(t, lanes - 1, 1))
    return h + RATE * k * (total - 6.0 * t)


def heat_kernel(cap, sizes, request, h, k, got, low, high, out, found, *rest):
    *send, held = rest
    count = lax.axis_size("gx")
    bx, by, bz = h.shape
    h0, k0 = h[...], k[...]
    read = side_reader(sizes, got, bx)
    me = lax.axis_index("gx")
    layers, lines = [], []
    for beside, inside in ((low, me > 0), (high, me < count - 1)):
        beside = jnp.where(inside, beside[...], 0.0)
        layers.append([beside[part * by : part * by + by, :][None] for part in range(3)])
        lines.append([beside[3 * by + n : 3 * by + n + 1, :] for n in range(4)])
    y_sides = [[read(d, 0, part) for part in range(3)] for d in (-1, 1)]
    z_sides = [[read(0, d, part) for part in range(3)] for d in (-1, 1)]
    corner = [[read(dy, dz) for dz in (-1, 1)] for dy in (-1, 1)]
    to_first = [[pltpu.roll(c[0], 1, 1), c[1]] for c in corner]
    y_inner = [sublanes(h0, 0), sublanes(h0, by - 1)]
    z_inner = [to_lanes(h0[:, :, 0:1]), to_lanes(h0[:, :, bz - 1 : bz])]

    sides = [temperature(layers[0][0]), temperature(layers[1][0])]
    sides += [temperature(side[0]) for side in y_sides + z_sides]
    h1 = conduct(h0, k0, *sides)
    next_sides = []
    for side in range(2):
        near, far, near_k = layers[side]
        across = [temperature(far), temperature(h0[0:1])]
        if side:
            across = [temperature(h0[bx - 1 : bx]), temperature(far)]
        next_sides.append(conduct(near, near_k, *across, *[temperature(line) for line in lines[side]]))
    for side in range(2):
        near, far, near_k = y_sides[side]
        ends = [to_first[side][0], pltpu.roll(to_first[side][1], bz - 1, 1)]
        next_sides.append(
            flat_step(near, near_k, y_inner[side], far, lines[0][side], lines[1][side], *ends, bz)
        )
    for side in range(2):
        near, far, near_k = z_sides[side]
        ends = [to_first[0][side], pltpu.roll(to_first[1][side], by - 1, 1)]
        next_sides.append(
            flat_step(near, near_k, z_inner[side], far, lines[0][2 + side], lines[1][2 + side], *ends, by)
        )
    h2 = conduct(h1, k0, *[temperature(side) for side in next_sides])
    out[...] = h2

    held[...] = temperature(h2).reshape(bx, by // CB, CB, bz)
    parts, deep = block_layout(cap)
    nby, nbz = by // CB, bz // CB
    group = iota((deep, CB, bz), 2) // CB
    for shift in range(count):
        total = jnp.zeros((deep, CB, bz), F32)
        for rank in range(cap):
            block = request[(count - shift) % count, rank]
            a, b, c = block // (nby * nbz), (block // nbz) % nby, block % nbz
            for part in range(parts):
                at = rank * parts + part
                patch = held[pl.ds(a * CB + part * deep, deep), b]
                moved = pltpu.roll(patch, (CB * at - CB * c + bz) % bz, 2)
                total = jnp.where(group == at, moved, total)
        total = total.reshape(deep * CB, bz)
        (send[shift - 1] if shift else found)[...] = total


def write_records(phase, solute, picks, own, own_edges, rows):
    flat = [f.reshape(SLOTS * TE, PLANE) for f in (phase, solute)]
    high, low = halves(jnp.concatenate(flat, axis=1))
    planes = dot(high, picks) + dot(low, picks)
    own[0:SLOTS] = planes[:, 0:128].reshape(SLOTS, TE, 128)
    own[SLOTS : 2 * SLOTS] = planes[:, 128:256].reshape(SLOTS, TE, 128)
    for part in range(4):
        rows[part] = flat[part // 2][:, part % 2 * 128 : part % 2 * 128 + 128]
    for part in range(4):
        low_face = rows[part, pl.ds(0, SLOTS, TE), :]
        high_face = rows[part, pl.ds(TE - 1, SLOTS, TE), :]
        for at, value in ((0, high_face), (4, low_face)):
            own_edges[pl.ds(at + part, SLOTS, 8), :] = value
            own_edges[pl.ds(8 * SLOTS + 4 - at + part, SLOTS, 8), :] = value


def merge_record(planes, edges, number):
    side = (iota((TE, 128), 1) % 64) // TE
    out = planes[number(2)]
    for face in range(3, 6):
        out = jnp.where(side == face - 2, planes[number(face)], out)
    first, second = [edges[pl.ds(pl.multiple_of(number(face) * 8, 8), 8), :] for face in range(2)]
    return out, jnp.where(iota((8, 128), 0) < 4, first, second)


def pack(own, own_edges, table, send):
    cap = send[0].shape[0] // REC
    records, faces, _ = table_sizes(len(send) + 1, cap)
    for record in range(records):
        out, row = send[record // cap], record % cap * REC
        planes, edge = merge_record(
            own, own_edges, lambda face: table[1 + face // faces, face % faces * records + record]
        )
        out[row : row + TE, :] = planes
        out[row + TE : row + REC, :] = edge


def first_pack_kernel(table, asked, phase, solute, picks, own, own_edges, asked_out, *rest):
    *send, rows = rest
    write_records(phase[...], solute[...], picks[...], own, own_edges, rows)
    pack(own, own_edges, table, send)
    asked_out[...] = asked[...]


def take_heat(cap, table, found, spreads, blocks, held, heat):
    parts, deep = block_layout(cap)
    for number, value in enumerate(found):
        blocks[number] = value[...]
    group = iota((CB, 128), 1) // CB
    for slot in range(SLOTS):
        back, rank = place_of(table, slot)
        for x in range(CB):
            row = (x % deep) * CB
            patch = blocks[back, row : row + CB, :]
            held[slot * CB + x] = jnp.where(group == rank * parts + x // deep, patch, 0.0)
    rows = held[...].reshape(SLOTS * CB * CB, 128)
    wide = dot(jnp.concatenate(halves(rows), axis=1), spreads)
    wide = wide.reshape(SLOTS * CB, CB, PLANE)
    keep = iota(wide.shape, 1) == iota(wide.shape, 2) // TE // 2
    coarse = jnp.sum(jnp.where(keep, wide, 0.0), axis=1)
    for half in range(2):
        for odd in range(2):
            heat[half, pl.ds(odd, SLOTS * CB, 2), :] = coarse[:, half * 128 : half * 128 + 128]


def inner_step(phase, solute, heat, stencil):
    row = iota((SLOTS, TE, PLANE), 1)
    lap = []
    for field in (phase, solute):
        high, low = halves(field.reshape(SLOTS * TE, PLANE))
        total = (dot(high, stencil) + dot(low, stencil)).reshape(SLOTS, TE, PLANE) - 6.0 * field
        total += jnp.where(row == 0, 0.0, pltpu.roll(field, 1, 1))
        total += jnp.where(row == TE - 1, 0.0, pltpu.roll(field, TE - 1, 1))
        lap.append(total)
    squared = 1.0 - phase * phase
    drive = solute if heat is None else heat + solute
    change = ORDER_SPEED * (
        lap[0] + phase - phase * phase * phase - COUPLING * drive * squared * squared
    )
    return phase + change, solute + SOLUTE_RATE * lap[1] + REJECTION * change


def wide_heat(heat):
    return jnp.concatenate([heat[0], heat[1]], axis=1).reshape(SLOTS, TE, PLANE)


def gather_ghosts(table, got, own, own_edges, planes, edges, ghosts, ghost_edges):
    records = planes.shape[0] - 2 * SLOTS
    cap = records // len(got)
    for record in range(records):
        value, row = got[record // cap], record % cap * REC
        planes[record] = value[row : row + TE, :]
        edges[record * 8 : record * 8 + 8, :] = value[row + TE : row + REC, :]
    planes[records:] = own[...]
    edges[records * 8 :, :] = own_edges[...]
    for slot in range(SLOTS):
        out, edge = merge_record(planes, edges, lambda face: table[0, face * SLOTS + slot])
        ghosts[slot] = out
        ghost_edges[slot] = edge


def ghost_shares(ghosts, ghost_edges, places):
    beside = jnp.concatenate(halves(ghosts[...].reshape(SLOTS * TE, 128)), axis=1)
    beside = dot(beside, places)
    rows = iota((SLOTS, TE, PLANE), 1)
    shares = []
    for number in range(2):
        share = beside[:, number * PLANE : number * PLANE + PLANE].reshape(SLOTS, TE, PLANE)
        for face, at_row in ((0, 0), (1, TE - 1)):
            at = face * 4 + number * 2
            side = [ghost_edges[:, row : row + 1, :] for row in (at, at + 1)]
            side = jnp.concatenate(side, axis=2)
            share += jnp.where(rows == at_row, side, 0.0)
        shares.append(share)
    return shares


def add_shares(phase, solute, shares, heat_share=None):
    change = ORDER_SPEED * shares[0]
    if heat_share is not None:
        change += heat_share
    return phase + change, solute + SOLUTE_RATE * shares[1] + REJECTION * change


def inner_kernel(has_heat, phase, solute, stencil, *rest):
    phase_out, solute_out = rest[-2:]
    heat = wide_heat(rest[0]) if has_heat else None
    phase_out[...], solute_out[...] = inner_step(phase[...], solute[...], heat, stencil[...])


def first_step_kernel(cap, table, old_phase, phase, solute, own, own_edges, picks, places, spreads, *rest):
    others = lax.axis_size("gx") - 1
    found, got, rest = rest[: others + 1], rest[others + 1 : 2 * others + 1], rest[2 * others + 1 :]
    phase_out, solute_out, heat_out, own_out, edges_out, *rest = rest
    send, (*records, ghosts, ghost_edges, rows, blocks, held) = rest[:others], rest[others:]
    take_heat(cap, table, found, spreads[...], blocks, held, heat_out)
    gather_ghosts(table, got, own, own_edges, *records, ghosts, ghost_edges)
    squared = 1.0 - old_phase[...] * old_phase[...]
    heat_share = (-ORDER_SPEED * COUPLING) * wide_heat(heat_out) * squared * squared
    new_phase, new_solute = add_shares(
        phase[...], solute[...], ghost_shares(ghosts, ghost_edges, places[...]), heat_share
    )
    phase_out[...] = new_phase
    solute_out[...] = new_solute
    write_records(new_phase, new_solute, picks[...], own_out, edges_out, rows)
    pack(own_out, edges_out, table, send)


def write_out_kernel(value, out, sem):
    copy = pltpu.make_async_copy(value, out, sem)
    copy.start()
    copy.wait()


def middle_step_kernel(table, phase, solute, own, own_edges, picks, places, *rest):
    others = lax.axis_size("gx") - 1
    got, (phase_out, solute_out, own_out, edges_out, *rest) = rest[:others], rest[others:]
    send, (*records, ghosts, ghost_edges, rows) = rest[:others], rest[others:]
    gather_ghosts(table, got, own, own_edges, *records, ghosts, ghost_edges)
    new_phase, new_solute = add_shares(phase[...], solute[...], ghost_shares(ghosts, ghost_edges, places[...]))
    phase_out[...] = new_phase
    solute_out[...] = new_solute
    write_records(new_phase, new_solute, picks[...], own_out, edges_out, rows)
    pack(own_out, edges_out, table, send)


def last_step_kernel(table, phase, solute, own, own_edges, places, *rest):
    others = lax.axis_size("gx") - 1
    got, (phase_out, solute_out, *records, ghosts, ghost_edges, _) = rest[:others], rest[others:]
    gather_ghosts(table, got, own, own_edges, *records, ghosts, ghost_edges)
    phase_out[...], solute_out[...] = add_shares(
        phase[...], solute[...], ghost_shares(ghosts, ghost_edges, places[...])
    )


def call(kernel, in_specs, out_shapes, scratch=(), out_specs=None, mib=16):
    return pl.pallas_call(
        kernel,
        out_shape=out_shapes,
        in_specs=in_specs,
        out_specs=out_specs or jax.tree.map(lambda _: VMEM, out_shapes),
        scratch_shapes=list(scratch),
        compiler_params=pltpu.CompilerParams(vmem_limit_bytes=mib * 1024 * 1024),
    )


def shape(*dims):
    return jax.ShapeDtypeStruct(dims, F32)


def local(enthalpy, conductivity, phase, solute, tile_source, tile_block, tile_neighbour):
    count = lax.axis_size("gx")
    sizes = (lax.axis_size("gy"), lax.axis_size("gz"))
    plane_cap = -(-SLOTS // (count - 1))
    block_cap = 2 * SLOTS // count
    others = count - 1
    records = others * plane_cap
    bx, by, bz = enthalpy.shape
    picks, stencil, places, spreads = tables()

    integers = functools.partial(jax.ShapeDtypeStruct, dtype=jnp.int32)
    sides, table, asked, *farther = call(
        functools.partial(sides_kernel, sizes, plane_cap),
        [ANY] * 5,
        [
            shape(sizes[0] * sizes[1], 3 * bx, 128),
            integers((table_sizes(count, plane_cap)[2], 128)),
            shape(count, 128),
            *[shape(8, 128)] * (count - 3),
        ],
        [
            pltpu.VMEM((1, SLOTS), jnp.int32),
            pltpu.VMEM((1, SLOTS), jnp.int32),
            pltpu.VMEM((FACES, 1, SLOTS), jnp.int32),
            pltpu.VMEM((bx, by, bz), F32),
            pltpu.VMEM((bx, by, bz), F32),
            pltpu.SemaphoreType.DMA((2 * bx + 3,)),
        ],
        mib=56,
    )(
        tile_source.reshape(1, SLOTS),
        tile_block.reshape(1, SLOTS),
        jnp.transpose(tile_neighbour, (0, 1, 4, 2, 3)).reshape(FACES, 1, SLOTS),
        enthalpy,
        conductivity,
    )
    sides = lax.all_to_all(sides, ("gy", "gz"), split_axis=0, concat_axis=0, tiled=True)

    def pass_on(value, shift):
        return lax.ppermute(value, "gx", [(i, (i + shift) % count) for i in range(count)])

    def exchange(values):
        return [pass_on(value, shift) for shift, value in enumerate(values, 1)]

    def swap_all(values):
        return [
            lax.ppermute(value, "gx", [(i, i ^ swap) for i in range(count)])
            for swap, value in zip(swap_order(count), values)
        ]

    farther = [pass_on(value, shift) for shift, value in enumerate(farther, 2)]

    phase_field = phase.reshape(SLOTS, TE, PLANE)
    solute_field = solute.reshape(SLOTS, TE, PLANE)
    own_shapes = [shape(2 * SLOTS, TE, 128), shape(2 * SLOTS * 8, 128)]
    send_shapes = [shape(plane_cap * REC, 128)] * others
    rows_scratch = pltpu.VMEM((4, SLOTS * TE, 128), F32)
    packed = call(
        first_pack_kernel,
        [SMEM] + [VMEM] * 4,
        [*own_shapes, shape(count, 128), *send_shapes],
        [rows_scratch],
    )(table, asked, phase_field, solute_field, picks)
    own, asked, packed = packed[:2], packed[2], packed[3:]

    layer = shape(3 * by + 8, bz)
    down, up = call(
        functools.partial(layers_kernel, sizes), [VMEM] * 4, [layer, layer]
    )(enthalpy, conductivity, sides, asked)
    from_low, from_high = pass_on(up, 1), pass_on(down, others)
    row = 3 * by + 4
    request = [asked[0], from_low[row], *[value[0] for value in farther], from_high[row]]
    request = jnp.stack([value[:block_cap] for value in request]).astype(jnp.int32)
    _, deep = block_layout(block_cap)
    brick = shape(bx, by, bz)
    got = swap_all(packed)
    heated, *found = call(
        functools.partial(heat_kernel, block_cap, sizes),
        [SMEM] + [VMEM] * 5,
        [brick] + [shape(deep * CB, 128)] * count,
        [pltpu.VMEM((bx, by // CB, CB, bz), F32)],
    )(request, enthalpy, conductivity, sides, from_low, from_high)
    found[1:] = exchange(found[1:])
    (heat_out,) = call(write_out_kernel, [ANY], [brick], [pltpu.SemaphoreType.DMA], [ANY])(heated)

    field = shape(SLOTS, TE, PLANE)
    step_scratch = [
        pltpu.VMEM((records + 2 * SLOTS, TE, 128), F32),
        pltpu.VMEM(((records + 2 * SLOTS) * 8, 128), F32),
        pltpu.VMEM((SLOTS, TE, 128), F32),
        pltpu.VMEM((SLOTS, 8, 128), F32),
        rows_scratch,
    ]
    def inner(phase_field, solute_field, *heat):
        return call(
            functools.partial(inner_kernel, bool(heat)), [VMEM] * (3 + len(heat)), [field, field]
        )(phase_field, solute_field, stencil, *heat)

    inner_fields = inner(phase_field, solute_field)
    phase_field, solute_field, heat, *rest = call(
        functools.partial(first_step_kernel, block_cap),
        [SMEM] + [VMEM] * (8 + count + others),
        [field, field, shape(2, SLOTS * TE, 128), *own_shapes, *send_shapes],
        step_scratch
        + [
            pltpu.VMEM((count, deep * CB, 128), F32),
            pltpu.VMEM((SLOTS * CB, CB, 128), F32),
        ],
    )(table, phase_field, *inner_fields, *own, picks, places, spreads, *found, *got)
    own, send = rest[:2], rest[2:]
    for _ in range(PHASE_STEPS - 2):
        got = swap_all(send)
        inner_fields = inner(phase_field, solute_field, heat)
        phase_field, solute_field, *rest = call(
            middle_step_kernel,
            [SMEM] + [VMEM] * (6 + others),
            [field, field, *own_shapes, *send_shapes],
            step_scratch,
        )(table, *inner_fields, *own, picks, places, *got)
        own, send = rest[:2], rest[2:]
    got = swap_all(send)
    inner_fields = inner(phase_field, solute_field, heat)
    phase_field, solute_field = call(
        last_step_kernel, [SMEM] + [VMEM] * (5 + others), [field, field], step_scratch
    )(table, *inner_fields, *own, places, *got)
    return heat_out, phase_field.reshape(phase.shape), solute_field.reshape(solute.shape)


def solution(mesh):
    grid = P("gx", "gy", "gz")
    tiles = P("gx", "gy", "gz", None, None, None)
    return jax.shard_map(
        local,
        mesh=mesh,
        in_specs=(
            grid,
            grid,
            tiles,
            tiles,
            P("gx", "gy", "gz", None, None),
            P("gx", "gy", "gz", None),
            P("gx", "gy", "gz", None, None),
        ),
        out_specs=(grid, tiles, tiles),
        check_vma=False,
    )
```

```python
import functools

import jax
import jax.numpy as jnp
import numpy as np
from jax import lax
from jax.experimental import pallas as pl
from jax.experimental.pallas import tpu as pltpu
from jax.sharding import PartitionSpec as P

CB = 8
TE = 16
PLANE = TE * TE
SLOTS = 16
FACES = 6
PHASE_STEPS = 4
REC = 24

RATE = 0.16
ORDER_SPEED = 0.1
SOLUTE_RATE = 0.15
COUPLING = 0.5
REJECTION = 0.5

F32 = jnp.float32
BF16 = jnp.bfloat16
VMEM = pl.BlockSpec(memory_space=pltpu.VMEM)
SMEM = pl.BlockSpec(memory_space=pltpu.SMEM)
ANY = pl.BlockSpec(memory_space=pl.ANY)


def plane_lane(face):
    j = np.arange(TE)
    return [j, PLANE - TE + j, j * TE, j * TE + TE - 1][face - 2]


def constant_tables():
    pick = np.zeros((2, PLANE, 256), np.float32)
    place = np.zeros((2, 128, PLANE), np.float32)
    for field in range(2):
        for face in range(2, 6):
            at = field * 64 + (face - 2) * TE + np.arange(TE)
            pick[field, plane_lane(face ^ 1), at] = 1.0
            pick[field, plane_lane(face), 128 + at] = 1.0
            place[field, at, plane_lane(face)] = 1.0
    y, z = np.divmod(np.arange(PLANE), TE)
    dy, dz = np.abs(y[:, None] - y[None, :]), np.abs(z[:, None] - z[None, :])
    stencil = ((dy + dz) == 1).astype(np.float32)
    lane = np.arange(128)
    spread = (lane[:, None] % CB == z[None, :] // 2).astype(np.float32)
    return pick, place, stencil, spread


def tables():
    pick, place, stencil, spread = constant_tables()
    place = np.concatenate([place[0], place[1]], axis=1)
    return (
        jnp.asarray(np.concatenate([pick[0], pick[1]], axis=0), BF16),
        jnp.asarray(stencil, BF16),
        jnp.asarray(np.concatenate([place, place], axis=0), BF16),
        jnp.asarray(np.concatenate([spread, spread], axis=0), BF16),
    )


def halves(value):
    high = value.astype(BF16)
    return high, (value - high.astype(F32)).astype(BF16)


def dot(a, b):
    return jnp.dot(a, b, preferred_element_type=F32)


def temperature(h):
    return jnp.minimum(h, 0.0) + jnp.maximum(h - 1.0, 0.0)


def iota(shape, dim):
    return lax.broadcasted_iota(jnp.int32, shape, dim)


def to_lanes(column):
    bx, by, _ = column.shape
    diagonal = iota((bx, by, 128), 1) == iota((bx, by, 128), 2)
    return jnp.sum(jnp.where(diagonal, column, 0.0), axis=1)


def to_column(line, by):
    bx = line.shape[0]
    diagonal = iota((bx, by, 128), 1) == iota((bx, by, 128), 2)
    return jnp.sum(jnp.where(diagonal, line[:, None, :], 0.0), axis=2, keepdims=True)


def conduct(h, k, xlo, xhi, ylo, yhi, zlo, zhi):
    bx, by, bz = h.shape
    t = temperature(h)
    row, lane = iota((bx, by, bz), 1), iota((bx, by, bz), 2)
    if bx > 1:
        total = jnp.concatenate([xlo, t[:-1]], axis=0) + jnp.concatenate([t[1:], xhi], axis=0)
    else:
        total = xlo + xhi
    total += jnp.where(row == 0, ylo[:, None, :], pltpu.roll(t, 1, 1))
    total += jnp.where(row == by - 1, yhi[:, None, :], pltpu.roll(t, by - 1, 1))
    total += jnp.where(lane == 0, to_column(zlo, by), pltpu.roll(t, 1, 2))
    total += jnp.where(lane == bz - 1, to_column(zhi, by), pltpu.roll(t, bz - 1, 2))
    return h + RATE * k * (total - 6.0 * t)


def sublanes(value, y):
    return jnp.concatenate([value[x, y : y + 1, :] for x in range(value.shape[0])], axis=0)


def side_blocks(h, k):
    by, bz = h.shape[1:]
    return [
        (sublanes(h, 0), sublanes(h, 1), sublanes(k, 0)),
        (sublanes(h, by - 1), sublanes(h, by - 2), sublanes(k, by - 1)),
        (to_lanes(h[:, :, 0:1]), to_lanes(h[:, :, 1:2]), to_lanes(k[:, :, 0:1])),
        (to_lanes(h[:, :, bz - 1 : bz]), to_lanes(h[:, :, bz - 2 : bz - 1]), to_lanes(k[:, :, bz - 1 : bz])),
    ]


def column_of(row):
    square = (row.shape[1], row.shape[1])
    return jnp.sum(jnp.where(iota(square, 0) == iota(square, 1), row, 0.0), axis=1, keepdims=True)


def table_sizes(count, plane_cap):
    records = (count - 1) * plane_cap
    faces = min(FACES, 128 // records)
    return records, faces, 1 + -(-FACES // faces)


def swap_order(count):
    return sorted(range(1, count), key=lambda s: (-s.bit_length(), s))


def place_of(table, slot):
    return table[0, FACES * SLOTS + slot], table[0, FACES * SLOTS + SLOTS + slot]


def write_tables(plane_cap, source, block, neighbour, asked, farther, table):
    here = lax.axis_index("gx")
    me = here.astype(F32)
    count = lax.axis_size("gx")
    records, faces, _ = table_sizes(count, plane_cap)
    cap = float(plane_cap)

    def position_of(swap):
        position = jnp.zeros(swap.shape, F32)
        for at, other in enumerate(swap_order(count)):
            position = jnp.where(swap == other, float(at), position)
        return position

    def wrapped(shift):
        return jnp.where(shift < 0.0, shift + float(count), shift)

    square = (SLOTS, SLOTS)
    before = iota(square, 0) < iota(square, 1)
    slot = iota((1, SLOTS), 1).astype(F32)
    source_row, block_column = source[...].astype(F32), column_of(block[...].astype(F32))
    source_column = column_of(source_row)
    rank = jnp.sum(
        jnp.where((source_column == source_row) & before, 1.0, 0.0), axis=0, keepdims=True
    )
    rank_column = column_of(rank)
    lane = iota((SLOTS, 128), 1).astype(F32)
    for shift in range(count):
        hit = (wrapped(source_column - me) == float(shift)) & (rank_column == lane)
        row = jnp.sum(jnp.where(hit, block_column, 0.0), axis=0, keepdims=True)
        asked[shift : shift + 1, :] = row
        if 2 <= shift < count - 1:
            farther[shift - 2][...] = jnp.broadcast_to(row, (8, 128))
    at = FACES * SLOTS
    swap = source[...] ^ here
    found = jnp.where(swap == 0, 0.0, 1.0 + position_of(swap))
    table[0:1, at : at + SLOTS] = found.astype(jnp.int32)
    table[0:1, at + SLOTS : at + 2 * SLOTS] = rank.astype(jnp.int32)
    slot_column = iota((SLOTS, records), 0).astype(F32)
    for face in range(FACES):
        number = neighbour[face]
        owner_row, number_row = (number >> 4).astype(F32), number.astype(F32)
        owner_column, number_column = column_of(owner_row), column_of(number_row)
        other_row = (number_row >= 0.0) & (owner_row != me)
        alike = (owner_column == owner_row) & (owner_column >= 0.0) & (owner_column != me)
        receive_rank = jnp.sum(
            jnp.where(alike & (number_column < number_row), 1.0, 0.0), axis=0, keepdims=True
        )
        send_rank = jnp.sum(jnp.where(alike & before, 1.0, 0.0), axis=0, keepdims=True)
        position = position_of(jnp.where(number < 0, 0, (number >> 4) ^ here))
        mine = records + (number_row - owner_row * SLOTS)
        there = position * cap + receive_rank
        receive = jnp.where(owner_row == me, mine, there)
        receive = jnp.where(number_row < 0.0, records + SLOTS + slot, receive)
        table[0:1, face * SLOTS : face * SLOTS + SLOTS] = receive.astype(jnp.int32)
        key = jnp.where(other_row, position * cap + send_rank, -1.0)
        hit = iota((SLOTS, records), 1).astype(F32) == column_of(key)
        tile = jnp.sum(jnp.where(hit, slot_column, 0.0), axis=0, keepdims=True)
        row, at = 1 + (face ^ 1) // faces, (face ^ 1) % faces * records
        table[row : row + 1, at : at + records] = tile.astype(jnp.int32)


def sides_kernel(
    sizes, plane_cap, source_far, block_far, neighbour_far, h_far, k_far, send, table, *rest
):
    asked, *farther, source, block, neighbour, h, k, sems = rest
    ny, nz = sizes
    my_y, my_z = lax.axis_index("gy"), lax.axis_index("gz")
    bx = h.shape[0]
    small = [(source_far, source), (block_far, block), (neighbour_far, neighbour)]
    copies = [pltpu.make_async_copy(*pair, sems.at[2 * bx + n]) for n, pair in enumerate(small)]
    large = []
    for x in range(bx):
        large.append(pltpu.make_async_copy(h_far.at[x], h.at[x], sems.at[x]))
        large.append(pltpu.make_async_copy(k_far.at[x], k.at[x], sems.at[bx + x]))
    for copy in copies + large:
        copy.start()
    for copy in copies:
        copy.wait()
    write_tables(plane_cap, source, block, neighbour, asked, farther, table)
    for copy in large:
        copy.wait()
    blocks = side_blocks(h[...], k[...])
    for y in range(ny):
        for z in range(nz):
            for part in range(3):
                ylo, yhi, zlo, zhi = [block[part] for block in blocks]
                chosen = jnp.where(
                    my_y == y, jnp.where(z < my_z, zlo, zhi), jnp.where(y < my_y, ylo, yhi)
                )
                send[y * nz + z, part * bx : part * bx + bx, :] = chosen


def side_reader(sizes, got, bx):
    ny, nz = sizes
    my_y, my_z = lax.axis_index("gy"), lax.axis_index("gz")

    def read(dy, dz, part=0):
        y, z = my_y + dy, my_z + dz
        inside = (y >= 0) & (y < ny) & (z >= 0) & (z < nz)
        at = jnp.where(inside, y * nz + z, 0)
        return jnp.where(inside, got[at, part * bx : part * bx + bx, :], 0.0)

    return read


def layers_kernel(sizes, h, k, got, asked, *rest):
    down, up = rest[-2:]
    bx, by, bz = h.shape
    read = side_reader(sizes, got, bx)
    around = [read(-1, 0), read(1, 0), read(0, -1), read(0, 1)]
    last = asked.shape[0] - 1
    for out, near, far, ask in ((down, 0, 1, last), (up, bx - 1, bx - 2, 1)):
        out[0:by, :] = h[near]
        out[by : 2 * by, :] = h[far]
        out[2 * by : 3 * by, :] = k[near]
        for number, side in enumerate(around):
            out[3 * by + number : 3 * by + number + 1, :] = side[near : near + 1, :]
        out[3 * by + 4 : 3 * by + 8, :] = jnp.broadcast_to(asked[ask : ask + 1, :], (4, bz))


def block_layout(cap):
    parts = 128 // CB // cap
    return parts, CB // parts


def flat_step(h, k, inner, outer, first, last, before, after, length):
    bx, lanes = h.shape
    t = temperature(h)
    row, lane = iota(h.shape, 0), iota(h.shape, 1)
    total = temperature(inner) + temperature(outer)
    total += jnp.where(row == 0, temperature(first), pltpu.roll(t, 1, 0))
    total += jnp.where(row == bx - 1, temperature(last), pltpu.roll(t, bx - 1, 0))
    total += jnp.where(lane == 0, temperature(before), pltpu.roll(t, 1, 1))
    total += jnp.where(lane == length - 1, temperature(after), pltpu.roll(t, lanes - 1, 1))
    return h + RATE * k * (total - 6.0 * t)


def heat_kernel(cap, sizes, request, h, k, got, low, high, out, found, *rest):
    *send, held = rest
    count = lax.axis_size("gx")
    bx, by, bz = h.shape
    h0, k0 = h[...], k[...]
    read = side_reader(sizes, got, bx)
    me = lax.axis_index("gx")
    layers, lines = [], []
    for beside, inside in ((low, me > 0), (high, me < count - 1)):
        beside = jnp.where(inside, beside[...], 0.0)
        layers.append([beside[part * by : part * by + by, :][None] for part in range(3)])
        lines.append([beside[3 * by + n : 3 * by + n + 1, :] for n in range(4)])
    y_sides = [[read(d, 0, part) for part in range(3)] for d in (-1, 1)]
    z_sides = [[read(0, d, part) for part in range(3)] for d in (-1, 1)]
    corner = [[read(dy, dz) for dz in (-1, 1)] for dy in (-1, 1)]
    to_first = [[pltpu.roll(c[0], 1, 1), c[1]] for c in corner]
    y_inner = [sublanes(h0, 0), sublanes(h0, by - 1)]
    z_inner = [to_lanes(h0[:, :, 0:1]), to_lanes(h0[:, :, bz - 1 : bz])]

    sides = [temperature(layers[0][0]), temperature(layers[1][0])]
    sides += [temperature(side[0]) for side in y_sides + z_sides]
    h1 = conduct(h0, k0, *sides)
    next_sides = []
    for side in range(2):
        near, far, near_k = layers[side]
        across = [temperature(far), temperature(h0[0:1])]
        if side:
            across = [temperature(h0[bx - 1 : bx]), temperature(far)]
        next_sides.append(conduct(near, near_k, *across, *[temperature(line) for line in lines[side]]))
    for side in range(2):
        near, far, near_k = y_sides[side]
        ends = [to_first[side][0], pltpu.roll(to_first[side][1], bz - 1, 1)]
        next_sides.append(
            flat_step(near, near_k, y_inner[side], far, lines[0][side], lines[1][side], *ends, bz)
        )
    for side in range(2):
        near, far, near_k = z_sides[side]
        ends = [to_first[0][side], pltpu.roll(to_first[1][side], by - 1, 1)]
        next_sides.append(
            flat_step(near, near_k, z_inner[side], far, lines[0][2 + side], lines[1][2 + side], *ends, by)
        )
    h2 = conduct(h1, k0, *[temperature(side) for side in next_sides])
    out[...] = h2

    held[...] = temperature(h2).reshape(bx, by // CB, CB, bz)
    parts, deep = block_layout(cap)
    nby, nbz = by // CB, bz // CB
    group = iota((deep, CB, bz), 2) // CB
    for out, swap in zip((found, *send), (0, *swap_order(count))):
        back = lax.rem(me - (me ^ swap) + count, count)
        total = jnp.zeros((deep, CB, bz), F32)
        for rank in range(cap):
            block = request[back, rank]
            a, b, c = block // (nby * nbz), (block // nbz) % nby, block % nbz
            for part in range(parts):
                at = rank * parts + part
                patch = held[pl.ds(a * CB + part * deep, deep), b]
                moved = pltpu.roll(patch, (CB * at - CB * c + bz) % bz, 2)
                total = jnp.where(group == at, moved, total)
        out[...] = total.reshape(deep * CB, bz)


def write_records(phase, solute, picks, own, own_edges, rows):
    flat = [f.reshape(SLOTS * TE, PLANE) for f in (phase, solute)]
    high, low = halves(jnp.concatenate(flat, axis=1))
    planes = dot(high, picks) + dot(low, picks)
    own[0:SLOTS] = planes[:, 0:128].reshape(SLOTS, TE, 128)
    own[SLOTS : 2 * SLOTS] = planes[:, 128:256].reshape(SLOTS, TE, 128)
    for part in range(4):
        rows[part] = flat[part // 2][:, part % 2 * 128 : part % 2 * 128 + 128]
    for part in range(4):
        low_face = rows[part, pl.ds(0, SLOTS, TE), :]
        high_face = rows[part, pl.ds(TE - 1, SLOTS, TE), :]
        for at, value in ((0, high_face), (4, low_face)):
            own_edges[pl.ds(at + part, SLOTS, 8), :] = value
            own_edges[pl.ds(8 * SLOTS + 4 - at + part, SLOTS, 8), :] = value


def merge_record(planes, edges, number):
    side = (iota((TE, 128), 1) % 64) // TE
    out = planes[number(2)]
    for face in range(3, 6):
        out = jnp.where(side == face - 2, planes[number(face)], out)
    first, second = [edges[pl.ds(pl.multiple_of(number(face) * 8, 8), 8), :] for face in range(2)]
    return out, jnp.where(iota((8, 128), 0) < 4, first, second)


def pack(own, own_edges, table, send):
    cap = send[0].shape[0] // REC
    records, faces, _ = table_sizes(len(send) + 1, cap)
    for record in range(records):
        out, row = send[record // cap], record % cap * REC
        planes, edge = merge_record(
            own, own_edges, lambda face: table[1 + face // faces, face % faces * records + record]
        )
        out[row : row + TE, :] = planes
        out[row + TE : row + REC, :] = edge


def first_pack_kernel(table, asked, phase, solute, picks, own, own_edges, asked_out, *rest):
    *send, rows = rest
    write_records(phase[...], solute[...], picks[...], own, own_edges, rows)
    pack(own, own_edges, table, send)
    asked_out[...] = asked[...]


def take_heat(cap, table, found, spreads, blocks, held, heat):
    parts, deep = block_layout(cap)
    for number, value in enumerate(found):
        blocks[number] = value[...]
    group = iota((CB, 128), 1) // CB
    for slot in range(SLOTS):
        back, rank = place_of(table, slot)
        for x in range(CB):
            row = (x % deep) * CB
            patch = blocks[back, row : row + CB, :]
            held[slot * CB + x] = jnp.where(group == rank * parts + x // deep, patch, 0.0)
    rows = held[...].reshape(SLOTS * CB * CB, 128)
    wide = dot(jnp.concatenate(halves(rows), axis=1), spreads)
    wide = wide.reshape(SLOTS * CB, CB, PLANE)
    keep = iota(wide.shape, 1) == iota(wide.shape, 2) // TE // 2
    coarse = jnp.sum(jnp.where(keep, wide, 0.0), axis=1)
    for half in range(2):
        for odd in range(2):
            heat[half, pl.ds(odd, SLOTS * CB, 2), :] = coarse[:, half * 128 : half * 128 + 128]


def inner_step(phase, solute, heat, stencil):
    row = iota((SLOTS, TE, PLANE), 1)
    lap = []
    for field in (phase, solute):
        high, low = halves(field.reshape(SLOTS * TE, PLANE))
        total = (dot(high, stencil) + dot(low, stencil)).reshape(SLOTS, TE, PLANE) - 6.0 * field
        total += jnp.where(row == 0, 0.0, pltpu.roll(field, 1, 1))
        total += jnp.where(row == TE - 1, 0.0, pltpu.roll(field, TE - 1, 1))
        lap.append(total)
    squared = 1.0 - phase * phase
    drive = solute if heat is None else heat + solute
    change = ORDER_SPEED * (
        lap[0] + phase - phase * phase * phase - COUPLING * drive * squared * squared
    )
    return phase + change, solute + SOLUTE_RATE * lap[1] + REJECTION * change


def wide_heat(heat):
    return jnp.concatenate([heat[0], heat[1]], axis=1).reshape(SLOTS, TE, PLANE)


def gather_ghosts(table, got, own, own_edges, planes, edges, ghosts, ghost_edges):
    records = planes.shape[0] - 2 * SLOTS
    cap = records // len(got)
    for record in range(records):
        value, row = got[record // cap], record % cap * REC
        planes[record] = value[row : row + TE, :]
        edges[record * 8 : record * 8 + 8, :] = value[row + TE : row + REC, :]
    planes[records:] = own[...]
    edges[records * 8 :, :] = own_edges[...]
    for slot in range(SLOTS):
        out, edge = merge_record(planes, edges, lambda face: table[0, face * SLOTS + slot])
        ghosts[slot] = out
        ghost_edges[slot] = edge


def ghost_shares(ghosts, ghost_edges, places):
    beside = jnp.concatenate(halves(ghosts[...].reshape(SLOTS * TE, 128)), axis=1)
    beside = dot(beside, places)
    half = TE // 2
    rows = iota((SLOTS, half, PLANE), 1)
    shares = []
    for number in range(2):
        share = beside[:, number * PLANE : number * PLANE + PLANE].reshape(SLOTS, TE, PLANE)
        parts = []
        for face, at_row in ((0, 0), (1, half - 1)):
            at = face * 4 + number * 2
            side = [ghost_edges[:, row : row + 1, :] for row in (at, at + 1)]
            side = jnp.where(rows == at_row, jnp.concatenate(side, axis=2), 0.0)
            parts.append(share[:, face * half : face * half + half] + side)
        shares.append(jnp.concatenate(parts, axis=1))
    return shares


def add_shares(phase, solute, shares, heat_share=None):
    change = ORDER_SPEED * shares[0]
    if heat_share is not None:
        change += heat_share
    return phase + change, solute + SOLUTE_RATE * shares[1] + REJECTION * change


def inner_kernel(has_heat, phase, solute, stencil, *rest):
    phase_out, solute_out = rest[-2:]
    heat = wide_heat(rest[0]) if has_heat else None
    phase_out[...], solute_out[...] = inner_step(phase[...], solute[...], heat, stencil[...])


def first_step_kernel(cap, table, old_phase, phase, solute, own, own_edges, picks, places, spreads, *rest):
    others = lax.axis_size("gx") - 1
    found, got, rest = rest[: others + 1], rest[others + 1 : 2 * others + 1], rest[2 * others + 1 :]
    phase_out, solute_out, heat_out, own_out, edges_out, *rest = rest
    send, (*records, ghosts, ghost_edges, rows, blocks, held) = rest[:others], rest[others:]
    take_heat(cap, table, found, spreads[...], blocks, held, heat_out)
    gather_ghosts(table, got, own, own_edges, *records, ghosts, ghost_edges)
    squared = 1.0 - old_phase[...] * old_phase[...]
    heat_share = (-ORDER_SPEED * COUPLING) * wide_heat(heat_out) * squared * squared
    new_phase, new_solute = add_shares(
        phase[...], solute[...], ghost_shares(ghosts, ghost_edges, places[...]), heat_share
    )
    phase_out[...] = new_phase
    solute_out[...] = new_solute
    write_records(new_phase, new_solute, picks[...], own_out, edges_out, rows)
    pack(own_out, edges_out, table, send)


def write_out_kernel(value, out, sem):
    copy = pltpu.make_async_copy(value, out, sem)
    copy.start()
    copy.wait()


def middle_step_kernel(table, phase, solute, own, own_edges, picks, places, *rest):
    others = lax.axis_size("gx") - 1
    got, (phase_out, solute_out, own_out, edges_out, *rest) = rest[:others], rest[others:]
    send, (*records, ghosts, ghost_edges, rows) = rest[:others], rest[others:]
    gather_ghosts(table, got, own, own_edges, *records, ghosts, ghost_edges)
    new_phase, new_solute = add_shares(phase[...], solute[...], ghost_shares(ghosts, ghost_edges, places[...]))
    phase_out[...] = new_phase
    solute_out[...] = new_solute
    write_records(new_phase, new_solute, picks[...], own_out, edges_out, rows)
    pack(own_out, edges_out, table, send)


def last_step_kernel(table, phase, solute, own, own_edges, places, *rest):
    others = lax.axis_size("gx") - 1
    got, (phase_out, solute_out, *records, ghosts, ghost_edges, _) = rest[:others], rest[others:]
    gather_ghosts(table, got, own, own_edges, *records, ghosts, ghost_edges)
    phase_out[...], solute_out[...] = add_shares(
        phase[...], solute[...], ghost_shares(ghosts, ghost_edges, places[...])
    )


def call(kernel, in_specs, out_shapes, scratch=(), out_specs=None, mib=16):
    return pl.pallas_call(
        kernel,
        out_shape=out_shapes,
        in_specs=in_specs,
        out_specs=out_specs or jax.tree.map(lambda _: VMEM, out_shapes),
        scratch_shapes=list(scratch),
        compiler_params=pltpu.CompilerParams(vmem_limit_bytes=mib * 1024 * 1024),
    )


def shape(*dims):
    return jax.ShapeDtypeStruct(dims, F32)


def local(enthalpy, conductivity, phase, solute, tile_source, tile_block, tile_neighbour):
    count = lax.axis_size("gx")
    sizes = (lax.axis_size("gy"), lax.axis_size("gz"))
    plane_cap = -(-SLOTS // (count - 1))
    block_cap = 2 * SLOTS // count
    others = count - 1
    records = others * plane_cap
    bx, by, bz = enthalpy.shape
    picks, stencil, places, spreads = tables()

    integers = functools.partial(jax.ShapeDtypeStruct, dtype=jnp.int32)
    sides, table, asked, *farther = call(
        functools.partial(sides_kernel, sizes, plane_cap),
        [ANY] * 5,
        [
            shape(sizes[0] * sizes[1], 3 * bx, 128),
            integers((table_sizes(count, plane_cap)[2], 128)),
            shape(count, 128),
            *[shape(8, 128)] * (count - 3),
        ],
        [
            pltpu.VMEM((1, SLOTS), jnp.int32),
            pltpu.VMEM((1, SLOTS), jnp.int32),
            pltpu.VMEM((FACES, 1, SLOTS), jnp.int32),
            pltpu.VMEM((bx, by, bz), F32),
            pltpu.VMEM((bx, by, bz), F32),
            pltpu.SemaphoreType.DMA((2 * bx + 3,)),
        ],
        mib=56,
    )(
        tile_source.reshape(1, SLOTS),
        tile_block.reshape(1, SLOTS),
        jnp.transpose(tile_neighbour, (0, 1, 4, 2, 3)).reshape(FACES, 1, SLOTS),
        enthalpy,
        conductivity,
    )
    sides = lax.all_to_all(sides, ("gy", "gz"), split_axis=0, concat_axis=0, tiled=True)

    def pass_on(value, shift):
        return lax.ppermute(value, "gx", [(i, (i + shift) % count) for i in range(count)])

    def swap_all(values):
        return [
            lax.ppermute(value, "gx", [(i, i ^ swap) for i in range(count)])
            for swap, value in zip(swap_order(count), values)
        ]

    farther = [pass_on(value, shift) for shift, value in enumerate(farther, 2)]

    phase_field = phase.reshape(SLOTS, TE, PLANE)
    solute_field = solute.reshape(SLOTS, TE, PLANE)
    own_shapes = [shape(2 * SLOTS, TE, 128), shape(2 * SLOTS * 8, 128)]
    send_shapes = [shape(plane_cap * REC, 128)] * others
    rows_scratch = pltpu.VMEM((4, SLOTS * TE, 128), F32)
    packed = call(
        first_pack_kernel,
        [SMEM] + [VMEM] * 4,
        [*own_shapes, shape(count, 128), *send_shapes],
        [rows_scratch],
    )(table, asked, phase_field, solute_field, picks)
    own, asked, packed = packed[:2], packed[2], packed[3:]

    layer = shape(3 * by + 8, bz)
    down, up = call(
        functools.partial(layers_kernel, sizes), [VMEM] * 4 + [ANY] * len(farther), [layer, layer]
    )(enthalpy, conductivity, sides, asked, *farther)
    from_low, from_high = pass_on(up, 1), pass_on(down, others)
    row = 3 * by + 4
    request = [asked[0], from_low[row], *[value[0] for value in farther], from_high[row]]
    request = jnp.stack([value[:block_cap] for value in request]).astype(jnp.int32)
    _, deep = block_layout(block_cap)
    brick = shape(bx, by, bz)
    got = swap_all(packed)
    heated, *found = call(
        functools.partial(heat_kernel, block_cap, sizes),
        [SMEM] + [VMEM] * 5,
        [brick] + [shape(deep * CB, 128)] * count,
        [pltpu.VMEM((bx, by // CB, CB, bz), F32)],
    )(request, enthalpy, conductivity, sides, from_low, from_high)
    found[1:] = swap_all(found[1:])
    (heat_out,) = call(write_out_kernel, [ANY], [brick], [pltpu.SemaphoreType.DMA], [ANY])(heated)

    field = shape(SLOTS, TE, PLANE)
    step_scratch = [
        pltpu.VMEM((records + 2 * SLOTS, TE, 128), F32),
        pltpu.VMEM(((records + 2 * SLOTS) * 8, 128), F32),
        pltpu.VMEM((SLOTS, TE, 128), F32),
        pltpu.VMEM((SLOTS, 8, 128), F32),
        rows_scratch,
    ]
    def inner(phase_field, solute_field, *heat):
        return call(
            functools.partial(inner_kernel, bool(heat)), [VMEM] * (3 + len(heat)), [field, field]
        )(phase_field, solute_field, stencil, *heat)

    inner_fields = inner(phase_field, solute_field)
    phase_field, solute_field, heat, *rest = call(
        functools.partial(first_step_kernel, block_cap),
        [SMEM] + [VMEM] * (8 + count + others),
        [field, field, shape(2, SLOTS * TE, 128), *own_shapes, *send_shapes],
        step_scratch
        + [
            pltpu.VMEM((count, deep * CB, 128), F32),
            pltpu.VMEM((SLOTS * CB, CB, 128), F32),
        ],
    )(table, phase_field, *inner_fields, *own, picks, places, spreads, *found, *got)
    own, send = rest[:2], rest[2:]
    for _ in range(PHASE_STEPS - 2):
        got = swap_all(send)
        inner_fields = inner(phase_field, solute_field, heat)
        phase_field, solute_field, *rest = call(
            middle_step_kernel,
            [SMEM] + [VMEM] * (6 + others),
            [field, field, *own_shapes, *send_shapes],
            step_scratch,
        )(table, *inner_fields, *own, picks, places, *got)
        own, send = rest[:2], rest[2:]
    got = swap_all(send)
    inner_fields = inner(phase_field, solute_field, heat)
    phase_field, solute_field = call(
        last_step_kernel, [SMEM] + [VMEM] * (5 + others), [field, field], step_scratch
    )(table, *inner_fields, *own, places, *got)
    return heat_out, phase_field.reshape(phase.shape), solute_field.reshape(solute.shape)


def solution(mesh):
    grid = P("gx", "gy", "gz")
    tiles = P("gx", "gy", "gz", None, None, None)
    return jax.shard_map(
        local,
        mesh=mesh,
        in_specs=(
            grid,
            grid,
            tiles,
            tiles,
            P("gx", "gy", "gz", None, None),
            P("gx", "gy", "gz", None),
            P("gx", "gy", "gz", None, None),
        ),
        out_specs=(grid, tiles, tiles),
        check_vma=False,
    )
```
